32 devices in a mesh: slab: 16 (over z, y, core), chan: 2 (over x).
Axes of the slice: x: 2, y: 2, z: 4, core: 2. Of those that a mesh axis runs over, the one named last changes fastest.
Arguments:
- field: bfloat16 [32, 64, 48, 128], P('chan', 'slab'), may hold values from -6 to 6
- out_grad: bfloat16 [32, 64, 48, 128], P(None, 'slab'), may hold values from -6 to 6
- first_weight: bfloat16 [32, 27, 32], P('chan'), may hold values from -0.21875 to 0.21875
- second_weight: bfloat16 [32, 27, 32], P('chan'), may hold values from -0.21875 to 0.21875
Outputs:
- input_grad: bfloat16 [32, 64, 48, 128], P('chan', 'slab')
- first_grad: float32 [32, 27, 32], P('chan')
- second_grad: float32 [32, 27, 32], P('chan')
The draws below stay inside these ranges and needn't reach their ends.
All inputs are finite; a program needn't handle non-finite values.
Results may differ from the reference program's by a relative error of at most 0.014.
Values may be sent and summed in bfloat16 or wider, within the bound.
No kernel may reach another device: no remote copies, remote signals or barrier semaphores. Data moves between devices by JAX's collectives and lax.ppermute only.
A program may use at most 320 MiB of HBM per device.

```python
import math
import jax
import jax.numpy as jnp
from jax import lax

C = 32
NY = 48
NZ = 128
NX = 64
N_CHAN = 2


def steps_of(own_key, extent, cuts, low, high):
    def one(position, blocks):
        steps = jax.random.uniform(jax.random.fold_in(jax.random.fold_in(own_key, 6), position), (blocks,), jnp.float32, low / len(cuts), high / len(cuts))
        return jnp.repeat(jnp.exp(steps), extent[position] // blocks).reshape((-1,) + (1,) * (len(extent) - position - 1))

    loudness = one(*cuts[0])
    for cut in cuts[1:]:
        loudness = loudness * one(*cut)
    return loudness


def normal_values(own_key, shape, deviation, limit, cuts=(), dtype=jnp.bfloat16):
    values = jax.random.normal(own_key, shape, jnp.float32) * deviation
    if len(cuts) > 0:
        values = steps_of(own_key, shape, cuts, -0.22, 0.18) * values
    return jnp.clip(values, min=-limit, max=limit).astype(dtype)


def setup_inputs(seed: int = 0) -> dict:
    seeds = jax.random.split(jax.random.key(seed), 5)
    return {
        "field": normal_values(seeds[0], (C, NX, NY, NZ), 1.0, 6.0, ((0, 2), (1, 16))),
        "out_grad": normal_values(seeds[1], (C, NX, NY, NZ), 1.0, 6.0, ((1, 16),)),
        "first_weight": normal_values(seeds[2], (C, 27, C), (27 * C) ** -0.5, 0.21875, ((0, 2),)),
        "second_weight": normal_values(seeds[3], (C, 27, C), (27 * C) ** -0.5, 0.21875, ((0, 2),)),
    }


def tap_stack(padded, first, planes):
    base = padded[:, first:first + planes]
    return jnp.stack([jnp.roll(base, (1 - b, 1 - e), axis=(2, 3)) for b in range(3) for e in range(3)])

def forward_sum(padded, weight):
    planes = padded.shape[1] - 2
    total = jnp.zeros((weight.shape[2], planes) + padded.shape[2:], jnp.float32)
    for a in range(3):
        stack = tap_stack(padded, a, planes).astype(jnp.float32)
        kernel = weight[:, 9 * a:9 * a + 9, :].astype(jnp.float32)
        total = total + jnp.einsum('jixyz,ijo->oxyz', stack, kernel)
    return total

def weight_sum(padded, delta):
    planes = padded.shape[1] - 2
    parts = []
    for a in range(3):
        stack = tap_stack(padded, a, planes).astype(jnp.float32)
        parts.append(jnp.einsum('jixyz,oxyz->ijo', stack, delta.astype(jnp.float32)))
    return jnp.concatenate(parts, axis=1)

def spread_back(padded_delta, weight):
    planes = padded_delta.shape[1] - 2
    total = jnp.zeros((weight.shape[0], planes) + padded_delta.shape[2:], jnp.float32)
    for a in range(3):
        base = padded_delta[:, 2 - a:2 - a + planes].astype(jnp.float32)
        kernel = weight[:, 9 * a:9 * a + 9, :].astype(jnp.float32)
        lifted = jnp.einsum('ijo,oxyz->jixyz', kernel, base)
        for j in range(9):
            b, e = (j // 3, j % 3)
            total = total + jnp.roll(lifted[j], (b - 1, e - 1), axis=(2, 3))
    return total

def wrap_pad(values):
    return jnp.concatenate([values[:, -1:], values, values[:, :1]], axis=1)

def silu_slope(values):
    sig = jax.nn.sigmoid(values)
    return sig * (1.0 + values * (1.0 - sig))

def grouped_sum(padded, weight):
    group = C // N_CHAN
    total = jnp.zeros((C, NX, NY, NZ), jnp.float32)
    for g in range(N_CHAN):
        low = g * group
        part = forward_sum(padded[low:low + group], weight[low:low + group]).astype(jnp.bfloat16)
        total = total + lax.optimization_barrier(part).astype(jnp.float32)
    return total

def reference(field, out_grad, first_weight, second_weight):
    group = C // N_CHAN
    field_pad = wrap_pad(field)
    first_sum = grouped_sum(field_pad, first_weight)
    hidden = jax.nn.silu(first_sum).astype(jnp.bfloat16)
    hidden_pad = wrap_pad(hidden)
    second_sum = grouped_sum(hidden_pad, second_weight)
    second_delta = (out_grad.astype(jnp.float32) * silu_slope(second_sum)).astype(jnp.bfloat16)
    delta_pad = wrap_pad(second_delta)
    second_raw = jnp.concatenate([weight_sum(hidden_pad[g * group:(g + 1) * group], second_delta) for g in range(N_CHAN)], axis=0)
    hidden_back = jnp.concatenate([spread_back(delta_pad, second_weight[g * group:(g + 1) * group]) for g in range(N_CHAN)], axis=0)
    first_delta = (hidden_back * silu_slope(first_sum)).astype(jnp.bfloat16)
    first_pad = wrap_pad(first_delta)
    first_raw = jnp.concatenate([weight_sum(field_pad[g * group:(g + 1) * group], first_delta) for g in range(N_CHAN)], axis=0)
    input_grad = jnp.concatenate([spread_back(first_pad, first_weight[g * group:(g + 1) * group]) for g in range(N_CHAN)], axis=0).astype(jnp.bfloat16)
    factor = 1.0 / math.sqrt(NX * NY * NZ)
    return (input_grad, first_raw * factor, second_raw * factor)
```

```python
import functools
import math

import jax
import jax.numpy as jnp
from jax import lax
from jax.experimental import pallas as pl
from jax.experimental.pallas import tpu as pltpu
from jax.sharding import PartitionSpec as P

F32 = jnp.float32
BF16 = jnp.bfloat16
LIMIT = 48 * 1024 * 1024


def call(kernel, outs, args, scratch=(), flops=0, moved=0):
    whole = pl.BlockSpec(memory_space=pltpu.VMEM)
    return pl.pallas_call(
        kernel,
        out_shape=outs,
        in_specs=[whole] * len(args),
        out_specs=[whole] * len(outs),
        scratch_shapes=list(scratch),
        compiler_params=pltpu.CompilerParams(vmem_limit_bytes=LIMIT),
        cost_estimate=pl.CostEstimate(flops=flops, bytes_accessed=moved, transcendentals=0),
    )(*args)


def turn_kernel(extent, shifts, share, margin, x_ref, *refs):
    count, planes, rows = x_ref.shape[0], x_ref.shape[1], x_ref.shape[2]
    outs, wide = refs[:-1], refs[-1]
    pairs = planes // 2

    def widen(i, _):
        for x in range(planes):
            start = pl.multiple_of((i * planes + x) * rows, 8)
            wide[pl.ds(start, rows), :] = x_ref[i, x].astype(F32)
        return 0

    lax.fori_loop(0, count, widen, 0)
    me = lax.axis_index("chan")
    for s, shift in enumerate(shifts):
        base = lax.rem(me + shift, extent) * share - margin + rows

        def turn(f, _, base=base, s=s):
            y = lax.rem(base + f, rows)
            for x in range(planes):
                tile = wide[pl.ds(x * rows + y, count, stride=planes * rows), :]
                outs[s * pairs + x // 2][f, x % 2] = tile.astype(BF16)
            return 0

        lax.fori_loop(0, share + 2 * margin, turn, 0)


def turned(x, extent, shifts, margin):
    count, planes, rows, depth = x.shape
    share = rows // extent
    piece = jax.ShapeDtypeStruct((share + 2 * margin, 2, count, depth), BF16)
    return call(
        functools.partial(turn_kernel, extent, shifts, share, margin),
        [piece] * (len(shifts) * planes // 2),
        [x],
        [pltpu.VMEM((count * planes * rows, depth), F32)],
        moved=x.size * 4,
    )


def columns(refs, row):
    sides = []
    for q in range(2):
        parts = []
        for ref in refs:
            part = ref[pl.ds(row + q, 3)]
            parts.append(part.reshape(6 * part.shape[2], part.shape[3]))
        sides.append(jnp.concatenate(parts, axis=0) if len(parts) > 1 else parts[0])
    return jnp.concatenate(sides, axis=1)


def taps(weight, refs, row):
    lifted = jnp.dot(weight, columns(refs, row), preferred_element_type=F32)
    third = lifted.shape[0] // 3
    depth = lifted.shape[1] // 2
    sums = []
    for q in range(2):
        side = lifted[:, q * depth : (q + 1) * depth]
        sums.append(
            side[third : 2 * third]
            + pltpu.roll(side[:third], 1, 1)
            + pltpu.roll(side[2 * third :], depth - 1, 1)
        )
    return sums


def silu_parts(v):
    sig = jax.nn.sigmoid(v)
    return sig, sig * (1.0 + v * (1.0 - sig))


def forward_kernel(groups, pairs, *refs):
    refs = list(refs)
    fields = [[refs.pop(0) for _ in range(groups)] for _ in range(pairs + 2)]
    grads = [refs.pop(0) for _ in range(pairs)]
    first, second = refs.pop(0), refs.pop(0)
    hiddens = [refs.pop(0) for _ in range(pairs + 1)]
    slopes = [refs.pop(0) for _ in range(pairs + 1)]
    deltas = [refs.pop(0) for _ in range(pairs)]

    def one(r, _):
        row = 2 * r
        for p in range(pairs + 1):
            for q, v in enumerate(taps(first[...], fields[p] + fields[p + 1], row)):
                sig, slope = silu_parts(v)
                shape = hiddens[p].shape[1:]
                hiddens[p][row + q] = (v * sig).astype(BF16).reshape(shape)
                slopes[p][row + q] = slope.astype(BF16).reshape(shape)
        return 0

    lax.fori_loop(0, hiddens[0].shape[0] // 2, one, 0)

    def two(r, _):
        row = 2 * r
        for p in range(pairs):
            for q, v in enumerate(taps(second[...], hiddens[p : p + 2], row)):
                shape = deltas[p].shape[1:]
                out_grad = grads[p][row + q].astype(F32)
                slope = silu_parts(v)[1].reshape(shape)
                deltas[p][row + q] = (out_grad * slope).astype(BF16)
        return 0

    lax.fori_loop(0, deltas[0].shape[0] // 2, two, 0)


def planes_of(pairs):
    return [(refs, x) for refs in pairs for x in range(2)]


def weight_loop(total, pieces, first_row, deltas, delta_row, count):
    total[...] = jnp.zeros_like(total)

    def step(r, _):
        left, right = [], []
        for x, ((delta,), place) in enumerate(deltas):
            rows = []
            for refs, side in pieces[x : x + 3]:
                for ref in refs:
                    part = ref[pl.ds(first_row + 2 * r, 4), side]
                    rows.append(part.reshape(4 * part.shape[1], part.shape[2]))
            left.append(jnp.concatenate(rows, axis=0))
            rows = []
            for q in range(2):
                wide = delta[delta_row + 2 * r + q, place]
                plain = wide.astype(F32)
                depth = plain.shape[1]
                rows += [
                    pltpu.roll(plain, depth - 1, 1).astype(BF16),
                    wide,
                    pltpu.roll(plain, 1, 1).astype(BF16),
                    jnp.zeros_like(wide),
                ]
            right.append(jnp.concatenate(rows, axis=0))
        total[...] += lax.dot_general(
            jnp.concatenate(left, axis=1),
            jnp.concatenate(right, axis=1),
            (((1,), (1,)), ((), ())),
            preferred_element_type=F32,
        )
        return 0

    lax.fori_loop(0, count // 2, step, 0)


def weight_fold(total, raw, groups):
    size = raw.shape[2]
    lanes = raw.shape[3]
    for a in range(3):
        for j in range(groups):
            for b in range(3):
                start = ((a * groups + j) * 4 + b) * size
                raw[j, 3 * a + b] = (
                    total[start : start + size, :lanes]
                    + total[start + size : start + 2 * size, lanes:]
                )


def second_kernel(share, pairs, *refs):
    refs = list(refs)
    hiddens = [[refs.pop(0)] for _ in range(pairs + 1)]
    deltas = [refs.pop(0) for _ in range(pairs)]
    raw, total = refs
    weight_loop(total, planes_of(hiddens), 2, planes_of([[d] for d in deltas]), 2, share)
    weight_fold(total, raw, 1)


def back_kernel(share, groups, pairs, *refs):
    refs = list(refs)
    deltas = [refs.pop(0) for _ in range(pairs + 2)]
    slopes = [refs.pop(0) for _ in range(pairs + 1)]
    fields = [[refs.pop(0) for _ in range(groups)] for _ in range(pairs + 2)]
    weight = refs.pop(0)
    firsts = [refs.pop(0) for _ in range(pairs + 1)]
    raw, total = refs

    def one(r, _):
        row = 2 * r
        for p in range(pairs + 1):
            for q, v in enumerate(taps(weight[...], deltas[p : p + 2], row)):
                shape = firsts[p].shape[1:]
                slope = slopes[p][row + 2 + q].astype(F32)
                firsts[p][row + q] = (v.reshape(shape) * slope).astype(BF16)
        return 0

    lax.fori_loop(0, firsts[0].shape[0] // 2, one, 0)
    near = planes_of(fields)[1:-1]
    own = planes_of([[first] for first in firsts])[1:-1]
    weight_loop(total, near, 3, own, 1, share)
    weight_fold(total, raw, groups)


def last_kernel(pairs, *refs):
    refs = list(refs)
    firsts = [refs.pop(0) for _ in range(pairs + 1)]
    weight = refs.pop(0)
    outs = refs

    def one(r, _):
        row = 2 * r
        for p in range(pairs):
            for q, v in enumerate(taps(weight[...], firsts[p : p + 2], row)):
                size = outs[0].shape[2]
                channels = len(outs) * size
                for x in range(2):
                    for j, out in enumerate(outs):
                        low = x * channels + j * size
                        out[row + q, 2 * p + x] = v[low : low + size].astype(BF16)
        return 0

    lax.fori_loop(0, outs[0].shape[0] // 2, one, 0)


def merge_kernel(extent, *refs):
    pieces, out, wide = refs[:-2], refs[-2], refs[-1]
    share, planes, size = pieces[0].shape[:3]
    rows = out.shape[2]
    me = lax.axis_index("chan")
    for j, piece in enumerate(pieces):
        base = lax.rem(me + extent - j, extent) * share

        def widen(f, _, piece=piece, base=base):
            for x in range(planes):
                start = ((base + f) * planes + x) * size
                start = pl.multiple_of(start, 8) if size % 8 == 0 else start
                wide[pl.ds(start, size), :] = piece[f, x].astype(F32)
            return 0

        lax.fori_loop(0, share, widen, 0)

    def turn(i, _):
        for x in range(planes):
            tile = wide[pl.ds(x * size + i, rows, stride=planes * size), :]
            out[i, x] = tile.astype(BF16)
        return 0

    lax.fori_loop(0, size, turn, 0)


def paired(weight):
    shifted = [jnp.pad(weight, ((0, 0), (x, 1 - x), (0, 0), (0, 0), (0, 0))) for x in range(2)]
    return jnp.transpose(jnp.stack(shifted), (4, 0, 5, 2, 3, 1))


def wide_columns(paired_weight, groups):
    e, x, out, four, b, count = paired_weight.shape
    split = paired_weight.reshape(e, x, out, 2, 2, b, groups, count // groups)
    return jnp.transpose(split, (0, 1, 2, 3, 6, 5, 4, 7)).reshape(e * x * out, four * b * count)


def slab_sum(values, axis):
    count = lax.axis_size(axis)
    if count & (count - 1) != 0:
        return lax.psum(values, axis)
    stride = 1
    while stride < count:
        radix = 4 if count % (4 * stride) == 0 else 2
        got = [values] + [
            lax.ppermute(values, axis, [(i, i ^ (m * stride)) for i in range(count)])
            for m in range(1, radix)
        ]
        values = got[0] + got[1]
        if radix == 4:
            values = values + (got[2] + got[3])
        stride *= radix
    return values


def body(field, out_grad, first_weight, second_weight):
    extent = lax.axis_size("chan")
    slabs = lax.axis_size("slab")
    me = lax.axis_index("chan")
    size, planes, rows, depth = field.shape
    channels = size * extent
    pairs = planes // 2
    share = rows // extent
    factor = 1.0 / math.sqrt(planes * slabs * rows * depth)

    def to_chan(value, shift):
        return lax.ppermute(value, "chan", [(i, (i + shift) % extent) for i in range(extent)])

    def to_next(value):
        return lax.ppermute(value, "slab", [(i, (i + 1) % slabs) for i in range(slabs)])

    def to_prev(value):
        return lax.ppermute(value, "slab", [((i + 1) % slabs, i) for i in range(slabs)])

    sent = turned(field, extent, list(range(extent)), 4)
    weights = jnp.stack([first_weight, second_weight])
    weight_parts = [weights] + [to_chan(weights, j) for j in range(1, extent)]
    parts = [sent[:pairs]]
    for j in range(1, extent):
        parts.append([to_chan(piece, j) for piece in sent[j * pairs : (j + 1) * pairs]])
    by_pair = [[parts[j][p] for j in range(extent)] for p in range(pairs)]
    groups = extent
    if size % 16 != 0:
        by_pair = [[jnp.concatenate(pieces, axis=2)] for pieces in by_pair]
        groups = 1
    before = [to_next(piece) for piece in by_pair[-1]]
    after = [to_prev(piece) for piece in by_pair[0]]
    fields = [before] + by_pair + [after]

    own_order = jnp.concatenate([part[0] for part in weight_parts], axis=0)
    second_all = jnp.zeros((channels,) + second_weight.shape[1:], BF16)
    for j, part in enumerate(weight_parts):
        place = lax.rem(me + extent - j, extent) * size
        second_all = lax.dynamic_update_slice(second_all, part[1], (place, 0, 0))
    first_five = own_order.reshape(channels, 3, 3, 3, channels)
    second_five = second_all.reshape(channels, 3, 3, 3, channels)

    def backward(five):
        return jnp.transpose(five[:, ::-1, ::-1, ::-1], (4, 1, 2, 3, 0))

    first_wide = wide_columns(paired(first_five), groups)
    second_wide = wide_columns(paired(second_five), 1)
    second_back = wide_columns(paired(backward(second_five)), 1)
    first_back = wide_columns(paired(backward(first_five)), 1)

    grads = turned(out_grad, extent, [0], 2)

    def many(count, rows_each, dtype=BF16):
        return [jax.ShapeDtypeStruct((rows_each, 2, channels, depth), dtype)] * count

    flat_fields = [piece for pieces in fields for piece in pieces]
    work = 2 * 27 * channels * channels * depth
    made = call(
        functools.partial(forward_kernel, groups, pairs),
        many(pairs + 1, share + 6) * 2 + many(pairs, share + 4),
        flat_fields + list(grads) + [first_wide, second_wide],
        flops=work * 2 * planes * share,
        moved=8 * planes * share * channels * depth,
    )
    hiddens = made[: pairs + 1]
    slopes = made[pairs + 1 : 2 * pairs + 2]
    deltas = made[2 * pairs + 2 :]
    all_deltas = [to_next(deltas[-1])] + list(deltas) + [to_prev(deltas[0])]

    def raw_shape(count):
        return jax.ShapeDtypeStruct((count, 9, channels // count, 4 * channels), F32)

    total = pltpu.VMEM((12 * channels, 8 * channels), F32)
    (second_raw,) = call(
        functools.partial(second_kernel, share, pairs),
        [raw_shape(1)],
        list(hiddens) + list(deltas),
        [total],
        flops=work * planes * share,
        moved=8 * planes * share * channels * depth,
    )
    made = call(
        functools.partial(back_kernel, share, groups, pairs),
        many(pairs + 1, share + 2) + [raw_shape(groups)],
        all_deltas + list(slopes) + flat_fields + [second_back],
        [total],
        flops=work * 2 * planes * share,
        moved=8 * planes * share * channels * depth,
    )
    firsts, first_raw = made[:-1], made[-1]

    first_groups = first_raw.reshape(groups, 9, channels // groups, 4 * channels)
    if groups != extent:
        first_groups = jnp.transpose(
            first_groups.reshape(9, extent, size, 4 * channels), (1, 0, 2, 3)
        )
    second_groups = second_raw.reshape(9, channels, 4 * channels)
    mine = None
    for j in range(extent):
        place = lax.rem(me + extent - j, extent) * size
        piece = jnp.stack(
            [
                first_groups[j],
                lax.dynamic_slice_in_dim(second_groups, place, size, axis=1),
            ]
        )[..., : 3 * channels]
        piece = piece if j == 0 else to_chan(piece, extent - j)
        mine = piece if mine is None else mine + piece
    both = slab_sum(mine, "slab") * factor
    both = both.reshape(2, 3, 3, size, 3, channels)
    both = jnp.transpose(both, (0, 3, 1, 2, 4, 5)).reshape(2, size, 27, channels)

    out_piece = jax.ShapeDtypeStruct((share, planes, size, depth), BF16)
    made = call(
        functools.partial(last_kernel, pairs),
        [out_piece] * extent,
        list(firsts) + [first_back],
        flops=work * planes * share,
        moved=4 * planes * share * channels * depth,
    )
    pieces = [made[0]] + [None] * (extent - 1)
    for j in range(1, extent):
        pieces[extent - j] = to_chan(made[j], extent - j)
    (input_grad,) = call(
        functools.partial(merge_kernel, extent),
        [jax.ShapeDtypeStruct(field.shape, BF16)],
        pieces,
        [pltpu.VMEM((rows * planes * size, depth), F32)],
        moved=4 * field.size,
    )
    return input_grad, both[0], both[1]


def solution(mesh):
    placed = (
        P("chan", "slab", None, None),
        P(None, "slab", None, None),
        P("chan", None, None),
        P("chan", None, None),
    )
    return jax.shard_map(
        body,
        mesh=mesh,
        in_specs=placed,
        out_specs=(P("chan", "slab", None, None), P("chan", None, None), P("chan", None, None)),
        check_vma=False,
    )
```

```python
import functools
import math

import jax
import jax.numpy as jnp
from jax import lax
from jax.experimental import pallas as pl
from jax.experimental.pallas import tpu as pltpu
from jax.sharding import PartitionSpec as P

F32 = jnp.float32
BF16 = jnp.bfloat16
LIMIT = 16 * 1024 * 1024


def call(kernel, outs, args, scratch=(), flops=0, moved=0):
    whole = pl.BlockSpec(memory_space=pltpu.VMEM)
    return pl.pallas_call(
        kernel,
        out_shape=outs,
        in_specs=[whole] * len(args),
        out_specs=[whole] * len(outs),
        scratch_shapes=list(scratch),
        compiler_params=pltpu.CompilerParams(vmem_limit_bytes=LIMIT),
        cost_estimate=pl.CostEstimate(flops=flops, bytes_accessed=moved, transcendentals=0),
    )(*args)


def widened(x_ref, wide):
    count, planes, rows = x_ref.shape[:3]

    def widen(i, _):
        for x in range(planes):
            start = pl.multiple_of((i * planes + x) * rows, 8)
            wide[pl.ds(start, rows), :] = x_ref[i, x].astype(F32)
        return 0

    lax.fori_loop(0, count, widen, 0)


def turn(wide, outs, shape, base, length):
    count, planes, rows = shape

    def one(f, _):
        y = lax.rem(base + f, rows)
        for x in range(planes):
            tile = wide[pl.ds(x * rows + y, count, stride=planes * rows), :]
            outs[x // 2][f, x % 2] = tile.astype(BF16)
        return 0

    lax.fori_loop(0, length, one, 0)


def field_kernel(extent, margin, x_ref, first, second, *refs):
    outs, packed, wide = refs[:-2], refs[-2], refs[-1]
    count, planes, rows = x_ref.shape[:3]
    pairs = planes // 2
    share = rows // extent
    widened(x_ref, wide)
    me = lax.axis_index("chan")
    for s in range(extent):
        base = lax.rem(me + s, extent) * share - margin + rows
        turn(
            wide,
            outs[s * pairs : (s + 1) * pairs],
            (count, planes, rows),
            base,
            share + 2 * margin,
        )
    blank = jnp.zeros(first.shape[1:], F32)
    for h in range(packed.shape[0]):
        parts = []
        for ref in (first, second):
            for t in (2 * h, 2 * h + 1):
                parts.append(ref[t].astype(F32) if t < ref.shape[0] else blank)
        packed[h] = jnp.concatenate(parts, axis=1).astype(BF16)


def grad_kernel(extent, margin, x_ref, *refs):
    outs, wide = refs[:-1], refs[-1]
    count, planes, rows = x_ref.shape[:3]
    share = rows // extent
    widened(x_ref, wide)
    base = lax.axis_index("chan") * share - margin + rows
    turn(wide, outs, (count, planes, rows), base, share + 2 * margin)


def matrix_kernel(extent, *refs):
    packs, outs = refs[:extent], refs[extent:]
    me = lax.axis_index("chan")
    halves = packs[0].shape[0]
    quarter = packs[0].shape[2] // 4
    taps = []
    turned = []
    for h in range(halves):
        tiles = [pack[h].astype(F32) for pack in packs]
        own = jnp.concatenate(tiles, axis=0)
        fixed = []
        for g in range(extent):
            place = lax.rem(me + extent - g, extent)
            tile = tiles[0]
            for j in range(1, extent):
                tile = jnp.where(place == j, tiles[j], tile)
            fixed.append(tile)
        both = jnp.concatenate(
            [own[:, : 2 * quarter], jnp.concatenate(fixed, axis=0)[:, 2 * quarter :]], axis=1
        )
        across = both.T
        for side in range(2):
            taps.append(
                [both[:, k * quarter : (k + 1) * quarter] for k in (side, side + 2)]
            )
            turned.append(
                [across[k * quarter : (k + 1) * quarter] for k in (side, side + 2)]
            )
    channels = quarter
    blank = jnp.zeros((channels, channels), F32)
    for k in range(2):
        for out, blocks, flip in ((outs[k], turned, False), (outs[2 + k], taps, True)):
            for e in range(3):
                for x in range(2):
                    chunks = []
                    for pair in range(2):
                        for b in range(3):
                            for side in range(2):
                                a = 2 * pair + side - x
                                t = 9 * a + 3 * b + e
                                inside = 0 <= a <= 2
                                t = 26 - t if flip else t
                                chunks.append(blocks[t][k] if inside else blank)
                    low = (2 * e + x) * channels
                    out[low : low + channels, :] = jnp.concatenate(chunks, axis=1).astype(BF16)


def stacked(refs, row, count):
    if len(refs) == 1:
        part = refs[0][pl.ds(row, count)]
        return part.reshape(-1, part.shape[-1])
    parts = [ref[row + b, x] for b in range(count) for x in range(2) for ref in refs]
    return jnp.concatenate(parts, axis=0)


def taps(weight, pairs, row):
    sides = []
    for p in range(len(pairs) - 1):
        for q in range(2):
            above = stacked(pairs[p], row + q, 3)
            below = stacked(pairs[p + 1], row + q, 3)
            sides.append(jnp.concatenate([above, below], axis=0))
    lifted = jnp.dot(weight, jnp.concatenate(sides, axis=1), preferred_element_type=F32)
    third = lifted.shape[0] // 3
    depth = sides[0].shape[1]
    sums = []
    for k in range(len(sides)):
        side = lifted[:, k * depth : (k + 1) * depth]
        sums.append(
            side[third : 2 * third]
            + pltpu.roll(side[:third], 1, 1)
            + pltpu.roll(side[2 * third :], depth - 1, 1)
        )
    return [sums[2 * p : 2 * p + 2] for p in range(len(pairs) - 1)]


def silu_parts(v):
    sig = jax.nn.sigmoid(v)
    return sig, sig * (1.0 + v * (1.0 - sig))


def forward_kernel(groups, pairs, *refs):
    refs = list(refs)
    fields = [[refs.pop(0) for _ in range(groups)] for _ in range(pairs + 2)]
    grads = [refs.pop(0) for _ in range(pairs)]
    first, second = refs.pop(0), refs.pop(0)
    hiddens = [refs.pop(0) for _ in range(pairs + 1)]
    slopes = [refs.pop(0) for _ in range(pairs + 1)]
    deltas = [refs.pop(0) for _ in range(pairs)]

    def one(r, _):
        row = 2 * r
        for p, sums in enumerate(taps(first[...], fields, row)):
            for q, v in enumerate(sums):
                sig, slope = silu_parts(v)
                shape = hiddens[p].shape[1:]
                hiddens[p][row + q] = (v * sig).astype(BF16).reshape(shape)
                slopes[p][row + q] = slope.astype(BF16).reshape(shape)
        return 0

    lax.fori_loop(0, hiddens[0].shape[0] // 2, one, 0)

    def two(r, _):
        row = 2 * r
        for p, sums in enumerate(taps(second[...], [[ref] for ref in hiddens], row)):
            for q, v in enumerate(sums):
                shape = deltas[p].shape[1:]
                out_grad = grads[p][row + q].astype(F32)
                slope = silu_parts(v)[1].reshape(shape)
                deltas[p][row + q] = (out_grad * slope).astype(BF16)
        return 0

    lax.fori_loop(0, deltas[0].shape[0] // 2, two, 0)


def planes_of(pairs):
    return [(refs, x) for refs in pairs for x in range(2)]


def weight_loop(total, pieces, first_row, deltas, delta_row, count):
    total[...] = jnp.zeros_like(total)

    def step(r, _):
        left, right = [], []
        for x, ((delta,), place) in enumerate(deltas):
            rows = []
            for q in range(2):
                wide = delta[delta_row + 2 * r + q, place]
                plain = wide.astype(F32)
                depth = plain.shape[1]
                rows += [
                    pltpu.roll(plain, depth - 1, 1).astype(BF16),
                    wide,
                    pltpu.roll(plain, 1, 1).astype(BF16),
                ]
            left.append(jnp.concatenate(rows, axis=0))
            rows = []
            for refs, side in pieces[x : x + 3]:
                for b in range(4):
                    for ref in refs:
                        rows.append(ref[first_row + 2 * r + b, side])
            right.append(jnp.concatenate(rows, axis=0))
        total[...] += lax.dot_general(
            jnp.concatenate(left, axis=1),
            jnp.concatenate(right, axis=1),
            (((1,), (1,)), ((), ())),
            preferred_element_type=F32,
        )
        return 0

    lax.fori_loop(0, count // 2, step, 0)


def weight_fold(total, size):
    lanes = total.shape[0] // 2
    channels = total.shape[1] // 12
    upper, lower = total[:lanes, :].T, total[lanes:, :].T
    parts = []
    for g in range(channels // size):
        taps_of = []
        for a in range(3):
            for b in range(3):
                start = (4 * a + b) * channels + g * size
                taps_of.append(
                    upper[start : start + size]
                    + lower[start + channels : start + channels + size]
                )
        parts.append(taps_of)
    return parts


def second_kernel(share, pairs, *refs):
    refs = list(refs)
    hiddens = [[refs.pop(0)] for _ in range(pairs + 1)]
    deltas = [refs.pop(0) for _ in range(pairs)]
    raw, total = refs
    weight_loop(total, planes_of(hiddens), 2, planes_of([[d] for d in deltas]), 2, share)
    for g, taps_of in enumerate(weight_fold(total, raw.shape[2])):
        for t, part in enumerate(taps_of):
            raw[g, t] = part


def back_kernel(share, groups, pairs, *refs):
    refs = list(refs)
    deltas = [[refs.pop(0)] for _ in range(pairs + 2)]
    slopes = [refs.pop(0) for _ in range(pairs + 1)]
    fields = [[refs.pop(0) for _ in range(groups)] for _ in range(pairs + 2)]
    weight, second = refs.pop(0), refs.pop(0)
    firsts = [refs.pop(0) for _ in range(pairs + 1)]
    keep, send, total = refs

    def one(r, _):
        row = 2 * r
        for p, sums in enumerate(taps(weight[...], deltas, row)):
            for q, v in enumerate(sums):
                shape = firsts[p].shape[1:]
                slope = slopes[p][row + 2 + q].astype(F32)
                firsts[p][row + q] = (v.reshape(shape) * slope).astype(BF16)
        return 0

    lax.fori_loop(0, firsts[0].shape[0] // 2, one, 0)
    near = planes_of(fields)[1:-1]
    own = planes_of([[first] for first in firsts])[1:-1]
    weight_loop(total, near, 3, own, 1, share)
    parts = weight_fold(total, keep.shape[2])
    extent = keep.shape[0]
    me = lax.axis_index("chan")
    odd = lax.rem(lax.axis_index("slab"), 2)

    def place(ours, theirs):
        for g, taps_of in enumerate(parts):
            there = lax.rem(me + extent - g, extent)
            for t, part in enumerate(taps_of):
                ours[g, t] = part
                theirs[g, t] = second[there, t]

    @pl.when(odd == 0)
    def _():
        place(keep, send)

    @pl.when(odd == 1)
    def _():
        place(send, keep)


def last_kernel(pairs, *refs):
    refs = list(refs)
    firsts = [refs.pop(0) for _ in range(pairs + 1)]
    weight = refs.pop(0)
    outs = refs

    def one(r, _):
        row = 2 * r
        size = outs[0].shape[2]
        channels = len(outs) * size
        for p, sums in enumerate(taps(weight[...], [[first] for first in firsts], row)):
            for q, v in enumerate(sums):
                for x in range(2):
                    for j, out in enumerate(outs):
                        low = x * channels + j * size
                        out[row + q, 2 * p + x] = v[low : low + size].astype(BF16)
        return 0

    lax.fori_loop(0, outs[0].shape[0] // 2, one, 0)


def merge_kernel(extent, *refs):
    pieces, out, wide = refs[:-2], refs[-2], refs[-1]
    share, planes, size = pieces[0].shape[:3]
    rows = out.shape[2]
    me = lax.axis_index("chan")
    for j, piece in enumerate(pieces):
        base = lax.rem(me + extent - j, extent) * share

        def widen(f, _, piece=piece, base=base):
            for x in range(planes):
                start = ((base + f) * planes + x) * size
                start = pl.multiple_of(start, 8) if size % 8 == 0 else start
                wide[pl.ds(start, size), :] = piece[f, x].astype(F32)
            return 0

        lax.fori_loop(0, share, widen, 0)

    def turn(i, _):
        for x in range(planes):
            tile = wide[pl.ds(x * size + i, rows, stride=planes * size), :]
            out[i, x] = tile.astype(BF16)
        return 0

    lax.fori_loop(0, size, turn, 0)


def pair_sum(values, axis, stride):
    count = lax.axis_size(axis)
    return values + lax.ppermute(values, axis, [(i, i ^ stride) for i in range(count)])


def body(field, out_grad, first_weight, second_weight):
    extent = lax.axis_size("chan")
    slabs = lax.axis_size("slab")
    me = lax.axis_index("chan")
    size, planes, rows, depth = field.shape
    channels = size * extent
    pairs = planes // 2
    share = rows // extent
    factor = 1.0 / math.sqrt(planes * slabs * rows * depth)

    def to_chan(value, shift):
        return lax.ppermute(value, "chan", [(i, (i + shift) % extent) for i in range(extent)])

    def to_next(value):
        return lax.ppermute(value, "slab", [(i, (i + 1) % slabs) for i in range(slabs)])

    def to_prev(value):
        return lax.ppermute(value, "slab", [((i + 1) % slabs, i) for i in range(slabs)])

    piece = jax.ShapeDtypeStruct((share + 8, 2, size, depth), BF16)
    halves = 14
    made = call(
        functools.partial(field_kernel, extent, 4),
        [piece] * (extent * pairs) + [jax.ShapeDtypeStruct((halves, size, 4 * channels), BF16)],
        [field, jnp.transpose(first_weight, (1, 0, 2)), jnp.transpose(second_weight, (1, 0, 2))],
        [pltpu.VMEM((size * planes * rows, depth), F32)],
        moved=field.size * 6,
    )
    parts = [made[:pairs]]
    for j in range(1, extent):
        parts.append([to_chan(piece, j) for piece in made[j * pairs : (j + 1) * pairs]])
    packs = [made[-1]] + [to_chan(made[-1], j) for j in range(1, extent)]
    by_pair = [[parts[j][p] for j in range(extent)] for p in range(pairs)]
    groups = extent
    if size % 16 != 0:
        by_pair = [[jnp.concatenate(pieces, axis=2)] for pieces in by_pair]
        groups = 1
    before = [to_next(piece) for piece in by_pair[-1]]
    after = [to_prev(piece) for piece in by_pair[0]]
    fields = [before] + by_pair + [after]
    matrix = jax.ShapeDtypeStruct((6 * channels, 12 * channels), BF16)
    first_wide, second_wide, first_back, second_back = call(
        functools.partial(matrix_kernel, extent), [matrix] * 4, packs, moved=matrix.size * 8
    )
    grad_piece = jax.ShapeDtypeStruct((share + 4, 2, channels, depth), BF16)
    grads = call(
        functools.partial(grad_kernel, extent, 2),
        [grad_piece] * pairs,
        [out_grad],
        [pltpu.VMEM((channels * planes * rows, depth), F32)],
        moved=out_grad.size * 4,
    )

    def many(count, rows_each, dtype=BF16):
        return [jax.ShapeDtypeStruct((rows_each, 2, channels, depth), dtype)] * count

    flat_fields = [piece for pieces in fields for piece in pieces]
    work = 2 * 27 * channels * channels * depth
    made = call(
        functools.partial(forward_kernel, groups, pairs),
        many(pairs + 1, share + 6) * 2 + many(pairs, share + 4),
        flat_fields + list(grads) + [first_wide, second_wide],
        flops=work * 2 * planes * share,
        moved=8 * planes * share * channels * depth,
    )
    hiddens = made[: pairs + 1]
    slopes = made[pairs + 1 : 2 * pairs + 2]
    deltas = made[2 * pairs + 2 :]
    all_deltas = [to_next(deltas[-1])] + list(deltas) + [to_prev(deltas[0])]

    raw = jax.ShapeDtypeStruct((extent, 9, size, 3 * channels), F32)
    total = pltpu.VMEM((6 * channels, 12 * channels), F32)
    (second_raw,) = call(
        functools.partial(second_kernel, share, pairs),
        [raw],
        list(hiddens) + list(deltas),
        [total],
        flops=work * planes * share,
        moved=8 * planes * share * channels * depth,
    )
    made = call(
        functools.partial(back_kernel, share, groups, pairs),
        many(pairs + 1, share + 2) + [raw] * 2,
        all_deltas + list(slopes) + flat_fields + [second_back, second_raw],
        [total],
        flops=work * 2 * planes * share,
        moved=8 * planes * share * channels * depth,
    )
    firsts, keep, send = made[:-2], made[-2], made[-1]

    if slabs & (slabs - 1) == 0 and slabs > 1:
        keep = keep + lax.ppermute(send, "slab", [(i, i ^ 1) for i in range(slabs)])
        mine = keep[0]
        for j in range(1, extent):
            mine = mine + to_chan(keep[j], extent - j)
        stride = 2
        while stride < slabs:
            mine = pair_sum(mine, "slab", stride)
            stride *= 2
        mine = mine * factor
        other = lax.ppermute(mine, "slab", [(i, i ^ 1) for i in range(slabs)])
    else:
        mine, other = keep[0], send[0]
        for j in range(1, extent):
            mine, other = mine + to_chan(keep[j], extent - j), other + to_chan(send[j], extent - j)
        even = lax.rem(lax.axis_index("slab"), 2) == 0
        mine, other = jnp.where(even, mine, other), jnp.where(even, other, mine)
        mine, other = lax.psum((mine, other), "slab")
        mine, other = mine * factor, other * factor
        mine, other = jnp.where(even, mine, other), jnp.where(even, other, mine)
    even = lax.rem(lax.axis_index("slab"), 2) == 0

    def laid(value):
        taps_first = jnp.transpose(value.reshape(9, size, 3, channels), (0, 2, 1, 3))
        return jnp.transpose(taps_first.reshape(27, size, channels), (1, 0, 2))

    first_grad = laid(jnp.where(even, mine, other))
    second_grad = laid(jnp.where(even, other, mine))

    out_piece = jax.ShapeDtypeStruct((share, planes, size, depth), BF16)
    made = call(
        functools.partial(last_kernel, pairs),
        [out_piece] * extent,
        list(firsts) + [first_back],
        flops=work * planes * share,
        moved=4 * planes * share * channels * depth,
    )
    pieces = [made[0]] + [None] * (extent - 1)
    for j in range(1, extent):
        pieces[extent - j] = to_chan(made[j], extent - j)
    (input_grad,) = call(
        functools.partial(merge_kernel, extent),
        [jax.ShapeDtypeStruct(field.shape, BF16)],
        pieces,
        [pltpu.VMEM((rows * planes * size, depth), F32)],
        moved=4 * field.size,
    )
    return input_grad, first_grad, second_grad


def solution(mesh):
    placed = (
        P("chan", "slab", None, None),
        P(None, "slab", None, None),
        P("chan", None, None),
        P("chan", None, None),
    )
    return jax.shard_map(
        body,
        mesh=mesh,
        in_specs=placed,
        out_specs=(P("chan", "slab", None, None), P("chan", None, None), P("chan", None, None)),
        check_vma=False,
    )
```

```python
import functools
import math

import jax
import jax.numpy as jnp
from jax import lax
from jax.experimental import pallas as pl
from jax.experimental.pallas import tpu as pltpu
from jax.sharding import PartitionSpec as P

F32 = jnp.float32
BF16 = jnp.bfloat16
LIMIT = 16 * 1024 * 1024


def call(kernel, outs, args, scratch=(), flops=0, moved=0, loose=0):
    whole = pl.BlockSpec(memory_space=pltpu.VMEM)
    still = pl.BlockSpec(memory_space=pl.ANY)
    return pl.pallas_call(
        kernel,
        out_shape=outs,
        in_specs=[still] * loose + [whole] * (len(args) - loose),
        out_specs=[whole] * len(outs),
        scratch_shapes=list(scratch),
        compiler_params=pltpu.CompilerParams(vmem_limit_bytes=LIMIT),
        cost_estimate=pl.CostEstimate(flops=flops, bytes_accessed=moved, transcendentals=0),
    )(*args)


def in_blocks(count, body):
    block = max(k for k in range(1, 8) if count % k == 0)
    if block < 4:
        block = min(count, 15)

    def several(r, _):
        for k in range(block):
            body(r * block + k)
        return 0

    lax.fori_loop(0, count // block, several, 0)
    for k in range(count // block * block, count):
        body(k)


def widened(x_ref, wide):
    count, planes, rows = x_ref.shape[:3]

    def widen(i):
        for x in range(planes):
            start = pl.multiple_of((i * planes + x) * rows, 8)
            wide[pl.ds(start, rows), :] = x_ref[i, x].astype(F32)

    in_blocks(count, widen)


def turn(wide, outs, shape, base, length):
    count, planes, rows = shape

    def one(f):
        y = lax.rem(base + f, rows)
        for x in range(planes):
            tile = wide[pl.ds(x * rows + y, count, stride=planes * rows), :]
            outs[x // 2][f, x % 2] = tile.astype(BF16)

    in_blocks(length, one)


def field_kernel(extent, margin, x_ref, *refs):
    outs, wide = refs[:-1], refs[-1]
    count, planes, rows = x_ref.shape[:3]
    pairs = planes // 2
    share = rows // extent
    widened(x_ref, wide)
    me = lax.axis_index("chan")
    for s in range(extent):
        base = lax.rem(me + s, extent) * share - margin + rows
        turn(
            wide,
            outs[s * pairs : (s + 1) * pairs],
            (count, planes, rows),
            base,
            share + 2 * margin,
        )


def pack_kernel(after, first, second, packed):
    del after
    blank = jnp.zeros(first.shape[1:], F32)
    for h in range(packed.shape[0]):
        parts = []
        for ref in (first, second):
            for t in (2 * h, 2 * h + 1):
                parts.append(ref[t].astype(F32) if t < ref.shape[0] else blank)
        packed[h] = jnp.concatenate(parts, axis=1).astype(BF16)


def grad_kernel(extent, margin, x_ref, *refs):
    outs, wide = refs[:-1], refs[-1]
    count, planes, rows = x_ref.shape[:3]
    share = rows // extent
    widened(x_ref, wide)
    base = lax.axis_index("chan") * share - margin + rows
    turn(wide, outs, (count, planes, rows), base, share + 2 * margin)


def matrix_kernel(extent, *refs):
    packs, outs = refs[:extent], refs[extent:]
    me = lax.axis_index("chan")
    halves = packs[0].shape[0]
    quarter = packs[0].shape[2] // 4
    taps = []
    turned = []
    for h in range(halves):
        tiles = [pack[h].astype(F32) for pack in packs]
        own = jnp.concatenate(tiles, axis=0)
        fixed = []
        for g in range(extent):
            place = lax.rem(me + extent - g, extent)
            tile = tiles[0]
            for j in range(1, extent):
                tile = jnp.where(place == j, tiles[j], tile)
            fixed.append(tile)
        both = jnp.concatenate(
            [own[:, : 2 * quarter], jnp.concatenate(fixed, axis=0)[:, 2 * quarter :]], axis=1
        )
        across = both.T
        for side in range(2):
            taps.append(
                [both[:, k * quarter : (k + 1) * quarter] for k in (side, side + 2)]
            )
            turned.append(
                [across[k * quarter : (k + 1) * quarter] for k in (side, side + 2)]
            )
    channels = quarter
    blank = jnp.zeros((channels, channels), F32)
    for k in range(2):
        for out, blocks, flip in ((outs[k], turned, False), (outs[2 + k], taps, True)):
            for e in range(3):
                for x in range(2):
                    chunks = []
                    for pair in range(2):
                        for b in range(3):
                            for side in range(2):
                                a = 2 * pair + side - x
                                t = 9 * a + 3 * b + e
                                inside = 0 <= a <= 2
                                t = 26 - t if flip else t
                                chunks.append(blocks[t][k] if inside else blank)
                    low = (2 * e + x) * channels
                    out[low : low + channels, :] = jnp.concatenate(chunks, axis=1).astype(BF16)


def stacked(refs, row, count):
    if len(refs) == 1:
        part = refs[0][pl.ds(row, count)]
        return part.reshape(-1, part.shape[-1])
    parts = [ref[row + b, x] for b in range(count) for x in range(2) for ref in refs]
    return jnp.concatenate(parts, axis=0)


def taps(weight, pairs, row):
    sides = []
    for p in range(len(pairs) - 1):
        for q in range(2):
            above = stacked(pairs[p], row + q, 3)
            below = stacked(pairs[p + 1], row + q, 3)
            sides.append(jnp.concatenate([above, below], axis=0))
    lifted = jnp.dot(weight, jnp.concatenate(sides, axis=1), preferred_element_type=F32)
    third = lifted.shape[0] // 3
    depth = sides[0].shape[1]
    sums = []
    for k in range(len(sides)):
        side = lifted[:, k * depth : (k + 1) * depth]
        sums.append(
            side[third : 2 * third]
            + pltpu.roll(side[:third], 1, 1)
            + pltpu.roll(side[2 * third :], depth - 1, 1)
        )
    return [sums[2 * p : 2 * p + 2] for p in range(len(pairs) - 1)]


def silu_parts(v):
    sig = jax.nn.sigmoid(v)
    return sig, sig * (1.0 + v * (1.0 - sig))


def forward_kernel(groups, pairs, *refs):
    refs = list(refs)
    fields = [[refs.pop(0) for _ in range(groups)] for _ in range(pairs + 2)]
    grads = [refs.pop(0) for _ in range(pairs)]
    first, second = refs.pop(0), refs.pop(0)
    hiddens = [refs.pop(0) for _ in range(pairs + 1)]
    slopes = [refs.pop(0) for _ in range(pairs + 1)]
    deltas = [refs.pop(0) for _ in range(pairs)]

    def one(r):
        row = 2 * r
        for p, sums in enumerate(taps(first[...], fields, row)):
            for q, v in enumerate(sums):
                sig, slope = silu_parts(v)
                shape = hiddens[p].shape[1:]
                hiddens[p][row + q] = (v * sig).astype(BF16).reshape(shape)
                slopes[p][row + q] = slope.astype(BF16).reshape(shape)

    in_blocks(hiddens[0].shape[0] // 2, one)

    def two(r):
        row = 2 * r
        for p, sums in enumerate(taps(second[...], [[ref] for ref in hiddens], row)):
            for q, v in enumerate(sums):
                shape = deltas[p].shape[1:]
                out_grad = grads[p][row + q].astype(F32)
                slope = silu_parts(v)[1].reshape(shape)
                deltas[p][row + q] = (out_grad * slope).astype(BF16)

    in_blocks(deltas[0].shape[0] // 2, two)


def planes_of(pairs):
    return [(refs, x) for refs in pairs for x in range(2)]


def weight_loop(total, pieces, first_row, deltas, delta_row, count):
    total[...] = jnp.zeros_like(total)

    together = max(k for k in range(1, 4) if (count // 2) % k == 0)

    def step(r, _):
        left, right = [], []
        for k in range(together):
            row = 2 * (r * together + k)
            for x, ((delta,), place) in enumerate(deltas):
                rows = []
                for q in range(2):
                    wide = delta[delta_row + row + q, place]
                    plain = wide.astype(F32)
                    depth = plain.shape[1]
                    rows += [
                        pltpu.roll(plain, depth - 1, 1).astype(BF16),
                        wide,
                        pltpu.roll(plain, 1, 1).astype(BF16),
                    ]
                left.append(jnp.concatenate(rows, axis=0))
                rows = []
                for refs, side in pieces[x : x + 3]:
                    for b in range(4):
                        for ref in refs:
                            rows.append(ref[first_row + row + b, side])
                right.append(jnp.concatenate(rows, axis=0))
        total[...] += lax.dot_general(
            jnp.concatenate(left, axis=1),
            jnp.concatenate(right, axis=1),
            (((1,), (1,)), ((), ())),
            preferred_element_type=F32,
        )
        return 0

    lax.fori_loop(0, count // 2 // together, step, 0)


def weight_fold(total, size):
    lanes = total.shape[0] // 2
    channels = total.shape[1] // 12
    upper, lower = total[:lanes, :].T, total[lanes:, :].T
    parts = []
    for g in range(channels // size):
        taps_of = []
        for a in range(3):
            for b in range(3):
                start = (4 * a + b) * channels + g * size
                taps_of.append(
                    upper[start : start + size]
                    + lower[start + channels : start + channels + size]
                )
        parts.append(taps_of)
    return parts


def second_kernel(share, pairs, *refs):
    refs = list(refs)
    hiddens = [[refs.pop(0)] for _ in range(pairs + 1)]
    deltas = [refs.pop(0) for _ in range(pairs)]
    raw, total = refs
    weight_loop(total, planes_of(hiddens), 2, planes_of([[d] for d in deltas]), 2, share)
    for g, taps_of in enumerate(weight_fold(total, raw.shape[2])):
        for t, part in enumerate(taps_of):
            raw[g, t] = part


def back_kernel(share, groups, pairs, *refs):
    refs = list(refs)
    deltas = [[refs.pop(0)] for _ in range(pairs + 2)]
    slopes = [refs.pop(0) for _ in range(pairs + 1)]
    fields = [[refs.pop(0) for _ in range(groups)] for _ in range(pairs + 2)]
    weight, second = refs.pop(0), refs.pop(0)
    firsts = [refs.pop(0) for _ in range(pairs + 1)]
    keep, send, total = refs

    def one(r):
        row = 2 * r
        for p, sums in enumerate(taps(weight[...], deltas, row)):
            for q, v in enumerate(sums):
                shape = firsts[p].shape[1:]
                slope = slopes[p][row + 2 + q].astype(F32)
                firsts[p][row + q] = (v.reshape(shape) * slope).astype(BF16)

    in_blocks(firsts[0].shape[0] // 2, one)
    near = planes_of(fields)[1:-1]
    own = planes_of([[first] for first in firsts])[1:-1]
    weight_loop(total, near, 3, own, 1, share)
    parts = weight_fold(total, keep.shape[2])
    extent = keep.shape[0]
    me = lax.axis_index("chan")
    odd = lax.rem(lax.axis_index("slab"), 2)

    def place(ours, theirs):
        for g, taps_of in enumerate(parts):
            there = lax.rem(me + extent - g, extent)
            for t, part in enumerate(taps_of):
                ours[g, t] = part
                theirs[g, t] = second[there, t]

    @pl.when(odd == 0)
    def _():
        place(keep, send)

    @pl.when(odd == 1)
    def _():
        place(send, keep)


def last_kernel(pairs, extent, *refs):
    refs = list(refs)
    shares = [refs.pop(0) for _ in range(extent)]
    added = refs.pop()
    value = shares[0][0]
    for j in range(1, extent):
        value = value + shares[j][...]
    added[...] = value
    firsts = [refs.pop(0) for _ in range(pairs + 1)]
    weight = refs.pop(0)
    outs = refs

    def one(r):
        row = 2 * r
        size = outs[0].shape[2]
        channels = len(outs) * size
        for p, sums in enumerate(taps(weight[...], [[first] for first in firsts], row)):
            for q, v in enumerate(sums):
                for x in range(2):
                    for j, out in enumerate(outs):
                        low = x * channels + j * size
                        out[row + q, 2 * p + x] = v[low : low + size].astype(BF16)

    in_blocks(outs[0].shape[0] // 2, one)


def merge_kernel(extent, one, two, *refs):
    pieces, out, added, wide = refs[:-3], refs[-3], refs[-2], refs[-1]
    added[...] = one[...] + two[...]
    share, planes, size = pieces[0].shape[:3]
    rows = out.shape[2]
    me = lax.axis_index("chan")
    for j, piece in enumerate(pieces):
        base = lax.rem(me + extent - j, extent) * share

        def widen(f, piece=piece, base=base):
            for x in range(planes):
                start = ((base + f) * planes + x) * size
                start = pl.multiple_of(start, 8) if size % 8 == 0 else start
                wide[pl.ds(start, size), :] = piece[f, x].astype(F32)

        in_blocks(share, widen)

    def back(i):
        for x in range(planes):
            tile = wide[pl.ds(x * size + i, rows, stride=planes * size), :]
            out[i, x] = tile.astype(BF16)

    in_blocks(size, back)


def body(field, out_grad, first_weight, second_weight):
    extent = lax.axis_size("chan")
    slabs = lax.axis_size("slab")
    me = lax.axis_index("chan")
    size, planes, rows, depth = field.shape
    channels = size * extent
    pairs = planes // 2
    share = rows // extent
    factor = 1.0 / math.sqrt(planes * slabs * rows * depth)

    def to_chan(value, shift):
        return lax.ppermute(value, "chan", [(i, (i + shift) % extent) for i in range(extent)])

    def to_next(value):
        return lax.ppermute(value, "slab", [(i, (i + 1) % slabs) for i in range(slabs)])

    def to_prev(value):
        return lax.ppermute(value, "slab", [((i + 1) % slabs, i) for i in range(slabs)])

    piece = jax.ShapeDtypeStruct((share + 8, 2, size, depth), BF16)
    halves = 14
    made = call(
        functools.partial(field_kernel, extent, 4),
        [piece] * (extent * pairs),
        [field],
        [pltpu.VMEM((size * planes * rows, depth), F32)],
        moved=field.size * 6,
    )
    parts = [made[:pairs]]
    for j in range(1, extent):
        parts.append([to_chan(piece, j) for piece in made[j * pairs : (j + 1) * pairs]])
    (pack,) = call(
        pack_kernel,
        [jax.ShapeDtypeStruct((halves, size, 4 * channels), BF16)],
        [made[0], jnp.transpose(first_weight, (1, 0, 2)), jnp.transpose(second_weight, (1, 0, 2))],
        loose=1,
    )
    packs = [pack] + [to_chan(pack, j) for j in range(1, extent)]
    by_pair = [[parts[j][p] for j in range(extent)] for p in range(pairs)]
    groups = extent
    if size % 16 != 0:
        by_pair = [[jnp.concatenate(pieces, axis=2)] for pieces in by_pair]
        groups = 1
    before = [to_next(piece) for piece in by_pair[-1]]
    after = [to_prev(piece) for piece in by_pair[0]]
    fields = [before] + by_pair + [after]
    matrix = jax.ShapeDtypeStruct((6 * channels, 12 * channels), BF16)
    first_wide, second_wide, first_back, second_back = call(
        functools.partial(matrix_kernel, extent), [matrix] * 4, packs, moved=matrix.size * 8
    )
    grad_piece = jax.ShapeDtypeStruct((share + 4, 2, channels, depth), BF16)
    grads = call(
        functools.partial(grad_kernel, extent, 2),
        [grad_piece] * pairs,
        [out_grad],
        [pltpu.VMEM((channels * planes * rows, depth), F32)],
        moved=out_grad.size * 4,
    )

    def many(count, rows_each, dtype=BF16):
        return [jax.ShapeDtypeStruct((rows_each, 2, channels, depth), dtype)] * count

    flat_fields = [piece for pieces in fields for piece in pieces]
    work = 2 * 27 * channels * channels * depth
    made = call(
        functools.partial(forward_kernel, groups, pairs),
        many(pairs + 1, share + 6) * 2 + many(pairs, share + 4),
        flat_fields + list(grads) + [first_wide, second_wide],
        flops=work * 2 * planes * share,
        moved=8 * planes * share * channels * depth,
    )
    hiddens = made[: pairs + 1]
    slopes = made[pairs + 1 : 2 * pairs + 2]
    deltas = made[2 * pairs + 2 :]
    all_deltas = [to_next(deltas[-1])] + list(deltas) + [to_prev(deltas[0])]

    raw = jax.ShapeDtypeStruct((extent, 9, size, 3 * channels), F32)
    total = pltpu.VMEM((6 * channels, 12 * channels), F32)
    (second_raw,) = call(
        functools.partial(second_kernel, share, pairs),
        [raw],
        list(hiddens) + list(deltas),
        [total],
        flops=work * planes * share,
        moved=8 * planes * share * channels * depth,
    )
    made = call(
        functools.partial(back_kernel, share, groups, pairs),
        many(pairs + 1, share + 2) + [raw] * 2,
        all_deltas + list(slopes) + flat_fields + [second_back, second_raw],
        [total],
        flops=work * 2 * planes * share,
        moved=8 * planes * share * channels * depth,
    )
    firsts, keep, send = made[:-2], made[-2], made[-1]

    def swapped(value, stride):
        return lax.ppermute(value, "slab", [(i, i ^ stride) for i in range(slabs)])

    plain = slabs & (slabs - 1) == 0 and slabs >= 4
    if plain:
        keep = keep + swapped(send, 1)
    out_piece = jax.ShapeDtypeStruct((share, planes, size, depth), BF16)
    portion = jax.ShapeDtypeStruct(keep.shape[1:], F32)
    made = call(
        functools.partial(last_kernel, pairs, extent),
        [out_piece] * extent + [portion],
        [keep]
        + [to_chan(keep[j], extent - j) for j in range(1, extent)]
        + list(firsts)
        + [first_back],
        flops=work * planes * share,
        moved=4 * planes * share * channels * depth,
    )
    mine = made[-1]
    pieces = [made[0]] + [None] * (extent - 1)
    for j in range(1, extent):
        pieces[extent - j] = to_chan(made[j], extent - j)
    if plain:
        stride = 2
        while 2 * stride < slabs:
            mine = mine + swapped(mine, stride)
            stride *= 2
        theirs = swapped(mine, stride)
    else:
        theirs = jnp.zeros_like(mine)
    input_grad, mine = call(
        functools.partial(merge_kernel, extent),
        [jax.ShapeDtypeStruct(field.shape, BF16), portion],
        [mine, theirs] + pieces,
        [pltpu.VMEM((rows * planes * size, depth), F32)],
        moved=4 * field.size,
    )
    if plain:
        mine = mine * factor
        other = swapped(mine, 1)
    else:
        other = send[0]
        for j in range(1, extent):
            other = other + to_chan(send[j], extent - j)
        even = lax.rem(lax.axis_index("slab"), 2) == 0
        mine, other = jnp.where(even, mine, other), jnp.where(even, other, mine)
        mine, other = lax.psum((mine, other), "slab")
        mine, other = mine * factor, other * factor
        mine, other = jnp.where(even, mine, other), jnp.where(even, other, mine)
    even = lax.rem(lax.axis_index("slab"), 2) == 0

    def laid(value):
        taps_first = jnp.transpose(value.reshape(9, size, 3, channels), (0, 2, 1, 3))
        return jnp.transpose(taps_first.reshape(27, size, channels), (1, 0, 2))

    first_grad = laid(jnp.where(even, mine, other))
    second_grad = laid(jnp.where(even, other, mine))
    return input_grad, first_grad, second_grad


def solution(mesh):
    placed = (
        P("chan", "slab", None, None),
        P(None, "slab", None, None),
        P("chan", None, None),
        P("chan", None, None),
    )
    return jax.shard_map(
        body,
        mesh=mesh,
        in_specs=placed,
        out_specs=(P("chan", "slab", None, None), P("chan", None, None), P("chan", None, None)),
        check_vma=False,
    )
```

```python
import functools
import math

import jax
import jax.numpy as jnp
from jax import lax
from jax.experimental import pallas as pl
from jax.experimental.pallas import tpu as pltpu
from jax.sharding import PartitionSpec as P

F32 = jnp.float32
BF16 = jnp.bfloat16
LIMIT = 16 * 1024 * 1024


def call(kernel, outs, args, scratch=(), flops=0, moved=0, loose=0, same=None):
    whole = pl.BlockSpec(memory_space=pltpu.VMEM)
    still = pl.BlockSpec(memory_space=pl.ANY)
    return pl.pallas_call(
        kernel,
        out_shape=outs,
        in_specs=[still] * loose + [whole] * (len(args) - loose),
        out_specs=[whole if same is None else still] * len(outs),
        input_output_aliases=same or {},
        scratch_shapes=list(scratch),
        compiler_params=pltpu.CompilerParams(vmem_limit_bytes=LIMIT),
        cost_estimate=pl.CostEstimate(flops=flops, bytes_accessed=moved, transcendentals=0),
    )(*args)


def in_blocks(count, body):
    block = max(k for k in range(1, 8) if count % k == 0)
    if block < 4:
        block = min(count, 15)

    def several(r, _):
        for k in range(block):
            body(r * block + k)
        return 0

    lax.fori_loop(0, count // block, several, 0)
    for k in range(count // block * block, count):
        body(k)


def widened(x_ref, wide):
    count, planes, rows = x_ref.shape[:3]

    def widen(i):
        for x in range(planes):
            start = pl.multiple_of((i * planes + x) * rows, 8)
            wide[pl.ds(start, rows), :] = x_ref[i, x].astype(F32)

    in_blocks(count, widen)


def turn(wide, outs, shape, base, length):
    count, planes, rows = shape

    def one(f):
        y = lax.rem(base + f, rows)
        for x in range(planes):
            tile = wide[pl.ds(x * rows + y, count, stride=planes * rows), :]
            outs[x // 2][f, x % 2] = tile.astype(BF16)

    in_blocks(length, one)


def field_kernel(extent, margin, x_ref, *refs):
    outs, wide = refs[:-1], refs[-1]
    count, planes, rows = x_ref.shape[:3]
    pairs = planes // 2
    share = rows // extent
    widened(x_ref, wide)
    me = lax.axis_index("chan")
    for s in range(extent):
        base = lax.rem(me + s, extent) * share - margin + rows
        turn(
            wide,
            outs[s * pairs : (s + 1) * pairs],
            (count, planes, rows),
            base,
            share + 2 * margin,
        )


def pack_kernel(after, first, second, packed):
    del after
    blank = jnp.zeros(first.shape[1:], F32)
    for h in range(packed.shape[0]):
        parts = []
        for ref in (first, second):
            for t in (2 * h, 2 * h + 1):
                parts.append(ref[t].astype(F32) if t < ref.shape[0] else blank)
        packed[h] = jnp.concatenate(parts, axis=1).astype(BF16)


def grad_kernel(extent, margin, x_ref, *refs):
    outs, wide = refs[:-1], refs[-1]
    count, planes, rows = x_ref.shape[:3]
    share = rows // extent
    widened(x_ref, wide)
    base = lax.axis_index("chan") * share - margin + rows
    turn(wide, outs, (count, planes, rows), base, share + 2 * margin)


def matrix_kernel(extent, *refs):
    packs, outs = refs[:extent], refs[extent:]
    me = lax.axis_index("chan")
    halves = packs[0].shape[0]
    quarter = packs[0].shape[2] // 4
    taps = []
    turned = []
    for h in range(halves):
        tiles = [pack[h].astype(F32) for pack in packs]
        own = jnp.concatenate(tiles, axis=0)
        fixed = []
        for g in range(extent):
            place = lax.rem(me + extent - g, extent)
            tile = tiles[0]
            for j in range(1, extent):
                tile = jnp.where(place == j, tiles[j], tile)
            fixed.append(tile)
        both = jnp.concatenate(
            [own[:, : 2 * quarter], jnp.concatenate(fixed, axis=0)[:, 2 * quarter :]], axis=1
        )
        across = both.T
        for side in range(2):
            taps.append(
                [both[:, k * quarter : (k + 1) * quarter] for k in (side, side + 2)]
            )
            turned.append(
                [across[k * quarter : (k + 1) * quarter] for k in (side, side + 2)]
            )
    channels = quarter
    blank = jnp.zeros((channels, channels), F32)
    for k in range(2):
        for out, blocks, flip in ((outs[k], turned, False), (outs[2 + k], taps, True)):
            for e in range(3):
                for x in range(2):
                    chunks = []
                    for pair in range(2):
                        for b in range(3):
                            for side in range(2):
                                a = 2 * pair + side - x
                                t = 9 * a + 3 * b + e
                                inside = 0 <= a <= 2
                                t = 26 - t if flip else t
                                chunks.append(blocks[t][k] if inside else blank)
                    low = (2 * e + x) * channels
                    out[low : low + channels, :] = jnp.concatenate(chunks, axis=1).astype(BF16)


def stacked(refs, row, count):
    if len(refs) == 1:
        part = refs[0][pl.ds(row, count)]
        return part.reshape(-1, part.shape[-1])
    parts = [ref[row + b, x] for b in range(count) for x in range(2) for ref in refs]
    return jnp.concatenate(parts, axis=0)


def taps(weight, pairs, row):
    sides = []
    for p in range(len(pairs) - 1):
        for q in range(2):
            above = stacked(pairs[p], row + q, 3)
            below = stacked(pairs[p + 1], row + q, 3)
            sides.append(jnp.concatenate([above, below], axis=0))
    lifted = jnp.dot(weight, jnp.concatenate(sides, axis=1), preferred_element_type=F32)
    third = lifted.shape[0] // 3
    depth = sides[0].shape[1]
    sums = []
    for k in range(len(sides)):
        side = lifted[:, k * depth : (k + 1) * depth]
        sums.append(
            side[third : 2 * third]
            + pltpu.roll(side[:third], 1, 1)
            + pltpu.roll(side[2 * third :], depth - 1, 1)
        )
    return [sums[2 * p : 2 * p + 2] for p in range(len(pairs) - 1)]


def silu_parts(v):
    sig = jax.nn.sigmoid(v)
    return sig, sig * (1.0 + v * (1.0 - sig))


def forward_kernel(groups, pairs, *refs):
    refs = list(refs)
    fields = [[refs.pop(0) for _ in range(groups)] for _ in range(pairs + 2)]
    grads = [refs.pop(0) for _ in range(pairs)]
    first, second = refs.pop(0), refs.pop(0)
    hiddens = [refs.pop(0) for _ in range(pairs + 1)]
    slopes = [refs.pop(0) for _ in range(pairs + 1)]
    deltas = [refs.pop(0) for _ in range(pairs)]

    def one(r):
        row = 2 * r
        for p, sums in enumerate(taps(first[...], fields, row)):
            for q, v in enumerate(sums):
                sig, slope = silu_parts(v)
                shape = hiddens[p].shape[1:]
                hiddens[p][row + q] = (v * sig).astype(BF16).reshape(shape)
                slopes[p][row + q] = slope.astype(BF16).reshape(shape)

    in_blocks(hiddens[0].shape[0] // 2, one)

    def two(r):
        row = 2 * r
        for p, sums in enumerate(taps(second[...], [[ref] for ref in hiddens], row)):
            for q, v in enumerate(sums):
                shape = deltas[p].shape[1:]
                out_grad = grads[p][row + q].astype(F32)
                slope = silu_parts(v)[1].reshape(shape)
                deltas[p][row + q] = (out_grad * slope).astype(BF16)

    in_blocks(deltas[0].shape[0] // 2, two)


def planes_of(pairs):
    return [(refs, x) for refs in pairs for x in range(2)]


def weight_loop(total, pieces, first_row, deltas, delta_row, count):
    total[...] = jnp.zeros_like(total)

    together = max(k for k in range(1, 4) if (count // 2) % k == 0)

    def step(r, _):
        left, right = [], []
        for k in range(together):
            row = 2 * (r * together + k)
            for x, ((delta,), place) in enumerate(deltas):
                rows = []
                for q in range(2):
                    wide = delta[delta_row + row + q, place]
                    plain = wide.astype(F32)
                    depth = plain.shape[1]
                    rows += [
                        pltpu.roll(plain, depth - 1, 1).astype(BF16),
                        wide,
                        pltpu.roll(plain, 1, 1).astype(BF16),
                    ]
                left.append(jnp.concatenate(rows, axis=0))
                rows = []
                for refs, side in pieces[x : x + 3]:
                    for b in range(4):
                        for ref in refs:
                            rows.append(ref[first_row + row + b, side])
                right.append(jnp.concatenate(rows, axis=0))
        total[...] += lax.dot_general(
            jnp.concatenate(left, axis=1),
            jnp.concatenate(right, axis=1),
            (((1,), (1,)), ((), ())),
            preferred_element_type=F32,
        )
        return 0

    lax.fori_loop(0, count // 2 // together, step, 0)


def weight_fold(total, size):
    lanes = total.shape[0] // 2
    channels = total.shape[1] // 12
    upper, lower = total[:lanes, :].T, total[lanes:, :].T
    groups = []
    for g in range(channels // size):
        taps_of = []
        for a in range(3):
            for b in range(3):
                start = (4 * a + b) * channels + g * size
                part = (
                    upper[start : start + size]
                    + lower[start + channels : start + channels + size]
                )
                taps_of += [part[:, e * channels : (e + 1) * channels] for e in range(3)]
        blank = jnp.zeros((size, channels), F32)
        taps_of += [blank] * 5
        groups.append([jnp.concatenate(taps_of[4 * h : 4 * h + 4], axis=1) for h in range(8)])
    return groups


def second_kernel(share, pairs, *refs):
    refs = list(refs)
    hiddens = [[refs.pop(0)] for _ in range(pairs + 1)]
    deltas = [refs.pop(0) for _ in range(pairs)]
    raw, total = refs
    weight_loop(total, planes_of(hiddens), 2, planes_of([[d] for d in deltas]), 2, share)
    for g, tiles in enumerate(weight_fold(total, raw.shape[2])):
        for h, tile in enumerate(tiles):
            raw[g, h] = tile


def back_kernel(share, groups, pairs, *refs):
    refs = list(refs)
    deltas = [[refs.pop(0)] for _ in range(pairs + 2)]
    slopes = [refs.pop(0) for _ in range(pairs + 1)]
    fields = [[refs.pop(0) for _ in range(groups)] for _ in range(pairs + 2)]
    weight, second = refs.pop(0), refs.pop(0)
    firsts = [refs.pop(0) for _ in range(pairs + 1)]
    sent, total = refs

    def one(r):
        row = 2 * r
        for p, sums in enumerate(taps(weight[...], deltas, row)):
            for q, v in enumerate(sums):
                shape = firsts[p].shape[1:]
                slope = slopes[p][row + 2 + q].astype(F32)
                firsts[p][row + q] = (v.reshape(shape) * slope).astype(BF16)

    in_blocks(firsts[0].shape[0] // 2, one)
    near = planes_of(fields)[1:-1]
    own = planes_of([[first] for first in firsts])[1:-1]
    weight_loop(total, near, 3, own, 1, share)
    extent, size = sent.shape[1:3]
    me = lax.axis_index("chan")
    for g, tiles in enumerate(weight_fold(total, size)):
        there = lax.rem(me + extent - g, extent)
        for h, tile in enumerate(tiles):
            sent[h, there] = tile
            sent[8 + h, g] = second[g, h]


def last_kernel(pairs, *refs):
    refs = list(refs)
    firsts = [refs.pop(0) for _ in range(pairs + 1)]
    weight = refs.pop(0)
    outs = refs

    def one(r):
        row = 2 * r
        size = outs[0].shape[2]
        channels = len(outs) * size
        for p, sums in enumerate(taps(weight[...], [[first] for first in firsts], row)):
            for q, v in enumerate(sums):
                for x in range(2):
                    for j, out in enumerate(outs):
                        low = x * channels + j * size
                        out[row + q, 2 * p + x] = v[low : low + size].astype(BF16)

    in_blocks(outs[0].shape[0] // 2, one)


def finish_kernel(factor, sums, first, second):
    channels = first.shape[2]
    for k, out in enumerate((first, second)):
        for t in range(27):
            low = t % 4 * channels
            out[t] = sums[8 * k + t // 4, :, low : low + channels] * factor


def relay_kernel(*refs):
    pass


def merge_kernel(extent, *refs):
    pieces, out, wide = refs[:-2], refs[-2], refs[-1]
    share, planes, size = pieces[0].shape[:3]
    rows = out.shape[2]
    me = lax.axis_index("chan")
    for j, piece in enumerate(pieces):
        base = lax.rem(me + extent - j, extent) * share

        def widen(f, piece=piece, base=base):
            for x in range(planes):
                start = ((base + f) * planes + x) * size
                start = pl.multiple_of(start, 8) if size % 8 == 0 else start
                wide[pl.ds(start, size), :] = piece[f, x].astype(F32)

        in_blocks(share, widen)

    def back(i):
        for x in range(planes):
            tile = wide[pl.ds(x * size + i, rows, stride=planes * size), :]
            out[i, x] = tile.astype(BF16)

    in_blocks(size, back)


def body(field, out_grad, first_weight, second_weight):
    extent = lax.axis_size("chan")
    slabs = lax.axis_size("slab")
    me = lax.axis_index("chan")
    size, planes, rows, depth = field.shape
    channels = size * extent
    pairs = planes // 2
    share = rows // extent
    factor = 1.0 / math.sqrt(planes * slabs * rows * depth)

    def to_chan(value, shift):
        return lax.ppermute(value, "chan", [(i, (i + shift) % extent) for i in range(extent)])

    def to_next(value):
        return lax.ppermute(value, "slab", [(i, (i + 1) % slabs) for i in range(slabs)])

    def to_prev(value):
        return lax.ppermute(value, "slab", [((i + 1) % slabs, i) for i in range(slabs)])

    piece = jax.ShapeDtypeStruct((share + 8, 2, size, depth), BF16)
    halves = 14
    made = call(
        functools.partial(field_kernel, extent, 4),
        [piece] * (extent * pairs),
        [field],
        [pltpu.VMEM((size * planes * rows, depth), F32)],
        moved=field.size * 6,
    )
    parts = [made[:pairs]]
    for j in range(1, extent):
        parts.append([to_chan(piece, j) for piece in made[j * pairs : (j + 1) * pairs]])
    (pack,) = call(
        pack_kernel,
        [jax.ShapeDtypeStruct((halves, size, 4 * channels), BF16)],
        [made[0], jnp.transpose(first_weight, (1, 0, 2)), jnp.transpose(second_weight, (1, 0, 2))],
        loose=1,
    )
    packs = [pack] + [to_chan(pack, j) for j in range(1, extent)]
    matrix = jax.ShapeDtypeStruct((6 * channels, 12 * channels), BF16)
    first_wide, second_wide, first_back, second_back = call(
        functools.partial(matrix_kernel, extent), [matrix] * 4, packs, moved=matrix.size * 8
    )
    grad_piece = jax.ShapeDtypeStruct((share + 4, 2, channels, depth), BF16)
    grads = call(
        functools.partial(grad_kernel, extent, 2),
        [grad_piece] * pairs,
        [out_grad],
        [pltpu.VMEM((channels * planes * rows, depth), F32)],
        moved=out_grad.size * 4,
    )
    if extent > 1:
        early = [parts[1][0], first_wide, grads[0]]
        (parts[1][0],) = call(relay_kernel, [piece], early, loose=3, same={0: 0})
    by_pair = [[parts[j][p] for j in range(extent)] for p in range(pairs)]
    groups = extent
    if size % 16 != 0:
        by_pair = [[jnp.concatenate(pieces, axis=2)] for pieces in by_pair]
        groups = 1
    before = [to_next(piece) for piece in by_pair[-1]]
    after = [to_prev(piece) for piece in by_pair[0]]
    fields = [before] + by_pair + [after]

    def many(count, rows_each, dtype=BF16):
        return [jax.ShapeDtypeStruct((rows_each, 2, channels, depth), dtype)] * count

    flat_fields = [piece for pieces in fields for piece in pieces]
    work = 2 * 27 * channels * channels * depth
    made = call(
        functools.partial(forward_kernel, groups, pairs),
        many(pairs + 1, share + 6) * 2 + many(pairs, share + 4),
        flat_fields + list(grads) + [first_wide, second_wide],
        flops=work * 2 * planes * share,
        moved=8 * planes * share * channels * depth,
    )
    hiddens = made[: pairs + 1]
    slopes = made[pairs + 1 : 2 * pairs + 2]
    deltas = made[2 * pairs + 2 :]
    all_deltas = [to_next(deltas[-1])] + list(deltas) + [to_prev(deltas[0])]

    raw = jax.ShapeDtypeStruct((extent, 8, size, 4 * channels), F32)
    ready = jax.ShapeDtypeStruct((16, extent, size, 4 * channels), F32)
    total = pltpu.VMEM((6 * channels, 12 * channels), F32)
    (second_raw,) = call(
        functools.partial(second_kernel, share, pairs),
        [raw],
        list(hiddens) + list(deltas),
        [total],
        flops=work * planes * share,
        moved=8 * planes * share * channels * depth,
    )
    made = call(
        functools.partial(back_kernel, share, groups, pairs),
        many(pairs + 1, share + 2) + [ready],
        all_deltas + list(slopes) + flat_fields + [second_back, second_raw],
        [total],
        flops=work * 2 * planes * share,
        moved=8 * planes * share * channels * depth,
    )
    firsts, sent = made[:-1], made[-1]

    wide = 4 * channels
    lines = 16 * size // slabs
    if lines * slabs == 16 * size:
        if lines != size:
            sent = jnp.swapaxes(sent, 0, 1).reshape(extent, slabs, lines, wide)
            sent = jnp.swapaxes(sent, 0, 1)
        sent = sent.reshape(slabs * extent, lines, wide)
        got = lax.all_to_all(sent, ("slab", "chan"), 0, 0, tiled=True)
        own = jnp.sum(got, axis=0, keepdims=True)
        sums = lax.all_to_all(
            jnp.broadcast_to(own, (slabs, lines, wide)), "slab", 0, 0, tiled=True
        )
    else:
        sums = lax.psum(sent, ("slab", "chan"))
        sums = lax.dynamic_index_in_dim(sums, me, axis=1, keepdims=False)
    sums = sums.reshape(16, size, wide)
    by_tap = jax.ShapeDtypeStruct((27, size, channels), F32)
    first_grad, second_grad = call(
        functools.partial(finish_kernel, factor), [by_tap] * 2, [sums]
    )
    first_grad, second_grad = (jnp.transpose(g, (1, 0, 2)) for g in (first_grad, second_grad))

    out_piece = jax.ShapeDtypeStruct((share, planes, size, depth), BF16)
    made = call(
        functools.partial(last_kernel, pairs),
        [out_piece] * extent,
        list(firsts) + [first_back],
        flops=work * planes * share,
        moved=4 * planes * share * channels * depth,
    )
    pieces = [made[0]] + [None] * (extent - 1)
    for j in range(1, extent):
        pieces[extent - j] = to_chan(made[j], extent - j)
    (input_grad,) = call(
        functools.partial(merge_kernel, extent),
        [jax.ShapeDtypeStruct(field.shape, BF16)],
        pieces,
        [pltpu.VMEM((rows * planes * size, depth), F32)],
        moved=4 * field.size,
    )
    return input_grad, first_grad, second_grad


def solution(mesh):
    placed = (
        P("chan", "slab", None, None),
        P(None, "slab", None, None),
        P("chan", None, None),
        P("chan", None, None),
    )
    return jax.shard_map(
        body,
        mesh=mesh,
        in_specs=placed,
        out_specs=(P("chan", "slab", None, None), P("chan", None, None), P("chan", None, None)),
        check_vma=False,
    )
```

```python
import functools
import math

import jax
import jax.numpy as jnp
from jax import lax
from jax.experimental import pallas as pl
from jax.experimental.pallas import tpu as pltpu
from jax.sharding import PartitionSpec as P

F32 = jnp.float32
BF16 = jnp.bfloat16
LIMIT = 16 * 1024 * 1024


def call(kernel, outs, args, scratch=(), flops=0, moved=0, loose=0, same=None, limit=LIMIT):
    whole = pl.BlockSpec(memory_space=pltpu.VMEM)
    still = pl.BlockSpec(memory_space=pl.ANY)
    return pl.pallas_call(
        kernel,
        out_shape=outs,
        in_specs=[still] * loose + [whole] * (len(args) - loose),
        out_specs=[whole if same is None else still] * len(outs),
        input_output_aliases=same or {},
        scratch_shapes=list(scratch),
        compiler_params=pltpu.CompilerParams(vmem_limit_bytes=limit),
        cost_estimate=pl.CostEstimate(flops=flops, bytes_accessed=moved, transcendentals=0),
    )(*args)


def in_blocks(count, body):
    block = max(k for k in range(1, 8) if count % k == 0)
    if block < 4:
        block = min(count, 15)

    def several(r, _):
        for k in range(block):
            body(r * block + k)
        return 0

    lax.fori_loop(0, count // block, several, 0)
    for k in range(count // block * block, count):
        body(k)


def widened(x_ref, wide, low, count):
    planes, rows = x_ref.shape[1:3]

    def widen(i):
        for x in range(planes):
            start = pl.multiple_of(((low + i) * planes + x) * rows, 8)
            wide[pl.ds(start, rows), :] = x_ref[low + i, x].astype(F32)

    in_blocks(count, widen)


def turn(wide, outs, shape, base, length):
    count, planes, rows = shape

    def one(f):
        y = lax.rem(base + f, rows)
        for x in range(planes):
            tile = wide[pl.ds(x * rows + y, count, stride=planes * rows), :]
            outs[x // 2][f, x % 2] = tile.astype(BF16)

    in_blocks(length, one)


def field_kernel(extent, margin, x_ref, first_ref, second_ref, *refs):
    outs = refs[:-6]
    wide, held, first, second, field_done, weight_done = refs[-6:]
    count, planes, rows = x_ref.shape[:3]
    pairs = planes // 2
    share = rows // extent
    length = share + 2 * margin
    cuts = field_done.shape[0]
    step = count // cuts
    fields = []
    for c in range(cuts):
        part = pl.ds(c * step, step)
        fields.append(pltpu.make_async_copy(x_ref.at[part], held.at[part], field_done.at[c]))
        fields[-1].start()
    weights = [
        pltpu.make_async_copy(first_ref, first, weight_done.at[0]),
        pltpu.make_async_copy(second_ref, second, weight_done.at[1]),
    ]
    for copy in weights:
        copy.start()
    for c in range(cuts):
        fields[c].wait()
        widened(held, wide, c * step, step)
    me = lax.axis_index("chan")
    for s in range(extent):
        base = lax.rem(me + s, extent) * share - margin + rows
        turn(wide, outs[s * pairs : (s + 1) * pairs], (count, planes, rows), base, length)
    for copy in weights:
        copy.wait()
    blank = jnp.zeros(first.shape[1:], F32)
    for h in range(14):
        parts = []
        for ref in (first, second):
            for t in (2 * h, 2 * h + 1):
                parts.append(ref[t].astype(F32) if t < 27 else blank)
        tile = jnp.concatenate(parts, axis=1).astype(BF16)
        for s in range(extent):
            outs[(s + 1) * pairs - 1][length + h // 2, h % 2] = tile


def grad_kernel(extent, margin, after, x_ref, *refs):
    del after
    outs, wide = refs[:-1], refs[-1]
    count, planes, rows = x_ref.shape[:3]
    share = rows // extent
    widened(x_ref, wide, 0, count)
    base = lax.axis_index("chan") * share - margin + rows
    turn(wide, outs, (count, planes, rows), base, share + 2 * margin)


def matrix_kernel(extent, *refs):
    pieces, outs = refs[:extent], refs[extent:]
    me = lax.axis_index("chan")
    quarter = pieces[0].shape[3] // 4
    length = pieces[0].shape[0] - 7
    taps = []
    turned = []
    for h in range(14):
        tiles = [piece[length + h // 2, h % 2].astype(F32) for piece in pieces]
        own = jnp.concatenate(tiles, axis=0)
        fixed = []
        for g in range(extent):
            place = lax.rem(me + extent - g, extent)
            tile = tiles[0]
            for j in range(1, extent):
                tile = jnp.where(place == j, tiles[j], tile)
            fixed.append(tile)
        both = jnp.concatenate(
            [own[:, : 2 * quarter], jnp.concatenate(fixed, axis=0)[:, 2 * quarter :]], axis=1
        )
        across = both.T
        for side in range(2):
            taps.append(
                [both[:, k * quarter : (k + 1) * quarter] for k in (side, side + 2)]
            )
            turned.append(
                [across[k * quarter : (k + 1) * quarter] for k in (side, side + 2)]
            )
    channels = quarter
    blank = jnp.zeros((channels, channels), F32)
    for k in range(2):
        for out, blocks, flip in ((outs[k], turned, False), (outs[2 + k], taps, True)):
            for e in range(3):
                for x in range(2):
                    chunks = []
                    for pair in range(2):
                        for b in range(3):
                            for side in range(2):
                                a = 2 * pair + side - x
                                t = 9 * a + 3 * b + e
                                inside = 0 <= a <= 2
                                t = 26 - t if flip else t
                                chunks.append(blocks[t][k] if inside else blank)
                    low = (2 * e + x) * channels
                    out[low : low + channels, :] = jnp.concatenate(chunks, axis=1).astype(BF16)


def stacked(refs, row, count):
    if len(refs) == 1:
        part = refs[0][pl.ds(row, count)]
        return part.reshape(-1, part.shape[-1])
    parts = [ref[row + b, x] for b in range(count) for x in range(2) for ref in refs]
    return jnp.concatenate(parts, axis=0)


def taps(weight, pairs, row):
    sides = []
    for p in range(len(pairs) - 1):
        for q in range(2):
            above = stacked(pairs[p], row + q, 3)
            below = stacked(pairs[p + 1], row + q, 3)
            sides.append(jnp.concatenate([above, below], axis=0))
    lifted = jnp.dot(weight, jnp.concatenate(sides, axis=1), preferred_element_type=F32)
    third = lifted.shape[0] // 3
    depth = sides[0].shape[1]
    sums = []
    for k in range(len(sides)):
        side = lifted[:, k * depth : (k + 1) * depth]
        sums.append(
            side[third : 2 * third]
            + pltpu.roll(side[:third], 1, 1)
            + pltpu.roll(side[2 * third :], depth - 1, 1)
        )
    return [sums[2 * p : 2 * p + 2] for p in range(len(pairs) - 1)]


def silu_parts(v):
    sig = jax.nn.sigmoid(v)
    return sig, sig * (1.0 + v * (1.0 - sig))


def forward_kernel(groups, fresh, ready, *refs):
    refs = list(refs)
    fields = [[refs.pop(0) for _ in range(groups)] for _ in range(fresh + 1)]
    hiddens = [refs.pop(0) for _ in range(ready)]
    count = fresh + ready - 1
    grads = [refs.pop(0) for _ in range(count)]
    first, second = refs.pop(0), refs.pop(0)
    made = [refs.pop(0) for _ in range(fresh)]
    slopes = [refs.pop(0) for _ in range(fresh)]
    deltas = refs
    hiddens = hiddens + made

    def one(r):
        row = 2 * r
        for p, sums in enumerate(taps(first[...], fields, row)):
            for q, v in enumerate(sums):
                sig, slope = silu_parts(v)
                shape = made[p].shape[1:]
                made[p][row + q] = (v * sig).astype(BF16).reshape(shape)
                slopes[p][row + q] = slope.astype(BF16).reshape(shape)

    in_blocks(made[0].shape[0] // 2, one)

    def two(r):
        row = 2 * r
        for p, sums in enumerate(taps(second[...], [[ref] for ref in hiddens], row)):
            for q, v in enumerate(sums):
                shape = deltas[p].shape[1:]
                out_grad = grads[p][row + q].astype(F32)
                slope = silu_parts(v)[1].reshape(shape)
                deltas[p][row + q] = (out_grad * slope).astype(BF16)

    if count > 0:
        in_blocks(deltas[0].shape[0] // 2, two)


def planes_of(pairs):
    return [(refs, x) for refs in pairs for x in range(2)]


def weight_loop(total, pieces, first_row, deltas, delta_row, count):
    total[...] = jnp.zeros_like(total)

    together = max(k for k in range(1, 4) if (count // 2) % k == 0)

    def step(r, _):
        left, right = [], []
        for k in range(together):
            row = 2 * (r * together + k)
            for x, ((delta,), place) in enumerate(deltas):
                rows = []
                for q in range(2):
                    wide = delta[delta_row + row + q, place]
                    plain = wide.astype(F32)
                    depth = plain.shape[1]
                    rows += [
                        pltpu.roll(plain, depth - 1, 1).astype(BF16),
                        wide,
                        pltpu.roll(plain, 1, 1).astype(BF16),
                    ]
                left.append(jnp.concatenate(rows, axis=0))
                rows = []
                for refs, side in pieces[x : x + 3]:
                    for b in range(4):
                        for ref in refs:
                            rows.append(ref[first_row + row + b, side])
                right.append(jnp.concatenate(rows, axis=0))
        total[...] += lax.dot_general(
            jnp.concatenate(left, axis=1),
            jnp.concatenate(right, axis=1),
            (((1,), (1,)), ((), ())),
            preferred_element_type=F32,
        )
        return 0

    lax.fori_loop(0, count // 2 // together, step, 0)


def weight_fold(total, size):
    lanes = total.shape[0] // 2
    channels = total.shape[1] // 12
    upper, lower = total[:lanes, :].T, total[lanes:, :].T
    groups = []
    for g in range(channels // size):
        taps_of = []
        for a in range(3):
            for b in range(3):
                start = (4 * a + b) * channels + g * size
                part = (
                    upper[start : start + size]
                    + lower[start + channels : start + channels + size]
                )
                taps_of += [part[:, e * channels : (e + 1) * channels] for e in range(3)]
        blank = jnp.zeros((size, channels), F32)
        taps_of.append(blank)
        groups.append([jnp.concatenate(taps_of[4 * h : 4 * h + 4], axis=1) for h in range(7)])
    return groups


def second_kernel(share, pairs, *refs):
    refs = list(refs)
    hiddens = [[refs.pop(0)] for _ in range(pairs + 1)]
    deltas = [refs.pop(0) for _ in range(pairs)]
    raw, total = refs
    weight_loop(total, planes_of(hiddens), 2, planes_of([[d] for d in deltas]), 2, share)
    for g, tiles in enumerate(weight_fold(total, raw.shape[2])):
        for h, tile in enumerate(tiles):
            raw[g, h] = tile


def first_deltas(weight, deltas, slopes, firsts):
    def one(r):
        row = 2 * r
        for p, sums in enumerate(taps(weight[...], [[delta] for delta in deltas], row)):
            for q, v in enumerate(sums):
                shape = firsts[p].shape[1:]
                slope = slopes[p][row + 2 + q].astype(F32)
                firsts[p][row + q] = (v.reshape(shape) * slope).astype(BF16)

    in_blocks(firsts[0].shape[0] // 2, one)


def back_kernel(count, *refs):
    weight, refs = refs[0], refs[1:]
    first_deltas(
        weight, refs[: count + 1], refs[count + 1 : 2 * count + 1], refs[2 * count + 1 :]
    )


def first_kernel(share, groups, pairs, *refs):
    refs = list(refs)
    weight = refs.pop(0)
    deltas = [refs.pop(0) for _ in range(2)]
    slope = refs.pop(0)
    later = [refs.pop(0) for _ in range(pairs)]
    fields = [[refs.pop(0) for _ in range(groups)] for _ in range(pairs + 2)]
    second = refs.pop(0)
    first, keep, send, total = refs
    first_deltas(weight, deltas, [slope], [first])
    near = planes_of(fields)[1:-1]
    own = planes_of([[ref] for ref in [first] + later])[1:-1]
    weight_loop(total, near, 3, own, 1, share)
    extent, halves, size = keep.shape[:3]
    me = lax.axis_index("chan")
    groups_of = weight_fold(total, size)

    def place(ours, theirs):
        for g, tiles in enumerate(groups_of):
            there = lax.rem(me + extent - g, extent)
            for h in range(halves):
                ours[g, h] = tiles[h]
                theirs[g, h] = second[there, h]

    odd = lax.rem(lax.axis_index("slab"), 2)

    @pl.when(odd == 0)
    def _():
        place(keep, send)

    @pl.when(odd == 1)
    def _():
        place(send, keep)


def last_kernel(pairs, *refs):
    refs = list(refs)
    firsts = [refs.pop(0) for _ in range(pairs + 1)]
    weight = refs.pop(0)
    outs = refs

    def one(r):
        row = 2 * r
        size = outs[0].shape[2]
        channels = len(outs) * size
        for p, sums in enumerate(taps(weight[...], [[first] for first in firsts], row)):
            for q, v in enumerate(sums):
                for x in range(2):
                    for j, out in enumerate(outs):
                        low = x * channels + j * size
                        out[row + q, 2 * p + x] = v[low : low + size].astype(BF16)

    in_blocks(outs[0].shape[0] // 2, one)


def finish_kernel(factor, mine, other, first, second):
    channels = first.shape[2]

    def place(ours, theirs):
        for out, sums in ((ours, mine), (theirs, other)):
            for t in range(27):
                low = t % 4 * channels
                out[t] = sums[t // 4, :, low : low + channels] * factor

    odd = lax.rem(lax.axis_index("slab"), 2)

    @pl.when(odd == 0)
    def _():
        place(first, second)

    @pl.when(odd == 1)
    def _():
        place(second, first)


def split_kernel(after, one, two, *outs):
    del after
    for g, out in enumerate(outs):
        out[...] = one[g] + two[g]


def add_kernel(*refs):
    values = [ref[...] for ref in refs[:-1]]
    while len(values) > 1:
        values = [sum(values[k + 1 : k + 2], values[k]) for k in range(0, len(values), 2)]
    refs[-1][...] = values[0]


def relay_kernel(*refs):
    pass


def merge_kernel(extent, *refs):
    pieces, out, wide = refs[:-2], refs[-2], refs[-1]
    share, planes, size = pieces[0].shape[:3]
    rows = out.shape[2]
    me = lax.axis_index("chan")
    for j, piece in enumerate(pieces):
        base = lax.rem(me + extent - j, extent) * share

        def widen(f, piece=piece, base=base):
            for x in range(planes):
                start = ((base + f) * planes + x) * size
                start = pl.multiple_of(start, 8) if size % 8 == 0 else start
                wide[pl.ds(start, size), :] = piece[f, x].astype(F32)

        in_blocks(share, widen)

    def back(i):
        for x in range(planes):
            tile = wide[pl.ds(x * size + i, rows, stride=planes * size), :]
            out[i, x] = tile.astype(BF16)

    in_blocks(size, back)


def body(field, out_grad, first_weight, second_weight):
    extent = lax.axis_size("chan")
    slabs = lax.axis_size("slab")
    me = lax.axis_index("chan")
    size, planes, rows, depth = field.shape
    channels = size * extent
    pairs = planes // 2
    share = rows // extent
    factor = 1.0 / math.sqrt(planes * slabs * rows * depth)

    def to_chan(value, shift):
        return lax.ppermute(value, "chan", [(i, (i + shift) % extent) for i in range(extent)])

    def to_next(value):
        return lax.ppermute(value, "slab", [(i, (i + 1) % slabs) for i in range(slabs)])

    def to_prev(value):
        return lax.ppermute(value, "slab", [((i + 1) % slabs, i) for i in range(slabs)])

    def relayed(value, *others):
        shape = jax.ShapeDtypeStruct(value.shape, value.dtype)
        early = [value, *others]
        return call(relay_kernel, [shape], early, loose=len(early), same={0: 0})[0]

    piece = jax.ShapeDtypeStruct((share + 8, 2, size, depth), BF16)
    longer = jax.ShapeDtypeStruct((share + 15, 2, size, depth), BF16)
    by_tap = (27, size, channels)
    cuts = 4 if size % 4 == 0 else 1
    made = call(
        functools.partial(field_kernel, extent, 4),
        ([piece] * (pairs - 1) + [longer]) * extent,
        [field, jnp.transpose(first_weight, (1, 0, 2)), jnp.transpose(second_weight, (1, 0, 2))],
        [
            pltpu.VMEM((size * planes * rows, depth), F32),
            pltpu.VMEM(field.shape, BF16),
            pltpu.VMEM(by_tap, BF16),
            pltpu.VMEM(by_tap, BF16),
            pltpu.SemaphoreType.DMA((cuts,)),
            pltpu.SemaphoreType.DMA((2,)),
        ],
        moved=field.size * 6,
        loose=3,
        limit=60 * 1024 * 1024,
    )
    parts = [list(made[:pairs])]
    for j in range(1, extent):
        sent = made[j * pairs : (j + 1) * pairs]
        parts.append([to_chan(value, j) for value in reversed(sent)][::-1])
    matrix = jax.ShapeDtypeStruct((6 * channels, 12 * channels), BF16)
    first_wide, second_wide, first_back, second_back = call(
        functools.partial(matrix_kernel, extent),
        [matrix] * 4,
        [part[-1] for part in parts],
        moved=matrix.size * 8,
    )
    arrived = parts[-1]
    grad_piece = jax.ShapeDtypeStruct((share + 4, 2, channels, depth), BF16)
    grads = call(
        functools.partial(grad_kernel, extent, 2),
        [grad_piece] * pairs,
        [arrived[-1], out_grad],
        [pltpu.VMEM((channels * planes * rows, depth), F32)],
        moved=out_grad.size * 4,
        loose=1,
    )
    if extent > 1 and pairs > 1:
        arrived[0] = relayed(arrived[0], grads[0])
    by_pair = [[parts[j][p] for j in range(extent)] for p in range(pairs)]
    groups = extent
    if size % 16 != 0:
        by_pair = [[jnp.concatenate(pieces, axis=2)] for pieces in by_pair]
        groups = 1
    before = [to_next(piece) for piece in by_pair[-1]]
    after = [to_prev(piece) for piece in by_pair[0]]
    fields = [before] + by_pair + [after]

    def many(count, rows_each):
        return [jax.ShapeDtypeStruct((rows_each, 2, channels, depth), BF16)] * count

    def flat(lists):
        return [piece for pieces in lists for piece in pieces]

    work = 27 * 2 * channels * channels * depth * 2
    space = 4 * channels * depth * share

    made = call(
        functools.partial(forward_kernel, groups, pairs, 0),
        many(2 * pairs, share + 6) + many(pairs - 1, share + 4),
        flat(fields[: pairs + 1]) + list(grads[: pairs - 1]) + [first_wide, second_wide],
        flops=work * (2 * pairs - 1) * share,
        moved=space * 4 * pairs,
    )
    hiddens, slopes, deltas = made[:pairs], made[pairs : 2 * pairs], made[2 * pairs :]
    made = call(
        functools.partial(forward_kernel, groups, 1, 1),
        many(2, share + 6) + many(1, share + 4),
        flat(fields[pairs:]) + [hiddens[-1], grads[-1], first_wide, second_wide],
        flops=work * 2 * share,
        moved=space * 6,
    )
    hiddens = list(hiddens) + [made[0]]
    slopes = list(slopes) + [made[1]]
    deltas = list(deltas) + [made[2]]
    delta_after = to_prev(deltas[0])
    delta_before = to_next(deltas[-1])

    raw = jax.ShapeDtypeStruct((extent, 7, size, 4 * channels), F32)
    total = pltpu.VMEM((6 * channels, 12 * channels), F32)
    (second_raw,) = call(
        functools.partial(second_kernel, share, pairs),
        [raw],
        hiddens + deltas,
        [total],
        flops=work * pairs * share,
        moved=space * 5,
    )
    later = call(
        functools.partial(back_kernel, pairs),
        many(pairs, share + 2),
        [second_back] + deltas + [delta_after] + slopes[1:],
        flops=work * pairs * share,
        moved=space * 3 * pairs,
    )
    first, keep, send = call(
        functools.partial(first_kernel, share, groups, pairs),
        many(1, share + 2) + [raw] * 2,
        [second_back, delta_before, deltas[0], slopes[0]]
        + list(later)
        + flat(fields)
        + [second_raw],
        [total],
        flops=work * (pairs + 1) * share,
        moved=space * 4 * pairs,
    )

    def stepped(value, stride, shift=0):
        if shift % extent == 0:
            return lax.ppermute(value, "slab", [(i, i ^ stride) for i in range(slabs)])
        pairs_of = []
        for i in range(slabs):
            for k in range(extent):
                there = (i ^ stride) * extent + (k + shift) % extent
                pairs_of.append((i * extent + k, there))
        return lax.ppermute(value, ("slab", "chan"), pairs_of)

    portion = jax.ShapeDtypeStruct(raw.shape[1:], F32)
    out_piece = jax.ShapeDtypeStruct((share, planes, size, depth), BF16)
    made = call(
        functools.partial(last_kernel, pairs),
        [out_piece] * extent,
        [first] + list(later) + [first_back],
        flops=work * pairs * share,
        moved=space * 2 * pairs,
    )
    plain = slabs & (slabs - 1) == 0 and slabs >= 4
    if plain:
        kept = call(split_kernel, [portion] * extent, [made[0], keep, stepped(send, 1)], loose=1)
        shares = [kept[0]] + [to_chan(kept[j], extent - j) for j in range(1, extent)]
        shares += [stepped(kept[j], 2, extent - j) for j in range(extent)]
        (mine,) = call(add_kernel, [portion], shares)
        made = [made[0]] + [relayed(value, mine) for value in made[1:]]
    pieces = [made[0]] + [None] * (extent - 1)
    for j in range(1, extent):
        pieces[extent - j] = to_chan(made[j], extent - j)
    if plain:
        stride = 4
        while stride < slabs:
            radix = 4 if slabs % (4 * stride) == 0 else 2
            got = [mine] + [stepped(mine, m * stride) for m in range(1, radix)]
            (mine,) = call(add_kernel, [portion], got)
            stride *= radix
        other = stepped(mine, 1)
    else:
        mine, other = keep[0], send[0]
        for j in range(1, extent):
            mine, other = mine + to_chan(keep[j], extent - j), other + to_chan(send[j], extent - j)
        even = lax.rem(lax.axis_index("slab"), 2) == 0
        mine, other = jnp.where(even, mine, other), jnp.where(even, other, mine)
        mine, other = lax.psum((mine, other), "slab")
        mine, other = jnp.where(even, mine, other), jnp.where(even, other, mine)
    first_grad, second_grad = call(
        functools.partial(finish_kernel, factor),
        [jax.ShapeDtypeStruct(by_tap, F32)] * 2,
        [mine, other],
    )
    first_grad, second_grad = (jnp.transpose(g, (1, 0, 2)) for g in (first_grad, second_grad))

    (input_grad,) = call(
        functools.partial(merge_kernel, extent),
        [jax.ShapeDtypeStruct(field.shape, BF16)],
        pieces,
        [pltpu.VMEM((rows * planes * size, depth), F32)],
        moved=4 * field.size,
    )
    return input_grad, first_grad, second_grad


def solution(mesh):
    placed = (
        P("chan", "slab", None, None),
        P(None, "slab", None, None),
        P("chan", None, None),
        P("chan", None, None),
    )
    return jax.shard_map(
        body,
        mesh=mesh,
        in_specs=placed,
        out_specs=(P("chan", "slab", None, None), P("chan", None, None), P("chan", None, None)),
        check_vma=False,
    )
```

```python
import functools
import math

import jax
import jax.numpy as jnp
from jax import lax
from jax.experimental import pallas as pl
from jax.experimental.pallas import tpu as pltpu
from jax.sharding import PartitionSpec as P

F32 = jnp.float32
BF16 = jnp.bfloat16
LIMIT = 16 * 1024 * 1024


def call(kernel, outs, args, scratch=(), flops=0, moved=0, loose=0, same=None):
    whole = pl.BlockSpec(memory_space=pltpu.VMEM)
    still = pl.BlockSpec(memory_space=pl.ANY)
    return pl.pallas_call(
        kernel,
        out_shape=outs,
        in_specs=[still] * loose + [whole] * (len(args) - loose),
        out_specs=[still if k in (same or {}).values() else whole for k in range(len(outs))],
        input_output_aliases=same or {},
        scratch_shapes=list(scratch),
        compiler_params=pltpu.CompilerParams(vmem_limit_bytes=LIMIT),
        cost_estimate=pl.CostEstimate(flops=flops, bytes_accessed=moved, transcendentals=0),
    )(*args)


def in_blocks(count, body):
    block = max(k for k in range(1, 8) if count % k == 0)
    if block < 4:
        block = min(count, 15)

    def several(r, _):
        for k in range(block):
            body(r * block + k)
        return 0

    lax.fori_loop(0, count // block, several, 0)
    for k in range(count // block * block, count):
        body(k)


def widened(x_ref, wide):
    count, planes, rows = x_ref.shape[:3]

    def widen(i):
        for x in range(planes):
            start = pl.multiple_of((i * planes + x) * rows, 8)
            wide[pl.ds(start, rows), :] = x_ref[i, x].astype(F32)

    in_blocks(count, widen)


def turn(wide, outs, shape, base, length):
    count, planes, rows = shape

    def one(f):
        y = lax.rem(base + f, rows)
        for x in range(planes):
            tile = wide[pl.ds(x * rows + y, count, stride=planes * rows), :]
            outs[x // 2][f, x % 2] = tile.astype(BF16)

    in_blocks(length, one)


def field_kernel(extent, margin, x_ref, *refs):
    outs, wide = refs[:-1], refs[-1]
    count, planes, rows = x_ref.shape[:3]
    pairs = planes // 2
    share = rows // extent
    widened(x_ref, wide)
    me = lax.axis_index("chan")
    for s in range(extent):
        base = lax.rem(me + s, extent) * share - margin + rows
        turn(
            wide,
            outs[s * pairs : (s + 1) * pairs],
            (count, planes, rows),
            base,
            share + 2 * margin,
        )


def pack_kernel(after, first, second, packed):
    del after
    blank = jnp.zeros(first.shape[1:], F32)
    for h in range(packed.shape[0]):
        parts = []
        for ref in (first, second):
            for t in (2 * h, 2 * h + 1):
                parts.append(ref[t].astype(F32) if t < ref.shape[0] else blank)
        packed[h] = jnp.concatenate(parts, axis=1).astype(BF16)


def grad_kernel(extent, margin, after, x_ref, *refs):
    del after
    outs, wide = refs[:-1], refs[-1]
    count, planes, rows = x_ref.shape[:3]
    share = rows // extent
    widened(x_ref, wide)
    base = lax.axis_index("chan") * share - margin + rows
    turn(wide, outs, (count, planes, rows), base, share + 2 * margin)


def matrix_kernel(extent, *refs):
    packs, outs = refs[:extent], refs[extent:]
    me = lax.axis_index("chan")
    halves = packs[0].shape[0]
    quarter = packs[0].shape[2] // 4
    taps = []
    turned = []
    for h in range(halves):
        tiles = [pack[h].astype(F32) for pack in packs]
        own = jnp.concatenate(tiles, axis=0)
        fixed = []
        for g in range(extent):
            place = lax.rem(me + extent - g, extent)
            tile = tiles[0]
            for j in range(1, extent):
                tile = jnp.where(place == j, tiles[j], tile)
            fixed.append(tile)
        both = jnp.concatenate(
            [own[:, : 2 * quarter], jnp.concatenate(fixed, axis=0)[:, 2 * quarter :]], axis=1
        )
        across = both.T
        for side in range(2):
            taps.append(
                [both[:, k * quarter : (k + 1) * quarter] for k in (side, side + 2)]
            )
            turned.append(
                [across[k * quarter : (k + 1) * quarter] for k in (side, side + 2)]
            )
    channels = quarter
    blank = jnp.zeros((channels, channels), F32)
    for k in range(2):
        for out, blocks, flip in ((outs[k], turned, False), (outs[2 + k], taps, True)):
            for e in range(3):
                for x in range(2):
                    chunks = []
                    for pair in range(2):
                        for b in range(3):
                            for side in range(2):
                                a = 2 * pair + side - x
                                t = 9 * a + 3 * b + e
                                inside = 0 <= a <= 2
                                t = 26 - t if flip else t
                                chunks.append(blocks[t][k] if inside else blank)
                    low = (2 * e + x) * channels
                    out[low : low + channels, :] = jnp.concatenate(chunks, axis=1).astype(BF16)


def stacked(refs, row, count):
    if len(refs) == 1:
        part = refs[0][pl.ds(row, count)]
        return part.reshape(-1, part.shape[-1])
    parts = [ref[row + b, x] for b in range(count) for x in range(2) for ref in refs]
    return jnp.concatenate(parts, axis=0)


def taps(weight, pairs, row):
    sides = []
    for p in range(len(pairs) - 1):
        for q in range(2):
            above = stacked(pairs[p], row + q, 3)
            below = stacked(pairs[p + 1], row + q, 3)
            sides.append(jnp.concatenate([above, below], axis=0))
    lifted = jnp.dot(weight, jnp.concatenate(sides, axis=1), preferred_element_type=F32)
    third = lifted.shape[0] // 3
    depth = sides[0].shape[1]
    sums = []
    for k in range(len(sides)):
        side = lifted[:, k * depth : (k + 1) * depth]
        sums.append(
            side[third : 2 * third]
            + pltpu.roll(side[:third], 1, 1)
            + pltpu.roll(side[2 * third :], depth - 1, 1)
        )
    return [sums[2 * p : 2 * p + 2] for p in range(len(pairs) - 1)]


def silu_parts(v):
    sig = jax.nn.sigmoid(v)
    return sig, sig * (1.0 + v * (1.0 - sig))


def forward_kernel(groups, fresh, ready, *refs):
    refs = list(refs)
    fields = [[refs.pop(0) for _ in range(groups)] for _ in range(fresh + 1)]
    hiddens = [refs.pop(0) for _ in range(ready)]
    count = fresh + ready - 1
    grads = [refs.pop(0) for _ in range(count)]
    first, second = refs.pop(0), refs.pop(0)
    made = [refs.pop(0) for _ in range(fresh)]
    slopes = [refs.pop(0) for _ in range(fresh)]
    deltas = refs
    hiddens = hiddens + made

    def one(r):
        row = 2 * r
        for p, sums in enumerate(taps(first[...], fields, row)):
            for q, v in enumerate(sums):
                sig, slope = silu_parts(v)
                shape = made[p].shape[1:]
                made[p][row + q] = (v * sig).astype(BF16).reshape(shape)
                slopes[p][row + q] = slope.astype(BF16).reshape(shape)

    in_blocks(made[0].shape[0] // 2, one)

    def two(r):
        row = 2 * r
        for p, sums in enumerate(taps(second[...], [[ref] for ref in hiddens], row)):
            for q, v in enumerate(sums):
                shape = deltas[p].shape[1:]
                out_grad = grads[p][row + q].astype(F32)
                slope = silu_parts(v)[1].reshape(shape)
                deltas[p][row + q] = (out_grad * slope).astype(BF16)

    if count > 0:
        in_blocks(deltas[0].shape[0] // 2, two)


def planes_of(pairs):
    return [(refs, x) for refs in pairs for x in range(2)]


def weight_loop(total, pieces, first_row, deltas, delta_row, count):
    blocks = [k for k in range(1, 13) if count // 2 % k == 0 and k * len(deltas) <= 12]
    together = max(blocks, default=1)

    def step(r, _):
        left, right = [], []
        for k in range(together):
            row = 2 * (r * together + k)
            for x, ((delta,), place) in enumerate(deltas):
                rows = []
                for q in range(2):
                    wide = delta[delta_row + row + q, place]
                    plain = wide.astype(F32)
                    depth = plain.shape[1]
                    rows += [
                        pltpu.roll(plain, depth - 1, 1).astype(BF16),
                        wide,
                        pltpu.roll(plain, 1, 1).astype(BF16),
                    ]
                left.append(jnp.concatenate(rows, axis=0))
                rows = []
                for refs, side in pieces[x : x + 3]:
                    for b in range(4):
                        for ref in refs:
                            rows.append(ref[first_row + row + b, side])
                right.append(jnp.concatenate(rows, axis=0))
        total[...] += lax.dot_general(
            jnp.concatenate(left, axis=1),
            jnp.concatenate(right, axis=1),
            (((1,), (1,)), ((), ())),
            preferred_element_type=F32,
        )
        return 0

    lax.fori_loop(0, count // 2 // together, step, 0)


def weight_fold(total, size):
    lanes = total.shape[0] // 2
    channels = total.shape[1] // 12
    upper, lower = total[:lanes, :].T, total[lanes:, :].T
    groups = []
    for g in range(channels // size):
        taps_of = []
        for a in range(3):
            for b in range(3):
                start = (4 * a + b) * channels + g * size
                part = (
                    upper[start : start + size]
                    + lower[start + channels : start + channels + size]
                )
                taps_of += [part[:, e * channels : (e + 1) * channels] for e in range(3)]
        blank = jnp.zeros((size, channels), F32)
        taps_of.append(blank)
        groups.append([jnp.concatenate(taps_of[4 * h : 4 * h + 4], axis=1) for h in range(7)])
    return groups


def second_kernel(share, pairs, *refs):
    refs = list(refs)
    hiddens = [[refs.pop(0)] for _ in range(pairs + 1)]
    deltas = [refs.pop(0) for _ in range(pairs)]
    raw, total = refs
    total[...] = jnp.zeros_like(total)
    weight_loop(total, planes_of(hiddens), 2, planes_of([[d] for d in deltas]), 2, share)
    for g, tiles in enumerate(weight_fold(total, raw.shape[2])):
        for h, tile in enumerate(tiles):
            raw[g, h] = tile


def first_deltas(weight, deltas, slopes, firsts):
    def one(r):
        row = 2 * r
        for p, sums in enumerate(taps(weight[...], [[delta] for delta in deltas], row)):
            for q, v in enumerate(sums):
                shape = firsts[p].shape[1:]
                slope = slopes[p][row + 2 + q].astype(F32)
                firsts[p][row + q] = (v.reshape(shape) * slope).astype(BF16)

    in_blocks(firsts[0].shape[0] // 2, one)


def back_kernel(share, groups, count, *refs):
    refs = list(refs)
    weight = refs.pop(0)
    deltas = [refs.pop(0) for _ in range(count + 1)]
    slopes = [refs.pop(0) for _ in range(count)]
    fields = [[refs.pop(0) for _ in range(groups)] for _ in range(count + 2)]
    firsts, total = refs[:-1], refs[-1]
    first_deltas(weight, deltas, slopes, firsts)
    total[...] = jnp.zeros_like(total)
    near = planes_of(fields)[2:-1]
    weight_loop(total, near, 3, planes_of([[ref] for ref in firsts])[:-1], 1, share)


def first_kernel(share, groups, after, *refs):
    del after
    refs = list(refs)
    weight = refs.pop(0)
    deltas = [refs.pop(0) for _ in range(2)]
    slope = refs.pop(0)
    fields = [[refs.pop(0) for _ in range(groups)] for _ in range(2)]
    later, second = refs.pop(0), refs.pop(0)
    first, keep, send, total = refs
    first_deltas(weight, deltas, [slope], [first])
    total[...] = later[...]
    weight_loop(total, planes_of(fields)[1:], 3, planes_of([[first]])[1:], 1, share)
    extent, halves, size = keep.shape[:3]
    me = lax.axis_index("chan")
    groups_of = weight_fold(total, size)

    def place(ours, theirs):
        for g, tiles in enumerate(groups_of):
            there = lax.rem(me + extent - g, extent)
            for h in range(halves):
                ours[g, h] = tiles[h]
                theirs[g, h] = second[there, h]

    odd = lax.rem(lax.axis_index("slab"), 2)

    @pl.when(odd == 0)
    def _():
        place(keep, send)

    @pl.when(odd == 1)
    def _():
        place(send, keep)


def last_kernel(pairs, *refs):
    refs = list(refs)
    firsts = [refs.pop(0) for _ in range(pairs + 1)]
    weight = refs.pop(0)
    outs = refs

    def one(r):
        row = 2 * r
        size = outs[0].shape[2]
        channels = len(outs) * size
        for p, sums in enumerate(taps(weight[...], [[first] for first in firsts], row)):
            for q, v in enumerate(sums):
                for x in range(2):
                    for j, out in enumerate(outs):
                        low = x * channels + j * size
                        out[row + q, 2 * p + x] = v[low : low + size].astype(BF16)

    in_blocks(outs[0].shape[0] // 2, one)


def finish_kernel(factor, mine, other, first, second):
    channels = first.shape[2]

    def place(ours, theirs):
        for out, sums in ((ours, mine), (theirs, other)):
            for t in range(27):
                low = t % 4 * channels
                out[t] = sums[t // 4, :, low : low + channels] * factor

    odd = lax.rem(lax.axis_index("slab"), 2)

    @pl.when(odd == 0)
    def _():
        place(first, second)

    @pl.when(odd == 1)
    def _():
        place(second, first)


def split_kernel(ahead, *refs):
    one, two, *outs = refs[ahead:]
    for g, out in enumerate(outs):
        out[...] = one[g] + two[g]


def add_kernel(*refs):
    values = [ref[...] for ref in refs[:-1]]
    while len(values) > 1:
        values = [sum(values[k + 1 : k + 2], values[k]) for k in range(0, len(values), 2)]
    refs[-1][...] = values[0]


def relay_kernel(*refs):
    pass


def merge_kernel(extent, *refs):
    pieces, out, wide = refs[1:-3], refs[-2], refs[-1]
    size, planes, rows = out.shape[:3]
    share = rows // extent
    me = lax.axis_index("chan")
    for j in range(extent):
        base = lax.rem(me + extent - j, extent) * share

        def widen(f, mine=pieces[j::extent], base=base):
            x = 0
            for piece in mine:
                for k in range(piece.shape[1]):
                    start = ((base + f) * planes + x) * size
                    start = pl.multiple_of(start, 8) if size % 8 == 0 else start
                    wide[pl.ds(start, size), :] = piece[f, k].astype(F32)
                    x += 1

        in_blocks(share, widen)

    def back(i):
        for x in range(planes):
            tile = wide[pl.ds(x * size + i, rows, stride=planes * size), :]
            out[i, x] = tile.astype(BF16)

    in_blocks(size, back)


def body(field, out_grad, first_weight, second_weight):
    extent = lax.axis_size("chan")
    slabs = lax.axis_size("slab")
    me = lax.axis_index("chan")
    size, planes, rows, depth = field.shape
    channels = size * extent
    pairs = planes // 2
    share = rows // extent
    factor = 1.0 / math.sqrt(planes * slabs * rows * depth)

    def to_chan(value, shift):
        return lax.ppermute(value, "chan", [(i, (i + shift) % extent) for i in range(extent)])

    def to_next(value):
        return lax.ppermute(value, "slab", [(i, (i + 1) % slabs) for i in range(slabs)])

    def to_prev(value):
        return lax.ppermute(value, "slab", [((i + 1) % slabs, i) for i in range(slabs)])

    def relayed(value, *others):
        shape = jax.ShapeDtypeStruct(value.shape, value.dtype)
        early = [value, *others]
        return call(relay_kernel, [shape], early, loose=len(early), same={0: 0})[0]

    piece = jax.ShapeDtypeStruct((share + 8, 2, size, depth), BF16)
    by_tap = (27, size, channels)
    made = call(
        functools.partial(field_kernel, extent, 4),
        [piece] * (extent * pairs),
        [field],
        [pltpu.VMEM((size * planes * rows, depth), F32)],
        moved=field.size * 6,
    )
    (pack,) = call(
        pack_kernel,
        [jax.ShapeDtypeStruct((14, size, 4 * channels), BF16)],
        [made[-1], jnp.transpose(first_weight, (1, 0, 2)), jnp.transpose(second_weight, (1, 0, 2))],
        loose=1,
    )
    packs = [pack] + [to_chan(pack, j) for j in range(1, extent)]
    parts = [list(made[:pairs])]
    whole = size % 16 == 0
    own_before, own_after = [], []
    if whole:
        for p in sorted({0, pairs - 1}):
            parts[0][p] = relayed(parts[0][p], pack)
        own_before, own_after = [to_next(parts[0][-1])], [to_prev(parts[0][0])]
    for j in range(1, extent):
        sent = list(made[j * pairs : (j + 1) * pairs])
        if whole and pairs > 1:
            sent[0] = relayed(sent[0], *packs[1:])
        parts.append([to_chan(value, j) for value in sent])
    matrix = jax.ShapeDtypeStruct((6 * channels, 12 * channels), BF16)
    first_wide, second_wide, first_back, second_back = call(
        functools.partial(matrix_kernel, extent),
        [matrix] * 4,
        packs,
        moved=matrix.size * 8,
    )
    arrived = parts[-1]
    grad_piece = jax.ShapeDtypeStruct((share + 4, 2, channels, depth), BF16)
    grads = call(
        functools.partial(grad_kernel, extent, 2),
        [grad_piece] * pairs,
        [own_after[0] if whole else arrived[-1], out_grad],
        [pltpu.VMEM((channels * planes * rows, depth), F32)],
        moved=out_grad.size * 4,
        loose=1,
    )
    if extent > 1 and pairs > 1:
        arrived[0] = relayed(arrived[0], grads[0], first_wide)
    by_pair = [[parts[j][p] for j in range(extent)] for p in range(pairs)]
    groups = extent
    if not whole:
        by_pair = [[jnp.concatenate(pieces, axis=2)] for pieces in by_pair]
        groups = 1
    before = own_before + [to_next(piece) for piece in by_pair[-1][len(own_before) :]]
    after = own_after + [to_prev(piece) for piece in by_pair[0][len(own_after) :]]
    fields = [before] + by_pair + [after]

    def many(count, rows_each):
        return [jax.ShapeDtypeStruct((rows_each, 2, channels, depth), BF16)] * count

    def flat(lists):
        return [piece for pieces in lists for piece in pieces]

    work = 27 * 2 * channels * channels * depth * 2
    space = 4 * channels * depth * share

    made = call(
        functools.partial(forward_kernel, groups, pairs, 0),
        many(2 * pairs, share + 6) + many(pairs - 1, share + 4),
        flat(fields[: pairs + 1]) + list(grads[: pairs - 1]) + [first_wide, second_wide],
        flops=work * (2 * pairs - 1) * share,
        moved=space * 4 * pairs,
    )
    hiddens, slopes, deltas = made[:pairs], made[pairs : 2 * pairs], made[2 * pairs :]
    made = call(
        functools.partial(forward_kernel, groups, 1, 1),
        many(2, share + 6) + many(1, share + 4),
        flat(fields[pairs:]) + [hiddens[-1], grads[-1], first_wide, second_wide],
        flops=work * 2 * share,
        moved=space * 6,
    )
    hiddens = list(hiddens) + [made[0]]
    slopes = list(slopes) + [made[1]]
    deltas = list(deltas) + [made[2]]
    delta_after = to_prev(deltas[0])
    delta_before = to_next(deltas[-1])

    raw = jax.ShapeDtypeStruct((extent, 7, size, 4 * channels), F32)
    total = pltpu.VMEM((6 * channels, 12 * channels), F32)
    (second_raw,) = call(
        functools.partial(second_kernel, share, pairs),
        [raw],
        hiddens + deltas,
        [total],
        flops=work * pairs * share,
        moved=space * 5,
    )
    partial_sum = jax.ShapeDtypeStruct((6 * channels, 12 * channels), F32)
    made = call(
        functools.partial(back_kernel, share, groups, pairs),
        many(pairs, share + 2) + [partial_sum],
        [second_back] + deltas + [delta_after] + slopes[1:] + flat(fields),
        flops=work * (2 * pairs - 1) * share,
        moved=space * 6 * pairs,
    )
    later, partial_total = list(made[:-1]), made[-1]

    def field_grad(firsts):
        count = len(firsts) - 1
        return list(
            call(
                functools.partial(last_kernel, count),
                [jax.ShapeDtypeStruct((share, 2 * count, size, depth), BF16)] * extent,
                firsts + [first_back],
                flops=work * count * share,
                moved=space * 2 * count,
            )
        )

    def exchanged(made):
        pieces = [made[0]] + [None] * (extent - 1)
        for j in range(1, extent):
            pieces[extent - j] = to_chan(made[j], extent - j)
        return pieces

    pieces, early = [], [later[0]]
    if pairs > 1:
        early = field_grad(later)
        pieces = exchanged(early)
    first, keep, send = call(
        functools.partial(first_kernel, share, groups),
        many(1, share + 2) + [raw] * 2,
        [early[0], second_back, delta_before, deltas[0], slopes[0]]
        + flat(fields[0:2])
        + [partial_total, second_raw],
        [total],
        flops=work * 2 * share,
        moved=space * 6,
        loose=1,
    )

    def stepped(value, stride, shift=0):
        if shift % extent == 0:
            return lax.ppermute(value, "slab", [(i, i ^ stride) for i in range(slabs)])
        pairs_of = []
        for i in range(slabs):
            for k in range(extent):
                there = (i ^ stride) * extent + (k + shift) % extent
                pairs_of.append((i * extent + k, there))
        return lax.ppermute(value, ("slab", "chan"), pairs_of)

    portion = jax.ShapeDtypeStruct(raw.shape[1:], F32)
    made = field_grad([first, later[0]])
    plain = slabs & (slabs - 1) == 0 and slabs >= 4
    if plain:
        ahead = made[:1] + pieces[1:2]
        kept = call(
            functools.partial(split_kernel, len(ahead)),
            [portion] * extent,
            ahead + [keep, stepped(send, 1)],
            loose=len(ahead),
        )
        shares = [kept[0]] + [to_chan(kept[j], extent - j) for j in range(1, extent)]
        shares += [stepped(kept[j], 2, extent - j) for j in range(extent)]
        (mine,) = call(add_kernel, [portion], shares)
        made = [made[0]] + [relayed(value, mine) for value in made[1:]]
    pieces = exchanged(made) + pieces

    def merged(value):
        return call(
            functools.partial(merge_kernel, extent),
            [
                jax.ShapeDtypeStruct(value.shape, value.dtype),
                jax.ShapeDtypeStruct(field.shape, BF16),
            ],
            [value] + pieces,
            [pltpu.VMEM((rows * planes * size, depth), F32)],
            moved=4 * field.size,
            loose=1,
            same={0: 0},
        )

    if plain:
        stride = 4
        while stride < slabs:
            radix = 4 if slabs % (4 * stride) == 0 else 2
            got = [mine] + [stepped(mine, m * stride) for m in range(1, radix)]
            (mine,) = call(add_kernel, [portion], got)
            stride *= radix
        mine, input_grad = merged(mine)
        other = stepped(mine, 1)
    else:
        mine, other = keep[0], send[0]
        for j in range(1, extent):
            mine, other = mine + to_chan(keep[j], extent - j), other + to_chan(send[j], extent - j)
        even = lax.rem(lax.axis_index("slab"), 2) == 0
        mine, other = jnp.where(even, mine, other), jnp.where(even, other, mine)
        mine, other = lax.psum((mine, other), "slab")
        mine, input_grad = merged(mine)
        mine, other = jnp.where(even, mine, other), jnp.where(even, other, mine)
    first_grad, second_grad = call(
        functools.partial(finish_kernel, factor),
        [jax.ShapeDtypeStruct(by_tap, F32)] * 2,
        [mine, other],
    )
    first_grad, second_grad = (jnp.transpose(g, (1, 0, 2)) for g in (first_grad, second_grad))
    return input_grad, first_grad, second_grad


def solution(mesh):
    placed = (
        P("chan", "slab", None, None),
        P(None, "slab", None, None),
        P("chan", None, None),
        P("chan", None, None),
    )
    return jax.shard_map(
        body,
        mesh=mesh,
        in_specs=placed,
        out_specs=(P("chan", "slab", None, None), P("chan", None, None), P("chan", None, None)),
        check_vma=False,
    )
```

```python
import functools
import math

import jax
import jax.numpy as jnp
from jax import lax
from jax.experimental import pallas as pl
from jax.experimental.pallas import tpu as pltpu
from jax.sharding import PartitionSpec as P

F32 = jnp.float32
BF16 = jnp.bfloat16
LIMIT = 16 * 1024 * 1024


def call(kernel, outs, args, scratch=(), flops=0, moved=0, loose=0, same=None):
    whole = pl.BlockSpec(memory_space=pltpu.VMEM)
    still = pl.BlockSpec(memory_space=pl.ANY)
    return pl.pallas_call(
        kernel,
        out_shape=outs,
        in_specs=[still] * loose + [whole] * (len(args) - loose),
        out_specs=[still if k in (same or {}).values() else whole for k in range(len(outs))],
        input_output_aliases=same or {},
        scratch_shapes=list(scratch),
        compiler_params=pltpu.CompilerParams(vmem_limit_bytes=LIMIT),
        cost_estimate=pl.CostEstimate(flops=flops, bytes_accessed=moved, transcendentals=0),
    )(*args)


def in_blocks(count, body):
    block = max(k for k in range(1, 8) if count % k == 0)
    if block < 4:
        block = min(count, 15)

    def several(r, _):
        for k in range(block):
            body(r * block + k)
        return 0

    lax.fori_loop(0, count // block, several, 0)
    for k in range(count // block * block, count):
        body(k)


def widened(x_ref, wide):
    count, planes, rows = x_ref.shape[:3]

    def widen(i):
        for x in range(planes):
            start = pl.multiple_of((i * planes + x) * rows, 8)
            wide[pl.ds(start, rows), :] = x_ref[i, x].astype(F32)

    in_blocks(count, widen)


def turn(wide, outs, shape, base, length):
    count, planes, rows = shape

    def one(f):
        y = lax.rem(base + f, rows)
        for x in range(planes):
            tile = wide[pl.ds(x * rows + y, count, stride=planes * rows), :]
            outs[x // 2][f, x % 2] = tile.astype(BF16)

    in_blocks(length, one)


def field_kernel(extent, margin, x_ref, *refs):
    outs, wide = refs[:-1], refs[-1]
    count, planes, rows = x_ref.shape[:3]
    pairs = planes // 2
    share = rows // extent
    widened(x_ref, wide)
    me = lax.axis_index("chan")
    for s in range(extent):
        base = lax.rem(me + s, extent) * share - margin + rows
        turn(
            wide,
            outs[s * pairs : (s + 1) * pairs],
            (count, planes, rows),
            base,
            share + 2 * margin,
        )


def pack_kernel(after, first, second, packed):
    del after
    blank = jnp.zeros(first.shape[1:], F32)
    for h in range(packed.shape[0]):
        parts = []
        for ref in (first, second):
            for t in (2 * h, 2 * h + 1):
                parts.append(ref[t].astype(F32) if t < ref.shape[0] else blank)
        packed[h] = jnp.concatenate(parts, axis=1).astype(BF16)


def grad_kernel(extent, margin, after, x_ref, *refs):
    del after
    outs, wide = refs[:-1], refs[-1]
    count, planes, rows = x_ref.shape[:3]
    share = rows // extent
    widened(x_ref, wide)
    base = lax.axis_index("chan") * share - margin + rows
    turn(wide, outs, (count, planes, rows), base, share + 2 * margin)


def matrix_kernel(extent, *refs):
    packs, outs = refs[:extent], refs[extent:]
    me = lax.axis_index("chan")
    halves = packs[0].shape[0]
    quarter = packs[0].shape[2] // 4
    taps = []
    turned = []
    for h in range(halves):
        tiles = [pack[h].astype(F32) for pack in packs]
        own = jnp.concatenate(tiles, axis=0)
        fixed = []
        for g in range(extent):
            place = lax.rem(me + extent - g, extent)
            tile = tiles[0]
            for j in range(1, extent):
                tile = jnp.where(place == j, tiles[j], tile)
            fixed.append(tile)
        both = jnp.concatenate(
            [own[:, : 2 * quarter], jnp.concatenate(fixed, axis=0)[:, 2 * quarter :]], axis=1
        )
        across = both.T
        for side in range(2):
            taps.append(
                [both[:, k * quarter : (k + 1) * quarter] for k in (side, side + 2)]
            )
            turned.append(
                [across[k * quarter : (k + 1) * quarter] for k in (side, side + 2)]
            )
    channels = quarter
    blank = jnp.zeros((channels, channels), F32)
    for k in range(2):
        for out, blocks, flip in ((outs[k], turned, False), (outs[2 + k], taps, True)):
            for e in range(3):
                for x in range(2):
                    chunks = []
                    for pair in range(2):
                        for b in range(3):
                            for side in range(2):
                                a = 2 * pair + side - x
                                t = 9 * a + 3 * b + e
                                inside = 0 <= a <= 2
                                t = 26 - t if flip else t
                                chunks.append(blocks[t][k] if inside else blank)
                    low = (2 * e + x) * channels
                    out[low : low + channels, :] = jnp.concatenate(chunks, axis=1).astype(BF16)


def stacked(refs, row, count):
    if len(refs) == 1:
        part = refs[0][pl.ds(row, count)]
        return part.reshape(-1, part.shape[-1])
    parts = [ref[row + b, x] for b in range(count) for x in range(2) for ref in refs]
    return jnp.concatenate(parts, axis=0)


def taps(weight, pairs, row):
    sides = []
    for p in range(len(pairs) - 1):
        for q in range(2):
            above = stacked(pairs[p], row + q, 3)
            below = stacked(pairs[p + 1], row + q, 3)
            sides.append(jnp.concatenate([above, below], axis=0))
    lifted = jnp.dot(weight, jnp.concatenate(sides, axis=1), preferred_element_type=F32)
    third = lifted.shape[0] // 3
    depth = sides[0].shape[1]
    sums = []
    for k in range(len(sides)):
        side = lifted[:, k * depth : (k + 1) * depth]
        sums.append(
            side[third : 2 * third]
            + pltpu.roll(side[:third], 1, 1)
            + pltpu.roll(side[2 * third :], depth - 1, 1)
        )
    return [sums[2 * p : 2 * p + 2] for p in range(len(pairs) - 1)]


def silu_parts(v):
    sig = jax.nn.sigmoid(v)
    return sig, sig * (1.0 + v * (1.0 - sig))


def forward_kernel(groups, fresh, ready, *refs):
    refs = list(refs)
    fields = [[refs.pop(0) for _ in range(groups)] for _ in range(fresh + 1)]
    hiddens = [refs.pop(0) for _ in range(ready)]
    count = fresh + ready - 1
    grads = [refs.pop(0) for _ in range(count)]
    first, second = refs.pop(0), refs.pop(0)
    made = [refs.pop(0) for _ in range(fresh)]
    slopes = [refs.pop(0) for _ in range(fresh)]
    deltas = refs
    hiddens = hiddens + made

    def one(r):
        row = 2 * r
        for p, sums in enumerate(taps(first[...], fields, row)):
            for q, v in enumerate(sums):
                sig, slope = silu_parts(v)
                shape = made[p].shape[1:]
                made[p][row + q] = (v * sig).astype(BF16).reshape(shape)
                slopes[p][row + q] = slope.astype(BF16).reshape(shape)

    in_blocks(made[0].shape[0] // 2, one)

    def two(r):
        row = 2 * r
        for p, sums in enumerate(taps(second[...], [[ref] for ref in hiddens], row)):
            for q, v in enumerate(sums):
                shape = deltas[p].shape[1:]
                out_grad = grads[p][row + q].astype(F32)
                slope = silu_parts(v)[1].reshape(shape)
                deltas[p][row + q] = (out_grad * slope).astype(BF16)

    if count > 0:
        in_blocks(deltas[0].shape[0] // 2, two)


def planes_of(pairs):
    return [(refs, x) for refs in pairs for x in range(2)]


def weight_loop(total, pieces, first_row, deltas, delta_row, count):
    blocks = [k for k in range(1, 13) if count // 2 % k == 0 and k * len(deltas) <= 12]
    together = max(blocks, default=1)

    def step(r, _):
        left, right = [], []
        for k in range(together):
            row = 2 * (r * together + k)
            for x, ((delta,), place) in enumerate(deltas):
                rows = []
                for q in range(2):
                    wide = delta[delta_row + row + q, place]
                    plain = wide.astype(F32)
                    depth = plain.shape[1]
                    rows += [
                        pltpu.roll(plain, depth - 1, 1).astype(BF16),
                        wide,
                        pltpu.roll(plain, 1, 1).astype(BF16),
                    ]
                left.append(jnp.concatenate(rows, axis=0))
                rows = []
                for refs, side in pieces[x : x + 3]:
                    for b in range(4):
                        for ref in refs:
                            rows.append(ref[first_row + row + b, side])
                right.append(jnp.concatenate(rows, axis=0))
        total[...] += lax.dot_general(
            jnp.concatenate(left, axis=1),
            jnp.concatenate(right, axis=1),
            (((1,), (1,)), ((), ())),
            preferred_element_type=F32,
        )
        return 0

    lax.fori_loop(0, count // 2 // together, step, 0)


def weight_fold(total, size):
    lanes = total.shape[0] // 2
    channels = total.shape[1] // 12
    upper, lower = total[:lanes, :].T, total[lanes:, :].T
    groups = []
    for g in range(channels // size):
        taps_of = []
        for a in range(3):
            for b in range(3):
                start = (4 * a + b) * channels + g * size
                part = (
                    upper[start : start + size]
                    + lower[start + channels : start + channels + size]
                )
                taps_of += [part[:, e * channels : (e + 1) * channels] for e in range(3)]
        blank = jnp.zeros((size, channels), F32)
        taps_of.append(blank)
        groups.append([jnp.concatenate(taps_of[4 * h : 4 * h + 4], axis=1) for h in range(7)])
    return groups


def second_kernel(share, pairs, *refs):
    refs = list(refs)
    hiddens = [[refs.pop(0)] for _ in range(pairs + 1)]
    deltas = [refs.pop(0) for _ in range(pairs)]
    raw, total = refs
    total[...] = jnp.zeros_like(total)
    weight_loop(total, planes_of(hiddens), 2, planes_of([[d] for d in deltas]), 2, share)
    for g, tiles in enumerate(weight_fold(total, raw.shape[2])):
        for h, tile in enumerate(tiles):
            raw[g, h] = tile


def first_deltas(weight, deltas, slopes, firsts):
    def one(r):
        row = 2 * r
        for p, sums in enumerate(taps(weight[...], [[delta] for delta in deltas], row)):
            for q, v in enumerate(sums):
                shape = firsts[p].shape[1:]
                slope = slopes[p][row + 2 + q].astype(F32)
                firsts[p][row + q] = (v.reshape(shape) * slope).astype(BF16)

    in_blocks(firsts[0].shape[0] // 2, one)


def back_kernel(share, groups, count, *refs):
    refs = list(refs)
    weight = refs.pop(0)
    deltas = [refs.pop(0) for _ in range(count + 1)]
    slopes = [refs.pop(0) for _ in range(count)]
    fields = [[refs.pop(0) for _ in range(groups)] for _ in range(count + 2)]
    firsts, total = refs[:-1], refs[-1]
    first_deltas(weight, deltas, slopes, firsts)
    total[...] = jnp.zeros_like(total)
    near = planes_of(fields)[2:-1]
    weight_loop(total, near, 3, planes_of([[ref] for ref in firsts])[:-1], 1, share)


def first_kernel(share, groups, after, *refs):
    del after
    refs = list(refs)
    weight = refs.pop(0)
    deltas = [refs.pop(0) for _ in range(2)]
    slope = refs.pop(0)
    fields = [[refs.pop(0) for _ in range(groups)] for _ in range(2)]
    later, second = refs.pop(0), refs.pop(0)
    first, keep, send, total = refs
    first_deltas(weight, deltas, [slope], [first])
    total[...] = later[...]
    weight_loop(total, planes_of(fields)[1:], 3, planes_of([[first]])[1:], 1, share)
    extent, halves, size = keep.shape[:3]
    me = lax.axis_index("chan")
    groups_of = weight_fold(total, size)

    def place(ours, theirs):
        for g, tiles in enumerate(groups_of):
            there = lax.rem(me + extent - g, extent)
            for h in range(halves):
                ours[g, h] = tiles[h]
                theirs[g, h] = second[there, h]

    odd = lax.rem(lax.axis_index("slab"), 2)

    @pl.when(odd == 0)
    def _():
        place(keep, send)

    @pl.when(odd == 1)
    def _():
        place(send, keep)


def last_kernel(pairs, *refs):
    refs = list(refs)
    firsts = [refs.pop(0) for _ in range(pairs + 1)]
    weight = refs.pop(0)
    outs = refs

    def one(r):
        row = 2 * r
        size = outs[0].shape[2]
        channels = len(outs) * size
        for p, sums in enumerate(taps(weight[...], [[first] for first in firsts], row)):
            for q, v in enumerate(sums):
                for x in range(2):
                    for j, out in enumerate(outs):
                        low = x * channels + j * size
                        out[row + q, 2 * p + x] = v[low : low + size].astype(BF16)

    in_blocks(outs[0].shape[0] // 2, one)


def finish_kernel(factor, mine, other, first, second):
    channels = first.shape[2]

    def place(ours, theirs):
        for out, sums in ((ours, mine), (theirs, other)):
            for t in range(27):
                low = t % 4 * channels
                out[t] = sums[t // 4, :, low : low + channels] * factor

    odd = lax.rem(lax.axis_index("slab"), 2)

    @pl.when(odd == 0)
    def _():
        place(first, second)

    @pl.when(odd == 1)
    def _():
        place(second, first)


def split_kernel(ahead, *refs):
    one, two, *outs = refs[ahead:]
    for g, out in enumerate(outs):
        out[...] = one[g] + two[g]


def add_kernel(*refs):
    values = [ref[...] for ref in refs[:-1]]
    while len(values) > 1:
        values = [sum(values[k + 1 : k + 2], values[k]) for k in range(0, len(values), 2)]
    refs[-1][...] = values[0]


def relay_kernel(*refs):
    pass


def merge_kernel(extent, *refs):
    pieces, out, wide = refs[1:-3], refs[-2], refs[-1]
    size, planes, rows = out.shape[:3]
    share = rows // extent
    me = lax.axis_index("chan")
    for j in range(extent):
        base = lax.rem(me + extent - j, extent) * share

        def widen(f, mine=pieces[j::extent], base=base):
            x = 0
            for piece in mine:
                for k in range(piece.shape[1]):
                    start = ((base + f) * planes + x) * size
                    start = pl.multiple_of(start, 8) if size % 8 == 0 else start
                    wide[pl.ds(start, size), :] = piece[f, k].astype(F32)
                    x += 1

        in_blocks(share, widen)

    def back(i):
        for x in range(planes):
            tile = wide[pl.ds(x * size + i, rows, stride=planes * size), :]
            out[i, x] = tile.astype(BF16)

    in_blocks(size, back)


def body(field, out_grad, first_weight, second_weight):
    extent = lax.axis_size("chan")
    slabs = lax.axis_size("slab")
    me = lax.axis_index("chan")
    size, planes, rows, depth = field.shape
    channels = size * extent
    pairs = planes // 2
    share = rows // extent
    factor = 1.0 / math.sqrt(planes * slabs * rows * depth)

    def to_chan(value, shift):
        return lax.ppermute(value, "chan", [(i, (i + shift) % extent) for i in range(extent)])

    def to_next(value):
        return lax.ppermute(value, "slab", [(i, (i + 1) % slabs) for i in range(slabs)])

    def to_prev(value):
        return lax.ppermute(value, "slab", [((i + 1) % slabs, i) for i in range(slabs)])

    def relayed(value, *others):
        shape = jax.ShapeDtypeStruct(value.shape, value.dtype)
        early = [value, *others]
        return call(relay_kernel, [shape], early, loose=len(early), same={0: 0})[0]

    piece = jax.ShapeDtypeStruct((share + 8, 2, size, depth), BF16)
    by_tap = (27, size, channels)
    made = call(
        functools.partial(field_kernel, extent, 4),
        [piece] * (extent * pairs),
        [field],
        [pltpu.VMEM((size * planes * rows, depth), F32)],
        moved=field.size * 6,
    )
    (pack,) = call(
        pack_kernel,
        [jax.ShapeDtypeStruct((14, size, 4 * channels), BF16)],
        [made[-1], jnp.transpose(first_weight, (1, 0, 2)), jnp.transpose(second_weight, (1, 0, 2))],
        loose=1,
    )
    packs = [pack] + [to_chan(pack, j) for j in range(1, extent)]
    parts = [list(made[:pairs])]
    whole = size % 16 == 0
    own_before, own_after = [], []
    if whole:
        own_before, own_after = [to_next(parts[0][-1])], [to_prev(parts[0][0])]
    for j in range(1, extent):
        sent = list(made[j * pairs : (j + 1) * pairs])
        if whole and pairs > 1:
            sent[0] = relayed(sent[0], *own_before, *packs[1:])
        parts.append([to_chan(value, j) for value in sent])
    grad_piece = jax.ShapeDtypeStruct((share + 4, 2, channels, depth), BF16)
    grads = call(
        functools.partial(grad_kernel, extent, 2),
        [grad_piece] * pairs,
        [own_after[0] if whole else pack, out_grad],
        [pltpu.VMEM((channels * planes * rows, depth), F32)],
        moved=out_grad.size * 4,
        loose=1,
    )
    matrix = jax.ShapeDtypeStruct((6 * channels, 12 * channels), BF16)
    first_wide, second_wide, first_back, second_back = call(
        functools.partial(matrix_kernel, extent),
        [matrix] * 4,
        packs,
        moved=matrix.size * 8,
    )
    arrived = parts[-1]
    if extent > 1 and pairs > 1:
        arrived[0] = relayed(arrived[0], grads[0], first_wide)
    by_pair = [[parts[j][p] for j in range(extent)] for p in range(pairs)]
    groups = extent
    if not whole:
        by_pair = [[jnp.concatenate(pieces, axis=2)] for pieces in by_pair]
        groups = 1
    before = own_before + [to_next(piece) for piece in by_pair[-1][len(own_before) :]]
    after = own_after + [to_prev(piece) for piece in by_pair[0][len(own_after) :]]
    fields = [before] + by_pair + [after]

    def many(count, rows_each):
        return [jax.ShapeDtypeStruct((rows_each, 2, channels, depth), BF16)] * count

    def flat(lists):
        return [piece for pieces in lists for piece in pieces]

    work = 27 * 2 * channels * channels * depth * 2
    space = 4 * channels * depth * share

    made = call(
        functools.partial(forward_kernel, groups, pairs, 0),
        many(2 * pairs, share + 6) + many(pairs - 1, share + 4),
        flat(fields[: pairs + 1]) + list(grads[: pairs - 1]) + [first_wide, second_wide],
        flops=work * (2 * pairs - 1) * share,
        moved=space * 4 * pairs,
    )
    hiddens, slopes, deltas = made[:pairs], made[pairs : 2 * pairs], made[2 * pairs :]
    made = call(
        functools.partial(forward_kernel, groups, 1, 1),
        many(2, share + 6) + many(1, share + 4),
        flat(fields[pairs:]) + [hiddens[-1], grads[-1], first_wide, second_wide],
        flops=work * 2 * share,
        moved=space * 6,
    )
    hiddens = list(hiddens) + [made[0]]
    slopes = list(slopes) + [made[1]]
    deltas = list(deltas) + [made[2]]
    delta_after = to_prev(deltas[0])
    delta_before = to_next(deltas[-1])

    raw = jax.ShapeDtypeStruct((extent, 7, size, 4 * channels), F32)
    total = pltpu.VMEM((6 * channels, 12 * channels), F32)
    (second_raw,) = call(
        functools.partial(second_kernel, share, pairs),
        [raw],
        hiddens + deltas,
        [total],
        flops=work * pairs * share,
        moved=space * 5,
    )
    partial_sum = jax.ShapeDtypeStruct((6 * channels, 12 * channels), F32)
    made = call(
        functools.partial(back_kernel, share, groups, pairs),
        many(pairs, share + 2) + [partial_sum],
        [second_back] + deltas + [delta_after] + slopes[1:] + flat(fields),
        flops=work * (2 * pairs - 1) * share,
        moved=space * 6 * pairs,
    )
    later, partial_total = list(made[:-1]), made[-1]

    def field_grad(firsts):
        count = len(firsts) - 1
        return list(
            call(
                functools.partial(last_kernel, count),
                [jax.ShapeDtypeStruct((share, 2 * count, size, depth), BF16)] * extent,
                firsts + [first_back],
                flops=work * count * share,
                moved=space * 2 * count,
            )
        )

    def exchanged(made):
        pieces = [made[0]] + [None] * (extent - 1)
        for j in range(1, extent):
            pieces[extent - j] = to_chan(made[j], extent - j)
        return pieces

    pieces, early = [], [later[0]]
    if pairs > 1:
        early = field_grad(later)
        pieces = exchanged(early)
    first, keep, send = call(
        functools.partial(first_kernel, share, groups),
        many(1, share + 2) + [raw] * 2,
        [early[0], second_back, delta_before, deltas[0], slopes[0]]
        + flat(fields[0:2])
        + [partial_total, second_raw],
        [total],
        flops=work * 2 * share,
        moved=space * 6,
        loose=1,
    )

    def stepped(value, stride, shift=0):
        if shift % extent == 0:
            return lax.ppermute(value, "slab", [(i, i ^ stride) for i in range(slabs)])
        pairs_of = []
        for i in range(slabs):
            for k in range(extent):
                there = (i ^ stride) * extent + (k + shift) % extent
                pairs_of.append((i * extent + k, there))
        return lax.ppermute(value, ("slab", "chan"), pairs_of)

    portion = jax.ShapeDtypeStruct(raw.shape[1:], F32)
    made = field_grad([first, later[0]])
    plain = slabs & (slabs - 1) == 0 and slabs >= 4
    if plain:
        ahead = made[:1] + pieces[1:2]
        kept = call(
            functools.partial(split_kernel, len(ahead)),
            [portion] * extent,
            ahead + [keep, stepped(send, 1)],
            loose=len(ahead),
        )
        shares = [kept[0]] + [to_chan(kept[j], extent - j) for j in range(1, extent)]
        shares += [stepped(kept[j], 2, extent - j) for j in range(extent)]
        (mine,) = call(add_kernel, [portion], shares)
        made = [made[0]] + [relayed(value, mine) for value in made[1:]]
    pieces = exchanged(made) + pieces

    def merged(value):
        return call(
            functools.partial(merge_kernel, extent),
            [
                jax.ShapeDtypeStruct(value.shape, value.dtype),
                jax.ShapeDtypeStruct(field.shape, BF16),
            ],
            [value] + pieces,
            [pltpu.VMEM((rows * planes * size, depth), F32)],
            moved=4 * field.size,
            loose=1,
            same={0: 0},
        )

    if plain:
        stride = 4
        while stride < slabs:
            radix = 4 if slabs % (4 * stride) == 0 else 2
            got = [mine] + [stepped(mine, m * stride) for m in range(1, radix)]
            (mine,) = call(add_kernel, [portion], got)
            stride *= radix
        mine, input_grad = merged(mine)
        other = stepped(mine, 1)
    else:
        mine, other = keep[0], send[0]
        for j in range(1, extent):
            mine, other = mine + to_chan(keep[j], extent - j), other + to_chan(send[j], extent - j)
        even = lax.rem(lax.axis_index("slab"), 2) == 0
        mine, other = jnp.where(even, mine, other), jnp.where(even, other, mine)
        mine, other = lax.psum((mine, other), "slab")
        mine, input_grad = merged(mine)
        mine, other = jnp.where(even, mine, other), jnp.where(even, other, mine)
    first_grad, second_grad = call(
        functools.partial(finish_kernel, factor),
        [jax.ShapeDtypeStruct(by_tap, F32)] * 2,
        [mine, other],
    )
    first_grad, second_grad = (jnp.transpose(g, (1, 0, 2)) for g in (first_grad, second_grad))
    return input_grad, first_grad, second_grad


def solution(mesh):
    placed = (
        P("chan", "slab", None, None),
        P(None, "slab", None, None),
        P("chan", None, None),
        P("chan", None, None),
    )
    return jax.shard_map(
        body,
        mesh=mesh,
        in_specs=placed,
        out_specs=(P("chan", "slab", None, None), P("chan", None, None), P("chan", None, None)),
        check_vma=False,
    )
```

```python
import functools
import math

import jax
import jax.numpy as jnp
from jax import lax
from jax.experimental import pallas as pl
from jax.experimental.pallas import tpu as pltpu
from jax.sharding import PartitionSpec as P

F32 = jnp.float32
BF16 = jnp.bfloat16
LIMIT = 16 * 1024 * 1024


def call(kernel, outs, args, scratch=(), flops=0, moved=0, loose=0, same=None):
    whole = pl.BlockSpec(memory_space=pltpu.VMEM)
    still = pl.BlockSpec(memory_space=pl.ANY)
    return pl.pallas_call(
        kernel,
        out_shape=outs,
        in_specs=[still] * loose + [whole] * (len(args) - loose),
        out_specs=[still if k in (same or {}).values() else whole for k in range(len(outs))],
        input_output_aliases=same or {},
        scratch_shapes=list(scratch),
        compiler_params=pltpu.CompilerParams(vmem_limit_bytes=LIMIT),
        cost_estimate=pl.CostEstimate(flops=flops, bytes_accessed=moved, transcendentals=0),
    )(*args)


def in_blocks(count, body):
    block = max(k for k in range(1, 8) if count % k == 0)
    if block < 4:
        block = min(count, 15)

    def several(r, _):
        for k in range(block):
            body(r * block + k)
        return 0

    lax.fori_loop(0, count // block, several, 0)
    for k in range(count // block * block, count):
        body(k)


def widened(x_ref, wide):
    count, planes, rows = x_ref.shape[:3]

    def widen(i):
        for x in range(planes):
            start = pl.multiple_of((i * planes + x) * rows, 8)
            wide[pl.ds(start, rows), :] = x_ref[i, x].astype(F32)

    in_blocks(count, widen)


def turn(wide, outs, shape, base, length):
    count, planes, rows = shape

    def one(f):
        y = lax.rem(base + f, rows)
        for x in range(planes):
            tile = wide[pl.ds(x * rows + y, count, stride=planes * rows), :]
            outs[x // 2][f, x % 2] = tile.astype(BF16)

    in_blocks(length, one)


def field_kernel(extent, margin, x_ref, *refs):
    outs, wide = refs[:-1], refs[-1]
    count, planes, rows = x_ref.shape[:3]
    pairs = planes // 2
    share = rows // extent
    widened(x_ref, wide)
    me = lax.axis_index("chan")
    for s in range(extent):
        base = lax.rem(me + s, extent) * share - margin + rows
        turn(
            wide,
            outs[s * pairs : (s + 1) * pairs],
            (count, planes, rows),
            base,
            share + 2 * margin,
        )


def pack_kernel(count, rows, *refs):
    first, second = refs[count : count + 2]
    pieces, packed, done = refs[count + 2 : -2], refs[-2], refs[-1]
    blank = jnp.zeros(first.shape[1:], F32)
    for h in range(14):
        parts = []
        for ref in (first, second):
            for t in (2 * h, 2 * h + 1):
                parts.append(ref[t].astype(F32) if t < ref.shape[0] else blank)
        packed[h // 2, h % 2] = jnp.concatenate(parts, axis=1).astype(BF16)
    copies = []
    for k, piece in enumerate(pieces):
        copies.append(pltpu.make_async_copy(packed, piece.at[pl.ds(rows, 7)], done.at[k]))
        copies[-1].start()
    for copy in copies:
        copy.wait()


def grad_kernel(extent, margin, one, two, x_ref, *refs):
    del one, two
    outs, wide = refs[:-1], refs[-1]
    count, planes, rows = x_ref.shape[:3]
    share = rows // extent
    widened(x_ref, wide)
    base = lax.axis_index("chan") * share - margin + rows
    turn(wide, outs, (count, planes, rows), base, share + 2 * margin)


def matrix_kernel(extent, *refs):
    packs, outs = refs[:extent], refs[extent:]
    me = lax.axis_index("chan")
    quarter = packs[0].shape[3] // 4
    taps = []
    turned = []
    for h in range(14):
        tiles = [
            pack[pack.shape[0] - 7 + h // 2, h % 2].astype(F32) for pack in packs
        ]
        own = jnp.concatenate(tiles, axis=0)
        fixed = []
        for g in range(extent):
            place = lax.rem(me + extent - g, extent)
            tile = tiles[0]
            for j in range(1, extent):
                tile = jnp.where(place == j, tiles[j], tile)
            fixed.append(tile)
        both = jnp.concatenate(
            [own[:, : 2 * quarter], jnp.concatenate(fixed, axis=0)[:, 2 * quarter :]], axis=1
        )
        across = both.T
        for side in range(2):
            taps.append(
                [both[:, k * quarter : (k + 1) * quarter] for k in (side, side + 2)]
            )
            turned.append(
                [across[k * quarter : (k + 1) * quarter] for k in (side, side + 2)]
            )
    channels = quarter
    blank = jnp.zeros((channels, channels), F32)
    for k in range(2):
        for out, blocks, flip in ((outs[k], turned, False), (outs[2 + k], taps, True)):
            for e in range(3):
                for x in range(2):
                    chunks = []
                    for pair in range(2):
                        for b in range(3):
                            for side in range(2):
                                a = 2 * pair + side - x
                                t = 9 * a + 3 * b + e
                                inside = 0 <= a <= 2
                                t = 26 - t if flip else t
                                chunks.append(blocks[t][k] if inside else blank)
                    low = (2 * e + x) * channels
                    out[low : low + channels, :] = jnp.concatenate(chunks, axis=1).astype(BF16)


def stacked(refs, row, count):
    if len(refs) == 1:
        part = refs[0][pl.ds(row, count)]
        return part.reshape(-1, part.shape[-1])
    parts = [ref[row + b, x] for b in range(count) for x in range(2) for ref in refs]
    return jnp.concatenate(parts, axis=0)


def taps(weight, pairs, row):
    sides = []
    for p in range(len(pairs) - 1):
        for q in range(2):
            above = stacked(pairs[p], row + q, 3)
            below = stacked(pairs[p + 1], row + q, 3)
            sides.append(jnp.concatenate([above, below], axis=0))
    lifted = jnp.dot(weight, jnp.concatenate(sides, axis=1), preferred_element_type=F32)
    third = lifted.shape[0] // 3
    depth = sides[0].shape[1]
    sums = []
    for k in range(len(sides)):
        side = lifted[:, k * depth : (k + 1) * depth]
        sums.append(
            side[third : 2 * third]
            + pltpu.roll(side[:third], 1, 1)
            + pltpu.roll(side[2 * third :], depth - 1, 1)
        )
    return [sums[2 * p : 2 * p + 2] for p in range(len(pairs) - 1)]


def silu_parts(v):
    sig = jax.nn.sigmoid(v)
    return sig, sig * (1.0 + v * (1.0 - sig))


def forward_kernel(groups, fresh, ready, *refs):
    refs = list(refs)
    fields = [[refs.pop(0) for _ in range(groups)] for _ in range(fresh + 1)]
    hiddens = [refs.pop(0) for _ in range(ready)]
    count = fresh + ready - 1
    grads = [refs.pop(0) for _ in range(count)]
    first, second = refs.pop(0), refs.pop(0)
    made = [refs.pop(0) for _ in range(fresh)]
    slopes = [refs.pop(0) for _ in range(fresh)]
    deltas = refs
    hiddens = hiddens + made

    def one(r):
        row = 2 * r
        for p, sums in enumerate(taps(first[...], fields, row)):
            for q, v in enumerate(sums):
                sig, slope = silu_parts(v)
                shape = made[p].shape[1:]
                made[p][row + q] = (v * sig).astype(BF16).reshape(shape)
                slopes[p][row + q] = slope.astype(BF16).reshape(shape)

    in_blocks(made[0].shape[0] // 2, one)

    def two(r):
        row = 2 * r
        for p, sums in enumerate(taps(second[...], [[ref] for ref in hiddens], row)):
            for q, v in enumerate(sums):
                shape = deltas[p].shape[1:]
                out_grad = grads[p][row + q].astype(F32)
                slope = silu_parts(v)[1].reshape(shape)
                deltas[p][row + q] = (out_grad * slope).astype(BF16)

    if count > 0:
        in_blocks(deltas[0].shape[0] // 2, two)


def planes_of(pairs):
    return [(refs, x) for refs in pairs for x in range(2)]


def weight_loop(total, pieces, first_row, deltas, delta_row, count):
    blocks = [k for k in range(1, 13) if count // 2 % k == 0 and k * len(deltas) <= 12]
    together = max(blocks, default=1)

    def step(r, _):
        left, right = [], []
        for k in range(together):
            row = 2 * (r * together + k)
            for x, ((delta,), place) in enumerate(deltas):
                rows = []
                for q in range(2):
                    wide = delta[delta_row + row + q, place]
                    plain = wide.astype(F32)
                    depth = plain.shape[1]
                    rows += [
                        pltpu.roll(plain, depth - 1, 1).astype(BF16),
                        wide,
                        pltpu.roll(plain, 1, 1).astype(BF16),
                    ]
                left.append(jnp.concatenate(rows, axis=0))
                rows = []
                for refs, side in pieces[x : x + 3]:
                    for b in range(4):
                        for ref in refs:
                            rows.append(ref[first_row + row + b, side])
                right.append(jnp.concatenate(rows, axis=0))
        total[...] += lax.dot_general(
            jnp.concatenate(left, axis=1),
            jnp.concatenate(right, axis=1),
            (((1,), (1,)), ((), ())),
            preferred_element_type=F32,
        )
        return 0

    lax.fori_loop(0, count // 2 // together, step, 0)


def weight_fold(total, size):
    lanes = total.shape[0] // 2
    channels = total.shape[1] // 12
    upper, lower = total[:lanes, :].T, total[lanes:, :].T
    groups = []
    for g in range(channels // size):
        taps_of = []
        for a in range(3):
            for b in range(3):
                start = (4 * a + b) * channels + g * size
                part = (
                    upper[start : start + size]
                    + lower[start + channels : start + channels + size]
                )
                taps_of += [part[:, e * channels : (e + 1) * channels] for e in range(3)]
        blank = jnp.zeros((size, channels), F32)
        taps_of.append(blank)
        groups.append([jnp.concatenate(taps_of[4 * h : 4 * h + 4], axis=1) for h in range(7)])
    return groups


def second_kernel(share, pairs, *refs):
    refs = list(refs)
    hiddens = [[refs.pop(0)] for _ in range(pairs + 1)]
    deltas = [refs.pop(0) for _ in range(pairs)]
    raw, total = refs
    total[...] = jnp.zeros_like(total)
    weight_loop(total, planes_of(hiddens), 2, planes_of([[d] for d in deltas]), 2, share)
    for g, tiles in enumerate(weight_fold(total, raw.shape[2])):
        for h, tile in enumerate(tiles):
            raw[g, h] = tile


def first_deltas(weight, deltas, slopes, firsts):
    def one(r):
        row = 2 * r
        for p, sums in enumerate(taps(weight[...], [[delta] for delta in deltas], row)):
            for q, v in enumerate(sums):
                shape = firsts[p].shape[1:]
                slope = slopes[p][row + 2 + q].astype(F32)
                firsts[p][row + q] = (v.reshape(shape) * slope).astype(BF16)

    in_blocks(firsts[0].shape[0] // 2, one)


def back_kernel(share, groups, count, after, *refs):
    del after
    refs = list(refs)
    weight = refs.pop(0)
    deltas = [refs.pop(0) for _ in range(count + 1)]
    slopes = [refs.pop(0) for _ in range(count)]
    fields = [[refs.pop(0) for _ in range(groups)] for _ in range(count + 2)]
    firsts, total = refs[:-1], refs[-1]
    first_deltas(weight, deltas, slopes, firsts)
    total[...] = jnp.zeros_like(total)
    near = planes_of(fields)[2:-1]
    weight_loop(total, near, 3, planes_of([[ref] for ref in firsts])[:-1], 1, share)


def first_kernel(share, groups, after, *refs):
    del after
    refs = list(refs)
    weight = refs.pop(0)
    deltas = [refs.pop(0) for _ in range(2)]
    slope = refs.pop(0)
    fields = [[refs.pop(0) for _ in range(groups)] for _ in range(2)]
    later, second = refs.pop(0), refs.pop(0)
    first, keep, send, total = refs
    first_deltas(weight, deltas, [slope], [first])
    total[...] = later[...]
    weight_loop(total, planes_of(fields)[1:], 3, planes_of([[first]])[1:], 1, share)
    extent, halves, size = keep.shape[:3]
    me = lax.axis_index("chan")
    groups_of = weight_fold(total, size)

    def place(ours, theirs):
        for g, tiles in enumerate(groups_of):
            there = lax.rem(me + extent - g, extent)
            for h in range(halves):
                ours[g, h] = tiles[h]
                theirs[g, h] = second[there, h]

    odd = lax.rem(lax.axis_index("slab"), 2)

    @pl.when(odd == 0)
    def _():
        place(keep, send)

    @pl.when(odd == 1)
    def _():
        place(send, keep)


def last_kernel(pairs, *refs):
    refs = list(refs)
    firsts = [refs.pop(0) for _ in range(pairs + 1)]
    weight = refs.pop(0)
    outs = refs

    def one(r):
        row = 2 * r
        size = outs[0].shape[2]
        channels = len(outs) * size
        for p, sums in enumerate(taps(weight[...], [[first] for first in firsts], row)):
            for q, v in enumerate(sums):
                for x in range(2):
                    for j, out in enumerate(outs):
                        low = x * channels + j * size
                        out[row + q, 2 * p + x] = v[low : low + size].astype(BF16)

    in_blocks(outs[0].shape[0] // 2, one)


def finish_kernel(factor, mine, other, first, second):
    channels = first.shape[2]

    def place(ours, theirs):
        for out, sums in ((ours, mine), (theirs, other)):
            for t in range(27):
                low = t % 4 * channels
                out[t] = sums[t // 4, :, low : low + channels] * factor

    odd = lax.rem(lax.axis_index("slab"), 2)

    @pl.when(odd == 0)
    def _():
        place(first, second)

    @pl.when(odd == 1)
    def _():
        place(second, first)


def split_kernel(ahead, *refs):
    one, two, *outs = refs[ahead:]
    for g, out in enumerate(outs):
        out[...] = one[g] + two[g]


def add_kernel(ahead, *refs):
    values = [ref[...] for ref in refs[ahead:-1]]
    while len(values) > 1:
        values = [sum(values[k + 1 : k + 2], values[k]) for k in range(0, len(values), 2)]
    refs[-1][...] = values[0]


def relay_kernel(*refs):
    pass


def merge_kernel(extent, *refs):
    pieces, token, out, wide = refs[:-3], refs[-3], refs[-2], refs[-1]
    token[...] = jnp.zeros_like(token)
    size, planes, rows = out.shape[:3]
    share = rows // extent
    me = lax.axis_index("chan")
    for j in range(extent):
        base = lax.rem(me + extent - j, extent) * share

        def widen(f, mine=pieces[j::extent], base=base):
            x = 0
            for piece in mine:
                for k in range(piece.shape[1]):
                    start = ((base + f) * planes + x) * size
                    start = pl.multiple_of(start, 8) if size % 8 == 0 else start
                    wide[pl.ds(start, size), :] = piece[f, k].astype(F32)
                    x += 1

        in_blocks(share, widen)

    def back(i):
        for x in range(planes):
            tile = wide[pl.ds(x * size + i, rows, stride=planes * size), :]
            out[i, x] = tile.astype(BF16)

    in_blocks(size, back)


def body(field, out_grad, first_weight, second_weight):
    extent = lax.axis_size("chan")
    slabs = lax.axis_size("slab")
    me = lax.axis_index("chan")
    size, planes, rows, depth = field.shape
    channels = size * extent
    pairs = planes // 2
    share = rows // extent
    factor = 1.0 / math.sqrt(planes * slabs * rows * depth)

    def to_chan(value, shift):
        return lax.ppermute(value, "chan", [(i, (i + shift) % extent) for i in range(extent)])

    def to_next(value):
        return lax.ppermute(value, "slab", [(i, (i + 1) % slabs) for i in range(slabs)])

    def to_prev(value):
        return lax.ppermute(value, "slab", [((i + 1) % slabs, i) for i in range(slabs)])

    def relayed(value, *others):
        shape = jax.ShapeDtypeStruct(value.shape, value.dtype)
        early = [value, *others]
        return call(relay_kernel, [shape], early, loose=len(early), same={0: 0})[0]

    piece = jax.ShapeDtypeStruct((share + 8, 2, size, depth), BF16)
    by_tap = (27, size, channels)
    longer = jax.ShapeDtypeStruct((share + 15, 2, size, depth), BF16)
    rest = [piece] * (pairs - 1)
    made = call(
        functools.partial(field_kernel, extent, 4),
        [piece] + rest + ([longer] + rest) * (extent - 1),
        [field],
        [pltpu.VMEM((size * planes * rows, depth), F32)],
        moved=field.size * 6,
    )
    first_sent = list(made[pairs::pairs])
    others = extent - 1
    packed = call(
        functools.partial(pack_kernel, others, share + 8),
        [longer] * others + [jax.ShapeDtypeStruct((7, 2, size, 4 * channels), BF16)],
        first_sent
        + [jnp.transpose(first_weight, (1, 0, 2)), jnp.transpose(second_weight, (1, 0, 2))],
        [pltpu.SemaphoreType.DMA((max(others, 1),))],
        loose=others,
        same={k: k for k in range(others)},
    )
    first_sent, pack = packed[:-1], packed[-1]
    parts = [list(made[:pairs])]
    whole = size % 16 == 0
    own_before, own_after = [], []
    if whole:
        own_before, own_after = [to_next(parts[0][-1])], [to_prev(parts[0][0])]
    for j in range(1, extent):
        sent = [first_sent[j - 1]] + list(made[j * pairs + 1 : (j + 1) * pairs])
        parts.append([to_chan(value, j) for value in sent])
    packs = [pack] + [part[0] for part in parts[1:]]
    grad_piece = jax.ShapeDtypeStruct((share + 4, 2, channels, depth), BF16)
    grads = call(
        functools.partial(grad_kernel, extent, 2),
        [grad_piece] * pairs,
        [own_before[0], own_after[0], out_grad] if whole else [pack, pack, out_grad],
        [pltpu.VMEM((channels * planes * rows, depth), F32)],
        moved=out_grad.size * 4,
        loose=2,
    )
    matrix = jax.ShapeDtypeStruct((6 * channels, 12 * channels), BF16)
    first_wide, second_wide, first_back, second_back = call(
        functools.partial(matrix_kernel, extent),
        [matrix] * 4,
        packs,
        moved=matrix.size * 8,
    )
    arrived = parts[-1]
    if extent > 1 and pairs > 1:
        arrived[0] = relayed(arrived[0], grads[0])
    by_pair = [[parts[j][p] for j in range(extent)] for p in range(pairs)]
    groups = extent
    if not whole:
        by_pair = [
            [jnp.concatenate([piece[: share + 8] for piece in pieces], axis=2)]
            for pieces in by_pair
        ]
        groups = 1
    before = own_before + [to_next(piece) for piece in by_pair[-1][len(own_before) :]]
    after = own_after + [to_prev(piece) for piece in by_pair[0][len(own_after) :]]
    fields = [before] + by_pair + [after]

    def many(count, rows_each):
        return [jax.ShapeDtypeStruct((rows_each, 2, channels, depth), BF16)] * count

    def flat(lists):
        return [piece for pieces in lists for piece in pieces]

    work = 27 * 2 * channels * channels * depth * 2
    space = 4 * channels * depth * share

    made = call(
        functools.partial(forward_kernel, groups, pairs, 0),
        many(2 * pairs, share + 6) + many(pairs - 1, share + 4),
        flat(fields[: pairs + 1]) + list(grads[: pairs - 1]) + [first_wide, second_wide],
        flops=work * (2 * pairs - 1) * share,
        moved=space * 4 * pairs,
    )
    hiddens, slopes, deltas = made[:pairs], made[pairs : 2 * pairs], made[2 * pairs :]
    made = call(
        functools.partial(forward_kernel, groups, 1, 1),
        many(2, share + 6) + many(1, share + 4),
        flat(fields[pairs:]) + [hiddens[-1], grads[-1], first_wide, second_wide],
        flops=work * 2 * share,
        moved=space * 6,
    )
    hiddens = list(hiddens) + [made[0]]
    slopes = list(slopes) + [made[1]]
    deltas = list(deltas) + [made[2]]
    delta_after = to_prev(deltas[0])
    delta_before = to_next(deltas[-1])

    raw = jax.ShapeDtypeStruct((extent, 7, size, 4 * channels), F32)
    total = pltpu.VMEM((6 * channels, 12 * channels), F32)
    (second_raw,) = call(
        functools.partial(second_kernel, share, pairs),
        [raw],
        hiddens + deltas,
        [total],
        flops=work * pairs * share,
        moved=space * 5,
    )
    partial_sum = jax.ShapeDtypeStruct((6 * channels, 12 * channels), F32)
    made = call(
        functools.partial(back_kernel, share, groups, pairs),
        many(pairs, share + 2) + [partial_sum],
        [second_raw, second_back] + deltas + [delta_after] + slopes[1:] + flat(fields),
        flops=work * (2 * pairs - 1) * share,
        moved=space * 6 * pairs,
        loose=1,
    )
    later, partial_total = list(made[:-1]), made[-1]

    def field_grad(firsts):
        count = len(firsts) - 1
        return list(
            call(
                functools.partial(last_kernel, count),
                [jax.ShapeDtypeStruct((share, 2 * count, size, depth), BF16)] * extent,
                firsts + [first_back],
                flops=work * count * share,
                moved=space * 2 * count,
            )
        )

    def exchanged(made):
        pieces = [made[0]] + [None] * (extent - 1)
        for j in range(1, extent):
            pieces[extent - j] = to_chan(made[j], extent - j)
        return pieces

    pieces, early = [], [later[0]]
    if pairs > 1:
        early = field_grad(later)
        pieces = exchanged(early)
    first, keep, send = call(
        functools.partial(first_kernel, share, groups),
        many(1, share + 2) + [raw] * 2,
        [early[0], second_back, delta_before, deltas[0], slopes[0]]
        + flat(fields[0:2])
        + [partial_total, second_raw],
        [total],
        flops=work * 2 * share,
        moved=space * 6,
        loose=1,
    )

    def stepped(value, stride, shift=0):
        if shift % extent == 0:
            return lax.ppermute(value, "slab", [(i, i ^ stride) for i in range(slabs)])
        pairs_of = []
        for i in range(slabs):
            for k in range(extent):
                there = (i ^ stride) * extent + (k + shift) % extent
                pairs_of.append((i * extent + k, there))
        return lax.ppermute(value, ("slab", "chan"), pairs_of)

    portion = jax.ShapeDtypeStruct(raw.shape[1:], F32)
    made = field_grad([first, later[0]])
    plain = slabs & (slabs - 1) == 0 and slabs >= 4
    if plain:
        ahead = made[:1] + pieces[1:2]
        kept = call(
            functools.partial(split_kernel, len(ahead)),
            [portion] * extent,
            ahead + [keep, stepped(send, 1)],
            loose=len(ahead),
        )
        shares = [kept[0]] + [to_chan(kept[j], extent - j) for j in range(1, extent)]
        shares += [stepped(kept[j], 2, extent - j) for j in range(extent)]
        (mine,) = call(functools.partial(add_kernel, 0), [portion], shares)
        made = [made[0]] + [relayed(value, mine) for value in made[1:]]
    pieces = exchanged(made) + pieces

    token, input_grad = call(
        functools.partial(merge_kernel, extent),
        [jax.ShapeDtypeStruct((8, 128), F32), jax.ShapeDtypeStruct(field.shape, BF16)],
        pieces,
        [pltpu.VMEM((rows * planes * size, depth), F32)],
        moved=4 * field.size,
    )
    if plain:
        stride = 4
        while stride < slabs:
            radix = 4 if slabs % (4 * stride) == 0 else 2
            got = [mine] + [stepped(mine, m * stride) for m in range(1, radix)]
            last = stride * radix == slabs
            ahead = [token] if last else []
            (mine,) = call(
                functools.partial(add_kernel, len(ahead)), [portion], ahead + got, loose=len(ahead)
            )
            stride *= radix
        other = stepped(mine, 1)
    else:
        mine, other = keep[0], send[0]
        for j in range(1, extent):
            mine, other = mine + to_chan(keep[j], extent - j), other + to_chan(send[j], extent - j)
        even = lax.rem(lax.axis_index("slab"), 2) == 0
        mine, other = jnp.where(even, mine, other), jnp.where(even, other, mine)
        mine, other = lax.psum((mine, other), "slab")
        mine, other = jnp.where(even, mine, other), jnp.where(even, other, mine)
    first_grad, second_grad = call(
        functools.partial(finish_kernel, factor),
        [jax.ShapeDtypeStruct(by_tap, F32)] * 2,
        [mine, other],
    )
    first_grad, second_grad = (jnp.transpose(g, (1, 0, 2)) for g in (first_grad, second_grad))
    return input_grad, first_grad, second_grad


def solution(mesh):
    placed = (
        P("chan", "slab", None, None),
        P(None, "slab", None, None),
        P("chan", None, None),
        P("chan", None, None),
    )
    return jax.shard_map(
        body,
        mesh=mesh,
        in_specs=placed,
        out_specs=(P("chan", "slab", None, None), P("chan", None, None), P("chan", None, None)),
        check_vma=False,
    )
```

```python
import functools
import math

import jax
import jax.numpy as jnp
from jax import lax
from jax.experimental import pallas as pl
from jax.experimental.pallas import tpu as pltpu
from jax.sharding import PartitionSpec as P

F32 = jnp.float32
BF16 = jnp.bfloat16
LIMIT = 16 * 1024 * 1024


def call(kernel, outs, args, scratch=(), flops=0, moved=0, loose=0, same=None):
    whole = pl.BlockSpec(memory_space=pltpu.VMEM)
    still = pl.BlockSpec(memory_space=pl.ANY)
    return pl.pallas_call(
        kernel,
        out_shape=outs,
        in_specs=[still] * loose + [whole] * (len(args) - loose),
        out_specs=[still if k in (same or {}).values() else whole for k in range(len(outs))],
        input_output_aliases=same or {},
        scratch_shapes=list(scratch),
        compiler_params=pltpu.CompilerParams(vmem_limit_bytes=LIMIT),
        cost_estimate=pl.CostEstimate(flops=flops, bytes_accessed=moved, transcendentals=0),
    )(*args)


def in_blocks(count, body):
    block = max(k for k in range(1, 8) if count % k == 0)
    if block < 4:
        block = min(count, 15)

    def several(r, _):
        for k in range(block):
            body(r * block + k)
        return 0

    lax.fori_loop(0, count // block, several, 0)
    for k in range(count // block * block, count):
        body(k)


def widened(x_ref, wide):
    count, planes, rows = x_ref.shape[:3]

    def widen(i):
        for x in range(planes):
            start = pl.multiple_of((i * planes + x) * rows, 8)
            wide[pl.ds(start, rows), :] = x_ref[i, x].astype(F32)

    in_blocks(count, widen)


def turn(wide, outs, shape, base, length):
    count, planes, rows = shape

    def one(f):
        y = lax.rem(base + f, rows)
        for x in range(planes):
            tile = wide[pl.ds(x * rows + y, count, stride=planes * rows), :]
            outs[x // 2][f, x % 2] = tile.astype(BF16)

    in_blocks(length, one)


def field_kernel(extent, margin, x_ref, *refs):
    outs, wide = refs[:-1], refs[-1]
    count, planes, rows = x_ref.shape[:3]
    pairs = planes // 2
    share = rows // extent
    widened(x_ref, wide)
    me = lax.axis_index("chan")
    for s in range(extent):
        base = lax.rem(me + s, extent) * share - margin + rows
        turn(
            wide,
            outs[s * pairs : (s + 1) * pairs],
            (count, planes, rows),
            base,
            share + 2 * margin,
        )


def pack_kernel(count, rows, *refs):
    first, second = refs[count : count + 2]
    pieces, packed, done = refs[count + 2 : -2], refs[-2], refs[-1]
    blank = jnp.zeros(first.shape[1:], F32)
    for h in range(14):
        parts = []
        for ref in (first, second):
            for t in (2 * h, 2 * h + 1):
                parts.append(ref[t].astype(F32) if t < ref.shape[0] else blank)
        packed[h // 2, h % 2] = jnp.concatenate(parts, axis=1).astype(BF16)
    copies = []
    for k, piece in enumerate(pieces):
        copies.append(pltpu.make_async_copy(packed, piece.at[pl.ds(rows, 7)], done.at[k]))
        copies[-1].start()
    for copy in copies:
        copy.wait()


def grad_kernel(extent, margin, after, x_ref, *refs):
    del after
    outs, wide = refs[:-1], refs[-1]
    count, planes, rows = x_ref.shape[:3]
    share = rows // extent
    widened(x_ref, wide)
    base = lax.axis_index("chan") * share - margin + rows
    turn(wide, outs, (count, planes, rows), base, share + 2 * margin)


def matrix_kernel(extent, *refs):
    packs, outs = refs[:extent], refs[extent:]
    me = lax.axis_index("chan")
    quarter = packs[0].shape[3] // 4
    taps = []
    turned = []
    for h in range(14):
        tiles = [
            pack[pack.shape[0] - 7 + h // 2, h % 2].astype(F32) for pack in packs
        ]
        own = jnp.concatenate(tiles, axis=0)
        fixed = []
        for g in range(extent):
            place = lax.rem(me + extent - g, extent)
            tile = tiles[0]
            for j in range(1, extent):
                tile = jnp.where(place == j, tiles[j], tile)
            fixed.append(tile)
        both = jnp.concatenate(
            [own[:, : 2 * quarter], jnp.concatenate(fixed, axis=0)[:, 2 * quarter :]], axis=1
        )
        across = both.T
        for side in range(2):
            taps.append(
                [both[:, k * quarter : (k + 1) * quarter] for k in (side, side + 2)]
            )
            turned.append(
                [across[k * quarter : (k + 1) * quarter] for k in (side, side + 2)]
            )
    channels = quarter
    blank = jnp.zeros((channels, channels), F32)
    for k in range(2):
        for out, blocks, flip in ((outs[k], turned, False), (outs[2 + k], taps, True)):
            for e in range(3):
                for x in range(2):
                    chunks = []
                    for pair in range(2):
                        for b in range(3):
                            for side in range(2):
                                a = 2 * pair + side - x
                                t = 9 * a + 3 * b + e
                                inside = 0 <= a <= 2
                                t = 26 - t if flip else t
                                chunks.append(blocks[t][k] if inside else blank)
                    low = (2 * e + x) * channels
                    out[low : low + channels, :] = jnp.concatenate(chunks, axis=1).astype(BF16)


def stacked(refs, row, count):
    if len(refs) == 1:
        part = refs[0][pl.ds(row, count)]
        return part.reshape(-1, part.shape[-1])
    parts = [ref[row + b, x] for b in range(count) for x in range(2) for ref in refs]
    return jnp.concatenate(parts, axis=0)


def taps(weight, pairs, row):
    sides = []
    for p in range(len(pairs) - 1):
        for q in range(2):
            above = stacked(pairs[p], row + q, 3)
            below = stacked(pairs[p + 1], row + q, 3)
            sides.append(jnp.concatenate([above, below], axis=0))
    lifted = jnp.dot(weight, jnp.concatenate(sides, axis=1), preferred_element_type=F32)
    third = lifted.shape[0] // 3
    depth = sides[0].shape[1]
    sums = []
    for k in range(len(sides)):
        side = lifted[:, k * depth : (k + 1) * depth]
        sums.append(
            side[third : 2 * third]
            + pltpu.roll(side[:third], 1, 1)
            + pltpu.roll(side[2 * third :], depth - 1, 1)
        )
    return [sums[2 * p : 2 * p + 2] for p in range(len(pairs) - 1)]


def silu_parts(v):
    sig = jax.nn.sigmoid(v)
    return sig, sig * (1.0 + v * (1.0 - sig))


def forward_kernel(groups, fresh, ready, *refs):
    refs = list(refs)
    fields = [[refs.pop(0) for _ in range(groups)] for _ in range(fresh + 1)]
    hiddens = [refs.pop(0) for _ in range(ready)]
    count = fresh + ready - 1
    grads = [refs.pop(0) for _ in range(count)]
    first, second = refs.pop(0), refs.pop(0)
    made = [refs.pop(0) for _ in range(fresh)]
    slopes = [refs.pop(0) for _ in range(fresh)]
    deltas = refs
    hiddens = hiddens + made

    def one(r):
        row = 2 * r
        for p, sums in enumerate(taps(first[...], fields, row)):
            for q, v in enumerate(sums):
                sig, slope = silu_parts(v)
                shape = made[p].shape[1:]
                made[p][row + q] = (v * sig).astype(BF16).reshape(shape)
                slopes[p][row + q] = slope.astype(BF16).reshape(shape)

    in_blocks(made[0].shape[0] // 2, one)

    def two(r):
        row = 2 * r
        for p, sums in enumerate(taps(second[...], [[ref] for ref in hiddens], row)):
            for q, v in enumerate(sums):
                shape = deltas[p].shape[1:]
                out_grad = grads[p][row + q].astype(F32)
                slope = silu_parts(v)[1].reshape(shape)
                deltas[p][row + q] = (out_grad * slope).astype(BF16)

    if count > 0:
        in_blocks(deltas[0].shape[0] // 2, two)


def planes_of(pairs):
    return [(refs, x) for refs in pairs for x in range(2)]


def weight_loop(total, pieces, first_row, deltas, delta_row, count):
    blocks = [k for k in range(1, 13) if count // 2 % k == 0 and k * len(deltas) <= 12]
    together = max(blocks, default=1)

    def step(r, _):
        left, right = [], []
        for k in range(together):
            row = 2 * (r * together + k)
            for x, ((delta,), place) in enumerate(deltas):
                rows = []
                for q in range(2):
                    wide = delta[delta_row + row + q, place]
                    plain = wide.astype(F32)
                    depth = plain.shape[1]
                    rows += [
                        pltpu.roll(plain, depth - 1, 1).astype(BF16),
                        wide,
                        pltpu.roll(plain, 1, 1).astype(BF16),
                    ]
                left.append(jnp.concatenate(rows, axis=0))
                rows = []
                for refs, side in pieces[x : x + 3]:
                    for b in range(4):
                        for ref in refs:
                            rows.append(ref[first_row + row + b, side])
                right.append(jnp.concatenate(rows, axis=0))
        total[...] += lax.dot_general(
            jnp.concatenate(left, axis=1),
            jnp.concatenate(right, axis=1),
            (((1,), (1,)), ((), ())),
            preferred_element_type=F32,
        )
        return 0

    lax.fori_loop(0, count // 2 // together, step, 0)


def weight_fold(total, size):
    lanes = total.shape[0] // 2
    channels = total.shape[1] // 12
    upper, lower = total[:lanes, :].T, total[lanes:, :].T
    groups = []
    for g in range(channels // size):
        taps_of = []
        for a in range(3):
            for b in range(3):
                start = (4 * a + b) * channels + g * size
                part = (
                    upper[start : start + size]
                    + lower[start + channels : start + channels + size]
                )
                taps_of += [part[:, e * channels : (e + 1) * channels] for e in range(3)]
        blank = jnp.zeros((size, channels), F32)
        taps_of.append(blank)
        groups.append([jnp.concatenate(taps_of[4 * h : 4 * h + 4], axis=1) for h in range(7)])
    return groups


def first_deltas(weight, deltas, slopes, firsts):
    def one(r):
        row = 2 * r
        for p, sums in enumerate(taps(weight[...], [[delta] for delta in deltas], row)):
            for q, v in enumerate(sums):
                shape = firsts[p].shape[1:]
                slope = slopes[p][row + 2 + q].astype(F32)
                firsts[p][row + q] = (v.reshape(shape) * slope).astype(BF16)

    in_blocks(firsts[0].shape[0] // 2, one)


def back_part(share, kept, weight, deltas, slopes, fields, firsts, total):
    first_deltas(weight, deltas, slopes, firsts)
    near = planes_of(fields)
    own = planes_of([[ref] for ref in firsts])
    low, high = kept
    weight_loop(total, near[low : high + 2], 3, own[low:high], 1, share)


def middle_kernel(share, groups, pairs, *refs):
    refs = list(refs)
    hiddens = [[refs.pop(0)] for _ in range(pairs + 1)]
    deltas = [refs.pop(0) for _ in range(pairs)]
    weight = refs.pop(0)
    count = pairs - 1
    slopes = [refs.pop(0) for _ in range(count)]
    fields = [[refs.pop(0) for _ in range(groups)] for _ in range(pairs)]
    raw, first_total = refs.pop(0), refs.pop(0)
    firsts, total = refs[:count], refs[-1]
    total[...] = jnp.zeros_like(total)
    weight_loop(total, planes_of(hiddens), 2, planes_of([[d] for d in deltas]), 2, share)
    for g, tiles in enumerate(weight_fold(total, raw.shape[2])):
        for h, tile in enumerate(tiles):
            raw[g, h] = tile
    first_total[...] = jnp.zeros_like(first_total)
    if count > 0:
        kept = (0, 2 * count)
        back_part(share, kept, weight, deltas, slopes, fields, firsts, first_total)


def back_kernel(share, groups, weight, one, two, slope, *refs):
    refs = list(refs)
    fields = [[refs.pop(0) for _ in range(groups)] for _ in range(2)]
    before, first, total = refs
    total[...] = before[...]
    back_part(share, (0, 1), weight, [one, two], [slope], fields, [first], total)


def first_kernel(share, groups, after, weight, one, two, slope, *refs):
    del after
    refs = list(refs)
    fields = [[refs.pop(0) for _ in range(groups)] for _ in range(2)]
    before, second = refs.pop(0), refs.pop(0)
    first, keep, send, total = refs
    total[...] = before[...]
    back_part(share, (1, 2), weight, [one, two], [slope], fields, [first], total)
    extent, halves, size = keep.shape[:3]
    me = lax.axis_index("chan")
    groups_of = weight_fold(total, size)

    def place(ours, theirs):
        for g, tiles in enumerate(groups_of):
            there = lax.rem(me + extent - g, extent)
            for h in range(halves):
                ours[g, h] = tiles[h]
                theirs[g, h] = second[there, h]

    odd = lax.rem(lax.axis_index("slab"), 2)

    @pl.when(odd == 0)
    def _():
        place(keep, send)

    @pl.when(odd == 1)
    def _():
        place(send, keep)


def last_kernel(pairs, *refs):
    refs = list(refs)
    firsts = [refs.pop(0) for _ in range(pairs + 1)]
    weight = refs.pop(0)
    outs = refs

    def one(r):
        row = 2 * r
        size = outs[0].shape[2]
        channels = len(outs) * size
        for p, sums in enumerate(taps(weight[...], [[first] for first in firsts], row)):
            for q, v in enumerate(sums):
                for x in range(2):
                    for j, out in enumerate(outs):
                        low = x * channels + j * size
                        out[row + q, 2 * p + x] = v[low : low + size].astype(BF16)

    in_blocks(outs[0].shape[0] // 2, one)


def finish_kernel(factor, mine, other, first, second):
    channels = first.shape[2]

    def place(ours, theirs):
        for out, sums in ((ours, mine), (theirs, other)):
            for t in range(27):
                low = t % 4 * channels
                out[t] = sums[t // 4, :, low : low + channels] * factor

    odd = lax.rem(lax.axis_index("slab"), 2)

    @pl.when(odd == 0)
    def _():
        place(first, second)

    @pl.when(odd == 1)
    def _():
        place(second, first)


def split_kernel(ahead, *refs):
    one, two, *outs = refs[ahead:]
    for g, out in enumerate(outs):
        out[...] = one[g] + two[g]


def add_kernel(ahead, *refs):
    values = [ref[...] for ref in refs[ahead:-1]]
    while len(values) > 1:
        values = [sum(values[k + 1 : k + 2], values[k]) for k in range(0, len(values), 2)]
    refs[-1][...] = values[0]


def relay_kernel(*refs):
    pass


def merge_kernel(extent, *refs):
    pieces, token, out, wide = refs[:-3], refs[-3], refs[-2], refs[-1]
    token[...] = jnp.zeros_like(token)
    size, planes, rows = out.shape[:3]
    share = rows // extent
    me = lax.axis_index("chan")
    for j in range(extent):
        base = lax.rem(me + extent - j, extent) * share

        def widen(f, mine=pieces[j::extent], base=base):
            x = 0
            for piece in mine:
                for k in range(piece.shape[1]):
                    start = ((base + f) * planes + x) * size
                    start = pl.multiple_of(start, 8) if size % 8 == 0 else start
                    wide[pl.ds(start, size), :] = piece[f, k].astype(F32)
                    x += 1

        in_blocks(share, widen)

    def back(i):
        for x in range(planes):
            tile = wide[pl.ds(x * size + i, rows, stride=planes * size), :]
            out[i, x] = tile.astype(BF16)

    in_blocks(size, back)


def body(field, out_grad, first_weight, second_weight):
    extent = lax.axis_size("chan")
    slabs = lax.axis_size("slab")
    me = lax.axis_index("chan")
    size, planes, rows, depth = field.shape
    channels = size * extent
    pairs = planes // 2
    share = rows // extent
    factor = 1.0 / math.sqrt(planes * slabs * rows * depth)

    def to_chan(value, shift):
        return lax.ppermute(value, "chan", [(i, (i + shift) % extent) for i in range(extent)])

    def to_next(value):
        return lax.ppermute(value, "slab", [(i, (i + 1) % slabs) for i in range(slabs)])

    def to_prev(value):
        return lax.ppermute(value, "slab", [((i + 1) % slabs, i) for i in range(slabs)])

    def relayed(value, *others):
        shape = jax.ShapeDtypeStruct(value.shape, value.dtype)
        early = [value, *others]
        return call(relay_kernel, [shape], early, loose=len(early), same={0: 0})[0]

    piece = jax.ShapeDtypeStruct((share + 8, 2, size, depth), BF16)
    by_tap = (27, size, channels)
    longer = jax.ShapeDtypeStruct((share + 15, 2, size, depth), BF16)
    rest = [piece] * (pairs - 1)
    made = call(
        functools.partial(field_kernel, extent, 4),
        [piece] + rest + ([longer] + rest) * (extent - 1),
        [field],
        [pltpu.VMEM((size * planes * rows, depth), F32)],
        moved=field.size * 6,
    )
    first_sent = list(made[pairs::pairs])
    others = extent - 1
    packed = call(
        functools.partial(pack_kernel, others, share + 8),
        [longer] * others + [jax.ShapeDtypeStruct((7, 2, size, 4 * channels), BF16)],
        first_sent
        + [jnp.transpose(first_weight, (1, 0, 2)), jnp.transpose(second_weight, (1, 0, 2))],
        [pltpu.SemaphoreType.DMA((max(others, 1),))],
        loose=others,
        same={k: k for k in range(others)},
    )
    first_sent, pack = packed[:-1], packed[-1]
    parts = [list(made[:pairs])]
    whole = size % 16 == 0
    own_before, own_after = [], []
    if whole:
        own_before, own_after = [to_next(parts[0][-1])], [to_prev(parts[0][0])]
    for j in range(1, extent):
        sent = [first_sent[j - 1]] + list(made[j * pairs + 1 : (j + 1) * pairs])
        parts.append([to_chan(value, j) for value in sent])
    packs = [pack] + [part[0] for part in parts[1:]]
    grad_piece = jax.ShapeDtypeStruct((share + 4, 2, channels, depth), BF16)
    grads = call(
        functools.partial(grad_kernel, extent, 2),
        [grad_piece] * pairs,
        [pack, out_grad],
        [pltpu.VMEM((channels * planes * rows, depth), F32)],
        moved=out_grad.size * 4,
        loose=1,
    )
    matrix = jax.ShapeDtypeStruct((6 * channels, 12 * channels), BF16)
    first_wide, second_wide, first_back, second_back = call(
        functools.partial(matrix_kernel, extent),
        [matrix] * 4,
        packs,
        moved=matrix.size * 8,
    )
    if whole and extent > 1 and pairs > 1:
        parts[1][-1] = relayed(parts[1][-1], grads[0])
        parts[1][0] = relayed(parts[1][0], own_after[0])
    by_pair = [[parts[j][p] for j in range(extent)] for p in range(pairs)]
    groups = extent
    if not whole:
        by_pair = [
            [jnp.concatenate([piece[: share + 8] for piece in pieces], axis=2)]
            for pieces in by_pair
        ]
        groups = 1
    before = own_before + [to_next(piece) for piece in by_pair[-1][len(own_before) :]]
    after = own_after + [to_prev(piece) for piece in by_pair[0][len(own_after) :]]
    fields = [before] + by_pair + [after]

    def many(count, rows_each):
        return [jax.ShapeDtypeStruct((rows_each, 2, channels, depth), BF16)] * count

    def flat(lists):
        return [piece for pieces in lists for piece in pieces]

    work = 27 * 2 * channels * channels * depth * 2
    space = 4 * channels * depth * share

    made = call(
        functools.partial(forward_kernel, groups, pairs, 0),
        many(2 * pairs, share + 6) + many(pairs - 1, share + 4),
        flat(fields[: pairs + 1]) + list(grads[: pairs - 1]) + [first_wide, second_wide],
        flops=work * (2 * pairs - 1) * share,
        moved=space * 4 * pairs,
    )
    hiddens, slopes, deltas = made[:pairs], made[pairs : 2 * pairs], made[2 * pairs :]
    made = call(
        functools.partial(forward_kernel, groups, 1, 1),
        many(2, share + 6) + many(1, share + 4),
        flat(fields[pairs:]) + [hiddens[-1], grads[-1], first_wide, second_wide],
        flops=work * 2 * share,
        moved=space * 6,
    )
    hiddens = list(hiddens) + [made[0]]
    slopes = list(slopes) + [made[1]]
    deltas = list(deltas) + [made[2]]
    delta_after = to_prev(deltas[0])
    delta_before = to_next(deltas[-1])

    raw = jax.ShapeDtypeStruct((extent, 7, size, 4 * channels), F32)
    whole_sum = (6 * channels, 12 * channels)
    sums = jax.ShapeDtypeStruct(whole_sum, F32)
    made = call(
        functools.partial(middle_kernel, share, groups, pairs),
        [raw, sums] + many(pairs - 1, share + 2),
        hiddens + deltas + [second_back] + slopes[1:pairs] + flat(fields[1:-1]),
        [pltpu.VMEM(whole_sum, F32)],
        flops=work * (3 * pairs - 2) * share,
        moved=space * 9,
    )
    second_raw, sums_then, later = made[0], made[1], list(made[2:])
    made = call(
        functools.partial(back_kernel, share, groups),
        many(1, share + 2) + [sums],
        [second_back, deltas[-1], delta_after, slopes[-1]] + flat(fields[-2:]) + [sums_then],
        flops=work * 2 * share,
        moved=space * 6,
    )
    later, sums_then = later + [made[0]], made[1]

    def field_grad(firsts):
        count = len(firsts) - 1
        return list(
            call(
                functools.partial(last_kernel, count),
                [jax.ShapeDtypeStruct((share, 2 * count, size, depth), BF16)] * extent,
                firsts + [first_back],
                flops=work * count * share,
                moved=space * 2 * count,
            )
        )

    def exchanged(made):
        pieces = [made[0]] + [None] * (extent - 1)
        for j in range(1, extent):
            pieces[extent - j] = to_chan(made[j], extent - j)
        return pieces

    pieces, early = [], [later[0]]
    if pairs > 1:
        early = field_grad(later)
        pieces = exchanged(early)
    first, keep, send = call(
        functools.partial(first_kernel, share, groups),
        many(1, share + 2) + [raw] * 2,
        [early[0], second_back, delta_before, deltas[0], slopes[0]]
        + flat(fields[0:2])
        + [sums_then, second_raw],
        [pltpu.VMEM(whole_sum, F32)],
        flops=work * 2 * share,
        moved=space * 6,
        loose=1,
    )

    def stepped(value, stride, shift=0):
        if shift % extent == 0:
            return lax.ppermute(value, "slab", [(i, i ^ stride) for i in range(slabs)])
        pairs_of = []
        for i in range(slabs):
            for k in range(extent):
                there = (i ^ stride) * extent + (k + shift) % extent
                pairs_of.append((i * extent + k, there))
        return lax.ppermute(value, ("slab", "chan"), pairs_of)

    portion = jax.ShapeDtypeStruct(raw.shape[1:], F32)
    made = field_grad([first, later[0]])
    plain = slabs & (slabs - 1) == 0 and slabs >= 4
    if plain:
        ahead = made[:1]
        kept = call(
            functools.partial(split_kernel, len(ahead)),
            [portion] * extent,
            ahead + [keep, stepped(send, 1)],
            loose=len(ahead),
        )
        shares = [kept[0]] + [to_chan(kept[j], extent - j) for j in range(1, extent)]
        shares += [stepped(kept[j], 2, extent - j) for j in range(extent)]
        ahead = pieces[1:2]
        (mine,) = call(
            functools.partial(add_kernel, len(ahead)), [portion], ahead + shares, loose=len(ahead)
        )
        made = [made[0]] + [relayed(value, mine) for value in made[1:]]
    pieces = exchanged(made) + pieces

    token, input_grad = call(
        functools.partial(merge_kernel, extent),
        [jax.ShapeDtypeStruct((8, 128), F32), jax.ShapeDtypeStruct(field.shape, BF16)],
        pieces,
        [pltpu.VMEM((rows * planes * size, depth), F32)],
        moved=4 * field.size,
    )
    if plain:
        stride = 4
        while stride < slabs:
            radix = 4 if slabs % (4 * stride) == 0 else 2
            got = [mine] + [stepped(mine, m * stride) for m in range(1, radix)]
            last = stride * radix == slabs
            ahead = [token] if last else []
            (mine,) = call(
                functools.partial(add_kernel, len(ahead)), [portion], ahead + got, loose=len(ahead)
            )
            stride *= radix
        other = stepped(mine, 1)
    else:
        mine, other = keep[0], send[0]
        for j in range(1, extent):
            mine, other = mine + to_chan(keep[j], extent - j), other + to_chan(send[j], extent - j)
        even = lax.rem(lax.axis_index("slab"), 2) == 0
        mine, other = jnp.where(even, mine, other), jnp.where(even, other, mine)
        mine, other = lax.psum((mine, other), "slab")
        mine, other = jnp.where(even, mine, other), jnp.where(even, other, mine)
    first_grad, second_grad = call(
        functools.partial(finish_kernel, factor),
        [jax.ShapeDtypeStruct(by_tap, F32)] * 2,
        [mine, other],
    )
    first_grad, second_grad = (jnp.transpose(g, (1, 0, 2)) for g in (first_grad, second_grad))
    return input_grad, first_grad, second_grad


def solution(mesh):
    placed = (
        P("chan", "slab", None, None),
        P(None, "slab", None, None),
        P("chan", None, None),
        P("chan", None, None),
    )
    return jax.shard_map(
        body,
        mesh=mesh,
        in_specs=placed,
        out_specs=(P("chan", "slab", None, None), P("chan", None, None), P("chan", None, None)),
        check_vma=False,
    )
```

```python
import functools
import math

import jax
import jax.numpy as jnp
from jax import lax
from jax.experimental import pallas as pl
from jax.experimental.pallas import tpu as pltpu
from jax.sharding import PartitionSpec as P

F32 = jnp.float32
BF16 = jnp.bfloat16
LIMIT = 16 * 1024 * 1024


def call(kernel, outs, args, scratch=(), flops=0, moved=0, loose=0, same=None):
    whole = pl.BlockSpec(memory_space=pltpu.VMEM)
    still = pl.BlockSpec(memory_space=pl.ANY)
    return pl.pallas_call(
        kernel,
        out_shape=outs,
        in_specs=[still] * loose + [whole] * (len(args) - loose),
        out_specs=[still if k in (same or {}).values() else whole for k in range(len(outs))],
        input_output_aliases=same or {},
        scratch_shapes=list(scratch),
        compiler_params=pltpu.CompilerParams(vmem_limit_bytes=LIMIT),
        cost_estimate=pl.CostEstimate(flops=flops, bytes_accessed=moved, transcendentals=0),
    )(*args)


def in_blocks(count, body):
    block = max(k for k in range(1, 8) if count % k == 0)
    if block < 4:
        block = min(count, 15)

    def several(r, _):
        for k in range(block):
            body(r * block + k)
        return 0

    lax.fori_loop(0, count // block, several, 0)
    for k in range(count // block * block, count):
        body(k)


def widened(x_ref, wide):
    count, planes, rows = x_ref.shape[:3]

    def widen(i):
        for x in range(planes):
            start = pl.multiple_of((i * planes + x) * rows, 8)
            wide[pl.ds(start, rows), :] = x_ref[i, x].astype(F32)

    in_blocks(count, widen)


def turn(wide, outs, shape, base, length):
    count, planes, rows = shape

    def one(f):
        y = lax.rem(base + f, rows)
        for x in range(planes):
            tile = wide[pl.ds(x * rows + y, count, stride=planes * rows), :]
            outs[x // 2][f, x % 2] = tile.astype(BF16)

    in_blocks(length, one)


def field_kernel(extent, margin, x_ref, *refs):
    outs, wide = refs[:-1], refs[-1]
    count, planes, rows = x_ref.shape[:3]
    pairs = planes // 2
    share = rows // extent
    widened(x_ref, wide)
    me = lax.axis_index("chan")
    for s in range(extent):
        base = lax.rem(me + s, extent) * share - margin + rows
        turn(
            wide,
            outs[s * pairs : (s + 1) * pairs],
            (count, planes, rows),
            base,
            share + 2 * margin,
        )


def pack_kernel(after, first, second, packed):
    del after
    blank = jnp.zeros(first.shape[1:], F32)
    for h in range(packed.shape[0]):
        parts = []
        for ref in (first, second):
            for t in (2 * h, 2 * h + 1):
                parts.append(ref[t].astype(F32) if t < ref.shape[0] else blank)
        packed[h] = jnp.concatenate(parts, axis=1).astype(BF16)


def grad_kernel(extent, margin, after, x_ref, *refs):
    del after
    outs, wide = refs[:-1], refs[-1]
    count, planes, rows = x_ref.shape[:3]
    share = rows // extent
    widened(x_ref, wide)
    base = lax.axis_index("chan") * share - margin + rows
    turn(wide, outs, (count, planes, rows), base, share + 2 * margin)


def matrix_kernel(extent, *refs):
    packs, outs = refs[:extent], refs[extent:]
    me = lax.axis_index("chan")
    quarter = packs[0].shape[2] // 4
    taps = []
    turned = []
    for h in range(packs[0].shape[0]):
        tiles = [pack[h].astype(F32) for pack in packs]
        own = jnp.concatenate(tiles, axis=0)
        fixed = []
        for g in range(extent):
            place = lax.rem(me + extent - g, extent)
            tile = tiles[0]
            for j in range(1, extent):
                tile = jnp.where(place == j, tiles[j], tile)
            fixed.append(tile)
        both = jnp.concatenate(
            [own[:, : 2 * quarter], jnp.concatenate(fixed, axis=0)[:, 2 * quarter :]], axis=1
        )
        across = both.T
        for side in range(2):
            taps.append(
                [both[:, k * quarter : (k + 1) * quarter] for k in (side, side + 2)]
            )
            turned.append(
                [across[k * quarter : (k + 1) * quarter] for k in (side, side + 2)]
            )
    channels = quarter
    blank = jnp.zeros((channels, channels), F32)
    for k in range(2):
        for out, blocks, flip in ((outs[k], turned, False), (outs[2 + k], taps, True)):
            for e in range(3):
                for x in range(2):
                    chunks = []
                    for pair in range(2):
                        for b in range(3):
                            for side in range(2):
                                a = 2 * pair + side - x
                                t = 9 * a + 3 * b + e
                                inside = 0 <= a <= 2
                                t = 26 - t if flip else t
                                chunks.append(blocks[t][k] if inside else blank)
                    low = (2 * e + x) * channels
                    out[low : low + channels, :] = jnp.concatenate(chunks, axis=1).astype(BF16)


def stacked(refs, row, count):
    if len(refs) == 1:
        part = refs[0][pl.ds(row, count)]
        return part.reshape(-1, part.shape[-1])
    parts = [ref[row + b, x] for b in range(count) for x in range(2) for ref in refs]
    return jnp.concatenate(parts, axis=0)


def taps(weight, pairs, row):
    sides = []
    for p in range(len(pairs) - 1):
        for q in range(2):
            above = stacked(pairs[p], row + q, 3)
            below = stacked(pairs[p + 1], row + q, 3)
            sides.append(jnp.concatenate([above, below], axis=0))
    lifted = jnp.dot(weight, jnp.concatenate(sides, axis=1), preferred_element_type=F32)
    third = lifted.shape[0] // 3
    depth = sides[0].shape[1]
    sums = []
    for k in range(len(sides)):
        side = lifted[:, k * depth : (k + 1) * depth]
        sums.append(
            side[third : 2 * third]
            + pltpu.roll(side[:third], 1, 1)
            + pltpu.roll(side[2 * third :], depth - 1, 1)
        )
    return [sums[2 * p : 2 * p + 2] for p in range(len(pairs) - 1)]


def silu_parts(v):
    sig = jax.nn.sigmoid(v)
    return sig, sig * (1.0 + v * (1.0 - sig))


def forward_kernel(groups, fresh, ready, *refs):
    refs = list(refs)
    fields = [[refs.pop(0) for _ in range(groups)] for _ in range(fresh + 1)]
    hiddens = [refs.pop(0) for _ in range(ready)]
    count = fresh + ready - 1
    grads = [refs.pop(0) for _ in range(count)]
    first, second = refs.pop(0), refs.pop(0)
    made = [refs.pop(0) for _ in range(fresh)]
    slopes = [refs.pop(0) for _ in range(fresh)]
    deltas = refs
    hiddens = hiddens + made

    def one(r):
        row = 2 * r
        for p, sums in enumerate(taps(first[...], fields, row)):
            for q, v in enumerate(sums):
                sig, slope = silu_parts(v)
                shape = made[p].shape[1:]
                made[p][row + q] = (v * sig).astype(BF16).reshape(shape)
                slopes[p][row + q] = slope.astype(BF16).reshape(shape)

    in_blocks(made[0].shape[0] // 2, one)

    def two(r):
        row = 2 * r
        for p, sums in enumerate(taps(second[...], [[ref] for ref in hiddens], row)):
            for q, v in enumerate(sums):
                shape = deltas[p].shape[1:]
                out_grad = grads[p][row + q].astype(F32)
                slope = silu_parts(v)[1].reshape(shape)
                deltas[p][row + q] = (out_grad * slope).astype(BF16)

    if count > 0:
        in_blocks(deltas[0].shape[0] // 2, two)


def planes_of(pairs):
    return [(refs, x) for refs in pairs for x in range(2)]


def weight_loop(total, pieces, first_row, deltas, delta_row, count):
    blocks = [k for k in range(1, 13) if count // 2 % k == 0 and k * len(deltas) <= 12]
    together = max(blocks, default=1)

    def step(r, _):
        left, right = [], []
        for k in range(together):
            row = 2 * (r * together + k)
            for x, ((delta,), place) in enumerate(deltas):
                rows = []
                for q in range(2):
                    wide = delta[delta_row + row + q, place]
                    plain = wide.astype(F32)
                    depth = plain.shape[1]
                    rows += [
                        pltpu.roll(plain, depth - 1, 1).astype(BF16),
                        wide,
                        pltpu.roll(plain, 1, 1).astype(BF16),
                    ]
                left.append(jnp.concatenate(rows, axis=0))
                rows = []
                for refs, side in pieces[x : x + 3]:
                    for b in range(4):
                        for ref in refs:
                            rows.append(ref[first_row + row + b, side])
                right.append(jnp.concatenate(rows, axis=0))
        total[...] += lax.dot_general(
            jnp.concatenate(left, axis=1),
            jnp.concatenate(right, axis=1),
            (((1,), (1,)), ((), ())),
            preferred_element_type=F32,
        )
        return 0

    lax.fori_loop(0, count // 2 // together, step, 0)


def weight_fold(total, size):
    lanes = total.shape[0] // 2
    channels = total.shape[1] // 12
    upper, lower = total[:lanes, :].T, total[lanes:, :].T
    groups = []
    for g in range(channels // size):
        taps_of = []
        for a in range(3):
            for b in range(3):
                start = (4 * a + b) * channels + g * size
                part = (
                    upper[start : start + size]
                    + lower[start + channels : start + channels + size]
                )
                taps_of += [part[:, e * channels : (e + 1) * channels] for e in range(3)]
        blank = jnp.zeros((size, channels), F32)
        taps_of.append(blank)
        groups.append([jnp.concatenate(taps_of[4 * h : 4 * h + 4], axis=1) for h in range(7)])
    return groups


def first_deltas(weight, deltas, slopes, firsts):
    def one(r):
        row = 2 * r
        for p, sums in enumerate(taps(weight[...], [[delta] for delta in deltas], row)):
            for q, v in enumerate(sums):
                shape = firsts[p].shape[1:]
                slope = slopes[p][row + 2 + q].astype(F32)
                firsts[p][row + q] = (v.reshape(shape) * slope).astype(BF16)

    in_blocks(firsts[0].shape[0] // 2, one)


def back_part(share, kept, weight, deltas, slopes, fields, firsts, total):
    first_deltas(weight, deltas, slopes, firsts)
    near = planes_of(fields)
    own = planes_of([[ref] for ref in firsts])
    low, high = kept
    weight_loop(total, near[low : high + 2], 3, own[low:high], 1, share)


def middle_kernel(share, groups, pairs, *refs):
    refs = list(refs)
    hiddens = [[refs.pop(0)] for _ in range(pairs + 1)]
    deltas = [refs.pop(0) for _ in range(pairs)]
    weight = refs.pop(0)
    count = pairs - 1
    slopes = [refs.pop(0) for _ in range(count)]
    fields = [[refs.pop(0) for _ in range(groups)] for _ in range(pairs)]
    raw, first_total = refs.pop(0), refs.pop(0)
    firsts, total = refs[:count], refs[-1]
    total[...] = jnp.zeros_like(total)
    weight_loop(total, planes_of(hiddens), 2, planes_of([[d] for d in deltas]), 2, share)
    for g, tiles in enumerate(weight_fold(total, raw.shape[2])):
        for h, tile in enumerate(tiles):
            raw[g, h] = tile
    first_total[...] = jnp.zeros_like(first_total)
    if count > 0:
        kept = (0, 2 * count)
        back_part(share, kept, weight, deltas, slopes, fields, firsts, first_total)


def back_kernel(share, groups, weight, one, two, slope, *refs):
    refs = list(refs)
    fields = [[refs.pop(0) for _ in range(groups)] for _ in range(2)]
    before, first, total = refs
    total[...] = before[...]
    back_part(share, (0, 1), weight, [one, two], [slope], fields, [first], total)


def first_kernel(share, groups, after, weight, one, two, slope, *refs):
    del after
    refs = list(refs)
    fields = [[refs.pop(0) for _ in range(groups)] for _ in range(2)]
    before, second = refs.pop(0), refs.pop(0)
    first, total = refs[0], refs[-1]
    extent = (len(refs) - 2) // 2
    keep, send = refs[1 : 1 + extent], refs[1 + extent : -1]
    total[...] = before[...]
    back_part(share, (1, 2), weight, [one, two], [slope], fields, [first], total)
    halves, size = keep[0].shape[:2]
    me = lax.axis_index("chan")
    groups_of = weight_fold(total, size)

    def place(ours, theirs):
        for g, tiles in enumerate(groups_of):
            there = lax.rem(me + extent - g, extent)
            for h in range(halves):
                ours[g][h] = tiles[h]
                theirs[g][h] = second[there, h]

    odd = lax.rem(lax.axis_index("slab"), 2)

    @pl.when(odd == 0)
    def _():
        place(keep, send)

    @pl.when(odd == 1)
    def _():
        place(send, keep)


def last_kernel(pairs, *refs):
    refs = list(refs)
    firsts = [refs.pop(0) for _ in range(pairs + 1)]
    weight = refs.pop(0)
    outs = refs

    def one(r):
        row = 2 * r
        size = outs[0].shape[2]
        channels = len(outs) * size
        for p, sums in enumerate(taps(weight[...], [[first] for first in firsts], row)):
            for q, v in enumerate(sums):
                for x in range(2):
                    for j, out in enumerate(outs):
                        low = x * channels + j * size
                        out[row + q, 2 * p + x] = v[low : low + size].astype(BF16)

    in_blocks(outs[0].shape[0] // 2, one)


def finish_kernel(factor, mine, other, first, second):
    channels = first.shape[2]

    def place(ours, theirs):
        for out, sums in ((ours, mine), (theirs, other)):
            for t in range(27):
                low = t % 4 * channels
                out[t] = sums[t // 4, :, low : low + channels] * factor

    odd = lax.rem(lax.axis_index("slab"), 2)

    @pl.when(odd == 0)
    def _():
        place(first, second)

    @pl.when(odd == 1)
    def _():
        place(second, first)


def add_kernel(ahead, *refs):
    values = [ref[...] for ref in refs[ahead:-1]]
    while len(values) > 1:
        values = [sum(values[k + 1 : k + 2], values[k]) for k in range(0, len(values), 2)]
    refs[-1][...] = values[0]


def relay_kernel(*refs):
    pass


def merge_kernel(extent, *refs):
    pieces, token, out, wide = refs[:-3], refs[-3], refs[-2], refs[-1]
    token[...] = jnp.zeros_like(token)
    size, planes, rows = out.shape[:3]
    share = rows // extent
    me = lax.axis_index("chan")
    for j in range(extent):
        base = lax.rem(me + extent - j, extent) * share

        def widen(f, mine=pieces[j::extent], base=base):
            x = 0
            for piece in mine:
                for k in range(piece.shape[1]):
                    start = ((base + f) * planes + x) * size
                    start = pl.multiple_of(start, 8) if size % 8 == 0 else start
                    wide[pl.ds(start, size), :] = piece[f, k].astype(F32)
                    x += 1

        in_blocks(share, widen)

    def back(i):
        for x in range(planes):
            tile = wide[pl.ds(x * size + i, rows, stride=planes * size), :]
            out[i, x] = tile.astype(BF16)

    in_blocks(size, back)


def body(field, out_grad, first_weight, second_weight):
    extent = lax.axis_size("chan")
    slabs = lax.axis_size("slab")
    me = lax.axis_index("chan")
    size, planes, rows, depth = field.shape
    channels = size * extent
    pairs = planes // 2
    share = rows // extent
    factor = 1.0 / math.sqrt(planes * slabs * rows * depth)

    def to_chan(value, shift):
        return lax.ppermute(value, "chan", [(i, (i + shift) % extent) for i in range(extent)])

    def to_next(value):
        return lax.ppermute(value, "slab", [(i, (i + 1) % slabs) for i in range(slabs)])

    def to_prev(value):
        return lax.ppermute(value, "slab", [((i + 1) % slabs, i) for i in range(slabs)])

    def relayed(value, *others):
        shape = jax.ShapeDtypeStruct(value.shape, value.dtype)
        early = [value, *others]
        return call(relay_kernel, [shape], early, loose=len(early), same={0: 0})[0]

    piece = jax.ShapeDtypeStruct((share + 8, 2, size, depth), BF16)
    by_tap = (27, size, channels)
    made = call(
        functools.partial(field_kernel, extent, 4),
        [piece] * (extent * pairs),
        [field],
        [pltpu.VMEM((size * planes * rows, depth), F32)],
        moved=field.size * 6,
    )
    parts = [list(made[:pairs])]
    for j in range(1, extent):
        parts.append([to_chan(value, j) for value in made[j * pairs : (j + 1) * pairs]])
    (pack,) = call(
        pack_kernel,
        [jax.ShapeDtypeStruct((14, size, 4 * channels), BF16)],
        [made[0], jnp.transpose(first_weight, (1, 0, 2)), jnp.transpose(second_weight, (1, 0, 2))],
        loose=1,
    )
    packs = [pack] + [to_chan(pack, j) for j in range(1, extent)]
    whole = size % 16 == 0
    own_before, own_after = [], []
    if whole:
        own_before, own_after = [to_next(parts[0][-1])], [to_prev(parts[0][0])]
    grad_piece = jax.ShapeDtypeStruct((share + 4, 2, channels, depth), BF16)
    grads = call(
        functools.partial(grad_kernel, extent, 2),
        [grad_piece] * pairs,
        [pack, out_grad],
        [pltpu.VMEM((channels * planes * rows, depth), F32)],
        moved=out_grad.size * 4,
        loose=1,
    )
    matrix = jax.ShapeDtypeStruct((6 * channels, 12 * channels), BF16)
    first_wide, second_wide, first_back, second_back = call(
        functools.partial(matrix_kernel, extent),
        [matrix] * 4,
        packs,
        moved=matrix.size * 8,
    )
    if whole and extent > 1 and pairs > 1:
        parts[1][-1] = relayed(parts[1][-1], grads[0])
        parts[1][0] = relayed(parts[1][0], own_after[0], *packs[1:])
    by_pair = [[parts[j][p] for j in range(extent)] for p in range(pairs)]
    groups = extent
    if not whole:
        by_pair = [[jnp.concatenate(pieces, axis=2)] for pieces in by_pair]
        groups = 1
    before = own_before + [to_next(piece) for piece in by_pair[-1][len(own_before) :]]
    after = own_after + [to_prev(piece) for piece in by_pair[0][len(own_after) :]]
    fields = [before] + by_pair + [after]

    def many(count, rows_each):
        return [jax.ShapeDtypeStruct((rows_each, 2, channels, depth), BF16)] * count

    def flat(lists):
        return [piece for pieces in lists for piece in pieces]

    work = 27 * 2 * channels * channels * depth * 2
    space = 4 * channels * depth * share

    made = call(
        functools.partial(forward_kernel, groups, pairs, 0),
        many(2 * pairs, share + 6) + many(pairs - 1, share + 4),
        flat(fields[: pairs + 1]) + list(grads[: pairs - 1]) + [first_wide, second_wide],
        flops=work * (2 * pairs - 1) * share,
        moved=space * 4 * pairs,
    )
    hiddens, slopes, deltas = made[:pairs], made[pairs : 2 * pairs], made[2 * pairs :]
    made = call(
        functools.partial(forward_kernel, groups, 1, 1),
        many(2, share + 6) + many(1, share + 4),
        flat(fields[pairs:]) + [hiddens[-1], grads[-1], first_wide, second_wide],
        flops=work * 2 * share,
        moved=space * 6,
    )
    hiddens = list(hiddens) + [made[0]]
    slopes = list(slopes) + [made[1]]
    deltas = list(deltas) + [made[2]]
    delta_after = to_prev(deltas[0])
    delta_before = to_next(deltas[-1])

    raw = jax.ShapeDtypeStruct((extent, 7, size, 4 * channels), F32)
    whole_sum = (6 * channels, 12 * channels)
    sums = jax.ShapeDtypeStruct(whole_sum, F32)
    made = call(
        functools.partial(middle_kernel, share, groups, pairs),
        [raw, sums] + many(pairs - 1, share + 2),
        hiddens + deltas + [second_back] + slopes[1:pairs] + flat(fields[1:-1]),
        [pltpu.VMEM(whole_sum, F32)],
        flops=work * (3 * pairs - 2) * share,
        moved=space * 9,
    )
    second_raw, sums_then, later = made[0], made[1], list(made[2:])
    made = call(
        functools.partial(back_kernel, share, groups),
        many(1, share + 2) + [sums],
        [second_back, deltas[-1], delta_after, slopes[-1]] + flat(fields[-2:]) + [sums_then],
        flops=work * 2 * share,
        moved=space * 6,
    )
    later, sums_then = later + [made[0]], made[1]

    def field_grad(firsts):
        count = len(firsts) - 1
        return list(
            call(
                functools.partial(last_kernel, count),
                [jax.ShapeDtypeStruct((share, 2 * count, size, depth), BF16)] * extent,
                firsts + [first_back],
                flops=work * count * share,
                moved=space * 2 * count,
            )
        )

    def exchanged(made):
        pieces = [made[0]] + [None] * (extent - 1)
        for j in range(1, extent):
            pieces[extent - j] = to_chan(made[j], extent - j)
        return pieces

    pieces, early = [], [later[0]]
    if pairs > 1:
        early = field_grad(later)
        pieces = exchanged(early)
    portion = jax.ShapeDtypeStruct(raw.shape[1:], F32)
    made = call(
        functools.partial(first_kernel, share, groups),
        many(1, share + 2) + [portion] * (2 * extent),
        [early[0], second_back, delta_before, deltas[0], slopes[0]]
        + flat(fields[0:2])
        + [sums_then, second_raw],
        [pltpu.VMEM(whole_sum, F32)],
        flops=work * 2 * share,
        moved=space * 6,
        loose=1,
    )

    first, keep, send = made[0], made[1 : 1 + extent], made[1 + extent :]

    def stepped(value, stride, shift=0):
        if shift % extent == 0:
            return lax.ppermute(value, "slab", [(i, i ^ stride) for i in range(slabs)])
        pairs_of = []
        for i in range(slabs):
            for k in range(extent):
                there = (i ^ stride) * extent + (k + shift) % extent
                pairs_of.append((i * extent + k, there))
        return lax.ppermute(value, ("slab", "chan"), pairs_of)

    made = field_grad([first, later[0]])
    plain = slabs & (slabs - 1) == 0 and slabs >= 4
    if plain:
        shares = [keep[0], stepped(send[0], 1)]
        for j in range(1, extent):
            shares += [to_chan(keep[j], extent - j), stepped(send[j], 1, extent - j)]
        ahead = made[:1] + pieces[1:2]
        (mine,) = call(
            functools.partial(add_kernel, len(ahead)), [portion], ahead + shares, loose=len(ahead)
        )
        made = [made[0]] + [relayed(value, mine) for value in made[1:]]
    pieces = exchanged(made) + pieces

    token, input_grad = call(
        functools.partial(merge_kernel, extent),
        [jax.ShapeDtypeStruct((8, 128), F32), jax.ShapeDtypeStruct(field.shape, BF16)],
        pieces,
        [pltpu.VMEM((rows * planes * size, depth), F32)],
        moved=4 * field.size,
    )
    if plain:
        stride = 2
        while stride < slabs:
            radix = 4 if slabs % (4 * stride) == 0 else 2
            got = [mine] + [stepped(mine, m * stride) for m in range(1, radix)]
            last = stride * radix == slabs
            ahead = [token] if last else []
            (mine,) = call(
                functools.partial(add_kernel, len(ahead)), [portion], ahead + got, loose=len(ahead)
            )
            stride *= radix
        other = stepped(mine, 1)
    else:
        mine, other = keep[0], send[0]
        for j in range(1, extent):
            mine, other = mine + to_chan(keep[j], extent - j), other + to_chan(send[j], extent - j)
        even = lax.rem(lax.axis_index("slab"), 2) == 0
        mine, other = jnp.where(even, mine, other), jnp.where(even, other, mine)
        mine, other = lax.psum((mine, other), "slab")
        mine, other = jnp.where(even, mine, other), jnp.where(even, other, mine)
    first_grad, second_grad = call(
        functools.partial(finish_kernel, factor),
        [jax.ShapeDtypeStruct(by_tap, F32)] * 2,
        [mine, other],
    )
    first_grad, second_grad = (jnp.transpose(g, (1, 0, 2)) for g in (first_grad, second_grad))
    return input_grad, first_grad, second_grad


def solution(mesh):
    placed = (
        P("chan", "slab", None, None),
        P(None, "slab", None, None),
        P("chan", None, None),
        P("chan", None, None),
    )
    return jax.shard_map(
        body,
        mesh=mesh,
        in_specs=placed,
        out_specs=(P("chan", "slab", None, None), P("chan", None, None), P("chan", None, None)),
        check_vma=False,
    )
```

```python
import functools
import math

import jax
import jax.numpy as jnp
from jax import lax
from jax.experimental import pallas as pl
from jax.experimental.pallas import tpu as pltpu
from jax.sharding import PartitionSpec as P

F32 = jnp.float32
BF16 = jnp.bfloat16
LIMIT = 16 * 1024 * 1024


def call(kernel, outs, args, scratch=(), flops=0, moved=0, loose=0, same=None):
    whole = pl.BlockSpec(memory_space=pltpu.VMEM)
    still = pl.BlockSpec(memory_space=pl.ANY)
    return pl.pallas_call(
        kernel,
        out_shape=outs,
        in_specs=[still] * loose + [whole] * (len(args) - loose),
        out_specs=[still if k in (same or {}).values() else whole for k in range(len(outs))],
        input_output_aliases=same or {},
        scratch_shapes=list(scratch),
        compiler_params=pltpu.CompilerParams(vmem_limit_bytes=LIMIT),
        cost_estimate=pl.CostEstimate(flops=flops, bytes_accessed=moved, transcendentals=0),
    )(*args)


def in_blocks(count, body):
    block = max(k for k in range(1, 8) if count % k == 0)
    if block < 4:
        block = min(count, 15)

    def several(r, _):
        for k in range(block):
            body(r * block + k)
        return 0

    lax.fori_loop(0, count // block, several, 0)
    for k in range(count // block * block, count):
        body(k)


def widened(x_ref, wide):
    count, planes, rows = x_ref.shape[:3]

    def widen(i):
        for x in range(planes):
            start = pl.multiple_of((i * planes + x) * rows, 8)
            wide[pl.ds(start, rows), :] = x_ref[i, x].astype(F32)

    in_blocks(count, widen)


def turn(wide, outs, shape, base, length):
    count, planes, rows = shape

    def one(f):
        y = lax.rem(base + f, rows)
        for x in range(planes):
            tile = wide[pl.ds(x * rows + y, count, stride=planes * rows), :]
            outs[x // 2][f, x % 2] = tile.astype(BF16)

    in_blocks(length, one)


def field_kernel(extent, margin, x_ref, *refs):
    outs, wide = refs[:-1], refs[-1]
    count, planes, rows = x_ref.shape[:3]
    pairs = planes // 2
    share = rows // extent
    widened(x_ref, wide)
    me = lax.axis_index("chan")
    for s in range(extent):
        base = lax.rem(me + s, extent) * share - margin + rows
        turn(
            wide,
            outs[s * pairs : (s + 1) * pairs],
            (count, planes, rows),
            base,
            share + 2 * margin,
        )


def pack_kernel(after, first, second, packed):
    del after
    blank = jnp.zeros(first.shape[1:], F32)
    for h in range(packed.shape[0]):
        parts = []
        for ref in (first, second):
            for t in (2 * h, 2 * h + 1):
                parts.append(ref[t].astype(F32) if t < ref.shape[0] else blank)
        packed[h] = jnp.concatenate(parts, axis=1).astype(BF16)


def grad_kernel(extent, margin, after, x_ref, *refs):
    del after
    outs, wide = refs[:-1], refs[-1]
    count, planes, rows = x_ref.shape[:3]
    share = rows // extent
    widened(x_ref, wide)
    base = lax.axis_index("chan") * share - margin + rows
    turn(wide, outs, (count, planes, rows), base, share + 2 * margin)


def matrix_kernel(extent, *refs):
    packs, outs = refs[:extent], refs[extent:]
    me = lax.axis_index("chan")
    quarter = packs[0].shape[2] // 4
    taps = []
    turned = []
    for h in range(packs[0].shape[0]):
        tiles = [pack[h].astype(F32) for pack in packs]
        own = jnp.concatenate(tiles, axis=0)
        fixed = []
        for g in range(extent):
            place = lax.rem(me + extent - g, extent)
            tile = tiles[0]
            for j in range(1, extent):
                tile = jnp.where(place == j, tiles[j], tile)
            fixed.append(tile)
        both = jnp.concatenate(
            [own[:, : 2 * quarter], jnp.concatenate(fixed, axis=0)[:, 2 * quarter :]], axis=1
        )
        across = both.T
        for side in range(2):
            taps.append(
                [both[:, k * quarter : (k + 1) * quarter] for k in (side, side + 2)]
            )
            turned.append(
                [across[k * quarter : (k + 1) * quarter] for k in (side, side + 2)]
            )
    channels = quarter
    blank = jnp.zeros((channels, channels), F32)
    for k in range(2):
        for out, blocks, flip in ((outs[k], turned, False), (outs[2 + k], taps, True)):
            for e in range(3):
                for x in range(2):
                    chunks = []
                    for pair in range(2):
                        for b in range(3):
                            for side in range(2):
                                a = 2 * pair + side - x
                                t = 9 * a + 3 * b + e
                                inside = 0 <= a <= 2
                                t = 26 - t if flip else t
                                chunks.append(blocks[t][k] if inside else blank)
                    low = (2 * e + x) * channels
                    out[low : low + channels, :] = jnp.concatenate(chunks, axis=1).astype(BF16)


def stacked(refs, row, count):
    if len(refs) == 1:
        part = refs[0][pl.ds(row, count)]
        return part.reshape(-1, part.shape[-1])
    parts = [ref[row + b, x] for b in range(count) for x in range(2) for ref in refs]
    return jnp.concatenate(parts, axis=0)


def taps(weight, inputs, row):
    sides = []
    for above, below in inputs:
        for q in range(2):
            sides.append(
                jnp.concatenate([stacked(above, row + q, 3), stacked(below, row + q, 3)], axis=0)
            )
    lifted = jnp.dot(weight, jnp.concatenate(sides, axis=1), preferred_element_type=F32)
    third = lifted.shape[0] // 3
    depth = sides[0].shape[1]
    sums = []
    for k in range(len(sides)):
        side = lifted[:, k * depth : (k + 1) * depth]
        sums.append(
            side[third : 2 * third]
            + pltpu.roll(side[:third], 1, 1)
            + pltpu.roll(side[2 * third :], depth - 1, 1)
        )
    return [sums[2 * p : 2 * p + 2] for p in range(len(inputs))]


def neighbours(pairs):
    return list(zip(pairs[:-1], pairs[1:]))


def silu_parts(v):
    sig = jax.nn.sigmoid(v)
    return sig, sig * (1.0 + v * (1.0 - sig))


def forward_kernel(groups, fresh, ready, *refs):
    refs = list(refs)
    fields = [[refs.pop(0) for _ in range(groups)] for _ in range(fresh + 1)]
    hiddens = [refs.pop(0) for _ in range(ready)]
    count = fresh + ready - 1
    grads = [refs.pop(0) for _ in range(count)]
    first, second = refs.pop(0), refs.pop(0)
    made = [refs.pop(0) for _ in range(fresh)]
    slopes = [refs.pop(0) for _ in range(fresh)]
    deltas = refs
    hiddens = hiddens + made

    def one(r):
        row = 2 * r
        for p, sums in enumerate(taps(first[...], neighbours(fields), row)):
            for q, v in enumerate(sums):
                sig, slope = silu_parts(v)
                shape = made[p].shape[1:]
                made[p][row + q] = (v * sig).astype(BF16).reshape(shape)
                slopes[p][row + q] = slope.astype(BF16).reshape(shape)

    in_blocks(made[0].shape[0] // 2, one)

    def two(r):
        row = 2 * r
        for p, sums in enumerate(taps(second[...], neighbours([[ref] for ref in hiddens]), row)):
            for q, v in enumerate(sums):
                shape = deltas[p].shape[1:]
                out_grad = grads[p][row + q].astype(F32)
                slope = silu_parts(v)[1].reshape(shape)
                deltas[p][row + q] = (out_grad * slope).astype(BF16)

    if count > 0:
        in_blocks(deltas[0].shape[0] // 2, two)


def planes_of(pairs):
    return [(refs, x) for refs in pairs for x in range(2)]


def weight_loop(total, pieces, first_row, deltas, delta_row, count):
    blocks = [k for k in range(1, 13) if count // 2 % k == 0 and k * len(deltas) <= 12]
    together = max(blocks, default=1)

    def step(r, _):
        left, right = [], []
        for k in range(together):
            row = 2 * (r * together + k)
            for x, ((delta,), place) in enumerate(deltas):
                rows = []
                for q in range(2):
                    wide = delta[delta_row + row + q, place]
                    plain = wide.astype(F32)
                    depth = plain.shape[1]
                    rows += [
                        pltpu.roll(plain, depth - 1, 1).astype(BF16),
                        wide,
                        pltpu.roll(plain, 1, 1).astype(BF16),
                    ]
                left.append(jnp.concatenate(rows, axis=0))
                rows = []
                for refs, side in pieces[x : x + 3]:
                    for b in range(4):
                        for ref in refs:
                            rows.append(ref[first_row + row + b, side])
                right.append(jnp.concatenate(rows, axis=0))
        total[...] += lax.dot_general(
            jnp.concatenate(left, axis=1),
            jnp.concatenate(right, axis=1),
            (((1,), (1,)), ((), ())),
            preferred_element_type=F32,
        )
        return 0

    lax.fori_loop(0, count // 2 // together, step, 0)


def weight_fold(total, size):
    lanes = total.shape[0] // 2
    channels = total.shape[1] // 12
    upper, lower = total[:lanes, :].T, total[lanes:, :].T
    groups = []
    for g in range(channels // size):
        taps_of = []
        for a in range(3):
            for b in range(3):
                start = (4 * a + b) * channels + g * size
                part = (
                    upper[start : start + size]
                    + lower[start + channels : start + channels + size]
                )
                taps_of += [part[:, e * channels : (e + 1) * channels] for e in range(3)]
        blank = jnp.zeros((size, channels), F32)
        taps_of.append(blank)
        groups.append([jnp.concatenate(taps_of[4 * h : 4 * h + 4], axis=1) for h in range(7)])
    return groups


def first_deltas(weight, inputs, slopes, firsts):
    def one(r):
        row = 2 * r
        for p, sums in enumerate(taps(weight[...], inputs, row)):
            for q, v in enumerate(sums):
                shape = firsts[p].shape[1:]
                slope = slopes[p][row + 2 + q].astype(F32)
                firsts[p][row + q] = (v.reshape(shape) * slope).astype(BF16)

    in_blocks(firsts[0].shape[0] // 2, one)


def gradient_kernel(share, groups, extent, pairs, *refs):
    refs = list(refs)
    hiddens = [[refs.pop(0)] for _ in range(pairs + 1)]
    deltas = [[refs.pop(0)] for _ in range(pairs)]
    weight = refs.pop(0)
    slopes = [refs.pop(0) for _ in range(pairs + 1)]
    fields = [[refs.pop(0) for _ in range(groups)] for _ in range(pairs + 2)]
    keep, send = refs.pop(0), refs.pop(0)
    inner = [refs.pop(0) for _ in range(pairs - 1)]
    head, tail, none, second_total, first_total = refs
    none[...] = jnp.zeros_like(none)
    second_total[...] = jnp.zeros_like(second_total)
    first_total[...] = jnp.zeros_like(first_total)
    weight_loop(second_total, planes_of(hiddens), 2, planes_of(deltas), 2, share)
    firsts = [head] + inner + [tail]
    first_deltas(weight, neighbours([[none]] + deltas + [[none]]), slopes, firsts)
    parts = planes_of([[first] for first in firsts])
    weight_loop(first_total, planes_of(fields), 3, parts, 1, share)
    halves, size = keep.shape[1:3]
    me = lax.axis_index("chan")
    of_first = weight_fold(first_total, size)
    of_second = weight_fold(second_total, size)

    def place(ours, theirs):
        for g in range(extent):
            there = lax.rem(me + extent - g, extent)
            for h in range(halves):
                ours[g, h] = of_first[g][h]
                theirs[there, h] = of_second[g][h]

    odd = lax.rem(lax.axis_index("slab"), 2)

    @pl.when(odd == 0)
    def _():
        place(keep, send)

    @pl.when(odd == 1)
    def _():
        place(send, keep)


def back_kernel(then, weight, one, two, slope, first):
    del then
    first_deltas(weight, [([one], [two])], [slope], [first])


def last_kernel(pairs, after, *refs):
    del after
    refs = list(refs)
    firsts = [refs.pop(0) for _ in range(pairs + 1)]
    weight = refs.pop(0)
    outs = refs

    def one(r):
        row = 2 * r
        size = outs[0].shape[2]
        channels = len(outs) * size
        for p, sums in enumerate(taps(weight[...], neighbours([[first] for first in firsts]), row)):
            for q, v in enumerate(sums):
                for x in range(2):
                    for j, out in enumerate(outs):
                        low = x * channels + j * size
                        out[row + q, 2 * p + x] = v[low : low + size].astype(BF16)

    in_blocks(outs[0].shape[0] // 2, one)


def finish_kernel(factor, mine, other, first, second):
    channels = first.shape[2]

    def place(ours, theirs):
        for out, sums in ((ours, mine), (theirs, other)):
            for t in range(27):
                low = t % 4 * channels
                out[t] = sums[t // 4, :, low : low + channels] * factor

    odd = lax.rem(lax.axis_index("slab"), 2)

    @pl.when(odd == 0)
    def _():
        place(first, second)

    @pl.when(odd == 1)
    def _():
        place(second, first)


def split_kernel(ahead, *refs):
    one, two, *outs = refs[ahead:]
    for g, out in enumerate(outs):
        out[...] = one[g] + two[g]


def add_kernel(ahead, *refs):
    values = [ref[...] for ref in refs[ahead:-1]]
    while len(values) > 1:
        values = [sum(values[k + 1 : k + 2], values[k]) for k in range(0, len(values), 2)]
    refs[-1][...] = values[0]


def relay_kernel(*refs):
    pass


def merge_kernel(extent, *refs):
    pieces, out, wide = refs[:-2], refs[-2], refs[-1]
    size, planes, rows = out.shape[:3]
    share = rows // extent
    me = lax.axis_index("chan")
    for j in range(extent):
        base = lax.rem(me + extent - j, extent) * share

        def widen(f, mine=pieces[j::extent], base=base):
            x = 0
            for piece in mine:
                for k in range(piece.shape[1]):
                    start = ((base + f) * planes + x) * size
                    start = pl.multiple_of(start, 8) if size % 8 == 0 else start
                    wide[pl.ds(start, size), :] = piece[f, k].astype(F32)
                    x += 1

        in_blocks(share, widen)

    def back(i):
        for x in range(planes):
            tile = wide[pl.ds(x * size + i, rows, stride=planes * size), :]
            out[i, x] = tile.astype(BF16)

    in_blocks(size, back)


def body(field, out_grad, first_weight, second_weight):
    extent = lax.axis_size("chan")
    slabs = lax.axis_size("slab")
    me = lax.axis_index("chan")
    size, planes, rows, depth = field.shape
    channels = size * extent
    pairs = planes // 2
    share = rows // extent
    factor = 1.0 / math.sqrt(planes * slabs * rows * depth)

    def to_chan(value, shift):
        return lax.ppermute(value, "chan", [(i, (i + shift) % extent) for i in range(extent)])

    def to_next(value):
        return lax.ppermute(value, "slab", [(i, (i + 1) % slabs) for i in range(slabs)])

    def to_prev(value):
        return lax.ppermute(value, "slab", [((i + 1) % slabs, i) for i in range(slabs)])

    def relayed(value, *others):
        shape = jax.ShapeDtypeStruct(value.shape, value.dtype)
        early = [value, *others]
        return call(relay_kernel, [shape], early, loose=len(early), same={0: 0})[0]

    piece = jax.ShapeDtypeStruct((share + 8, 2, size, depth), BF16)
    by_tap = (27, size, channels)
    made = call(
        functools.partial(field_kernel, extent, 4),
        [piece] * (extent * pairs),
        [field],
        [pltpu.VMEM((size * planes * rows, depth), F32)],
        moved=field.size * 6,
    )
    parts = [list(made[:pairs])]
    for j in range(1, extent):
        parts.append([to_chan(value, j) for value in made[j * pairs : (j + 1) * pairs]])
    (pack,) = call(
        pack_kernel,
        [jax.ShapeDtypeStruct((14, size, 4 * channels), BF16)],
        [made[0], jnp.transpose(first_weight, (1, 0, 2)), jnp.transpose(second_weight, (1, 0, 2))],
        loose=1,
    )
    packs = [pack] + [to_chan(pack, j) for j in range(1, extent)]
    whole = size % 16 == 0
    own_before, own_after = [], []
    if whole:
        own_before, own_after = [to_next(parts[0][-1])], [to_prev(parts[0][0])]
    grad_piece = jax.ShapeDtypeStruct((share + 4, 2, channels, depth), BF16)
    grads = call(
        functools.partial(grad_kernel, extent, 2),
        [grad_piece] * pairs,
        [pack, out_grad],
        [pltpu.VMEM((channels * planes * rows, depth), F32)],
        moved=out_grad.size * 4,
        loose=1,
    )
    matrix = jax.ShapeDtypeStruct((6 * channels, 12 * channels), BF16)
    first_wide, second_wide, first_back, second_back = call(
        functools.partial(matrix_kernel, extent),
        [matrix] * 4,
        packs,
        moved=matrix.size * 8,
    )
    if whole and extent > 1 and pairs > 1:
        parts[1][-1] = relayed(parts[1][-1], grads[0])
        parts[1][0] = relayed(parts[1][0], own_after[0], *packs[1:])
    by_pair = [[parts[j][p] for j in range(extent)] for p in range(pairs)]
    groups = extent
    if not whole:
        by_pair = [[jnp.concatenate(pieces, axis=2)] for pieces in by_pair]
        groups = 1
    before = own_before + [to_next(piece) for piece in by_pair[-1][len(own_before) :]]
    after = own_after + [to_prev(piece) for piece in by_pair[0][len(own_after) :]]
    fields = [before] + by_pair + [after]

    def many(count, rows_each):
        return [jax.ShapeDtypeStruct((rows_each, 2, channels, depth), BF16)] * count

    def flat(lists):
        return [piece for pieces in lists for piece in pieces]

    work = 27 * 2 * channels * channels * depth * 2
    space = 4 * channels * depth * share

    made = call(
        functools.partial(forward_kernel, groups, pairs, 0),
        many(2 * pairs, share + 6) + many(pairs - 1, share + 4),
        flat(fields[: pairs + 1]) + list(grads[: pairs - 1]) + [first_wide, second_wide],
        flops=work * (2 * pairs - 1) * share,
        moved=space * 4 * pairs,
    )
    hiddens, slopes, deltas = made[:pairs], made[pairs : 2 * pairs], made[2 * pairs :]
    made = call(
        functools.partial(forward_kernel, groups, 1, 1),
        many(2, share + 6) + many(1, share + 4),
        flat(fields[pairs:]) + [hiddens[-1], grads[-1], first_wide, second_wide],
        flops=work * 2 * share,
        moved=space * 6,
    )
    hiddens = list(hiddens) + [made[0]]
    slopes = list(slopes) + [made[1]]
    deltas = list(deltas) + [made[2]]
    delta_after = to_prev(deltas[0])
    delta_before = to_next(deltas[-1])

    raw = jax.ShapeDtypeStruct((extent, 7, size, 4 * channels), F32)
    portion = jax.ShapeDtypeStruct(raw.shape[1:], F32)
    total = pltpu.VMEM((6 * channels, 12 * channels), F32)

    def room(rows_each):
        return pltpu.VMEM((rows_each, 2, channels, depth), BF16)

    made = call(
        functools.partial(gradient_kernel, share, groups, extent, pairs),
        [raw] * 2 + many(pairs - 1, share + 2),
        hiddens + deltas + [second_back] + slopes + flat(fields),
        [room(share + 2), room(share + 2), room(share + 4), total, total],
    )
    keep, send, inner = made[0], made[1], list(made[2:])
    def outer(then, one, two, slope):
        return call(
            back_kernel,
            many(1, share + 2),
            [then, second_back, one, two, slope],
            flops=work * share,
            moved=space * 2,
            loose=1,
        )[0]

    last = outer(keep, deltas[-1], delta_after, slopes[-1])

    def field_grad(firsts, after):
        count = len(firsts) - 1
        return list(
            call(
                functools.partial(last_kernel, count),
                [jax.ShapeDtypeStruct((share, 2 * count, size, depth), BF16)] * extent,
                [after] + firsts + [first_back],
                flops=work * count * share,
                moved=space * 2 * count,
                loose=1,
            )
        )

    def exchanged(made):
        pieces = [made[0]] + [None] * (extent - 1)
        for j in range(1, extent):
            pieces[extent - j] = to_chan(made[j], extent - j)
        return pieces

    def stepped(value, stride, shift=0):
        if shift % extent == 0:
            return lax.ppermute(value, "slab", [(i, i ^ stride) for i in range(slabs)])
        pairs_of = []
        for i in range(slabs):
            for k in range(extent):
                there = (i ^ stride) * extent + (k + shift) % extent
                pairs_of.append((i * extent + k, there))
        return lax.ppermute(value, ("slab", "chan"), pairs_of)

    plain = slabs & (slabs - 1) == 0 and slabs >= 4
    if plain:
        ahead = [last]
        kept = call(
            functools.partial(split_kernel, len(ahead)),
            [portion] * extent,
            ahead + [keep, stepped(send, 1)],
            loose=len(ahead),
        )
        shares = [kept[0]] + [to_chan(kept[j], extent - j) for j in range(1, extent)]
        shares += [stepped(kept[j], 2, extent - j) for j in range(extent)]
        after = kept[0]
    else:
        after = keep
    first = outer(after, delta_before, deltas[0], slopes[0])
    firsts = [first] + inner + [last]
    halves = [field_grad(firsts[:2], after)]
    if pairs > 1:
        halves.append(field_grad(firsts[1:], after))
    if plain:
        ahead = [made[0] for made in halves]
        (mine,) = call(
            functools.partial(add_kernel, len(ahead)), [portion], ahead + shares, loose=len(ahead)
        )
        halves = [made[:1] + [relayed(value, mine) for value in made[1:]] for made in halves]
    pieces = [piece for made in halves for piece in exchanged(made)]
    if plain:
        stride = 4
        while stride < slabs:
            radix = 4 if slabs % (4 * stride) == 0 else 2
            got = [mine] + [stepped(mine, m * stride) for m in range(1, radix)]
            (mine,) = call(functools.partial(add_kernel, 0), [portion], got)
            stride *= radix
        other = stepped(mine, 1)
    else:
        mine, other = keep[0], send[0]
        for j in range(1, extent):
            mine, other = mine + to_chan(keep[j], extent - j), other + to_chan(send[j], extent - j)
        even = lax.rem(lax.axis_index("slab"), 2) == 0
        mine, other = jnp.where(even, mine, other), jnp.where(even, other, mine)
        mine, other = lax.psum((mine, other), "slab")
        mine, other = jnp.where(even, mine, other), jnp.where(even, other, mine)
    (input_grad,) = call(
        functools.partial(merge_kernel, extent),
        [jax.ShapeDtypeStruct(field.shape, BF16)],
        pieces,
        [pltpu.VMEM((rows * planes * size, depth), F32)],
        moved=4 * field.size,
    )
    first_grad, second_grad = call(
        functools.partial(finish_kernel, factor),
        [jax.ShapeDtypeStruct(by_tap, F32)] * 2,
        [mine, other],
    )
    first_grad, second_grad = (jnp.transpose(g, (1, 0, 2)) for g in (first_grad, second_grad))
    return input_grad, first_grad, second_grad


def solution(mesh):
    placed = (
        P("chan", "slab", None, None),
        P(None, "slab", None, None),
        P("chan", None, None),
        P("chan", None, None),
    )
    return jax.shard_map(
        body,
        mesh=mesh,
        in_specs=placed,
        out_specs=(P("chan", "slab", None, None), P("chan", None, None), P("chan", None, None)),
        check_vma=False,
    )
```

```python
import functools
import math

import jax
import jax.numpy as jnp
from jax import lax
from jax.experimental import pallas as pl
from jax.experimental.pallas import tpu as pltpu
from jax.sharding import PartitionSpec as P

F32 = jnp.float32
BF16 = jnp.bfloat16
LIMIT = 16 * 1024 * 1024


def call(kernel, outs, args, scratch=(), flops=0, moved=0, loose=0, same=None):
    whole = pl.BlockSpec(memory_space=pltpu.VMEM)
    still = pl.BlockSpec(memory_space=pl.ANY)
    return pl.pallas_call(
        kernel,
        out_shape=outs,
        in_specs=[still] * loose + [whole] * (len(args) - loose),
        out_specs=[still if k in (same or {}).values() else whole for k in range(len(outs))],
        input_output_aliases=same or {},
        scratch_shapes=list(scratch),
        compiler_params=pltpu.CompilerParams(vmem_limit_bytes=LIMIT),
        cost_estimate=pl.CostEstimate(flops=flops, bytes_accessed=moved, transcendentals=0),
    )(*args)


def in_blocks(count, body):
    block = max(k for k in range(1, 8) if count % k == 0)
    if block < 4:
        block = min(count, 15)

    def several(r, _):
        for k in range(block):
            body(r * block + k)
        return 0

    lax.fori_loop(0, count // block, several, 0)
    for k in range(count // block * block, count):
        body(k)


def widened(x_ref, wide):
    count, planes, rows = x_ref.shape[:3]

    def widen(i):
        for x in range(planes):
            start = pl.multiple_of((i * planes + x) * rows, 8)
            wide[pl.ds(start, rows), :] = x_ref[i, x].astype(F32)

    in_blocks(count, widen)


def turn(wide, outs, shape, base, length):
    count, planes, rows = shape

    def one(f):
        y = lax.rem(base + f, rows)
        for x in range(planes):
            tile = wide[pl.ds(x * rows + y, count, stride=planes * rows), :]
            outs[x // 2][f, x % 2] = tile.astype(BF16)

    in_blocks(length, one)


def field_kernel(extent, margin, x_ref, *refs):
    outs, wide = refs[:-1], refs[-1]
    count, planes, rows = x_ref.shape[:3]
    pairs = planes // 2
    share = rows // extent
    widened(x_ref, wide)
    me = lax.axis_index("chan")
    for s in range(extent):
        base = lax.rem(me + s, extent) * share - margin + rows
        turn(
            wide,
            outs[s * pairs : (s + 1) * pairs],
            (count, planes, rows),
            base,
            share + 2 * margin,
        )


def pack_kernel(after, first, second, packed):
    del after
    blank = jnp.zeros(first.shape[1:], F32)
    for h in range(packed.shape[0]):
        parts = []
        for ref in (first, second):
            for t in (2 * h, 2 * h + 1):
                parts.append(ref[t].astype(F32) if t < ref.shape[0] else blank)
        packed[h] = jnp.concatenate(parts, axis=1).astype(BF16)


def grad_kernel(extent, margin, after, x_ref, *refs):
    del after
    outs, wide = refs[:-1], refs[-1]
    count, planes, rows = x_ref.shape[:3]
    share = rows // extent
    widened(x_ref, wide)
    base = lax.axis_index("chan") * share - margin + rows
    turn(wide, outs, (count, planes, rows), base, share + 2 * margin)


def matrix_kernel(extent, *refs):
    packs, outs = refs[:extent], refs[extent:]
    me = lax.axis_index("chan")
    quarter = packs[0].shape[2] // 4
    taps = []
    turned = []
    for h in range(packs[0].shape[0]):
        tiles = [pack[h].astype(F32) for pack in packs]
        own = jnp.concatenate(tiles, axis=0)
        fixed = []
        for g in range(extent):
            place = lax.rem(me + extent - g, extent)
            tile = tiles[0]
            for j in range(1, extent):
                tile = jnp.where(place == j, tiles[j], tile)
            fixed.append(tile)
        both = jnp.concatenate(
            [own[:, : 2 * quarter], jnp.concatenate(fixed, axis=0)[:, 2 * quarter :]], axis=1
        )
        across = both.T
        for side in range(2):
            taps.append(
                [both[:, k * quarter : (k + 1) * quarter] for k in (side, side + 2)]
            )
            turned.append(
                [across[k * quarter : (k + 1) * quarter] for k in (side, side + 2)]
            )
    channels = quarter
    blank = jnp.zeros((channels, channels), F32)
    for k in range(2):
        for out, blocks, flip in ((outs[k], turned, False), (outs[2 + k], taps, True)):
            for e in range(3):
                for x in range(2):
                    chunks = []
                    for pair in range(2):
                        for b in range(3):
                            for side in range(2):
                                a = 2 * pair + side - x
                                t = 9 * a + 3 * b + e
                                inside = 0 <= a <= 2
                                t = 26 - t if flip else t
                                chunks.append(blocks[t][k] if inside else blank)
                    low = (2 * e + x) * channels
                    out[low : low + channels, :] = jnp.concatenate(chunks, axis=1).astype(BF16)


def stacked(refs, row, count):
    if len(refs) == 1:
        part = refs[0][pl.ds(row, count)]
        return part.reshape(-1, part.shape[-1])
    parts = [ref[row + b, x] for b in range(count) for x in range(2) for ref in refs]
    return jnp.concatenate(parts, axis=0)


def taps(weight, inputs, row):
    sides = []
    for above, below in inputs:
        for q in range(2):
            sides.append(
                jnp.concatenate([stacked(above, row + q, 3), stacked(below, row + q, 3)], axis=0)
            )
    lifted = jnp.dot(weight, jnp.concatenate(sides, axis=1), preferred_element_type=F32)
    third = lifted.shape[0] // 3
    depth = sides[0].shape[1]
    sums = []
    for k in range(len(sides)):
        side = lifted[:, k * depth : (k + 1) * depth]
        sums.append(
            side[third : 2 * third]
            + pltpu.roll(side[:third], 1, 1)
            + pltpu.roll(side[2 * third :], depth - 1, 1)
        )
    return [sums[2 * p : 2 * p + 2] for p in range(len(inputs))]


def neighbours(pairs):
    return list(zip(pairs[:-1], pairs[1:]))


def silu_parts(v):
    sig = jax.nn.sigmoid(v)
    return sig, sig * (1.0 + v * (1.0 - sig))


def forward_kernel(groups, fresh, ready, *refs):
    refs = list(refs)
    fields = [[refs.pop(0) for _ in range(groups)] for _ in range(fresh + 1)]
    hiddens = [refs.pop(0) for _ in range(ready)]
    count = fresh + ready - 1
    grads = [refs.pop(0) for _ in range(count)]
    first, second = refs.pop(0), refs.pop(0)
    made = [refs.pop(0) for _ in range(fresh)]
    slopes = [refs.pop(0) for _ in range(fresh)]
    deltas = refs
    hiddens = hiddens + made

    def one(r):
        row = 2 * r
        for p, sums in enumerate(taps(first[...], neighbours(fields), row)):
            for q, v in enumerate(sums):
                sig, slope = silu_parts(v)
                shape = made[p].shape[1:]
                made[p][row + q] = (v * sig).astype(BF16).reshape(shape)
                slopes[p][row + q] = slope.astype(BF16).reshape(shape)

    in_blocks(made[0].shape[0] // 2, one)

    def two(r):
        row = 2 * r
        for p, sums in enumerate(taps(second[...], neighbours([[ref] for ref in hiddens]), row)):
            for q, v in enumerate(sums):
                shape = deltas[p].shape[1:]
                out_grad = grads[p][row + q].astype(F32)
                slope = silu_parts(v)[1].reshape(shape)
                deltas[p][row + q] = (out_grad * slope).astype(BF16)

    if count > 0:
        in_blocks(deltas[0].shape[0] // 2, two)


def planes_of(pairs):
    return [(refs, x) for refs in pairs for x in range(2)]


def weight_loop(total, pieces, first_row, deltas, delta_row, count):
    blocks = [k for k in range(1, 13) if count // 2 % k == 0 and k * len(deltas) <= 12]
    together = max(blocks, default=1)

    def step(r, _):
        left, right = [], []
        for k in range(together):
            row = 2 * (r * together + k)
            for x, ((delta,), place) in enumerate(deltas):
                rows = []
                for q in range(2):
                    wide = delta[delta_row + row + q, place]
                    depth = wide.shape[1]
                    rows += [pltpu.roll(wide, depth - 1, 1), wide, pltpu.roll(wide, 1, 1)]
                left.append(jnp.concatenate(rows, axis=0))
                rows = []
                for refs, side in pieces[x : x + 3]:
                    for b in range(4):
                        for ref in refs:
                            rows.append(ref[first_row + row + b, side])
                right.append(jnp.concatenate(rows, axis=0))
        total[...] += lax.dot_general(
            jnp.concatenate(left, axis=1),
            jnp.concatenate(right, axis=1),
            (((1,), (1,)), ((), ())),
            preferred_element_type=F32,
        )
        return 0

    lax.fori_loop(0, count // 2 // together, step, 0)


def weight_fold(total, size):
    lanes = total.shape[0] // 2
    channels = total.shape[1] // 12
    upper, lower = total[:lanes, :].T, total[lanes:, :].T
    groups = []
    for g in range(channels // size):
        taps_of = []
        for a in range(3):
            for b in range(3):
                start = (4 * a + b) * channels + g * size
                part = (
                    upper[start : start + size]
                    + lower[start + channels : start + channels + size]
                )
                taps_of += [part[:, e * channels : (e + 1) * channels] for e in range(3)]
        blank = jnp.zeros((size, channels), F32)
        taps_of.append(blank)
        groups.append([jnp.concatenate(taps_of[4 * h : 4 * h + 4], axis=1) for h in range(7)])
    return groups


def first_deltas(weight, inputs, slopes, firsts):
    def one(r):
        row = 2 * r
        for p, sums in enumerate(taps(weight[...], inputs, row)):
            for q, v in enumerate(sums):
                shape = firsts[p].shape[1:]
                slope = slopes[p][row + 2 + q].astype(F32)
                firsts[p][row + q] = (v.reshape(shape) * slope).astype(BF16)

    in_blocks(firsts[0].shape[0] // 2, one)


def gradient_kernel(share, groups, extent, pairs, *refs):
    refs = list(refs)
    hiddens = [[refs.pop(0)] for _ in range(pairs + 1)]
    deltas = [[refs.pop(0)] for _ in range(pairs)]
    weight = refs.pop(0)
    slopes = [refs.pop(0) for _ in range(pairs + 1)]
    fields = [[refs.pop(0) for _ in range(groups)] for _ in range(pairs + 2)]
    keep, send = refs.pop(0), refs.pop(0)
    inner = [refs.pop(0) for _ in range(pairs - 1)]
    head, tail, none, second_total, first_total = refs
    none[...] = jnp.zeros_like(none)
    second_total[...] = jnp.zeros_like(second_total)
    first_total[...] = jnp.zeros_like(first_total)
    weight_loop(second_total, planes_of(hiddens), 2, planes_of(deltas), 2, share)
    firsts = [head] + inner + [tail]
    first_deltas(weight, neighbours([[none]] + deltas + [[none]]), slopes, firsts)
    parts = planes_of([[first] for first in firsts])
    weight_loop(first_total, planes_of(fields), 3, parts, 1, share)
    halves, size = keep.shape[1:3]
    me = lax.axis_index("chan")
    of_first = weight_fold(first_total, size)
    of_second = weight_fold(second_total, size)

    def place(ours, theirs):
        for g in range(extent):
            there = lax.rem(me + extent - g, extent)
            for h in range(halves):
                ours[g, h] = of_first[g][h]
                theirs[there, h] = of_second[g][h]

    odd = lax.rem(lax.axis_index("slab"), 2)

    @pl.when(odd == 0)
    def _():
        place(keep, send)

    @pl.when(odd == 1)
    def _():
        place(send, keep)


def field_kernel_back(inner, groups, after, *refs):
    del after
    refs = list(refs)
    back, weight = refs.pop(0), refs.pop(0)
    before, first, last, behind = [[refs.pop(0)] for _ in range(4)]
    slopes = [refs.pop(0) for _ in range(2)]
    middle = [refs.pop(0) for _ in range(inner)]
    outs, ends = refs[:groups], refs[groups:]
    first_deltas(back, [(before, first), (last, behind)], slopes, ends)
    firsts = [ends[0]] + middle + [ends[1]]

    def one(r):
        row = 2 * r
        size = outs[0].shape[2]
        channels = len(outs) * size
        for p, sums in enumerate(taps(weight[...], neighbours([[ref] for ref in firsts]), row)):
            for q, v in enumerate(sums):
                for x in range(2):
                    for j, out in enumerate(outs):
                        low = x * channels + j * size
                        out[row + q, 2 * p + x] = v[low : low + size].astype(BF16)

    in_blocks(outs[0].shape[0] // 2, one)


def finish_kernel(factor, after, mine, other, first, second):
    del after
    channels = first.shape[2]

    def place(ours, theirs):
        for out, sums in ((ours, mine), (theirs, other)):
            for t in range(27):
                low = t % 4 * channels
                out[t] = sums[t // 4, :, low : low + channels] * factor

    odd = lax.rem(lax.axis_index("slab"), 2)

    @pl.when(odd == 0)
    def _():
        place(first, second)

    @pl.when(odd == 1)
    def _():
        place(second, first)


def split_kernel(one, two, *outs):
    for g, out in enumerate(outs):
        out[...] = one[g] + two[g]


def add_kernel(ahead, *refs):
    values = [ref[...] for ref in refs[ahead:-1]]
    while len(values) > 1:
        values = [sum(values[k + 1 : k + 2], values[k]) for k in range(0, len(values), 2)]
    refs[-1][...] = values[0]


def relay_kernel(*refs):
    pass


def merge_kernel(extent, *refs):
    pieces, token, out, wide = refs[:-3], refs[-3], refs[-2], refs[-1]
    token[...] = jnp.zeros_like(token)
    size, planes, rows = out.shape[:3]
    share = rows // extent
    me = lax.axis_index("chan")
    for j in range(extent):
        base = lax.rem(me + extent - j, extent) * share

        def widen(f, mine=pieces[j::extent], base=base):
            x = 0
            for piece in mine:
                for k in range(piece.shape[1]):
                    start = ((base + f) * planes + x) * size
                    start = pl.multiple_of(start, 8) if size % 8 == 0 else start
                    wide[pl.ds(start, size), :] = piece[f, k].astype(F32)
                    x += 1

        in_blocks(share, widen)

    def back(i):
        for x in range(planes):
            tile = wide[pl.ds(x * size + i, rows, stride=planes * size), :]
            out[i, x] = tile.astype(BF16)

    in_blocks(size, back)


def body(field, out_grad, first_weight, second_weight):
    extent = lax.axis_size("chan")
    slabs = lax.axis_size("slab")
    me = lax.axis_index("chan")
    size, planes, rows, depth = field.shape
    channels = size * extent
    pairs = planes // 2
    share = rows // extent
    factor = 1.0 / math.sqrt(planes * slabs * rows * depth)

    def to_chan(value, shift):
        return lax.ppermute(value, "chan", [(i, (i + shift) % extent) for i in range(extent)])

    def to_next(value):
        return lax.ppermute(value, "slab", [(i, (i + 1) % slabs) for i in range(slabs)])

    def to_prev(value):
        return lax.ppermute(value, "slab", [((i + 1) % slabs, i) for i in range(slabs)])

    def relayed(value, *others):
        shape = jax.ShapeDtypeStruct(value.shape, value.dtype)
        early = [value, *others]
        return call(relay_kernel, [shape], early, loose=len(early), same={0: 0})[0]

    piece = jax.ShapeDtypeStruct((share + 8, 2, size, depth), BF16)
    by_tap = (27, size, channels)
    made = call(
        functools.partial(field_kernel, extent, 4),
        [piece] * (extent * pairs),
        [field],
        [pltpu.VMEM((size * planes * rows, depth), F32)],
        moved=field.size * 6,
    )
    parts = [list(made[:pairs])]
    for j in range(1, extent):
        parts.append([to_chan(value, j) for value in made[j * pairs : (j + 1) * pairs]])
    (pack,) = call(
        pack_kernel,
        [jax.ShapeDtypeStruct((14, size, 4 * channels), BF16)],
        [made[0], jnp.transpose(first_weight, (1, 0, 2)), jnp.transpose(second_weight, (1, 0, 2))],
        loose=1,
    )
    packs = [pack] + [to_chan(pack, j) for j in range(1, extent)]
    whole = size % 16 == 0
    own_before, own_after = [], []
    if whole:
        own_before, own_after = [to_next(parts[0][-1])], [to_prev(parts[0][0])]
    grad_piece = jax.ShapeDtypeStruct((share + 4, 2, channels, depth), BF16)
    grads = call(
        functools.partial(grad_kernel, extent, 2),
        [grad_piece] * pairs,
        [pack, out_grad],
        [pltpu.VMEM((channels * planes * rows, depth), F32)],
        moved=out_grad.size * 4,
        loose=1,
    )
    matrix = jax.ShapeDtypeStruct((6 * channels, 12 * channels), BF16)
    first_wide, second_wide, first_back, second_back = call(
        functools.partial(matrix_kernel, extent),
        [matrix] * 4,
        packs,
        moved=matrix.size * 8,
    )
    if whole and extent > 1 and pairs > 1:
        parts[1][-1] = relayed(parts[1][-1], grads[0])
        parts[1][0] = relayed(parts[1][0], own_after[0], *packs[1:])
    by_pair = [[parts[j][p] for j in range(extent)] for p in range(pairs)]
    groups = extent
    if not whole:
        by_pair = [[jnp.concatenate(pieces, axis=2)] for pieces in by_pair]
        groups = 1
    before = own_before + [to_next(piece) for piece in by_pair[-1][len(own_before) :]]
    after = own_after + [to_prev(piece) for piece in by_pair[0][len(own_after) :]]
    fields = [before] + by_pair + [after]

    def many(count, rows_each):
        return [jax.ShapeDtypeStruct((rows_each, 2, channels, depth), BF16)] * count

    def flat(lists):
        return [piece for pieces in lists for piece in pieces]

    work = 27 * 2 * channels * channels * depth * 2
    space = 4 * channels * depth * share

    made = call(
        functools.partial(forward_kernel, groups, pairs, 0),
        many(2 * pairs, share + 6) + many(pairs - 1, share + 4),
        flat(fields[: pairs + 1]) + list(grads[: pairs - 1]) + [first_wide, second_wide],
        flops=work * (2 * pairs - 1) * share,
        moved=space * 4 * pairs,
    )
    hiddens, slopes, deltas = made[:pairs], made[pairs : 2 * pairs], made[2 * pairs :]
    made = call(
        functools.partial(forward_kernel, groups, 1, 1),
        many(2, share + 6) + many(1, share + 4),
        flat(fields[pairs:]) + [hiddens[-1], grads[-1], first_wide, second_wide],
        flops=work * 2 * share,
        moved=space * 6,
    )
    hiddens = list(hiddens) + [made[0]]
    slopes = list(slopes) + [made[1]]
    deltas = list(deltas) + [made[2]]
    delta_after = to_prev(deltas[0])
    delta_before = to_next(deltas[-1])

    raw = jax.ShapeDtypeStruct((extent, 7, size, 4 * channels), F32)
    portion = jax.ShapeDtypeStruct(raw.shape[1:], F32)
    total = pltpu.VMEM((6 * channels, 12 * channels), F32)

    def room(rows_each):
        return pltpu.VMEM((rows_each, 2, channels, depth), BF16)

    made = call(
        functools.partial(gradient_kernel, share, groups, extent, pairs),
        [raw] * 2 + many(pairs - 1, share + 2),
        hiddens + deltas + [second_back] + slopes + flat(fields),
        [room(share + 2), room(share + 2), room(share + 4), total, total],
    )
    keep, send, inner = made[0], made[1], list(made[2:])
    def exchanged(made):
        pieces = [made[0]] + [None] * (extent - 1)
        for j in range(1, extent):
            pieces[extent - j] = to_chan(made[j], extent - j)
        return pieces

    def stepped(value, stride, shift=0):
        if shift % extent == 0:
            return lax.ppermute(value, "slab", [(i, i ^ stride) for i in range(slabs)])
        pairs_of = []
        for i in range(slabs):
            for k in range(extent):
                there = (i ^ stride) * extent + (k + shift) % extent
                pairs_of.append((i * extent + k, there))
        return lax.ppermute(value, ("slab", "chan"), pairs_of)

    plain = slabs & (slabs - 1) == 0 and slabs >= 4
    if plain:
        kept = call(split_kernel, [portion] * extent, [keep, stepped(send, 1)])
        shares = [kept[0]] + [to_chan(kept[j], extent - j) for j in range(1, extent)]
        shares += [stepped(kept[j], 2, extent - j) for j in range(extent)]
        after = kept[0]
    else:
        after = keep
    made = call(
        functools.partial(field_kernel_back, pairs - 1, extent),
        [jax.ShapeDtypeStruct((share, planes, size, depth), BF16)] * extent,
        [after, second_back, first_back]
        + [delta_before, deltas[0], deltas[-1], delta_after, slopes[0], slopes[-1]]
        + inner,
        [room(share + 2), room(share + 2)],
        flops=work * (pairs + 2) * share,
        moved=space * 6,
        loose=1,
    )
    if plain:
        ahead = list(made[:1])
        (mine,) = call(
            functools.partial(add_kernel, len(ahead)), [portion], ahead + shares, loose=len(ahead)
        )
        made = list(made[:1]) + [relayed(value, mine) for value in made[1:]]
    pieces = exchanged(made)
    if plain:
        stride = 4
        while stride < slabs:
            radix = 4 if slabs % (4 * stride) == 0 else 2
            got = [mine] + [stepped(mine, m * stride) for m in range(1, radix)]
            (mine,) = call(functools.partial(add_kernel, 0), [portion], got)
            stride *= radix
        other = stepped(mine, 1)
    else:
        mine, other = keep[0], send[0]
        for j in range(1, extent):
            mine, other = mine + to_chan(keep[j], extent - j), other + to_chan(send[j], extent - j)
        even = lax.rem(lax.axis_index("slab"), 2) == 0
        mine, other = jnp.where(even, mine, other), jnp.where(even, other, mine)
        mine, other = lax.psum((mine, other), "slab")
        mine, other = jnp.where(even, mine, other), jnp.where(even, other, mine)
    token, input_grad = call(
        functools.partial(merge_kernel, extent),
        [jax.ShapeDtypeStruct((8, 128), F32), jax.ShapeDtypeStruct(field.shape, BF16)],
        pieces,
        [pltpu.VMEM((rows * planes * size, depth), F32)],
        moved=4 * field.size,
    )
    first_grad, second_grad = call(
        functools.partial(finish_kernel, factor),
        [jax.ShapeDtypeStruct(by_tap, F32)] * 2,
        [token, mine, other],
        loose=1,
    )
    first_grad, second_grad = (jnp.transpose(g, (1, 0, 2)) for g in (first_grad, second_grad))
    return input_grad, first_grad, second_grad


def solution(mesh):
    placed = (
        P("chan", "slab", None, None),
        P(None, "slab", None, None),
        P("chan", None, None),
        P("chan", None, None),
    )
    return jax.shard_map(
        body,
        mesh=mesh,
        in_specs=placed,
        out_specs=(P("chan", "slab", None, None), P("chan", None, None), P("chan", None, None)),
        check_vma=False,
    )
```

```python
import functools
import math

import jax
import jax.numpy as jnp
from jax import lax
from jax.experimental import pallas as pl
from jax.experimental.pallas import tpu as pltpu
from jax.sharding import PartitionSpec as P

F32 = jnp.float32
BF16 = jnp.bfloat16
LIMIT = 16 * 1024 * 1024


def call(kernel, outs, args, scratch=(), flops=0, moved=0, loose=0, same=None):
    whole = pl.BlockSpec(memory_space=pltpu.VMEM)
    still = pl.BlockSpec(memory_space=pl.ANY)
    return pl.pallas_call(
        kernel,
        out_shape=outs,
        in_specs=[still] * loose + [whole] * (len(args) - loose),
        out_specs=[still if k in (same or {}).values() else whole for k in range(len(outs))],
        input_output_aliases=same or {},
        scratch_shapes=list(scratch),
        compiler_params=pltpu.CompilerParams(vmem_limit_bytes=LIMIT),
        cost_estimate=pl.CostEstimate(flops=flops, bytes_accessed=moved, transcendentals=0),
    )(*args)


def in_blocks(count, body):
    block = max(k for k in range(1, 17) if count % k == 0)

    def several(r, _):
        for k in range(block):
            body(r * block + k)
        return 0

    lax.fori_loop(0, count // block, several, 0)
    for k in range(count // block * block, count):
        body(k)


def widened(x_ref, wide):
    count, planes, rows = x_ref.shape[:3]

    def widen(i):
        for x in range(planes):
            start = pl.multiple_of((i * planes + x) * rows, 8)
            wide[pl.ds(start, rows), :] = x_ref[i, x].astype(F32)

    in_blocks(count, widen)


def turn(wide, outs, shape, base, length):
    count, planes, rows = shape

    def one(f):
        y = lax.rem(base + f, rows)
        for x in range(planes):
            tile = wide[pl.ds(x * rows + y, count, stride=planes * rows), :]
            outs[x // 2][f, x % 2] = tile.astype(BF16)

    in_blocks(length, one)


def field_kernel(extent, margin, x_ref, *refs):
    outs, wide = refs[:-1], refs[-1]
    count, planes, rows = x_ref.shape[:3]
    pairs = planes // 2
    share = rows // extent
    widened(x_ref, wide)
    me = lax.axis_index("chan")
    for s in range(extent):
        base = lax.rem(me + s, extent) * share - margin + rows
        turn(
            wide,
            outs[s * pairs : (s + 1) * pairs],
            (count, planes, rows),
            base,
            share + 2 * margin,
        )


def pack_kernel(after, first, second, packed):
    del after
    blank = jnp.zeros(first.shape[1:], F32)
    for h in range(packed.shape[0]):
        parts = []
        for ref in (first, second):
            for t in (2 * h, 2 * h + 1):
                parts.append(ref[t].astype(F32) if t < ref.shape[0] else blank)
        packed[h] = jnp.concatenate(parts, axis=1).astype(BF16)


def grad_kernel(extent, margin, after, x_ref, *refs):
    del after
    outs, wide = refs[:-1], refs[-1]
    count, planes, rows = x_ref.shape[:3]
    share = rows // extent
    widened(x_ref, wide)
    base = lax.axis_index("chan") * share - margin + rows
    turn(wide, outs, (count, planes, rows), base, share + 2 * margin)


def matrix_kernel(extent, *refs):
    packs, outs = refs[:extent], refs[extent:]
    me = lax.axis_index("chan")
    quarter = packs[0].shape[2] // 4
    taps = []
    turned = []
    for h in range(packs[0].shape[0]):
        tiles = [pack[h].astype(F32) for pack in packs]
        own = jnp.concatenate(tiles, axis=0)
        fixed = []
        for g in range(extent):
            place = lax.rem(me + extent - g, extent)
            tile = tiles[0]
            for j in range(1, extent):
                tile = jnp.where(place == j, tiles[j], tile)
            fixed.append(tile)
        both = jnp.concatenate(
            [own[:, : 2 * quarter], jnp.concatenate(fixed, axis=0)[:, 2 * quarter :]], axis=1
        )
        across = both.T
        for side in range(2):
            taps.append(
                [both[:, k * quarter : (k + 1) * quarter] for k in (side, side + 2)]
            )
            turned.append(
                [across[k * quarter : (k + 1) * quarter] for k in (side, side + 2)]
            )
    channels = quarter
    blank = jnp.zeros((channels, channels), F32)
    for k in range(2):
        for out, blocks, flip in ((outs[k], turned, False), (outs[2 + k], taps, True)):
            for e in range(3):
                for x in range(2):
                    chunks = []
                    for pair in range(2):
                        for b in range(3):
                            for side in range(2):
                                a = 2 * pair + side - x
                                t = 9 * a + 3 * b + e
                                inside = 0 <= a <= 2
                                t = 26 - t if flip else t
                                chunks.append(blocks[t][k] if inside else blank)
                    low = (2 * e + x) * channels
                    out[low : low + channels, :] = jnp.concatenate(chunks, axis=1).astype(BF16)


def stacked(refs, row, count):
    if len(refs) == 1:
        part = refs[0][pl.ds(row, count)]
        return part.reshape(-1, part.shape[-1])
    parts = [ref[row + b, x] for b in range(count) for x in range(2) for ref in refs]
    return jnp.concatenate(parts, axis=0)


def taps(weight, inputs, row):
    sides = []
    for above, below in inputs:
        for q in range(2):
            sides.append(
                jnp.concatenate([stacked(above, row + q, 3), stacked(below, row + q, 3)], axis=0)
            )
    lifted = jnp.dot(weight, jnp.concatenate(sides, axis=1), preferred_element_type=F32)
    third = lifted.shape[0] // 3
    depth = sides[0].shape[1]
    sums = []
    for k in range(len(sides)):
        side = lifted[:, k * depth : (k + 1) * depth]
        sums.append(
            side[third : 2 * third]
            + pltpu.roll(side[:third], 1, 1)
            + pltpu.roll(side[2 * third :], depth - 1, 1)
        )
    return [sums[2 * p : 2 * p + 2] for p in range(len(inputs))]


def neighbours(pairs):
    return list(zip(pairs[:-1], pairs[1:]))


def silu_parts(v):
    sig = jax.nn.sigmoid(v)
    return sig, sig * (1.0 + v * (1.0 - sig))


def forward_kernel(groups, fresh, ready, *refs):
    refs = list(refs)
    fields = [[refs.pop(0) for _ in range(groups)] for _ in range(fresh + 1)]
    hiddens = [refs.pop(0) for _ in range(ready)]
    count = fresh + ready - 1
    grads = [refs.pop(0) for _ in range(count)]
    first, second = refs.pop(0), refs.pop(0)
    made = [refs.pop(0) for _ in range(fresh)]
    slopes = [refs.pop(0) for _ in range(fresh)]
    deltas = refs
    hiddens = hiddens + made

    def one(r):
        row = 2 * r
        for p, sums in enumerate(taps(first[...], neighbours(fields), row)):
            for q, v in enumerate(sums):
                sig, slope = silu_parts(v)
                shape = made[p].shape[1:]
                made[p][row + q] = (v * sig).astype(BF16).reshape(shape)
                slopes[p][row + q] = slope.astype(BF16).reshape(shape)

    in_blocks(made[0].shape[0] // 2, one)

    def two(r):
        row = 2 * r
        for p, sums in enumerate(taps(second[...], neighbours([[ref] for ref in hiddens]), row)):
            for q, v in enumerate(sums):
                shape = deltas[p].shape[1:]
                out_grad = grads[p][row + q].astype(F32)
                slope = silu_parts(v)[1].reshape(shape)
                deltas[p][row + q] = (out_grad * slope).astype(BF16)

    if count > 0:
        in_blocks(deltas[0].shape[0] // 2, two)


def planes_of(pairs):
    return [(refs, x) for refs in pairs for x in range(2)]


def weight_loop(total, pieces, first_row, deltas, delta_row, count):
    blocks = [k for k in range(1, 13) if count // 2 % k == 0 and k * len(deltas) <= 12]
    together = max(blocks, default=1)

    def step(r, _):
        left, right = [], []
        for k in range(together):
            row = 2 * (r * together + k)
            for x, ((delta,), place) in enumerate(deltas):
                rows = []
                for q in range(2):
                    wide = delta[delta_row + row + q, place]
                    depth = wide.shape[1]
                    rows += [pltpu.roll(wide, depth - 1, 1), wide, pltpu.roll(wide, 1, 1)]
                    rows.append(jnp.zeros_like(wide))
                right.append(jnp.concatenate(rows, axis=0))
                rows = []
                for refs, side in pieces[x : x + 3]:
                    for b in range(4):
                        for ref in refs:
                            rows.append(ref[first_row + row + b, side])
                left.append(jnp.concatenate(rows, axis=0))
        total[...] += lax.dot_general(
            jnp.concatenate(left, axis=1),
            jnp.concatenate(right, axis=1),
            (((1,), (1,)), ((), ())),
            preferred_element_type=F32,
        )
        return 0

    lax.fori_loop(0, count // 2 // together, step, 0)


def weight_fold(total, size):
    lanes = total.shape[1] // 2
    channels = total.shape[0] // 12
    upper, lower = total[:, :lanes], total[:, lanes:]
    groups = []
    for g in range(channels // size):
        taps_of = []
        for a in range(3):
            for b in range(3):
                start = (4 * a + b) * channels + g * size
                part = (
                    upper[start : start + size]
                    + lower[start + channels : start + channels + size]
                )
                taps_of += [part[:, e * channels : (e + 1) * channels] for e in range(3)]
        blank = jnp.zeros((size, channels), F32)
        taps_of.append(blank)
        groups.append([jnp.concatenate(taps_of[4 * h : 4 * h + 4], axis=1) for h in range(7)])
    return groups


def first_deltas(weight, inputs, slopes, firsts):
    def one(r):
        row = 2 * r
        for p, sums in enumerate(taps(weight[...], inputs, row)):
            for q, v in enumerate(sums):
                shape = firsts[p].shape[1:]
                slope = slopes[p][row + 2 + q].astype(F32)
                firsts[p][row + q] = (v.reshape(shape) * slope).astype(BF16)

    in_blocks(firsts[0].shape[0] // 2, one)


def gradient_kernel(share, groups, extent, pairs, *refs):
    refs = list(refs)
    hiddens = [[refs.pop(0)] for _ in range(pairs + 1)]
    deltas = [[refs.pop(0)] for _ in range(pairs)]
    weight = refs.pop(0)
    slopes = [refs.pop(0) for _ in range(pairs + 1)]
    fields = [[refs.pop(0) for _ in range(groups)] for _ in range(pairs + 2)]
    keep, send = refs.pop(0), refs.pop(0)
    inner = [refs.pop(0) for _ in range(pairs - 1)]
    head, tail, none, second_total, first_total = refs
    none[...] = jnp.zeros_like(none)
    second_total[...] = jnp.zeros_like(second_total)
    first_total[...] = jnp.zeros_like(first_total)
    weight_loop(second_total, planes_of(hiddens), 2, planes_of(deltas), 2, share)
    firsts = [head] + inner + [tail]
    first_deltas(weight, neighbours([[none]] + deltas + [[none]]), slopes, firsts)
    parts = planes_of([[first] for first in firsts])
    weight_loop(first_total, planes_of(fields), 3, parts, 1, share)
    halves, size = keep.shape[1:3]
    me = lax.axis_index("chan")
    of_first = weight_fold(first_total, size)
    of_second = weight_fold(second_total, size)

    def place(ours, theirs):
        for g in range(extent):
            there = lax.rem(me + extent - g, extent)
            for h in range(halves):
                ours[g, h] = of_first[g][h]
                theirs[there, h] = of_second[g][h]

    odd = lax.rem(lax.axis_index("slab"), 2)

    @pl.when(odd == 0)
    def _():
        place(keep, send)

    @pl.when(odd == 1)
    def _():
        place(send, keep)


def field_kernel_back(inner, groups, after, *refs):
    del after
    refs = list(refs)
    back, weight = refs.pop(0), refs.pop(0)
    before, first, last, behind = [[refs.pop(0)] for _ in range(4)]
    slopes = [refs.pop(0) for _ in range(2)]
    middle = [refs.pop(0) for _ in range(inner)]
    outs, ends = refs[:groups], refs[groups:]
    first_deltas(back, [(before, first), (last, behind)], slopes, ends)
    firsts = [ends[0]] + middle + [ends[1]]

    def one(r):
        row = 2 * r
        size = outs[0].shape[2]
        channels = len(outs) * size
        for p, sums in enumerate(taps(weight[...], neighbours([[ref] for ref in firsts]), row)):
            for q, v in enumerate(sums):
                for x in range(2):
                    for j, out in enumerate(outs):
                        low = x * channels + j * size
                        out[row + q, 2 * p + x] = v[low : low + size].astype(BF16)

    in_blocks(outs[0].shape[0] // 2, one)


def finish_kernel(factor, after, mine, other, first, second):
    del after
    channels = first.shape[2]

    def place(ours, theirs):
        for out, sums in ((ours, mine), (theirs, other)):
            for t in range(27):
                low = t % 4 * channels
                out[t] = sums[t // 4, :, low : low + channels] * factor

    odd = lax.rem(lax.axis_index("slab"), 2)

    @pl.when(odd == 0)
    def _():
        place(first, second)

    @pl.when(odd == 1)
    def _():
        place(second, first)


def split_kernel(one, two, *outs):
    for g, out in enumerate(outs):
        out[...] = one[g] + two[g]


def add_kernel(ahead, *refs):
    values = [ref[...] for ref in refs[ahead:-1]]
    while len(values) > 1:
        values = [sum(values[k + 1 : k + 2], values[k]) for k in range(0, len(values), 2)]
    refs[-1][...] = values[0]


def relay_kernel(*refs):
    pass


def merge_kernel(extent, *refs):
    pieces, token, out, wide = refs[:-3], refs[-3], refs[-2], refs[-1]
    token[...] = jnp.zeros_like(token)
    size, planes, rows = out.shape[:3]
    share = rows // extent
    me = lax.axis_index("chan")
    for j in range(extent):
        base = lax.rem(me + extent - j, extent) * share

        def widen(f, mine=pieces[j::extent], base=base):
            x = 0
            for piece in mine:
                for k in range(piece.shape[1]):
                    start = ((base + f) * planes + x) * size
                    start = pl.multiple_of(start, 8) if size % 8 == 0 else start
                    wide[pl.ds(start, size), :] = piece[f, k].astype(F32)
                    x += 1

        in_blocks(share, widen)

    def back(i):
        for x in range(planes):
            tile = wide[pl.ds(x * size + i, rows, stride=planes * size), :]
            out[i, x] = tile.astype(BF16)

    in_blocks(size, back)


def body(field, out_grad, first_weight, second_weight):
    extent = lax.axis_size("chan")
    slabs = lax.axis_size("slab")
    me = lax.axis_index("chan")
    size, planes, rows, depth = field.shape
    channels = size * extent
    pairs = planes // 2
    share = rows // extent
    factor = 1.0 / math.sqrt(planes * slabs * rows * depth)

    def to_chan(value, shift):
        return lax.ppermute(value, "chan", [(i, (i + shift) % extent) for i in range(extent)])

    def to_next(value):
        return lax.ppermute(value, "slab", [(i, (i + 1) % slabs) for i in range(slabs)])

    def to_prev(value):
        return lax.ppermute(value, "slab", [((i + 1) % slabs, i) for i in range(slabs)])

    def relayed(value, *others):
        shape = jax.ShapeDtypeStruct(value.shape, value.dtype)
        early = [value, *others]
        return call(relay_kernel, [shape], early, loose=len(early), same={0: 0})[0]

    piece = jax.ShapeDtypeStruct((share + 8, 2, size, depth), BF16)
    by_tap = (27, size, channels)
    made = call(
        functools.partial(field_kernel, extent, 4),
        [piece] * (extent * pairs),
        [field],
        [pltpu.VMEM((size * planes * rows, depth), F32)],
        moved=field.size * 6,
    )
    parts = [list(made[:pairs])]
    for j in range(1, extent):
        parts.append([to_chan(value, j) for value in made[j * pairs : (j + 1) * pairs]])
    (pack,) = call(
        pack_kernel,
        [jax.ShapeDtypeStruct((14, size, 4 * channels), BF16)],
        [made[0], jnp.transpose(first_weight, (1, 0, 2)), jnp.transpose(second_weight, (1, 0, 2))],
        loose=1,
    )
    packs = [pack] + [to_chan(pack, j) for j in range(1, extent)]
    whole = size % 16 == 0
    own_before, own_after = [], []
    if whole:
        own_before, own_after = [to_next(parts[0][-1])], [to_prev(parts[0][0])]
    grad_piece = jax.ShapeDtypeStruct((share + 4, 2, channels, depth), BF16)
    grads = call(
        functools.partial(grad_kernel, extent, 2),
        [grad_piece] * pairs,
        [pack, out_grad],
        [pltpu.VMEM((channels * planes * rows, depth), F32)],
        moved=out_grad.size * 4,
        loose=1,
    )
    matrix = jax.ShapeDtypeStruct((6 * channels, 12 * channels), BF16)
    first_wide, second_wide, first_back, second_back = call(
        functools.partial(matrix_kernel, extent),
        [matrix] * 4,
        packs,
        moved=matrix.size * 8,
    )
    if whole and extent > 1 and pairs > 1:
        parts[1][-1] = relayed(parts[1][-1], grads[0])
        parts[1][0] = relayed(parts[1][0], own_after[0], *packs[1:])
    by_pair = [[parts[j][p] for j in range(extent)] for p in range(pairs)]
    groups = extent
    if not whole:
        by_pair = [[jnp.concatenate(pieces, axis=2)] for pieces in by_pair]
        groups = 1
    before = own_before + [to_next(piece) for piece in by_pair[-1][len(own_before) :]]
    after = own_after + [to_prev(piece) for piece in by_pair[0][len(own_after) :]]
    fields = [before] + by_pair + [after]

    def many(count, rows_each):
        return [jax.ShapeDtypeStruct((rows_each, 2, channels, depth), BF16)] * count

    def flat(lists):
        return [piece for pieces in lists for piece in pieces]

    work = 27 * 2 * channels * channels * depth * 2
    space = 4 * channels * depth * share

    made = call(
        functools.partial(forward_kernel, groups, pairs, 0),
        many(2 * pairs, share + 6) + many(pairs - 1, share + 4),
        flat(fields[: pairs + 1]) + list(grads[: pairs - 1]) + [first_wide, second_wide],
        flops=work * (2 * pairs - 1) * share,
        moved=space * 4 * pairs,
    )
    hiddens, slopes, deltas = made[:pairs], made[pairs : 2 * pairs], made[2 * pairs :]
    made = call(
        functools.partial(forward_kernel, groups, 1, 1),
        many(2, share + 6) + many(1, share + 4),
        flat(fields[pairs:]) + [hiddens[-1], grads[-1], first_wide, second_wide],
        flops=work * 2 * share,
        moved=space * 6,
    )
    hiddens = list(hiddens) + [made[0]]
    slopes = list(slopes) + [made[1]]
    deltas = list(deltas) + [made[2]]
    delta_after = to_prev(deltas[0])
    delta_before = to_next(deltas[-1])

    raw = jax.ShapeDtypeStruct((extent, 7, size, 4 * channels), F32)
    portion = jax.ShapeDtypeStruct(raw.shape[1:], F32)
    total = pltpu.VMEM((12 * channels, 8 * channels), F32)

    def room(rows_each):
        return pltpu.VMEM((rows_each, 2, channels, depth), BF16)

    made = call(
        functools.partial(gradient_kernel, share, groups, extent, pairs),
        [raw] * 2 + many(pairs - 1, share + 2),
        hiddens + deltas + [second_back] + slopes + flat(fields),
        [room(share + 2), room(share + 2), room(share + 4), total, total],
    )
    keep, send, inner = made[0], made[1], list(made[2:])
    def exchanged(made):
        pieces = [made[0]] + [None] * (extent - 1)
        for j in range(1, extent):
            pieces[extent - j] = to_chan(made[j], extent - j)
        return pieces

    def stepped(value, stride, shift=0):
        if shift % extent == 0:
            return lax.ppermute(value, "slab", [(i, i ^ stride) for i in range(slabs)])
        pairs_of = []
        for i in range(slabs):
            for k in range(extent):
                there = (i ^ stride) * extent + (k + shift) % extent
                pairs_of.append((i * extent + k, there))
        return lax.ppermute(value, ("slab", "chan"), pairs_of)

    plain = slabs & (slabs - 1) == 0 and slabs >= 4
    if plain:
        kept = call(split_kernel, [portion] * extent, [keep, stepped(send, 1)])
        shares = [kept[0]] + [to_chan(kept[j], extent - j) for j in range(1, extent)]
        shares += [stepped(kept[j], 2, extent - j) for j in range(extent)]
        after = kept[0]
    else:
        after = keep
    made = call(
        functools.partial(field_kernel_back, pairs - 1, extent),
        [jax.ShapeDtypeStruct((share, planes, size, depth), BF16)] * extent,
        [after, second_back, first_back]
        + [delta_before, deltas[0], deltas[-1], delta_after, slopes[0], slopes[-1]]
        + inner,
        [room(share + 2), room(share + 2)],
        flops=work * (pairs + 2) * share,
        moved=space * 6,
        loose=1,
    )
    if plain:
        ahead = list(made[:1])
        (mine,) = call(
            functools.partial(add_kernel, len(ahead)), [portion], ahead + shares, loose=len(ahead)
        )
        made = list(made[:1]) + [relayed(value, mine) for value in made[1:]]
    pieces = exchanged(made)
    if plain:
        stride = 4
        while stride < slabs:
            radix = 4 if slabs % (4 * stride) == 0 else 2
            got = [mine] + [stepped(mine, m * stride) for m in range(1, radix)]
            (mine,) = call(functools.partial(add_kernel, 0), [portion], got)
            stride *= radix
        other = stepped(mine, 1)
    else:
        mine, other = keep[0], send[0]
        for j in range(1, extent):
            mine, other = mine + to_chan(keep[j], extent - j), other + to_chan(send[j], extent - j)
        even = lax.rem(lax.axis_index("slab"), 2) == 0
        mine, other = jnp.where(even, mine, other), jnp.where(even, other, mine)
        mine, other = lax.psum((mine, other), "slab")
        mine, other = jnp.where(even, mine, other), jnp.where(even, other, mine)
    token, input_grad = call(
        functools.partial(merge_kernel, extent),
        [jax.ShapeDtypeStruct((8, 128), F32), jax.ShapeDtypeStruct(field.shape, BF16)],
        pieces,
        [pltpu.VMEM((rows * planes * size, depth), F32)],
        moved=4 * field.size,
    )
    first_grad, second_grad = call(
        functools.partial(finish_kernel, factor),
        [jax.ShapeDtypeStruct(by_tap, F32)] * 2,
        [token, mine, other],
        loose=1,
    )
    first_grad, second_grad = (jnp.transpose(g, (1, 0, 2)) for g in (first_grad, second_grad))
    return input_grad, first_grad, second_grad


def solution(mesh):
    placed = (
        P("chan", "slab", None, None),
        P(None, "slab", None, None),
        P("chan", None, None),
        P("chan", None, None),
    )
    return jax.shard_map(
        body,
        mesh=mesh,
        in_specs=placed,
        out_specs=(P("chan", "slab", None, None), P("chan", None, None), P("chan", None, None)),
        check_vma=False,
    )
```

```python
import functools
import math

import jax
import jax.numpy as jnp
from jax import lax
from jax.experimental import pallas as pl
from jax.experimental.pallas import tpu as pltpu
from jax.sharding import PartitionSpec as P

F32 = jnp.float32
BF16 = jnp.bfloat16
LIMIT = 16 * 1024 * 1024


def call(kernel, outs, args, scratch=(), flops=0, moved=0, loose=0, same=None):
    whole = pl.BlockSpec(memory_space=pltpu.VMEM)
    still = pl.BlockSpec(memory_space=pl.ANY)
    return pl.pallas_call(
        kernel,
        out_shape=outs,
        in_specs=[still] * loose + [whole] * (len(args) - loose),
        out_specs=[still if k in (same or {}).values() else whole for k in range(len(outs))],
        input_output_aliases=same or {},
        scratch_shapes=list(scratch),
        compiler_params=pltpu.CompilerParams(vmem_limit_bytes=LIMIT),
        cost_estimate=pl.CostEstimate(flops=flops, bytes_accessed=moved, transcendentals=0),
    )(*args)


def in_blocks(count, body):
    block = max(k for k in range(1, 17) if count % k == 0)

    def several(r, _):
        for k in range(block):
            body(r * block + k)
        return 0

    lax.fori_loop(0, count // block, several, 0)
    for k in range(count // block * block, count):
        body(k)


def widened(x_ref, wide):
    count, planes, rows = x_ref.shape[:3]

    def widen(i):
        for x in range(planes):
            start = pl.multiple_of((i * planes + x) * rows, 8)
            wide[pl.ds(start, rows), :] = x_ref[i, x].astype(F32)

    in_blocks(count, widen)


def turn(wide, outs, shape, base, length):
    count, planes, rows = shape

    def one(f):
        y = lax.rem(base + f, rows)
        for x in range(planes):
            tile = wide[pl.ds(x * rows + y, count, stride=planes * rows), :]
            outs[x // 2][f, x % 2] = tile.astype(BF16)

    in_blocks(length, one)


def field_kernel(extent, margin, x_ref, *refs):
    outs, wide = refs[:-1], refs[-1]
    count, planes, rows = x_ref.shape[:3]
    pairs = planes // 2
    share = rows // extent
    widened(x_ref, wide)
    me = lax.axis_index("chan")
    for s in range(extent):
        base = lax.rem(me + s, extent) * share - margin + rows
        turn(
            wide,
            outs[s * pairs : (s + 1) * pairs],
            (count, planes, rows),
            base,
            share + 2 * margin,
        )


def pack_kernel(after, first, second, packed):
    del after
    blank = jnp.zeros(first.shape[1:], F32)
    for h in range(packed.shape[0]):
        parts = []
        for ref in (first, second):
            for t in (2 * h, 2 * h + 1):
                parts.append(ref[t].astype(F32) if t < ref.shape[0] else blank)
        packed[h] = jnp.concatenate(parts, axis=1).astype(BF16)


def grad_kernel(extent, margin, after, x_ref, *refs):
    del after
    outs, wide = refs[:-1], refs[-1]
    count, planes, rows = x_ref.shape[:3]
    share = rows // extent
    widened(x_ref, wide)
    base = lax.axis_index("chan") * share - margin + rows
    turn(wide, outs, (count, planes, rows), base, share + 2 * margin)


def matrix_kernel(extent, *refs):
    packs, outs = refs[:extent], refs[extent:]
    me = lax.axis_index("chan")
    quarter = packs[0].shape[2] // 4
    taps = []
    turned = []
    for h in range(packs[0].shape[0]):
        tiles = [pack[h].astype(F32) for pack in packs]
        own = jnp.concatenate(tiles, axis=0)
        fixed = []
        for g in range(extent):
            place = lax.rem(me + extent - g, extent)
            tile = tiles[0]
            for j in range(1, extent):
                tile = jnp.where(place == j, tiles[j], tile)
            fixed.append(tile)
        both = jnp.concatenate(
            [own[:, : 2 * quarter], jnp.concatenate(fixed, axis=0)[:, 2 * quarter :]], axis=1
        )
        across = both.T
        for side in range(2):
            taps.append(
                [both[:, k * quarter : (k + 1) * quarter] for k in (side, side + 2)]
            )
            turned.append(
                [across[k * quarter : (k + 1) * quarter] for k in (side, side + 2)]
            )
    channels = quarter
    blank = jnp.zeros((channels, channels), F32)
    for k in range(2):
        for out, blocks, flip in ((outs[k], turned, False), (outs[2 + k], taps, True)):
            for e in range(3):
                for x in range(2):
                    chunks = []
                    for pair in range(2):
                        for b in range(3):
                            for side in range(2):
                                a = 2 * pair + side - x
                                t = 9 * a + 3 * b + e
                                inside = 0 <= a <= 2
                                t = 26 - t if flip else t
                                chunks.append(blocks[t][k] if inside else blank)
                    low = (2 * e + x) * channels
                    out[low : low + channels, :] = jnp.concatenate(chunks, axis=1).astype(BF16)


def stacked(refs, row, count):
    if len(refs) == 1:
        part = refs[0][pl.ds(row, count)]
        return part.reshape(-1, part.shape[-1])
    parts = [ref[row + b, x] for b in range(count) for x in range(2) for ref in refs]
    return jnp.concatenate(parts, axis=0)


def taps(weight, inputs, row):
    sides = []
    for above, below in inputs:
        for q in range(2):
            sides.append(
                jnp.concatenate([stacked(above, row + q, 3), stacked(below, row + q, 3)], axis=0)
            )
    lifted = jnp.dot(weight, jnp.concatenate(sides, axis=1), preferred_element_type=F32)
    third = lifted.shape[0] // 3
    depth = sides[0].shape[1]
    sums = []
    for k in range(len(sides)):
        side = lifted[:, k * depth : (k + 1) * depth]
        sums.append(
            side[third : 2 * third]
            + pltpu.roll(side[:third], 1, 1)
            + pltpu.roll(side[2 * third :], depth - 1, 1)
        )
    return [sums[2 * p : 2 * p + 2] for p in range(len(inputs))]


def neighbours(pairs):
    return list(zip(pairs[:-1], pairs[1:]))


def silu_parts(v):
    sig = jax.nn.sigmoid(v)
    return sig, sig * (1.0 + v * (1.0 - sig))


def forward_kernel(groups, fresh, ready, *refs):
    refs = list(refs)
    fields = [[refs.pop(0) for _ in range(groups)] for _ in range(fresh + 1)]
    hiddens = [refs.pop(0) for _ in range(ready)]
    count = fresh + ready - 1
    grads = [refs.pop(0) for _ in range(count)]
    first, second = refs.pop(0), refs.pop(0)
    made = [refs.pop(0) for _ in range(fresh)]
    slopes = [refs.pop(0) for _ in range(fresh)]
    deltas = refs
    hiddens = hiddens + made

    def one(r):
        row = 2 * r
        for p, sums in enumerate(taps(first[...], neighbours(fields), row)):
            for q, v in enumerate(sums):
                sig, slope = silu_parts(v)
                shape = made[p].shape[1:]
                made[p][row + q] = (v * sig).astype(BF16).reshape(shape)
                slopes[p][row + q] = slope.astype(BF16).reshape(shape)

    in_blocks(made[0].shape[0] // 2, one)

    def two(r):
        row = 2 * r
        for p, sums in enumerate(taps(second[...], neighbours([[ref] for ref in hiddens]), row)):
            for q, v in enumerate(sums):
                shape = deltas[p].shape[1:]
                out_grad = grads[p][row + q].astype(F32)
                slope = silu_parts(v)[1].reshape(shape)
                deltas[p][row + q] = (out_grad * slope).astype(BF16)

    if count > 0:
        in_blocks(deltas[0].shape[0] // 2, two)


def planes_of(pairs):
    return [(refs, x) for refs in pairs for x in range(2)]


def weight_loop(total, pieces, first_row, deltas, delta_row, count):
    blocks = [k for k in range(1, 13) if count // 2 % k == 0 and k * len(deltas) <= 12]
    together = max(blocks, default=1)

    def step(r, _):
        left, right = [], []
        for k in range(together):
            row = 2 * (r * together + k)
            for x, ((delta,), place) in enumerate(deltas):
                rows = []
                for q in range(2):
                    wide = delta[delta_row + row + q, place]
                    depth = wide.shape[1]
                    rows += [pltpu.roll(wide, depth - 1, 1), wide, pltpu.roll(wide, 1, 1)]
                    rows.append(jnp.zeros_like(wide))
                right.append(jnp.concatenate(rows, axis=0))
                rows = []
                for refs, side in pieces[x : x + 3]:
                    for b in range(4):
                        for ref in refs:
                            rows.append(ref[first_row + row + b, side])
                left.append(jnp.concatenate(rows, axis=0))
        total[...] += lax.dot_general(
            jnp.concatenate(left, axis=1),
            jnp.concatenate(right, axis=1),
            (((1,), (1,)), ((), ())),
            preferred_element_type=F32,
        )
        return 0

    lax.fori_loop(0, count // 2 // together, step, 0)


def weight_fold(total, size):
    lanes = total.shape[1] // 2
    channels = total.shape[0] // 12
    upper, lower = total[:, :lanes], total[:, lanes:]
    groups = []
    for g in range(channels // size):
        taps_of = []
        for a in range(3):
            for b in range(3):
                start = (4 * a + b) * channels + g * size
                part = (
                    upper[start : start + size]
                    + lower[start + channels : start + channels + size]
                )
                taps_of += [part[:, e * channels : (e + 1) * channels] for e in range(3)]
        blank = jnp.zeros((size, channels), F32)
        taps_of.append(blank)
        groups.append([jnp.concatenate(taps_of[4 * h : 4 * h + 4], axis=1) for h in range(7)])
    return groups


def first_deltas(weight, inputs, slopes, firsts):
    def one(r):
        row = 2 * r
        for p, sums in enumerate(taps(weight[...], inputs, row)):
            for q, v in enumerate(sums):
                shape = firsts[p].shape[1:]
                slope = slopes[p][row + 2 + q].astype(F32)
                firsts[p][row + q] = (v.reshape(shape) * slope).astype(BF16)

    in_blocks(firsts[0].shape[0] // 2, one)


def gradient_kernel(share, groups, extent, pairs, *refs):
    refs = list(refs)
    hiddens = [[refs.pop(0)] for _ in range(pairs + 1)]
    deltas = [[refs.pop(0)] for _ in range(pairs)]
    weight = refs.pop(0)
    slopes = [refs.pop(0) for _ in range(pairs + 1)]
    fields = [[refs.pop(0) for _ in range(groups)] for _ in range(pairs + 2)]
    keep, send = refs.pop(0), refs.pop(0)
    inner = [refs.pop(0) for _ in range(pairs - 1)]
    head, tail, none, second_total, first_total = refs
    none[...] = jnp.zeros_like(none)
    second_total[...] = jnp.zeros_like(second_total)
    first_total[...] = jnp.zeros_like(first_total)
    weight_loop(second_total, planes_of(hiddens), 2, planes_of(deltas), 2, share)
    firsts = [head] + inner + [tail]
    first_deltas(weight, neighbours([[none]] + deltas + [[none]]), slopes, firsts)
    parts = planes_of([[first] for first in firsts])
    weight_loop(first_total, planes_of(fields), 3, parts, 1, share)
    halves, size = keep.shape[1:3]
    me = lax.axis_index("chan")
    of_first = weight_fold(first_total, size)
    of_second = weight_fold(second_total, size)

    def place(ours, theirs):
        for g in range(extent):
            there = lax.rem(me + extent - g, extent)
            for h in range(halves):
                ours[g, h] = of_first[g][h]
                theirs[there, h] = of_second[g][h]

    odd = lax.rem(lax.axis_index("slab"), 2)

    @pl.when(odd == 0)
    def _():
        place(keep, send)

    @pl.when(odd == 1)
    def _():
        place(send, keep)


def field_kernel_back(inner, groups, after, *refs):
    del after
    refs = list(refs)
    back, weight = refs.pop(0), refs.pop(0)
    before, first, last, behind = [[refs.pop(0)] for _ in range(4)]
    slopes = [refs.pop(0) for _ in range(2)]
    middle = [refs.pop(0) for _ in range(inner)]
    outs, ends = refs[:groups], refs[groups:]
    first_deltas(back, [(before, first), (last, behind)], slopes, ends)
    firsts = [ends[0]] + middle + [ends[1]]

    def one(r):
        row = 2 * r
        size = outs[0].shape[2]
        channels = len(outs) * size
        for p, sums in enumerate(taps(weight[...], neighbours([[ref] for ref in firsts]), row)):
            for q, v in enumerate(sums):
                for x in range(2):
                    for j, out in enumerate(outs):
                        low = x * channels + j * size
                        out[row + q, 2 * p + x] = v[low : low + size].astype(BF16)

    in_blocks(outs[0].shape[0] // 2, one)


def finish_kernel(factor, after, mine, other, first, second):
    del after
    channels = first.shape[2]

    def place(ours, theirs):
        for out, sums in ((ours, mine), (theirs, other)):
            for t in range(27):
                low = t % 4 * channels
                out[t] = sums[t // 4, :, low : low + channels] * factor

    odd = lax.rem(lax.axis_index("slab"), 2)

    @pl.when(odd == 0)
    def _():
        place(first, second)

    @pl.when(odd == 1)
    def _():
        place(second, first)


def split_kernel(after, one, two, *outs):
    del after
    for g, out in enumerate(outs):
        out[...] = one[g] + two[g]


def add_kernel(ahead, *refs):
    values = [ref[...] for ref in refs[ahead:-1]]
    while len(values) > 1:
        values = [sum(values[k + 1 : k + 2], values[k]) for k in range(0, len(values), 2)]
    refs[-1][...] = values[0]


def relay_kernel(*refs):
    pass


def merge_kernel(extent, *refs):
    pieces, token, out, wide = refs[:-3], refs[-3], refs[-2], refs[-1]
    token[...] = jnp.zeros_like(token)
    size, planes, rows = out.shape[:3]
    share = rows // extent
    me = lax.axis_index("chan")
    for j in range(extent):
        base = lax.rem(me + extent - j, extent) * share

        def widen(f, mine=pieces[j::extent], base=base):
            x = 0
            for piece in mine:
                for k in range(piece.shape[1]):
                    start = ((base + f) * planes + x) * size
                    start = pl.multiple_of(start, 8) if size % 8 == 0 else start
                    wide[pl.ds(start, size), :] = piece[f, k].astype(F32)
                    x += 1

        in_blocks(share, widen)

    def back(i):
        for x in range(planes):
            tile = wide[pl.ds(x * size + i, rows, stride=planes * size), :]
            out[i, x] = tile.astype(BF16)

    in_blocks(size, back)


def body(field, out_grad, first_weight, second_weight):
    extent = lax.axis_size("chan")
    slabs = lax.axis_size("slab")
    me = lax.axis_index("chan")
    size, planes, rows, depth = field.shape
    channels = size * extent
    pairs = planes // 2
    share = rows // extent
    factor = 1.0 / math.sqrt(planes * slabs * rows * depth)

    def to_chan(value, shift):
        return lax.ppermute(value, "chan", [(i, (i + shift) % extent) for i in range(extent)])

    def to_next(value):
        return lax.ppermute(value, "slab", [(i, (i + 1) % slabs) for i in range(slabs)])

    def to_prev(value):
        return lax.ppermute(value, "slab", [((i + 1) % slabs, i) for i in range(slabs)])

    def relayed(value, *others):
        shape = jax.ShapeDtypeStruct(value.shape, value.dtype)
        early = [value, *others]
        return call(relay_kernel, [shape], early, loose=len(early), same={0: 0})[0]

    piece = jax.ShapeDtypeStruct((share + 8, 2, size, depth), BF16)
    by_tap = (27, size, channels)
    made = call(
        functools.partial(field_kernel, extent, 4),
        [piece] * (extent * pairs),
        [field],
        [pltpu.VMEM((size * planes * rows, depth), F32)],
        moved=field.size * 6,
    )
    parts = [list(made[:pairs])]
    for j in range(1, extent):
        parts.append([to_chan(value, j) for value in made[j * pairs : (j + 1) * pairs]])
    (pack,) = call(
        pack_kernel,
        [jax.ShapeDtypeStruct((14, size, 4 * channels), BF16)],
        [made[0], jnp.transpose(first_weight, (1, 0, 2)), jnp.transpose(second_weight, (1, 0, 2))],
        loose=1,
    )
    packs = [pack] + [to_chan(pack, j) for j in range(1, extent)]
    whole = size % 16 == 0
    own_before, own_after = [], []
    if whole:
        own_before, own_after = [to_next(parts[0][-1])], [to_prev(parts[0][0])]
    grad_piece = jax.ShapeDtypeStruct((share + 4, 2, channels, depth), BF16)
    grads = call(
        functools.partial(grad_kernel, extent, 2),
        [grad_piece] * pairs,
        [pack, out_grad],
        [pltpu.VMEM((channels * planes * rows, depth), F32)],
        moved=out_grad.size * 4,
        loose=1,
    )
    matrix = jax.ShapeDtypeStruct((6 * channels, 12 * channels), BF16)
    first_wide, second_wide, first_back, second_back = call(
        functools.partial(matrix_kernel, extent),
        [matrix] * 4,
        packs,
        moved=matrix.size * 8,
    )
    if whole and extent > 1 and pairs > 1:
        parts[1][-1] = relayed(parts[1][-1], pack)
        parts[1][0] = relayed(relayed(parts[1][0], grads[0], *packs[1:]), own_after[0])
    by_pair = [[parts[j][p] for j in range(extent)] for p in range(pairs)]
    groups = extent
    if not whole:
        by_pair = [[jnp.concatenate(pieces, axis=2)] for pieces in by_pair]
        groups = 1
    before = own_before + [to_next(piece) for piece in by_pair[-1][len(own_before) :]]
    after = own_after + [to_prev(piece) for piece in by_pair[0][len(own_after) :]]
    fields = [before] + by_pair + [after]

    def many(count, rows_each):
        return [jax.ShapeDtypeStruct((rows_each, 2, channels, depth), BF16)] * count

    def flat(lists):
        return [piece for pieces in lists for piece in pieces]

    work = 27 * 2 * channels * channels * depth * 2
    space = 4 * channels * depth * share

    made = call(
        functools.partial(forward_kernel, groups, pairs, 0),
        many(2 * pairs, share + 6) + many(pairs - 1, share + 4),
        flat(fields[: pairs + 1]) + list(grads[: pairs - 1]) + [first_wide, second_wide],
        flops=work * (2 * pairs - 1) * share,
        moved=space * 4 * pairs,
    )
    hiddens, slopes, deltas = made[:pairs], made[pairs : 2 * pairs], made[2 * pairs :]
    made = call(
        functools.partial(forward_kernel, groups, 1, 1),
        many(2, share + 6) + many(1, share + 4),
        flat(fields[pairs:]) + [hiddens[-1], grads[-1], first_wide, second_wide],
        flops=work * 2 * share,
        moved=space * 6,
    )
    hiddens = list(hiddens) + [made[0]]
    slopes = list(slopes) + [made[1]]
    deltas = list(deltas) + [made[2]]
    delta_after = to_prev(deltas[0])
    delta_before = to_next(deltas[-1])

    raw = jax.ShapeDtypeStruct((extent, 7, size, 4 * channels), F32)
    portion = jax.ShapeDtypeStruct(raw.shape[1:], F32)
    total = pltpu.VMEM((12 * channels, 8 * channels), F32)

    def room(rows_each):
        return pltpu.VMEM((rows_each, 2, channels, depth), BF16)

    made = call(
        functools.partial(gradient_kernel, share, groups, extent, pairs),
        [raw] * 2 + many(pairs - 1, share + 2),
        hiddens + deltas + [second_back] + slopes + flat(fields),
        [room(share + 2), room(share + 2), room(share + 4), total, total],
    )
    keep, send, inner = made[0], made[1], list(made[2:])
    def exchanged(made):
        pieces = [made[0]] + [None] * (extent - 1)
        for j in range(1, extent):
            pieces[extent - j] = to_chan(made[j], extent - j)
        return pieces

    def stepped(value, stride, shift=0):
        if shift % extent == 0:
            return lax.ppermute(value, "slab", [(i, i ^ stride) for i in range(slabs)])
        pairs_of = []
        for i in range(slabs):
            for k in range(extent):
                there = (i ^ stride) * extent + (k + shift) % extent
                pairs_of.append((i * extent + k, there))
        return lax.ppermute(value, ("slab", "chan"), pairs_of)

    plain = slabs & (slabs - 1) == 0 and slabs >= 4
    if plain:
        kept = call(
            split_kernel, [portion] * extent, [delta_after, keep, stepped(send, 1)], loose=1
        )
        shares = [kept[0]] + [to_chan(kept[j], extent - j) for j in range(1, extent)]
        shares += [stepped(kept[j], 2, extent - j) for j in range(extent)]
        after = kept[0]
    else:
        after = keep
    made = call(
        functools.partial(field_kernel_back, pairs - 1, extent),
        [jax.ShapeDtypeStruct((share, planes, size, depth), BF16)] * extent,
        [after, second_back, first_back]
        + [delta_before, deltas[0], deltas[-1], delta_after, slopes[0], slopes[-1]]
        + inner,
        [room(share + 2), room(share + 2)],
        flops=work * (pairs + 2) * share,
        moved=space * 6,
        loose=1,
    )
    if plain:
        ahead = list(made[:1])
        (mine,) = call(
            functools.partial(add_kernel, len(ahead)), [portion], ahead + shares, loose=len(ahead)
        )
        made = list(made[:1]) + [relayed(value, mine) for value in made[1:]]
    pieces = exchanged(made)
    if plain:
        stride = 4
        while stride < slabs:
            radix = 4 if slabs % (4 * stride) == 0 else 2
            got = [mine] + [stepped(mine, m * stride) for m in range(1, radix)]
            (mine,) = call(functools.partial(add_kernel, 0), [portion], got)
            stride *= radix
        other = stepped(mine, 1)
    else:
        mine, other = keep[0], send[0]
        for j in range(1, extent):
            mine, other = mine + to_chan(keep[j], extent - j), other + to_chan(send[j], extent - j)
        even = lax.rem(lax.axis_index("slab"), 2) == 0
        mine, other = jnp.where(even, mine, other), jnp.where(even, other, mine)
        mine, other = lax.psum((mine, other), "slab")
        mine, other = jnp.where(even, mine, other), jnp.where(even, other, mine)
    token, input_grad = call(
        functools.partial(merge_kernel, extent),
        [jax.ShapeDtypeStruct((8, 128), F32), jax.ShapeDtypeStruct(field.shape, BF16)],
        pieces,
        [pltpu.VMEM((rows * planes * size, depth), F32)],
        moved=4 * field.size,
    )
    first_grad, second_grad = call(
        functools.partial(finish_kernel, factor),
        [jax.ShapeDtypeStruct(by_tap, F32)] * 2,
        [token, mine, other],
        loose=1,
    )
    first_grad, second_grad = (jnp.transpose(g, (1, 0, 2)) for g in (first_grad, second_grad))
    return input_grad, first_grad, second_grad


def solution(mesh):
    placed = (
        P("chan", "slab", None, None),
        P(None, "slab", None, None),
        P("chan", None, None),
        P("chan", None, None),
    )
    return jax.shard_map(
        body,
        mesh=mesh,
        in_specs=placed,
        out_specs=(P("chan", "slab", None, None), P("chan", None, None), P("chan", None, None)),
        check_vma=False,
    )
```

```python
import functools
import math

import jax
import jax.numpy as jnp
from jax import lax
from jax.experimental import pallas as pl
from jax.experimental.pallas import tpu as pltpu
from jax.sharding import PartitionSpec as P

F32 = jnp.float32
BF16 = jnp.bfloat16
LIMIT = 16 * 1024 * 1024


def call(kernel, outs, args, scratch=(), flops=0, moved=0, loose=0, same=None):
    whole = pl.BlockSpec(memory_space=pltpu.VMEM)
    still = pl.BlockSpec(memory_space=pl.ANY)
    return pl.pallas_call(
        kernel,
        out_shape=outs,
        in_specs=[still] * loose + [whole] * (len(args) - loose),
        out_specs=[still if k in (same or {}).values() else whole for k in range(len(outs))],
        input_output_aliases=same or {},
        scratch_shapes=list(scratch),
        compiler_params=pltpu.CompilerParams(vmem_limit_bytes=LIMIT),
        cost_estimate=pl.CostEstimate(flops=flops, bytes_accessed=moved, transcendentals=0),
    )(*args)


def in_blocks(count, body):
    block = max(k for k in range(1, 17) if count % k == 0)

    def several(r, _):
        for k in range(block):
            body(r * block + k)
        return 0

    lax.fori_loop(0, count // block, several, 0)
    for k in range(count // block * block, count):
        body(k)


def widened(x_ref, wide):
    count, planes, rows = x_ref.shape[:3]

    def widen(i):
        for x in range(planes):
            start = pl.multiple_of((i * planes + x) * rows, 8)
            wide[pl.ds(start, rows), :] = x_ref[i, x].astype(F32)

    in_blocks(count, widen)


def turn(wide, outs, shape, base, length):
    count, planes, rows = shape

    def one(f):
        y = lax.rem(base + f, rows)
        for x in range(planes):
            tile = wide[pl.ds(x * rows + y, count, stride=planes * rows), :]
            outs[x // 2][f, x % 2] = tile.astype(BF16)

    in_blocks(length, one)


def field_kernel(extent, margin, x_ref, *refs):
    outs, wide = refs[:-1], refs[-1]
    count, planes, rows = x_ref.shape[:3]
    pairs = planes // 2
    share = rows // extent
    widened(x_ref, wide)
    me = lax.axis_index("chan")
    for s in range(extent):
        base = lax.rem(me + s, extent) * share - margin + rows
        turn(
            wide,
            outs[s * pairs : (s + 1) * pairs],
            (count, planes, rows),
            base,
            share + 2 * margin,
        )


def pack_kernel(after, first, second, packed):
    del after
    blank = jnp.zeros(first.shape[1:], F32)
    for h in range(packed.shape[0]):
        parts = []
        for ref in (first, second):
            for t in (2 * h, 2 * h + 1):
                parts.append(ref[t].astype(F32) if t < ref.shape[0] else blank)
        packed[h] = jnp.concatenate(parts, axis=1).astype(BF16)


def grad_kernel(extent, margin, after, x_ref, *refs):
    del after
    outs, wide = refs[:-1], refs[-1]
    count, planes, rows = x_ref.shape[:3]
    share = rows // extent
    widened(x_ref, wide)
    base = lax.axis_index("chan") * share - margin + rows
    turn(wide, outs, (count, planes, rows), base, share + 2 * margin)


def matrix_kernel(extent, *refs):
    packs, outs = refs[:extent], refs[extent:]
    me = lax.axis_index("chan")
    quarter = packs[0].shape[2] // 4
    taps = []
    turned = []
    for h in range(packs[0].shape[0]):
        tiles = [pack[h].astype(F32) for pack in packs]
        own = jnp.concatenate(tiles, axis=0)
        fixed = []
        for g in range(extent):
            place = lax.rem(me + extent - g, extent)
            tile = tiles[0]
            for j in range(1, extent):
                tile = jnp.where(place == j, tiles[j], tile)
            fixed.append(tile)
        both = jnp.concatenate(
            [own[:, : 2 * quarter], jnp.concatenate(fixed, axis=0)[:, 2 * quarter :]], axis=1
        )
        across = both.T
        for side in range(2):
            taps.append(
                [both[:, k * quarter : (k + 1) * quarter] for k in (side, side + 2)]
            )
            turned.append(
                [across[k * quarter : (k + 1) * quarter] for k in (side, side + 2)]
            )
    channels = quarter
    blank = jnp.zeros((channels, channels), F32)
    for k in range(2):
        for out, blocks, flip in ((outs[k], turned, False), (outs[2 + k], taps, True)):
            for e in range(3):
                for x in range(2):
                    chunks = []
                    for pair in range(2):
                        for b in range(3):
                            for side in range(2):
                                a = 2 * pair + side - x
                                t = 9 * a + 3 * b + e
                                inside = 0 <= a <= 2
                                t = 26 - t if flip else t
                                chunks.append(blocks[t][k] if inside else blank)
                    low = (2 * e + x) * channels
                    out[low : low + channels, :] = jnp.concatenate(chunks, axis=1).astype(BF16)


def stacked(refs, row, count):
    if len(refs) == 1:
        part = refs[0][pl.ds(row, count)]
        return part.reshape(-1, part.shape[-1])
    parts = [ref[row + b, x] for b in range(count) for x in range(2) for ref in refs]
    return jnp.concatenate(parts, axis=0)


def taps(weight, inputs, row):
    sides = []
    for above, below in inputs:
        for q in range(2):
            sides.append(
                jnp.concatenate([stacked(above, row + q, 3), stacked(below, row + q, 3)], axis=0)
            )
    lifted = jnp.dot(weight, jnp.concatenate(sides, axis=1), preferred_element_type=F32)
    third = lifted.shape[0] // 3
    depth = sides[0].shape[1]
    sums = []
    for k in range(len(sides)):
        side = lifted[:, k * depth : (k + 1) * depth]
        sums.append(
            side[third : 2 * third]
            + pltpu.roll(side[:third], 1, 1)
            + pltpu.roll(side[2 * third :], depth - 1, 1)
        )
    return [sums[2 * p : 2 * p + 2] for p in range(len(inputs))]


def neighbours(pairs):
    return list(zip(pairs[:-1], pairs[1:]))


def silu_parts(v):
    sig = jax.nn.sigmoid(v)
    return sig, sig * (1.0 + v * (1.0 - sig))


def forward_kernel(groups, fresh, ready, *refs):
    refs = list(refs)
    fields = [[refs.pop(0) for _ in range(groups)] for _ in range(fresh + 1)]
    hiddens = [refs.pop(0) for _ in range(ready)]
    count = fresh + ready - 1
    grads = [refs.pop(0) for _ in range(count)]
    first, second = refs.pop(0), refs.pop(0)
    made = [refs.pop(0) for _ in range(fresh)]
    slopes = [refs.pop(0) for _ in range(fresh)]
    deltas = refs
    hiddens = hiddens + made

    def one(r):
        row = 2 * r
        for p, sums in enumerate(taps(first[...], neighbours(fields), row)):
            for q, v in enumerate(sums):
                sig, slope = silu_parts(v)
                shape = made[p].shape[1:]
                made[p][row + q] = (v * sig).astype(BF16).reshape(shape)
                slopes[p][row + q] = slope.astype(BF16).reshape(shape)

    in_blocks(made[0].shape[0] // 2, one)

    def two(r):
        row = 2 * r
        for p, sums in enumerate(taps(second[...], neighbours([[ref] for ref in hiddens]), row)):
            for q, v in enumerate(sums):
                shape = deltas[p].shape[1:]
                out_grad = grads[p][row + q].astype(F32)
                slope = silu_parts(v)[1].reshape(shape)
                deltas[p][row + q] = (out_grad * slope).astype(BF16)

    if count > 0:
        in_blocks(deltas[0].shape[0] // 2, two)


def planes_of(pairs):
    return [(refs, x) for refs in pairs for x in range(2)]


def weight_loop(total, pieces, first_row, deltas, delta_row, count):
    blocks = [k for k in range(1, 13) if count // 2 % k == 0 and k * len(deltas) <= 12]
    together = max(blocks, default=1)

    def product(r):
        left, right = [], []
        for k in range(together):
            row = 2 * (r * together + k)
            for x, ((delta,), place) in enumerate(deltas):
                rows = []
                for q in range(2):
                    wide = delta[delta_row + row + q, place]
                    depth = wide.shape[1]
                    rows += [pltpu.roll(wide, depth - 1, 1), wide, pltpu.roll(wide, 1, 1)]
                    rows.append(jnp.zeros_like(wide))
                right.append(jnp.concatenate(rows, axis=0))
                rows = []
                for refs, side in pieces[x : x + 3]:
                    for b in range(4):
                        for ref in refs:
                            rows.append(ref[first_row + row + b, side])
                left.append(jnp.concatenate(rows, axis=0))
        return lax.dot_general(
            jnp.concatenate(left, axis=1),
            jnp.concatenate(right, axis=1),
            (((1,), (1,)), ((), ())),
            preferred_element_type=F32,
        )

    value = total[...]
    for r in range(count // 2 // together):
        value = value + product(r)
    total[...] = value


def weight_fold(total, size):
    lanes = total.shape[1] // 2
    channels = total.shape[0] // 12
    upper, lower = total[:, :lanes], total[:, lanes:]
    groups = []
    for g in range(channels // size):
        taps_of = []
        for a in range(3):
            for b in range(3):
                start = (4 * a + b) * channels + g * size
                part = (
                    upper[start : start + size]
                    + lower[start + channels : start + channels + size]
                )
                taps_of += [part[:, e * channels : (e + 1) * channels] for e in range(3)]
        blank = jnp.zeros((size, channels), F32)
        taps_of.append(blank)
        groups.append([jnp.concatenate(taps_of[4 * h : 4 * h + 4], axis=1) for h in range(7)])
    return groups


def first_deltas(weight, inputs, slopes, firsts):
    def one(r):
        row = 2 * r
        for p, sums in enumerate(taps(weight[...], inputs, row)):
            for q, v in enumerate(sums):
                shape = firsts[p].shape[1:]
                slope = slopes[p][row + 2 + q].astype(F32)
                firsts[p][row + q] = (v.reshape(shape) * slope).astype(BF16)

    in_blocks(firsts[0].shape[0] // 2, one)


def gradient_kernel(share, groups, extent, pairs, *refs):
    refs = list(refs)
    hiddens = [[refs.pop(0)] for _ in range(pairs + 1)]
    deltas = [[refs.pop(0)] for _ in range(pairs)]
    weight = refs.pop(0)
    slopes = [refs.pop(0) for _ in range(pairs + 1)]
    fields = [[refs.pop(0) for _ in range(groups)] for _ in range(pairs + 2)]
    keep, send = refs.pop(0), refs.pop(0)
    inner = [refs.pop(0) for _ in range(pairs - 1)]
    head, tail, none, second_total, first_total = refs
    none[...] = jnp.zeros_like(none)
    second_total[...] = jnp.zeros_like(second_total)
    first_total[...] = jnp.zeros_like(first_total)
    weight_loop(second_total, planes_of(hiddens), 2, planes_of(deltas), 2, share)
    firsts = [head] + inner + [tail]
    first_deltas(weight, neighbours([[none]] + deltas + [[none]]), slopes, firsts)
    parts = planes_of([[first] for first in firsts])
    weight_loop(first_total, planes_of(fields), 3, parts, 1, share)
    halves, size = keep.shape[1:3]
    me = lax.axis_index("chan")
    of_first = weight_fold(first_total, size)
    of_second = weight_fold(second_total, size)

    def place(ours, theirs):
        for g in range(extent):
            there = lax.rem(me + extent - g, extent)
            for h in range(halves):
                ours[g, h] = of_first[g][h]
                theirs[there, h] = of_second[g][h]

    odd = lax.rem(lax.axis_index("slab"), 2)

    @pl.when(odd == 0)
    def _():
        place(keep, send)

    @pl.when(odd == 1)
    def _():
        place(send, keep)


def field_kernel_back(inner, groups, after, *refs):
    del after
    refs = list(refs)
    back, weight = refs.pop(0), refs.pop(0)
    before, first, last, behind = [[refs.pop(0)] for _ in range(4)]
    slopes = [refs.pop(0) for _ in range(2)]
    middle = [refs.pop(0) for _ in range(inner)]
    outs, ends = refs[:groups], refs[groups:]
    first_deltas(back, [(before, first), (last, behind)], slopes, ends)
    firsts = [ends[0]] + middle + [ends[1]]

    def one(r):
        row = 2 * r
        size = outs[0].shape[2]
        channels = len(outs) * size
        for p, sums in enumerate(taps(weight[...], neighbours([[ref] for ref in firsts]), row)):
            for q, v in enumerate(sums):
                for x in range(2):
                    for j, out in enumerate(outs):
                        low = x * channels + j * size
                        out[row + q, 2 * p + x] = v[low : low + size].astype(BF16)

    in_blocks(outs[0].shape[0] // 2, one)


def split_kernel(after, one, two, *outs):
    del after
    for g, out in enumerate(outs):
        out[...] = one[g] + two[g]


def add_kernel(ahead, *refs):
    values = [ref[...] for ref in refs[ahead:-1]]
    while len(values) > 1:
        values = [sum(values[k + 1 : k + 2], values[k]) for k in range(0, len(values), 2)]
    refs[-1][...] = values[0]


def relay_kernel(*refs):
    pass


def merge_kernel(extent, factor, *refs):
    mine, other, *pieces = refs[:-4]
    out, first, second, wide = refs[-4:]
    channels = first.shape[2]

    def place(ours, theirs):
        for result, sums in ((ours, mine), (theirs, other)):
            for t in range(27):
                low = t % 4 * channels
                result[t] = sums[t // 4, :, low : low + channels] * factor

    odd = lax.rem(lax.axis_index("slab"), 2)

    @pl.when(odd == 0)
    def _():
        place(first, second)

    @pl.when(odd == 1)
    def _():
        place(second, first)

    size, planes, rows = out.shape[:3]
    share = rows // extent
    me = lax.axis_index("chan")
    for j in range(extent):
        base = lax.rem(me + extent - j, extent) * share

        def widen(f, mine=pieces[j::extent], base=base):
            x = 0
            for piece in mine:
                for k in range(piece.shape[1]):
                    start = ((base + f) * planes + x) * size
                    start = pl.multiple_of(start, 8) if size % 8 == 0 else start
                    wide[pl.ds(start, size), :] = piece[f, k].astype(F32)
                    x += 1

        in_blocks(share, widen)

    def back(i):
        for x in range(planes):
            tile = wide[pl.ds(x * size + i, rows, stride=planes * size), :]
            out[i, x] = tile.astype(BF16)

    in_blocks(size, back)


def body(field, out_grad, first_weight, second_weight):
    extent = lax.axis_size("chan")
    slabs = lax.axis_size("slab")
    me = lax.axis_index("chan")
    size, planes, rows, depth = field.shape
    channels = size * extent
    pairs = planes // 2
    share = rows // extent
    factor = 1.0 / math.sqrt(planes * slabs * rows * depth)

    def to_chan(value, shift):
        return lax.ppermute(value, "chan", [(i, (i + shift) % extent) for i in range(extent)])

    def to_next(value):
        return lax.ppermute(value, "slab", [(i, (i + 1) % slabs) for i in range(slabs)])

    def to_prev(value):
        return lax.ppermute(value, "slab", [((i + 1) % slabs, i) for i in range(slabs)])

    def relayed(value, *others):
        shape = jax.ShapeDtypeStruct(value.shape, value.dtype)
        early = [value, *others]
        return call(relay_kernel, [shape], early, loose=len(early), same={0: 0})[0]

    piece = jax.ShapeDtypeStruct((share + 8, 2, size, depth), BF16)
    by_tap = (27, size, channels)
    made = call(
        functools.partial(field_kernel, extent, 4),
        [piece] * (extent * pairs),
        [field],
        [pltpu.VMEM((size * planes * rows, depth), F32)],
        moved=field.size * 6,
    )
    parts = [list(made[:pairs])]
    for j in range(1, extent):
        parts.append([to_chan(value, j) for value in made[j * pairs : (j + 1) * pairs]])
    (pack,) = call(
        pack_kernel,
        [jax.ShapeDtypeStruct((14, size, 4 * channels), BF16)],
        [made[0], jnp.transpose(first_weight, (1, 0, 2)), jnp.transpose(second_weight, (1, 0, 2))],
        loose=1,
    )
    packs = [pack] + [to_chan(pack, j) for j in range(1, extent)]
    whole = size % 16 == 0
    own_before, own_after = [], []
    if whole:
        own_before, own_after = [to_next(parts[0][-1])], [to_prev(parts[0][0])]
    grad_piece = jax.ShapeDtypeStruct((share + 4, 2, channels, depth), BF16)
    grads = call(
        functools.partial(grad_kernel, extent, 2),
        [grad_piece] * pairs,
        [pack, out_grad],
        [pltpu.VMEM((channels * planes * rows, depth), F32)],
        moved=out_grad.size * 4,
        loose=1,
    )
    matrix = jax.ShapeDtypeStruct((6 * channels, 12 * channels), BF16)
    first_wide, second_wide, first_back, second_back = call(
        functools.partial(matrix_kernel, extent),
        [matrix] * 4,
        packs,
        moved=matrix.size * 8,
    )
    if whole and extent > 1 and pairs > 1:
        parts[1][-1] = relayed(parts[1][-1], *packs[1:])
        parts[1][0] = relayed(relayed(parts[1][0], grads[0], first_wide), own_after[0])
    by_pair = [[parts[j][p] for j in range(extent)] for p in range(pairs)]
    groups = extent
    if not whole:
        by_pair = [[jnp.concatenate(pieces, axis=2)] for pieces in by_pair]
        groups = 1
    before = own_before + [to_next(piece) for piece in by_pair[-1][len(own_before) :]]
    after = own_after + [to_prev(piece) for piece in by_pair[0][len(own_after) :]]
    fields = [before] + by_pair + [after]

    def many(count, rows_each):
        return [jax.ShapeDtypeStruct((rows_each, 2, channels, depth), BF16)] * count

    def flat(lists):
        return [piece for pieces in lists for piece in pieces]

    work = 27 * 2 * channels * channels * depth * 2
    space = 4 * channels * depth * share

    made = call(
        functools.partial(forward_kernel, groups, pairs, 0),
        many(2 * pairs, share + 6) + many(pairs - 1, share + 4),
        flat(fields[: pairs + 1]) + list(grads[: pairs - 1]) + [first_wide, second_wide],
        flops=work * (2 * pairs - 1) * share,
        moved=space * 4 * pairs,
    )
    hiddens, slopes, deltas = made[:pairs], made[pairs : 2 * pairs], made[2 * pairs :]
    made = call(
        functools.partial(forward_kernel, groups, 1, 1),
        many(2, share + 6) + many(1, share + 4),
        flat(fields[pairs:]) + [hiddens[-1], grads[-1], first_wide, second_wide],
        flops=work * 2 * share,
        moved=space * 6,
    )
    hiddens = list(hiddens) + [made[0]]
    slopes = list(slopes) + [made[1]]
    deltas = list(deltas) + [made[2]]
    delta_after = to_prev(deltas[0])
    delta_before = to_next(deltas[-1])

    raw = jax.ShapeDtypeStruct((extent, 7, size, 4 * channels), F32)
    portion = jax.ShapeDtypeStruct(raw.shape[1:], F32)
    total = pltpu.VMEM((12 * channels, 8 * channels), F32)

    def room(rows_each):
        return pltpu.VMEM((rows_each, 2, channels, depth), BF16)

    made = call(
        functools.partial(gradient_kernel, share, groups, extent, pairs),
        [raw] * 2 + many(pairs - 1, share + 2),
        hiddens + deltas + [second_back] + slopes + flat(fields),
        [room(share + 2), room(share + 2), room(share + 4), total, total],
    )
    keep, send, inner = made[0], made[1], list(made[2:])
    def exchanged(made):
        pieces = [made[0]] + [None] * (extent - 1)
        for j in range(1, extent):
            pieces[extent - j] = to_chan(made[j], extent - j)
        return pieces

    def stepped(value, stride, shift=0):
        if shift % extent == 0:
            return lax.ppermute(value, "slab", [(i, i ^ stride) for i in range(slabs)])
        pairs_of = []
        for i in range(slabs):
            for k in range(extent):
                there = (i ^ stride) * extent + (k + shift) % extent
                pairs_of.append((i * extent + k, there))
        return lax.ppermute(value, ("slab", "chan"), pairs_of)

    plain = slabs & (slabs - 1) == 0 and slabs >= 4
    if plain:
        kept = call(
            split_kernel, [portion] * extent, [delta_after, keep, stepped(send, 1)], loose=1
        )
        shares = [kept[0]] + [to_chan(kept[j], extent - j) for j in range(1, extent)]
        shares += [stepped(kept[j], 2, extent - j) for j in range(extent)]
        after = kept[0]
    else:
        after = keep
    made = call(
        functools.partial(field_kernel_back, pairs - 1, extent),
        [jax.ShapeDtypeStruct((share, planes, size, depth), BF16)] * extent,
        [after, second_back, first_back]
        + [delta_before, deltas[0], deltas[-1], delta_after, slopes[0], slopes[-1]]
        + inner,
        [room(share + 2), room(share + 2)],
        flops=work * (pairs + 2) * share,
        moved=space * 6,
        loose=1,
    )
    if plain:
        ahead = list(made[:1])
        (mine,) = call(
            functools.partial(add_kernel, len(ahead)), [portion], ahead + shares, loose=len(ahead)
        )
        made = list(made[:1]) + [relayed(value, mine) for value in made[1:]]
    pieces = exchanged(made)
    if plain:
        stride = 4
        while stride < slabs:
            radix = 4 if slabs % (4 * stride) == 0 else 2
            got = [mine] + [stepped(mine, m * stride) for m in range(1, radix)]
            (mine,) = call(functools.partial(add_kernel, 0), [portion], got)
            stride *= radix
        other = stepped(mine, 1)
    else:
        mine, other = keep[0], send[0]
        for j in range(1, extent):
            mine, other = mine + to_chan(keep[j], extent - j), other + to_chan(send[j], extent - j)
        even = lax.rem(lax.axis_index("slab"), 2) == 0
        mine, other = jnp.where(even, mine, other), jnp.where(even, other, mine)
        mine, other = lax.psum((mine, other), "slab")
        mine, other = jnp.where(even, mine, other), jnp.where(even, other, mine)
    input_grad, first_grad, second_grad = call(
        functools.partial(merge_kernel, extent, factor),
        [jax.ShapeDtypeStruct(field.shape, BF16)] + [jax.ShapeDtypeStruct(by_tap, F32)] * 2,
        [mine, other] + pieces,
        [pltpu.VMEM((rows * planes * size, depth), F32)],
        moved=4 * field.size,
    )
    first_grad, second_grad = (jnp.transpose(g, (1, 0, 2)) for g in (first_grad, second_grad))
    return input_grad, first_grad, second_grad


def solution(mesh):
    placed = (
        P("chan", "slab", None, None),
        P(None, "slab", None, None),
        P("chan", None, None),
        P("chan", None, None),
    )
    return jax.shard_map(
        body,
        mesh=mesh,
        in_specs=placed,
        out_specs=(P("chan", "slab", None, None), P("chan", None, None), P("chan", None, None)),
        check_vma=False,
    )
```

```python
import functools
import math

import jax
import jax.numpy as jnp
from jax import lax
from jax.experimental import pallas as pl
from jax.experimental.pallas import tpu as pltpu
from jax.sharding import PartitionSpec as P

F32 = jnp.float32
BF16 = jnp.bfloat16
LIMIT = 16 * 1024 * 1024


def call(kernel, outs, args, scratch=(), flops=0, moved=0, loose=0, same=None):
    whole = pl.BlockSpec(memory_space=pltpu.VMEM)
    still = pl.BlockSpec(memory_space=pl.ANY)
    return pl.pallas_call(
        kernel,
        out_shape=outs,
        in_specs=[still] * loose + [whole] * (len(args) - loose),
        out_specs=[still if k in (same or {}).values() else whole for k in range(len(outs))],
        input_output_aliases=same or {},
        scratch_shapes=list(scratch),
        compiler_params=pltpu.CompilerParams(vmem_limit_bytes=LIMIT),
        cost_estimate=pl.CostEstimate(flops=flops, bytes_accessed=moved, transcendentals=0),
    )(*args)


def in_blocks(count, body):
    block = max(k for k in range(1, 17) if count % k == 0)

    def several(r, _):
        for k in range(block):
            body(r * block + k)
        return 0

    lax.fori_loop(0, count // block, several, 0)
    for k in range(count // block * block, count):
        body(k)


def widened(x_ref, wide):
    count, planes, rows = x_ref.shape[:3]

    def widen(i):
        for x in range(planes):
            start = pl.multiple_of((i * planes + x) * rows, 8)
            wide[pl.ds(start, rows), :] = x_ref[i, x].astype(F32)

    in_blocks(count, widen)


def turn(wide, outs, shape, base, length):
    count, planes, rows = shape

    def one(f):
        y = lax.rem(base + f, rows)
        for x in range(planes):
            tile = wide[pl.ds(x * rows + y, count, stride=planes * rows), :]
            outs[x // 2][f, x % 2] = tile.astype(BF16)

    in_blocks(length, one)


def field_kernel(extent, margin, x_ref, *refs):
    outs, wide = refs[:-1], refs[-1]
    count, planes, rows = x_ref.shape[:3]
    pairs = planes // 2
    share = rows // extent
    widened(x_ref, wide)
    me = lax.axis_index("chan")
    for s in range(extent):
        base = lax.rem(me + s, extent) * share - margin + rows
        turn(
            wide,
            outs[s * pairs : (s + 1) * pairs],
            (count, planes, rows),
            base,
            share + 2 * margin,
        )


def pack_kernel(after, first, second, packed):
    del after
    blank = jnp.zeros(first.shape[1:], F32)
    for h in range(packed.shape[0]):
        parts = []
        for ref in (first, second):
            for t in (2 * h, 2 * h + 1):
                parts.append(ref[t].astype(F32) if t < ref.shape[0] else blank)
        packed[h] = jnp.concatenate(parts, axis=1).astype(BF16)


def grad_kernel(extent, margin, after, x_ref, *refs):
    del after
    outs, wide = refs[:-1], refs[-1]
    count, planes, rows = x_ref.shape[:3]
    share = rows // extent
    widened(x_ref, wide)
    base = lax.axis_index("chan") * share - margin + rows
    turn(wide, outs, (count, planes, rows), base, share + 2 * margin)


def matrix_kernel(extent, *refs):
    packs, outs = refs[:extent], refs[extent:]
    me = lax.axis_index("chan")
    quarter = packs[0].shape[2] // 4
    taps = []
    turned = []
    for h in range(packs[0].shape[0]):
        tiles = [pack[h].astype(F32) for pack in packs]
        own = jnp.concatenate(tiles, axis=0)
        fixed = []
        for g in range(extent):
            place = lax.rem(me + extent - g, extent)
            tile = tiles[0]
            for j in range(1, extent):
                tile = jnp.where(place == j, tiles[j], tile)
            fixed.append(tile)
        both = jnp.concatenate(
            [own[:, : 2 * quarter], jnp.concatenate(fixed, axis=0)[:, 2 * quarter :]], axis=1
        )
        across = both.T
        for side in range(2):
            taps.append(
                [both[:, k * quarter : (k + 1) * quarter] for k in (side, side + 2)]
            )
            turned.append(
                [across[k * quarter : (k + 1) * quarter] for k in (side, side + 2)]
            )
    channels = quarter
    blank = jnp.zeros((channels, channels), F32)
    for k in range(2):
        for out, blocks, flip in ((outs[k], turned, False), (outs[2 + k], taps, True)):
            for e in range(3):
                for x in range(2):
                    chunks = []
                    for pair in range(2):
                        for b in range(3):
                            for side in range(2):
                                a = 2 * pair + side - x
                                t = 9 * a + 3 * b + e
                                inside = 0 <= a <= 2
                                t = 26 - t if flip else t
                                chunks.append(blocks[t][k] if inside else blank)
                    low = (2 * e + x) * channels
                    out[low : low + channels, :] = jnp.concatenate(chunks, axis=1).astype(BF16)


def stacked(refs, row, count):
    if len(refs) == 1:
        part = refs[0][pl.ds(row, count)]
        return part.reshape(-1, part.shape[-1])
    parts = [ref[row + b, x] for b in range(count) for x in range(2) for ref in refs]
    return jnp.concatenate(parts, axis=0)


def taps(weight, inputs, row):
    sides = []
    for above, below in inputs:
        for q in range(2):
            sides.append(
                jnp.concatenate([stacked(above, row + q, 3), stacked(below, row + q, 3)], axis=0)
            )
    lifted = jnp.dot(weight, jnp.concatenate(sides, axis=1), preferred_element_type=F32)
    third = lifted.shape[0] // 3
    depth = sides[0].shape[1]
    sums = []
    for k in range(len(sides)):
        side = lifted[:, k * depth : (k + 1) * depth]
        sums.append(
            side[third : 2 * third]
            + pltpu.roll(side[:third], 1, 1)
            + pltpu.roll(side[2 * third :], depth - 1, 1)
        )
    return [sums[2 * p : 2 * p + 2] for p in range(len(inputs))]


def neighbours(pairs):
    return list(zip(pairs[:-1], pairs[1:]))


def silu_parts(v):
    sig = jax.nn.sigmoid(v)
    return sig, sig * (1.0 + v * (1.0 - sig))


def forward_kernel(groups, fresh, ready, *refs):
    refs = list(refs)
    fields = [[refs.pop(0) for _ in range(groups)] for _ in range(fresh + 1)]
    hiddens = [refs.pop(0) for _ in range(ready)]
    count = fresh + ready - 1
    grads = [refs.pop(0) for _ in range(count)]
    first, second = refs.pop(0), refs.pop(0)
    made = [refs.pop(0) for _ in range(fresh)]
    slopes = [refs.pop(0) for _ in range(fresh)]
    deltas = refs
    hiddens = hiddens + made

    def one(r):
        row = 2 * r
        for p, sums in enumerate(taps(first[...], neighbours(fields), row)):
            for q, v in enumerate(sums):
                sig, slope = silu_parts(v)
                shape = made[p].shape[1:]
                made[p][row + q] = (v * sig).astype(BF16).reshape(shape)
                slopes[p][row + q] = slope.astype(BF16).reshape(shape)

    in_blocks(made[0].shape[0] // 2, one)

    def two(r):
        row = 2 * r
        for p, sums in enumerate(taps(second[...], neighbours([[ref] for ref in hiddens]), row)):
            for q, v in enumerate(sums):
                shape = deltas[p].shape[1:]
                out_grad = grads[p][row + q].astype(F32)
                slope = silu_parts(v)[1].reshape(shape)
                deltas[p][row + q] = (out_grad * slope).astype(BF16)

    if count > 0:
        in_blocks(deltas[0].shape[0] // 2, two)


def planes_of(pairs):
    return [(refs, x) for refs in pairs for x in range(2)]


def weight_loop(total, pieces, first_row, deltas, delta_row, count):
    blocks = [k for k in range(1, 13) if count // 2 % k == 0 and k * len(deltas) <= 12]
    together = max(blocks, default=1)

    def product(r):
        left, right = [], []
        for k in range(together):
            row = 2 * (r * together + k)
            for x, ((delta,), place) in enumerate(deltas):
                rows = []
                for q in range(2):
                    wide = delta[delta_row + row + q, place]
                    depth = wide.shape[1]
                    rows += [pltpu.roll(wide, depth - 1, 1), wide, pltpu.roll(wide, 1, 1)]
                    rows.append(jnp.zeros_like(wide))
                right.append(jnp.concatenate(rows, axis=0))
                rows = []
                for refs, side in pieces[x : x + 3]:
                    for b in range(4):
                        for ref in refs:
                            rows.append(ref[first_row + row + b, side])
                left.append(jnp.concatenate(rows, axis=0))
        return lax.dot_general(
            jnp.concatenate(left, axis=1),
            jnp.concatenate(right, axis=1),
            (((1,), (1,)), ((), ())),
            preferred_element_type=F32,
        )

    value = total[...]
    for r in range(count // 2 // together):
        value = value + product(r)
    total[...] = value


def weight_fold(total, size):
    lanes = total.shape[1] // 2
    channels = total.shape[0] // 12
    upper, lower = total[:, :lanes], total[:, lanes:]
    groups = []
    for g in range(channels // size):
        taps_of = []
        for a in range(3):
            for b in range(3):
                start = (4 * a + b) * channels + g * size
                part = (
                    upper[start : start + size]
                    + lower[start + channels : start + channels + size]
                )
                taps_of += [part[:, e * channels : (e + 1) * channels] for e in range(3)]
        blank = jnp.zeros((size, channels), F32)
        taps_of.append(blank)
        groups.append([jnp.concatenate(taps_of[4 * h : 4 * h + 4], axis=1) for h in range(7)])
    return groups


def first_deltas(weight, inputs, slopes, firsts):
    def one(r):
        row = 2 * r
        for p, sums in enumerate(taps(weight[...], inputs, row)):
            for q, v in enumerate(sums):
                shape = firsts[p].shape[1:]
                slope = slopes[p][row + 2 + q].astype(F32)
                firsts[p][row + q] = (v.reshape(shape) * slope).astype(BF16)

    in_blocks(firsts[0].shape[0] // 2, one)


def gradient_kernel(share, groups, extent, pairs, *refs):
    refs = list(refs)
    hiddens = [[refs.pop(0)] for _ in range(pairs + 1)]
    deltas = [[refs.pop(0)] for _ in range(pairs)]
    weight = refs.pop(0)
    slopes = [refs.pop(0) for _ in range(pairs + 1)]
    fields = [[refs.pop(0) for _ in range(groups)] for _ in range(pairs + 2)]
    keep, send = refs.pop(0), refs.pop(0)
    inner = [refs.pop(0) for _ in range(pairs - 1)]
    head, tail, none, second_total, first_total = refs
    none[...] = jnp.zeros_like(none)
    second_total[...] = jnp.zeros_like(second_total)
    first_total[...] = jnp.zeros_like(first_total)
    weight_loop(second_total, planes_of(hiddens), 2, planes_of(deltas), 2, share)
    firsts = [head] + inner + [tail]
    first_deltas(weight, neighbours([[none]] + deltas + [[none]]), slopes, firsts)
    parts = planes_of([[first] for first in firsts])
    weight_loop(first_total, planes_of(fields), 3, parts, 1, share)
    halves, size = keep.shape[1:3]
    me = lax.axis_index("chan")
    of_first = weight_fold(first_total, size)
    of_second = weight_fold(second_total, size)

    def place(ours, theirs):
        for g in range(extent):
            there = lax.rem(me + extent - g, extent)
            for h in range(halves):
                ours[g, h] = of_first[g][h]
                theirs[there, h] = of_second[g][h]

    odd = lax.rem(lax.axis_index("slab"), 2)

    @pl.when(odd == 0)
    def _():
        place(keep, send)

    @pl.when(odd == 1)
    def _():
        place(send, keep)


def field_kernel_back(inner, groups, after, *refs):
    del after
    refs = list(refs)
    back, weight = refs.pop(0), refs.pop(0)
    before, first, last, behind = [[refs.pop(0)] for _ in range(4)]
    slopes = [refs.pop(0) for _ in range(2)]
    middle = [refs.pop(0) for _ in range(inner)]
    outs, ends = refs[:groups], refs[groups:]
    first_deltas(back, [(before, first), (last, behind)], slopes, ends)
    firsts = [ends[0]] + middle + [ends[1]]

    def one(r):
        row = 2 * r
        size = outs[0].shape[2]
        channels = len(outs) * size
        for p, sums in enumerate(taps(weight[...], neighbours([[ref] for ref in firsts]), row)):
            for q, v in enumerate(sums):
                for x in range(2):
                    for j, out in enumerate(outs):
                        low = x * channels + j * size
                        out[row + q, 2 * p + x] = v[low : low + size].astype(BF16)

    in_blocks(outs[0].shape[0] // 2, one)


def split_kernel(after, one, two, *outs):
    del after
    for g, out in enumerate(outs):
        out[...] = one[g] + two[g]


def add_kernel(ahead, *refs):
    values = [ref[...] for ref in refs[ahead:-1]]
    while len(values) > 1:
        values = [sum(values[k + 1 : k + 2], values[k]) for k in range(0, len(values), 2)]
    refs[-1][...] = values[0]


def relay_kernel(*refs):
    pass


def merge_kernel(extent, factor, *refs):
    mine, other, *pieces = refs[:-4]
    out, first, second, wide = refs[-4:]
    channels = first.shape[2]

    def place(ours, theirs):
        for result, sums in ((ours, mine), (theirs, other)):
            for t in range(27):
                low = t % 4 * channels
                result[t] = sums[t // 4, :, low : low + channels] * factor

    odd = lax.rem(lax.axis_index("slab"), 2)

    @pl.when(odd == 0)
    def _():
        place(first, second)

    @pl.when(odd == 1)
    def _():
        place(second, first)

    size, planes, rows = out.shape[:3]
    share = rows // extent
    me = lax.axis_index("chan")
    for j in range(extent):
        base = lax.rem(me + extent - j, extent) * share

        def widen(f, mine=pieces[j::extent], base=base):
            x = 0
            for piece in mine:
                for k in range(piece.shape[1]):
                    start = ((base + f) * planes + x) * size
                    start = pl.multiple_of(start, 8) if size % 8 == 0 else start
                    wide[pl.ds(start, size), :] = piece[f, k].astype(F32)
                    x += 1

        in_blocks(share, widen)

    def back(i):
        for x in range(planes):
            tile = wide[pl.ds(x * size + i, rows, stride=planes * size), :]
            out[i, x] = tile.astype(BF16)

    in_blocks(size, back)


def body(field, out_grad, first_weight, second_weight):
    extent = lax.axis_size("chan")
    slabs = lax.axis_size("slab")
    me = lax.axis_index("chan")
    size, planes, rows, depth = field.shape
    channels = size * extent
    pairs = planes // 2
    share = rows // extent
    factor = 1.0 / math.sqrt(planes * slabs * rows * depth)

    def to_chan(value, shift):
        return lax.ppermute(value, "chan", [(i, (i + shift) % extent) for i in range(extent)])

    def to_next(value):
        return lax.ppermute(value, "slab", [(i, (i + 1) % slabs) for i in range(slabs)])

    def to_prev(value):
        return lax.ppermute(value, "slab", [((i + 1) % slabs, i) for i in range(slabs)])

    def relayed(value, *others):
        shape = jax.ShapeDtypeStruct(value.shape, value.dtype)
        early = [value, *others]
        return call(relay_kernel, [shape], early, loose=len(early), same={0: 0})[0]

    piece = jax.ShapeDtypeStruct((share + 8, 2, size, depth), BF16)
    by_tap = (27, size, channels)
    made = call(
        functools.partial(field_kernel, extent, 4),
        [piece] * (extent * pairs),
        [field],
        [pltpu.VMEM((size * planes * rows, depth), F32)],
        moved=field.size * 6,
    )
    parts = [list(made[:pairs])]
    for j in range(1, extent):
        parts.append([to_chan(value, j) for value in made[j * pairs : (j + 1) * pairs]])
    (pack,) = call(
        pack_kernel,
        [jax.ShapeDtypeStruct((14, size, 4 * channels), BF16)],
        [made[0], jnp.transpose(first_weight, (1, 0, 2)), jnp.transpose(second_weight, (1, 0, 2))],
        loose=1,
    )
    packs = [pack] + [to_chan(pack, j) for j in range(1, extent)]
    whole = size % 16 == 0
    own_before, own_after = [], []
    if whole:
        own_before, own_after = [to_next(parts[0][-1])], [to_prev(parts[0][0])]
    grad_piece = jax.ShapeDtypeStruct((share + 4, 2, channels, depth), BF16)
    grads = call(
        functools.partial(grad_kernel, extent, 2),
        [grad_piece] * pairs,
        [pack, out_grad],
        [pltpu.VMEM((channels * planes * rows, depth), F32)],
        moved=out_grad.size * 4,
        loose=1,
    )
    matrix = jax.ShapeDtypeStruct((6 * channels, 12 * channels), BF16)
    first_wide, second_wide, first_back, second_back = call(
        functools.partial(matrix_kernel, extent),
        [matrix] * 4,
        packs,
        moved=matrix.size * 8,
    )
    if whole and extent > 1 and pairs > 1:
        parts[1][-1] = relayed(parts[1][-1], pack)
        parts[1][0] = relayed(relayed(parts[1][0], grads[0], *packs[1:]), own_after[0])
    by_pair = [[parts[j][p] for j in range(extent)] for p in range(pairs)]
    groups = extent
    if not whole:
        by_pair = [[jnp.concatenate(pieces, axis=2)] for pieces in by_pair]
        groups = 1
    before = own_before + [to_next(piece) for piece in by_pair[-1][len(own_before) :]]
    after = own_after + [to_prev(piece) for piece in by_pair[0][len(own_after) :]]
    fields = [before] + by_pair + [after]

    def many(count, rows_each):
        return [jax.ShapeDtypeStruct((rows_each, 2, channels, depth), BF16)] * count

    def flat(lists):
        return [piece for pieces in lists for piece in pieces]

    work = 27 * 2 * channels * channels * depth * 2
    space = 4 * channels * depth * share

    made = call(
        functools.partial(forward_kernel, groups, pairs, 0),
        many(2 * pairs, share + 6) + many(pairs - 1, share + 4),
        flat(fields[: pairs + 1]) + list(grads[: pairs - 1]) + [first_wide, second_wide],
        flops=work * (2 * pairs - 1) * share,
        moved=space * 4 * pairs,
    )
    hiddens, slopes, deltas = made[:pairs], made[pairs : 2 * pairs], made[2 * pairs :]
    made = call(
        functools.partial(forward_kernel, groups, 1, 1),
        many(2, share + 6) + many(1, share + 4),
        flat(fields[pairs:]) + [hiddens[-1], grads[-1], first_wide, second_wide],
        flops=work * 2 * share,
        moved=space * 6,
    )
    hiddens = list(hiddens) + [made[0]]
    slopes = list(slopes) + [made[1]]
    deltas = list(deltas) + [made[2]]
    delta_after = to_prev(deltas[0])
    delta_before = to_next(deltas[-1])

    raw = jax.ShapeDtypeStruct((extent, 7, size, 4 * channels), F32)
    portion = jax.ShapeDtypeStruct(raw.shape[1:], F32)
    total = pltpu.VMEM((12 * channels, 8 * channels), F32)

    def room(rows_each):
        return pltpu.VMEM((rows_each, 2, channels, depth), BF16)

    made = call(
        functools.partial(gradient_kernel, share, groups, extent, pairs),
        [raw] * 2 + many(pairs - 1, share + 2),
        hiddens + deltas + [second_back] + slopes + flat(fields),
        [room(share + 2), room(share + 2), room(share + 4), total, total],
    )
    keep, send, inner = made[0], made[1], list(made[2:])
    def exchanged(made):
        pieces = [made[0]] + [None] * (extent - 1)
        for j in range(1, extent):
            pieces[extent - j] = to_chan(made[j], extent - j)
        return pieces

    def stepped(value, stride, shift=0):
        if shift % extent == 0:
            return lax.ppermute(value, "slab", [(i, i ^ stride) for i in range(slabs)])
        pairs_of = []
        for i in range(slabs):
            for k in range(extent):
                there = (i ^ stride) * extent + (k + shift) % extent
                pairs_of.append((i * extent + k, there))
        return lax.ppermute(value, ("slab", "chan"), pairs_of)

    plain = slabs & (slabs - 1) == 0 and slabs >= 4
    if plain:
        kept = call(
            split_kernel, [portion] * extent, [delta_after, keep, stepped(send, 1)], loose=1
        )
        shares = [kept[0]] + [to_chan(kept[j], extent - j) for j in range(1, extent)]
        shares += [stepped(kept[j], 2, extent - j) for j in range(extent)]
        after = kept[0]
    else:
        after = keep
    made = call(
        functools.partial(field_kernel_back, pairs - 1, extent),
        [jax.ShapeDtypeStruct((share, planes, size, depth), BF16)] * extent,
        [after, second_back, first_back]
        + [delta_before, deltas[0], deltas[-1], delta_after, slopes[0], slopes[-1]]
        + inner,
        [room(share + 2), room(share + 2)],
        flops=work * (pairs + 2) * share,
        moved=space * 6,
        loose=1,
    )
    if plain:
        ahead = list(made[:1])
        (mine,) = call(
            functools.partial(add_kernel, len(ahead)), [portion], ahead + shares, loose=len(ahead)
        )
        made = list(made[:1]) + [relayed(value, mine) for value in made[1:]]
    pieces = exchanged(made)
    if plain:
        stride = 4
        while stride < slabs:
            radix = 4 if slabs % (4 * stride) == 0 else 2
            got = [mine] + [stepped(mine, m * stride) for m in range(1, radix)]
            (mine,) = call(functools.partial(add_kernel, 0), [portion], got)
            stride *= radix
        other = stepped(mine, 1)
    else:
        mine, other = keep[0], send[0]
        for j in range(1, extent):
            mine, other = mine + to_chan(keep[j], extent - j), other + to_chan(send[j], extent - j)
        even = lax.rem(lax.axis_index("slab"), 2) == 0
        mine, other = jnp.where(even, mine, other), jnp.where(even, other, mine)
        mine, other = lax.psum((mine, other), "slab")
        mine, other = jnp.where(even, mine, other), jnp.where(even, other, mine)
    input_grad, first_grad, second_grad = call(
        functools.partial(merge_kernel, extent, factor),
        [jax.ShapeDtypeStruct(field.shape, BF16)] + [jax.ShapeDtypeStruct(by_tap, F32)] * 2,
        [mine, other] + pieces,
        [pltpu.VMEM((rows * planes * size, depth), F32)],
        moved=4 * field.size,
    )
    first_grad, second_grad = (jnp.transpose(g, (1, 0, 2)) for g in (first_grad, second_grad))
    return input_grad, first_grad, second_grad


def solution(mesh):
    placed = (
        P("chan", "slab", None, None),
        P(None, "slab", None, None),
        P("chan", None, None),
        P("chan", None, None),
    )
    return jax.shard_map(
        body,
        mesh=mesh,
        in_specs=placed,
        out_specs=(P("chan", "slab", None, None), P("chan", None, None), P("chan", None, None)),
        check_vma=False,
    )
```

```python
import functools
import math

import jax
import jax.numpy as jnp
from jax import lax
from jax.experimental import pallas as pl
from jax.experimental.pallas import tpu as pltpu
from jax.sharding import PartitionSpec as P

F32 = jnp.float32
BF16 = jnp.bfloat16
LIMIT = 16 * 1024 * 1024


def call(kernel, outs, args, scratch=(), flops=0, moved=0, loose=0, same=None):
    whole = pl.BlockSpec(memory_space=pltpu.VMEM)
    still = pl.BlockSpec(memory_space=pl.ANY)
    return pl.pallas_call(
        kernel,
        out_shape=outs,
        in_specs=[still] * loose + [whole] * (len(args) - loose),
        out_specs=[still if k in (same or {}).values() else whole for k in range(len(outs))],
        input_output_aliases=same or {},
        scratch_shapes=list(scratch),
        compiler_params=pltpu.CompilerParams(vmem_limit_bytes=LIMIT),
        cost_estimate=pl.CostEstimate(flops=flops, bytes_accessed=moved, transcendentals=0),
    )(*args)


def in_blocks(count, body):
    block = max(k for k in range(1, 17) if count % k == 0)

    def several(r, _):
        for k in range(block):
            body(r * block + k)
        return 0

    lax.fori_loop(0, count // block, several, 0)
    for k in range(count // block * block, count):
        body(k)


def widened(x_ref, wide):
    count, planes, rows = x_ref.shape[:3]

    def widen(i):
        for x in range(planes):
            start = pl.multiple_of((i * planes + x) * rows, 8)
            wide[pl.ds(start, rows), :] = x_ref[i, x].astype(F32)

    in_blocks(count, widen)


def turn(wide, outs, shape, base, length):
    count, planes, rows = shape

    def one(f):
        y = lax.rem(base + f, rows)
        for x in range(planes):
            tile = wide[pl.ds(x * rows + y, count, stride=planes * rows), :]
            outs[x // 2][f, x % 2] = tile.astype(BF16)

    in_blocks(length, one)


def field_kernel(extent, margin, x_ref, *refs):
    outs, wide = refs[:-1], refs[-1]
    count, planes, rows = x_ref.shape[:3]
    pairs = planes // 2
    share = rows // extent
    widened(x_ref, wide)
    me = lax.axis_index("chan")
    for s in range(extent):
        base = lax.rem(me + s, extent) * share - margin + rows
        turn(
            wide,
            outs[s * pairs : (s + 1) * pairs],
            (count, planes, rows),
            base,
            share + 2 * margin,
        )


def pack_kernel(after, first, second, packed):
    del after
    blank = jnp.zeros(first.shape[1:], F32)
    for h in range(packed.shape[0]):
        parts = []
        for ref in (first, second):
            for t in (2 * h, 2 * h + 1):
                parts.append(ref[t].astype(F32) if t < ref.shape[0] else blank)
        packed[h] = jnp.concatenate(parts, axis=1).astype(BF16)


def grad_kernel(extent, margin, after, x_ref, *refs):
    del after
    outs, wide = refs[:-1], refs[-1]
    count, planes, rows = x_ref.shape[:3]
    share = rows // extent
    widened(x_ref, wide)
    base = lax.axis_index("chan") * share - margin + rows
    turn(wide, outs, (count, planes, rows), base, share + 2 * margin)


def matrix_kernel(extent, *refs):
    packs, outs = refs[:extent], refs[extent:]
    me = lax.axis_index("chan")
    quarter = packs[0].shape[2] // 4
    taps = []
    turned = []
    for h in range(packs[0].shape[0]):
        tiles = [pack[h].astype(F32) for pack in packs]
        own = jnp.concatenate(tiles, axis=0)
        fixed = []
        for g in range(extent):
            place = lax.rem(me + extent - g, extent)
            tile = tiles[0]
            for j in range(1, extent):
                tile = jnp.where(place == j, tiles[j], tile)
            fixed.append(tile)
        both = jnp.concatenate(
            [own[:, : 2 * quarter], jnp.concatenate(fixed, axis=0)[:, 2 * quarter :]], axis=1
        )
        across = both.T
        for side in range(2):
            taps.append(
                [both[:, k * quarter : (k + 1) * quarter] for k in (side, side + 2)]
            )
            turned.append(
                [across[k * quarter : (k + 1) * quarter] for k in (side, side + 2)]
            )
    channels = quarter
    blank = jnp.zeros((channels, channels), F32)
    for k in range(2):
        for out, blocks, flip in ((outs[k], turned, False), (outs[2 + k], taps, True)):
            for e in range(3):
                for x in range(2):
                    chunks = []
                    for pair in range(2):
                        for b in range(3):
                            for side in range(2):
                                a = 2 * pair + side - x
                                t = 9 * a + 3 * b + e
                                inside = 0 <= a <= 2
                                t = 26 - t if flip else t
                                chunks.append(blocks[t][k] if inside else blank)
                    low = (2 * e + x) * channels
                    out[low : low + channels, :] = jnp.concatenate(chunks, axis=1).astype(BF16)


def stacked(refs, row, count):
    if len(refs) == 1:
        part = refs[0][pl.ds(row, count)]
        return part.reshape(-1, part.shape[-1])
    parts = [ref[row + b, x] for b in range(count) for x in range(2) for ref in refs]
    return jnp.concatenate(parts, axis=0)


def taps(weight, inputs, row):
    sides = []
    for above, below in inputs:
        for q in range(2):
            sides.append(
                jnp.concatenate([stacked(above, row + q, 3), stacked(below, row + q, 3)], axis=0)
            )
    lifted = jnp.dot(weight, jnp.concatenate(sides, axis=1), preferred_element_type=F32)
    third = lifted.shape[0] // 3
    depth = sides[0].shape[1]
    sums = []
    for k in range(len(sides)):
        side = lifted[:, k * depth : (k + 1) * depth]
        sums.append(
            side[third : 2 * third]
            + pltpu.roll(side[:third], 1, 1)
            + pltpu.roll(side[2 * third :], depth - 1, 1)
        )
    return [sums[2 * p : 2 * p + 2] for p in range(len(inputs))]


def neighbours(pairs):
    return list(zip(pairs[:-1], pairs[1:]))


def silu_parts(v):
    sig = jax.nn.sigmoid(v)
    return sig, sig * (1.0 + v * (1.0 - sig))


def forward_kernel(groups, fresh, ready, *refs):
    refs = list(refs)
    fields = [[refs.pop(0) for _ in range(groups)] for _ in range(fresh + 1)]
    hiddens = [refs.pop(0) for _ in range(ready)]
    count = fresh + ready - 1
    grads = [refs.pop(0) for _ in range(count)]
    first, second = refs.pop(0), refs.pop(0)
    made = [refs.pop(0) for _ in range(fresh)]
    slopes = [refs.pop(0) for _ in range(fresh)]
    deltas = refs
    hiddens = hiddens + made

    def one(r):
        row = 2 * r
        for p, sums in enumerate(taps(first[...], neighbours(fields), row)):
            for q, v in enumerate(sums):
                sig, slope = silu_parts(v)
                shape = made[p].shape[1:]
                made[p][row + q] = (v * sig).astype(BF16).reshape(shape)
                slopes[p][row + q] = slope.astype(BF16).reshape(shape)

    in_blocks(made[0].shape[0] // 2, one)

    def two(r):
        row = 2 * r
        for p, sums in enumerate(taps(second[...], neighbours([[ref] for ref in hiddens]), row)):
            for q, v in enumerate(sums):
                shape = deltas[p].shape[1:]
                out_grad = grads[p][row + q].astype(F32)
                slope = silu_parts(v)[1].reshape(shape)
                deltas[p][row + q] = (out_grad * slope).astype(BF16)

    if count > 0:
        in_blocks(deltas[0].shape[0] // 2, two)


def planes_of(pairs):
    return [(refs, x) for refs in pairs for x in range(2)]


def weight_loop(total, pieces, first_row, deltas, delta_row, count):
    blocks = [k for k in range(1, 13) if count // 2 % k == 0 and k * len(deltas) <= 12]
    together = max(blocks, default=1)

    def product(r):
        left, right = [], []
        for k in range(together):
            row = 2 * (r * together + k)
            for x, ((delta,), place) in enumerate(deltas):
                rows = []
                for q in range(2):
                    wide = delta[delta_row + row + q, place]
                    depth = wide.shape[1]
                    rows += [pltpu.roll(wide, depth - 1, 1), wide, pltpu.roll(wide, 1, 1)]
                    rows.append(jnp.zeros_like(wide))
                right.append(jnp.concatenate(rows, axis=0))
                rows = []
                for refs, side in pieces[x : x + 3]:
                    for b in range(4):
                        for ref in refs:
                            rows.append(ref[first_row + row + b, side])
                left.append(jnp.concatenate(rows, axis=0))
        return lax.dot_general(
            jnp.concatenate(left, axis=1),
            jnp.concatenate(right, axis=1),
            (((1,), (1,)), ((), ())),
            preferred_element_type=F32,
        )

    value = total[...]
    for r in range(count // 2 // together):
        value = value + product(r)
    total[...] = value


def weight_fold(total, size):
    lanes = total.shape[1] // 2
    channels = total.shape[0] // 12
    upper, lower = total[:, :lanes], total[:, lanes:]
    groups = []
    for g in range(channels // size):
        taps_of = []
        for a in range(3):
            for b in range(3):
                start = (4 * a + b) * channels + g * size
                part = (
                    upper[start : start + size]
                    + lower[start + channels : start + channels + size]
                )
                taps_of += [part[:, e * channels : (e + 1) * channels] for e in range(3)]
        blank = jnp.zeros((size, channels), F32)
        taps_of.append(blank)
        groups.append([jnp.concatenate(taps_of[4 * h : 4 * h + 4], axis=1) for h in range(7)])
    return groups


def first_deltas(weight, inputs, slopes, firsts):
    def one(r):
        row = 2 * r
        for p, sums in enumerate(taps(weight[...], inputs, row)):
            for q, v in enumerate(sums):
                shape = firsts[p].shape[1:]
                slope = slopes[p][row + 2 + q].astype(F32)
                firsts[p][row + q] = (v.reshape(shape) * slope).astype(BF16)

    in_blocks(firsts[0].shape[0] // 2, one)


def gradient_kernel(share, groups, extent, pairs, *refs):
    refs = list(refs)
    hiddens = [[refs.pop(0)] for _ in range(pairs + 1)]
    deltas = [[refs.pop(0)] for _ in range(pairs)]
    weight = refs.pop(0)
    slopes = [refs.pop(0) for _ in range(pairs + 1)]
    fields = [[refs.pop(0) for _ in range(groups)] for _ in range(pairs + 2)]
    keep, send = refs.pop(0), refs.pop(0)
    inner = [refs.pop(0) for _ in range(pairs - 1)]
    head, tail, none, second_total, first_total = refs
    none[...] = jnp.zeros_like(none)
    second_total[...] = jnp.zeros_like(second_total)
    first_total[...] = jnp.zeros_like(first_total)
    weight_loop(second_total, planes_of(hiddens), 2, planes_of(deltas), 2, share)
    firsts = [head] + inner + [tail]
    first_deltas(weight, neighbours([[none]] + deltas + [[none]]), slopes, firsts)
    parts = planes_of([[first] for first in firsts])
    weight_loop(first_total, planes_of(fields), 3, parts, 1, share)
    halves, size = keep.shape[1:3]
    me = lax.axis_index("chan")
    of_first = weight_fold(first_total, size)
    of_second = weight_fold(second_total, size)

    def place(ours, theirs):
        for g in range(extent):
            there = lax.rem(me + extent - g, extent)
            for h in range(halves):
                ours[g, h] = of_first[g][h]
                theirs[there, h] = of_second[g][h]

    odd = lax.rem(lax.axis_index("slab"), 2)

    @pl.when(odd == 0)
    def _():
        place(keep, send)

    @pl.when(odd == 1)
    def _():
        place(send, keep)


def field_kernel_back(inner, groups, after, *refs):
    del after
    refs = list(refs)
    back, weight = refs.pop(0), refs.pop(0)
    before, first, last, behind = [[refs.pop(0)] for _ in range(4)]
    slopes = [refs.pop(0) for _ in range(2)]
    middle = [refs.pop(0) for _ in range(inner)]
    outs, ends = refs[:groups], refs[groups:]
    first_deltas(back, [(before, first), (last, behind)], slopes, ends)
    firsts = [ends[0]] + middle + [ends[1]]

    def one(r):
        row = 2 * r
        size = outs[0].shape[2]
        channels = len(outs) * size
        for p, sums in enumerate(taps(weight[...], neighbours([[ref] for ref in firsts]), row)):
            for q, v in enumerate(sums):
                for x in range(2):
                    for j, out in enumerate(outs):
                        low = x * channels + j * size
                        out[row + q, 2 * p + x] = v[low : low + size].astype(BF16)

    in_blocks(outs[0].shape[0] // 2, one)


def split_kernel(after, one, two, *outs):
    del after
    for g, out in enumerate(outs):
        out[...] = one[g] + two[g]


def add_kernel(ahead, *refs):
    values = [ref[...] for ref in refs[ahead:-1]]
    while len(values) > 1:
        values = [sum(values[k + 1 : k + 2], values[k]) for k in range(0, len(values), 2)]
    refs[-1][...] = values[0]


def relay_kernel(*refs):
    pass


def finish_kernel(factor, after, mine, other, first, second):
    del after
    channels = first.shape[2]

    def place(ours, theirs):
        for result, sums in ((ours, mine), (theirs, other)):
            for t in range(27):
                low = t % 4 * channels
                result[t] = sums[t // 4, :, low : low + channels] * factor

    odd = lax.rem(lax.axis_index("slab"), 2)

    @pl.when(odd == 0)
    def _():
        place(first, second)

    @pl.when(odd == 1)
    def _():
        place(second, first)


def merge_kernel(extent, *refs):
    pieces, token, out, wide = refs[:-3], refs[-3], refs[-2], refs[-1]
    token[...] = jnp.zeros_like(token)
    size, planes, rows = out.shape[:3]
    share = rows // extent
    me = lax.axis_index("chan")
    for j in range(extent):
        base = lax.rem(me + extent - j, extent) * share

        def widen(f, mine=pieces[j::extent], base=base):
            x = 0
            for piece in mine:
                for k in range(piece.shape[1]):
                    start = ((base + f) * planes + x) * size
                    start = pl.multiple_of(start, 8) if size % 8 == 0 else start
                    wide[pl.ds(start, size), :] = piece[f, k].astype(F32)
                    x += 1

        in_blocks(share, widen)

    def back(i):
        for x in range(planes):
            tile = wide[pl.ds(x * size + i, rows, stride=planes * size), :]
            out[i, x] = tile.astype(BF16)

    in_blocks(size, back)


def body(field, out_grad, first_weight, second_weight):
    extent = lax.axis_size("chan")
    slabs = lax.axis_size("slab")
    me = lax.axis_index("chan")
    size, planes, rows, depth = field.shape
    channels = size * extent
    pairs = planes // 2
    share = rows // extent
    factor = 1.0 / math.sqrt(planes * slabs * rows * depth)

    def to_chan(value, shift):
        return lax.ppermute(value, "chan", [(i, (i + shift) % extent) for i in range(extent)])

    def to_next(value):
        return lax.ppermute(value, "slab", [(i, (i + 1) % slabs) for i in range(slabs)])

    def to_prev(value):
        return lax.ppermute(value, "slab", [((i + 1) % slabs, i) for i in range(slabs)])

    def relayed(value, *others):
        shape = jax.ShapeDtypeStruct(value.shape, value.dtype)
        early = [value, *others]
        return call(relay_kernel, [shape], early, loose=len(early), same={0: 0})[0]

    piece = jax.ShapeDtypeStruct((share + 8, 2, size, depth), BF16)
    by_tap = (27, size, channels)
    made = call(
        functools.partial(field_kernel, extent, 4),
        [piece] * (extent * pairs),
        [field],
        [pltpu.VMEM((size * planes * rows, depth), F32)],
        moved=field.size * 6,
    )
    parts = [list(made[:pairs])]
    for j in range(1, extent):
        parts.append([to_chan(value, j) for value in made[j * pairs : (j + 1) * pairs]])
    (pack,) = call(
        pack_kernel,
        [jax.ShapeDtypeStruct((14, size, 4 * channels), BF16)],
        [made[0], jnp.transpose(first_weight, (1, 0, 2)), jnp.transpose(second_weight, (1, 0, 2))],
        loose=1,
    )
    packs = [pack] + [to_chan(pack, j) for j in range(1, extent)]
    whole = size % 16 == 0
    own_before, own_after = [], []
    if whole:
        own_before, own_after = [to_next(parts[0][-1])], [to_prev(parts[0][0])]
    grad_piece = jax.ShapeDtypeStruct((share + 4, 2, channels, depth), BF16)
    grads = call(
        functools.partial(grad_kernel, extent, 2),
        [grad_piece] * pairs,
        [pack, out_grad],
        [pltpu.VMEM((channels * planes * rows, depth), F32)],
        moved=out_grad.size * 4,
        loose=1,
    )
    matrix = jax.ShapeDtypeStruct((6 * channels, 12 * channels), BF16)
    first_wide, second_wide, first_back, second_back = call(
        functools.partial(matrix_kernel, extent),
        [matrix] * 4,
        packs,
        moved=matrix.size * 8,
    )
    if whole and extent > 1 and pairs > 1:
        parts[1][-1] = relayed(parts[1][-1], pack)
        parts[1][0] = relayed(relayed(parts[1][0], grads[0], *packs[1:]), own_after[0])
    by_pair = [[parts[j][p] for j in range(extent)] for p in range(pairs)]
    groups = extent
    if not whole:
        by_pair = [[jnp.concatenate(pieces, axis=2)] for pieces in by_pair]
        groups = 1
    before = own_before + [to_next(piece) for piece in by_pair[-1][len(own_before) :]]
    after = own_after + [to_prev(piece) for piece in by_pair[0][len(own_after) :]]
    fields = [before] + by_pair + [after]

    def many(count, rows_each):
        return [jax.ShapeDtypeStruct((rows_each, 2, channels, depth), BF16)] * count

    def flat(lists):
        return [piece for pieces in lists for piece in pieces]

    work = 27 * 2 * channels * channels * depth * 2
    space = 4 * channels * depth * share

    made = call(
        functools.partial(forward_kernel, groups, pairs, 0),
        many(2 * pairs, share + 6) + many(pairs - 1, share + 4),
        flat(fields[: pairs + 1]) + list(grads[: pairs - 1]) + [first_wide, second_wide],
        flops=work * (2 * pairs - 1) * share,
        moved=space * 4 * pairs,
    )
    hiddens, slopes, deltas = made[:pairs], made[pairs : 2 * pairs], made[2 * pairs :]
    made = call(
        functools.partial(forward_kernel, groups, 1, 1),
        many(2, share + 6) + many(1, share + 4),
        flat(fields[pairs:]) + [hiddens[-1], grads[-1], first_wide, second_wide],
        flops=work * 2 * share,
        moved=space * 6,
    )
    hiddens = list(hiddens) + [made[0]]
    slopes = list(slopes) + [made[1]]
    deltas = list(deltas) + [made[2]]
    delta_after = to_prev(deltas[0])
    delta_before = to_next(deltas[-1])

    raw = jax.ShapeDtypeStruct((extent, 7, size, 4 * channels), F32)
    portion = jax.ShapeDtypeStruct(raw.shape[1:], F32)
    total = pltpu.VMEM((12 * channels, 8 * channels), F32)

    def room(rows_each):
        return pltpu.VMEM((rows_each, 2, channels, depth), BF16)

    made = call(
        functools.partial(gradient_kernel, share, groups, extent, pairs),
        [raw] * 2 + many(pairs - 1, share + 2),
        hiddens + deltas + [second_back] + slopes + flat(fields),
        [room(share + 2), room(share + 2), room(share + 4), total, total],
    )
    keep, send, inner = made[0], made[1], list(made[2:])
    def exchanged(made):
        pieces = [made[0]] + [None] * (extent - 1)
        for j in range(1, extent):
            pieces[extent - j] = to_chan(made[j], extent - j)
        return pieces

    def stepped(value, stride, shift=0):
        if shift % extent == 0:
            return lax.ppermute(value, "slab", [(i, i ^ stride) for i in range(slabs)])
        pairs_of = []
        for i in range(slabs):
            for k in range(extent):
                there = (i ^ stride) * extent + (k + shift) % extent
                pairs_of.append((i * extent + k, there))
        return lax.ppermute(value, ("slab", "chan"), pairs_of)

    plain = slabs & (slabs - 1) == 0 and slabs >= 4
    if plain:
        kept = call(
            split_kernel, [portion] * extent, [delta_after, keep, stepped(send, 1)], loose=1
        )
        shares = [kept[0]] + [to_chan(kept[j], extent - j) for j in range(1, extent)]
        shares += [stepped(kept[j], 2, extent - j) for j in range(extent)]
        after = kept[0]
    else:
        after = keep
    made = call(
        functools.partial(field_kernel_back, pairs - 1, extent),
        [jax.ShapeDtypeStruct((share, planes, size, depth), BF16)] * extent,
        [after, second_back, first_back]
        + [delta_before, deltas[0], deltas[-1], delta_after, slopes[0], slopes[-1]]
        + inner,
        [room(share + 2), room(share + 2)],
        flops=work * (pairs + 2) * share,
        moved=space * 6,
        loose=1,
    )
    if plain:
        ahead = list(made[:1])
        (mine,) = call(
            functools.partial(add_kernel, len(ahead)), [portion], ahead + shares, loose=len(ahead)
        )
        made = list(made[:1]) + [relayed(value, mine) for value in made[1:]]
    pieces = exchanged(made)
    if plain:
        stride = 4
        while stride < slabs:
            got = [mine, stepped(mine, stride)]
            (mine,) = call(functools.partial(add_kernel, 0), [portion], got)
            stride *= 2
        other = stepped(mine, 1)
    else:
        mine, other = keep[0], send[0]
        for j in range(1, extent):
            mine, other = mine + to_chan(keep[j], extent - j), other + to_chan(send[j], extent - j)
        even = lax.rem(lax.axis_index("slab"), 2) == 0
        mine, other = jnp.where(even, mine, other), jnp.where(even, other, mine)
        mine, other = lax.psum((mine, other), "slab")
        mine, other = jnp.where(even, mine, other), jnp.where(even, other, mine)
    token, input_grad = call(
        functools.partial(merge_kernel, extent),
        [jax.ShapeDtypeStruct((8, 128), F32), jax.ShapeDtypeStruct(field.shape, BF16)],
        pieces,
        [pltpu.VMEM((rows * planes * size, depth), F32)],
        moved=4 * field.size,
    )
    first_grad, second_grad = call(
        functools.partial(finish_kernel, factor),
        [jax.ShapeDtypeStruct(by_tap, F32)] * 2,
        [token, mine, other],
        loose=1,
    )
    first_grad, second_grad = (jnp.transpose(g, (1, 0, 2)) for g in (first_grad, second_grad))
    return input_grad, first_grad, second_grad


def solution(mesh):
    placed = (
        P("chan", "slab", None, None),
        P(None, "slab", None, None),
        P("chan", None, None),
        P("chan", None, None),
    )
    return jax.shard_map(
        body,
        mesh=mesh,
        in_specs=placed,
        out_specs=(P("chan", "slab", None, None), P("chan", None, None), P("chan", None, None)),
        check_vma=False,
    )
```

```python
import functools
import math

import jax
import jax.numpy as jnp
from jax import lax
from jax.experimental import pallas as pl
from jax.experimental.pallas import tpu as pltpu
from jax.sharding import PartitionSpec as P

F32 = jnp.float32
BF16 = jnp.bfloat16
LIMIT = 16 * 1024 * 1024


def call(kernel, outs, args, scratch=(), flops=0, moved=0, loose=0, same=None):
    whole = pl.BlockSpec(memory_space=pltpu.VMEM)
    still = pl.BlockSpec(memory_space=pl.ANY)
    return pl.pallas_call(
        kernel,
        out_shape=outs,
        in_specs=[still] * loose + [whole] * (len(args) - loose),
        out_specs=[still if k in (same or {}).values() else whole for k in range(len(outs))],
        input_output_aliases=same or {},
        scratch_shapes=list(scratch),
        compiler_params=pltpu.CompilerParams(vmem_limit_bytes=LIMIT),
        cost_estimate=pl.CostEstimate(flops=flops, bytes_accessed=moved, transcendentals=0),
    )(*args)


def in_blocks(count, body):
    block = max(k for k in range(1, 17) if count % k == 0)

    def several(r, _):
        for k in range(block):
            body(r * block + k)
        return 0

    lax.fori_loop(0, count // block, several, 0)
    for k in range(count // block * block, count):
        body(k)


def widened(x_ref, wide, low, high):
    count, _, rows = x_ref.shape[:3]

    def widen(i):
        for x in range(low, high):
            start = pl.multiple_of((i * (high - low) + x - low) * rows, 8)
            wide[pl.ds(start, rows), :] = x_ref[i, x].astype(F32)

    in_blocks(count, widen)


def turn(wide, outs, shape, base, length):
    count, planes, rows = shape

    def one(f):
        y = lax.rem(base + f, rows)
        for x in range(planes):
            tile = wide[pl.ds(x * rows + y, count, stride=planes * rows), :]
            outs[x // 2][f, x % 2] = tile.astype(BF16)

    in_blocks(length, one)


def field_kernel(extent, margin, low, high, after, x_ref, *refs):
    del after
    outs, wide = refs[:-1], refs[-1]
    count, _, rows = x_ref.shape[:3]
    planes = high - low
    pairs = planes // 2
    share = rows // extent
    widened(x_ref, wide, low, high)
    me = lax.axis_index("chan")
    for s in range(extent):
        base = lax.rem(me + s, extent) * share - margin + rows
        turn(
            wide,
            outs[s * pairs : (s + 1) * pairs],
            (count, planes, rows),
            base,
            share + 2 * margin,
        )


def pack_kernel(after, first, second, packed):
    del after
    blank = jnp.zeros(first.shape[1:], F32)
    for h in range(packed.shape[0]):
        parts = []
        for ref in (first, second):
            for t in (2 * h, 2 * h + 1):
                parts.append(ref[t].astype(F32) if t < ref.shape[0] else blank)
        packed[h] = jnp.concatenate(parts, axis=1).astype(BF16)


def grad_kernel(extent, margin, after, x_ref, *refs):
    del after
    outs, wide = refs[:-1], refs[-1]
    count, planes, rows = x_ref.shape[:3]
    share = rows // extent
    widened(x_ref, wide, 0, planes)
    base = lax.axis_index("chan") * share - margin + rows
    turn(wide, outs, (count, planes, rows), base, share + 2 * margin)


def matrix_kernel(extent, *refs):
    packs, outs = refs[:extent], refs[extent:]
    me = lax.axis_index("chan")
    quarter = packs[0].shape[2] // 4
    taps = []
    turned = []
    for h in range(packs[0].shape[0]):
        tiles = [pack[h].astype(F32) for pack in packs]
        own = jnp.concatenate(tiles, axis=0)
        fixed = []
        for g in range(extent):
            place = lax.rem(me + extent - g, extent)
            tile = tiles[0]
            for j in range(1, extent):
                tile = jnp.where(place == j, tiles[j], tile)
            fixed.append(tile)
        both = jnp.concatenate(
            [own[:, : 2 * quarter], jnp.concatenate(fixed, axis=0)[:, 2 * quarter :]], axis=1
        )
        across = both.T
        for side in range(2):
            taps.append(
                [both[:, k * quarter : (k + 1) * quarter] for k in (side, side + 2)]
            )
            turned.append(
                [across[k * quarter : (k + 1) * quarter] for k in (side, side + 2)]
            )
    channels = quarter
    blank = jnp.zeros((channels, channels), F32)
    for k in range(2):
        for out, blocks, flip in ((outs[k], turned, False), (outs[2 + k], taps, True)):
            for e in range(3):
                for x in range(2):
                    chunks = []
                    for pair in range(2):
                        for b in range(3):
                            for side in range(2):
                                a = 2 * pair + side - x
                                t = 9 * a + 3 * b + e
                                inside = 0 <= a <= 2
                                t = 26 - t if flip else t
                                chunks.append(blocks[t][k] if inside else blank)
                    low = (2 * e + x) * channels
                    line = jnp.concatenate(chunks, axis=1).astype(BF16)
                    out[low : low + channels, :] = line
                    if k == 1 and flip:
                        half = line.shape[1] // 2
                        outs[4][low : low + channels, :] = line[:, :half]
                        outs[5][low : low + channels, :] = line[:, half:]


def stacked(refs, row, count):
    if len(refs) == 1:
        part = refs[0][pl.ds(row, count)]
        return part.reshape(-1, part.shape[-1])
    parts = [ref[row + b, x] for b in range(count) for x in range(2) for ref in refs]
    return jnp.concatenate(parts, axis=0)


def taps(weight, inputs, row):
    sides = []
    for pair in inputs:
        for q in range(2):
            parts = [stacked(refs, row + q, 3) for refs in pair]
            sides.append(jnp.concatenate(parts, axis=0) if len(parts) > 1 else parts[0])
    lifted = jnp.dot(weight, jnp.concatenate(sides, axis=1), preferred_element_type=F32)
    third = lifted.shape[0] // 3
    depth = sides[0].shape[1]
    sums = []
    for k in range(len(sides)):
        side = lifted[:, k * depth : (k + 1) * depth]
        sums.append(
            side[third : 2 * third]
            + pltpu.roll(side[:third], 1, 1)
            + pltpu.roll(side[2 * third :], depth - 1, 1)
        )
    return [sums[2 * p : 2 * p + 2] for p in range(len(inputs))]


def neighbours(pairs):
    return list(zip(pairs[:-1], pairs[1:]))


def silu_parts(v):
    sig = jax.nn.sigmoid(v)
    return sig, sig * (1.0 + v * (1.0 - sig))


def forward_kernel(groups, fresh, ready, *refs):
    refs = list(refs)
    fields = [[refs.pop(0) for _ in range(groups)] for _ in range(fresh + 1)]
    hiddens = [refs.pop(0) for _ in range(ready)]
    count = fresh + ready - 1
    grads = [refs.pop(0) for _ in range(count)]
    first, second = refs.pop(0), refs.pop(0)
    made = [refs.pop(0) for _ in range(fresh)]
    slopes = [refs.pop(0) for _ in range(fresh)]
    deltas = refs
    hiddens = hiddens + made

    def one(r):
        row = 2 * r
        for p, sums in enumerate(taps(first[...], neighbours(fields), row)):
            for q, v in enumerate(sums):
                sig, slope = silu_parts(v)
                shape = made[p].shape[1:]
                made[p][row + q] = (v * sig).astype(BF16).reshape(shape)
                slopes[p][row + q] = slope.astype(BF16).reshape(shape)

    in_blocks(made[0].shape[0] // 2, one)

    def two(r):
        row = 2 * r
        for p, sums in enumerate(taps(second[...], neighbours([[ref] for ref in hiddens]), row)):
            for q, v in enumerate(sums):
                shape = deltas[p].shape[1:]
                out_grad = grads[p][row + q].astype(F32)
                slope = silu_parts(v)[1].reshape(shape)
                deltas[p][row + q] = (out_grad * slope).astype(BF16)

    if count > 0:
        in_blocks(deltas[0].shape[0] // 2, two)


def planes_of(pairs):
    return [(refs, x) for refs in pairs for x in range(2)]


def weight_loop(total, pieces, first_row, deltas, delta_row, count):
    blocks = [k for k in range(1, 13) if count // 2 % k == 0 and k * len(deltas) <= 12]
    together = max(blocks, default=1)

    def product(r):
        left, right = [], []
        for k in range(together):
            row = 2 * (r * together + k)
            for x, ((delta,), place) in enumerate(deltas):
                rows = []
                for q in range(2):
                    wide = delta[delta_row + row + q, place]
                    depth = wide.shape[1]
                    rows += [pltpu.roll(wide, depth - 1, 1), wide, pltpu.roll(wide, 1, 1)]
                    rows.append(jnp.zeros_like(wide))
                right.append(jnp.concatenate(rows, axis=0))
                rows = []
                for refs, side in pieces[x : x + 3]:
                    for b in range(4):
                        for ref in refs:
                            rows.append(ref[first_row + row + b, side])
                left.append(jnp.concatenate(rows, axis=0))
        return lax.dot_general(
            jnp.concatenate(left, axis=1),
            jnp.concatenate(right, axis=1),
            (((1,), (1,)), ((), ())),
            preferred_element_type=F32,
        )

    value = total[...]
    for r in range(count // 2 // together):
        value = value + product(r)
    total[...] = value


def weight_fold(total, size):
    lanes = total.shape[1] // 2
    channels = total.shape[0] // 12
    upper, lower = total[:, :lanes], total[:, lanes:]
    groups = []
    for g in range(channels // size):
        taps_of = []
        for a in range(3):
            for b in range(3):
                start = (4 * a + b) * channels + g * size
                part = (
                    upper[start : start + size]
                    + lower[start + channels : start + channels + size]
                )
                taps_of += [part[:, e * channels : (e + 1) * channels] for e in range(3)]
        blank = jnp.zeros((size, channels), F32)
        taps_of.append(blank)
        groups.append([jnp.concatenate(taps_of[4 * h : 4 * h + 4], axis=1) for h in range(7)])
    return groups


def first_deltas(weight, inputs, slopes, firsts):
    def one(r):
        row = 2 * r
        for p, sums in enumerate(taps(weight[...], inputs, row)):
            for q, v in enumerate(sums):
                shape = firsts[p].shape[1:]
                slope = slopes[p][row + 2 + q].astype(F32)
                firsts[p][row + q] = (v.reshape(shape) * slope).astype(BF16)

    in_blocks(firsts[0].shape[0] // 2, one)


def gradient_kernel(share, groups, extent, pairs, *refs):
    refs = list(refs)
    hiddens = [[refs.pop(0)] for _ in range(pairs + 1)]
    deltas = [[refs.pop(0)] for _ in range(pairs)]
    weight, from_above, from_below = [refs.pop(0) for _ in range(3)]
    slopes = [refs.pop(0) for _ in range(pairs + 1)]
    fields = [[refs.pop(0) for _ in range(groups)] for _ in range(pairs + 2)]
    keep, send = refs.pop(0), refs.pop(0)
    inner = [refs.pop(0) for _ in range(pairs - 1)]
    head, tail, second_total, first_total = refs
    second_total[...] = jnp.zeros_like(second_total)
    first_total[...] = jnp.zeros_like(first_total)
    weight_loop(second_total, planes_of(hiddens), 2, planes_of(deltas), 2, share)
    firsts = [head] + inner + [tail]
    first_deltas(from_below, [(deltas[0],)], slopes[:1], [head])
    if inner:
        first_deltas(weight, neighbours(deltas), slopes[1:-1], inner)
    first_deltas(from_above, [(deltas[-1],)], slopes[-1:], [tail])
    parts = planes_of([[first] for first in firsts])
    weight_loop(first_total, planes_of(fields), 3, parts, 1, share)
    halves, size = keep.shape[1:3]
    me = lax.axis_index("chan")
    of_first = weight_fold(first_total, size)
    of_second = weight_fold(second_total, size)

    def place(ours, theirs):
        for g in range(extent):
            there = lax.rem(me + extent - g, extent)
            for h in range(halves):
                ours[g, h] = of_first[g][h]
                theirs[there, h] = of_second[g][h]

    odd = lax.rem(lax.axis_index("slab"), 2)

    @pl.when(odd == 0)
    def _():
        place(keep, send)

    @pl.when(odd == 1)
    def _():
        place(send, keep)


def field_kernel_back(inner, groups, after, *refs):
    del after
    refs = list(refs)
    back, weight = refs.pop(0), refs.pop(0)
    before, first, last, behind = [[refs.pop(0)] for _ in range(4)]
    slopes = [refs.pop(0) for _ in range(2)]
    middle = [refs.pop(0) for _ in range(inner)]
    outs, ends = refs[:groups], refs[groups:]
    first_deltas(back, [(before, first), (last, behind)], slopes, ends)
    firsts = [ends[0]] + middle + [ends[1]]

    def one(r):
        row = 2 * r
        size = outs[0].shape[2]
        channels = len(outs) * size
        for p, sums in enumerate(taps(weight[...], neighbours([[ref] for ref in firsts]), row)):
            for q, v in enumerate(sums):
                for x in range(2):
                    for j, out in enumerate(outs):
                        low = x * channels + j * size
                        out[row + q, 2 * p + x] = v[low : low + size].astype(BF16)

    in_blocks(outs[0].shape[0] // 2, one)


def split_kernel(after, one, two, *outs):
    del after
    for g, out in enumerate(outs):
        out[...] = one[g] + two[g]


def add_kernel(ahead, *refs):
    values = [ref[...] for ref in refs[ahead:-1]]
    while len(values) > 1:
        values = [sum(values[k + 1 : k + 2], values[k]) for k in range(0, len(values), 2)]
    refs[-1][...] = values[0]


def relay_kernel(*refs):
    pass


def finish_kernel(factor, after, mine, other, first, second):
    del after
    channels = first.shape[2]

    def place(ours, theirs):
        for result, sums in ((ours, mine), (theirs, other)):
            for t in range(27):
                low = t % 4 * channels
                result[t] = sums[t // 4, :, low : low + channels] * factor

    odd = lax.rem(lax.axis_index("slab"), 2)

    @pl.when(odd == 0)
    def _():
        place(first, second)

    @pl.when(odd == 1)
    def _():
        place(second, first)


def merge_kernel(extent, *refs):
    pieces, token, out, wide = refs[:-3], refs[-3], refs[-2], refs[-1]
    token[...] = jnp.zeros_like(token)
    size, planes, rows = out.shape[:3]
    share = rows // extent
    me = lax.axis_index("chan")
    for j in range(extent):
        base = lax.rem(me + extent - j, extent) * share

        def widen(f, mine=pieces[j::extent], base=base):
            x = 0
            for piece in mine:
                for k in range(piece.shape[1]):
                    start = ((base + f) * planes + x) * size
                    start = pl.multiple_of(start, 8) if size % 8 == 0 else start
                    wide[pl.ds(start, size), :] = piece[f, k].astype(F32)
                    x += 1

        in_blocks(share, widen)

    def back(i):
        for x in range(planes):
            tile = wide[pl.ds(x * size + i, rows, stride=planes * size), :]
            out[i, x] = tile.astype(BF16)

    in_blocks(size, back)


def body(field, out_grad, first_weight, second_weight):
    extent = lax.axis_size("chan")
    slabs = lax.axis_size("slab")
    me = lax.axis_index("chan")
    size, planes, rows, depth = field.shape
    channels = size * extent
    pairs = planes // 2
    share = rows // extent
    factor = 1.0 / math.sqrt(planes * slabs * rows * depth)

    def to_chan(value, shift):
        return lax.ppermute(value, "chan", [(i, (i + shift) % extent) for i in range(extent)])

    def to_next(value):
        return lax.ppermute(value, "slab", [(i, (i + 1) % slabs) for i in range(slabs)])

    def to_prev(value):
        return lax.ppermute(value, "slab", [((i + 1) % slabs, i) for i in range(slabs)])

    def relayed(value, *others):
        shape = jax.ShapeDtypeStruct(value.shape, value.dtype)
        early = [value, *others]
        return call(relay_kernel, [shape], early, loose=len(early), same={0: 0})[0]

    piece = jax.ShapeDtypeStruct((share + 8, 2, size, depth), BF16)
    by_tap = (27, size, channels)
    def field_pieces(low, high, after):
        count = (high - low) // 2
        made = call(
            functools.partial(field_kernel, extent, 4, low, high),
            [piece] * (extent * count),
            [after, field],
            [pltpu.VMEM((size * (high - low) * rows, depth), F32)],
            moved=field.size * 3,
            loose=1,
        )
        return [list(made[j * count : (j + 1) * count]) for j in range(extent)]

    made = field_pieces(planes - 2, planes, field)
    if pairs > 1:
        others = field_pieces(0, planes - 2, made[0][0])
        made = [first + last for first, last in zip(others, made)]
    parts = [made[0]]
    for j in range(1, extent):
        parts.append([to_chan(value, j) for value in made[j]])
    (pack,) = call(
        pack_kernel,
        [jax.ShapeDtypeStruct((14, size, 4 * channels), BF16)],
        [made[0][0], jnp.transpose(first_weight, (1, 0, 2)), jnp.transpose(second_weight, (1, 0, 2))],
        loose=1,
    )
    packs = [pack] + [to_chan(pack, j) for j in range(1, extent)]
    whole = size % 16 == 0
    own_before, own_after = [], []
    if whole:
        own_before, own_after = [to_next(parts[0][-1])], [to_prev(parts[0][0])]
    grad_piece = jax.ShapeDtypeStruct((share + 4, 2, channels, depth), BF16)
    grads = call(
        functools.partial(grad_kernel, extent, 2),
        [grad_piece] * pairs,
        [pack, out_grad],
        [pltpu.VMEM((channels * planes * rows, depth), F32)],
        moved=out_grad.size * 4,
        loose=1,
    )
    matrix = jax.ShapeDtypeStruct((6 * channels, 12 * channels), BF16)
    half = jax.ShapeDtypeStruct((6 * channels, 6 * channels), BF16)
    first_wide, second_wide, first_back, second_back, from_above, from_below = call(
        functools.partial(matrix_kernel, extent),
        [matrix] * 4 + [half] * 2,
        packs,
        moved=matrix.size * 8,
    )
    if whole and extent > 1 and pairs > 1:
        parts[1][-1] = relayed(parts[1][-1], pack)
        parts[1][0] = relayed(relayed(parts[1][0], grads[0], *packs[1:]), own_after[0])
    by_pair = [[parts[j][p] for j in range(extent)] for p in range(pairs)]
    groups = extent
    if not whole:
        by_pair = [[jnp.concatenate(pieces, axis=2)] for pieces in by_pair]
        groups = 1
    before = own_before + [to_next(piece) for piece in by_pair[-1][len(own_before) :]]
    after = own_after + [to_prev(piece) for piece in by_pair[0][len(own_after) :]]
    fields = [before] + by_pair + [after]

    def many(count, rows_each):
        return [jax.ShapeDtypeStruct((rows_each, 2, channels, depth), BF16)] * count

    def flat(lists):
        return [piece for pieces in lists for piece in pieces]

    work = 27 * 2 * channels * channels * depth * 2
    space = 4 * channels * depth * share

    made = call(
        functools.partial(forward_kernel, groups, pairs, 0),
        many(2 * pairs, share + 6) + many(pairs - 1, share + 4),
        flat(fields[: pairs + 1]) + list(grads[: pairs - 1]) + [first_wide, second_wide],
        flops=work * (2 * pairs - 1) * share,
        moved=space * 4 * pairs,
    )
    hiddens, slopes, deltas = made[:pairs], made[pairs : 2 * pairs], made[2 * pairs :]
    made = call(
        functools.partial(forward_kernel, groups, 1, 1),
        many(2, share + 6) + many(1, share + 4),
        flat(fields[pairs:]) + [hiddens[-1], grads[-1], first_wide, second_wide],
        flops=work * 2 * share,
        moved=space * 6,
    )
    hiddens = list(hiddens) + [made[0]]
    slopes = list(slopes) + [made[1]]
    deltas = list(deltas) + [made[2]]
    delta_after = to_prev(deltas[0])
    delta_before = to_next(deltas[-1])

    raw = jax.ShapeDtypeStruct((extent, 7, size, 4 * channels), F32)
    portion = jax.ShapeDtypeStruct(raw.shape[1:], F32)
    total = pltpu.VMEM((12 * channels, 8 * channels), F32)

    def room(rows_each):
        return pltpu.VMEM((rows_each, 2, channels, depth), BF16)

    made = call(
        functools.partial(gradient_kernel, share, groups, extent, pairs),
        [raw] * 2 + many(pairs - 1, share + 2),
        hiddens + deltas + [second_back, from_above, from_below] + slopes + flat(fields),
        [room(share + 2), room(share + 2), total, total],
    )
    keep, send, inner = made[0], made[1], list(made[2:])
    def exchanged(made):
        pieces = [made[0]] + [None] * (extent - 1)
        for j in range(1, extent):
            pieces[extent - j] = to_chan(made[j], extent - j)
        return pieces

    def stepped(value, stride, shift=0):
        if shift % extent == 0:
            return lax.ppermute(value, "slab", [(i, i ^ stride) for i in range(slabs)])
        pairs_of = []
        for i in range(slabs):
            for k in range(extent):
                there = (i ^ stride) * extent + (k + shift) % extent
                pairs_of.append((i * extent + k, there))
        return lax.ppermute(value, ("slab", "chan"), pairs_of)

    plain = slabs & (slabs - 1) == 0 and slabs >= 4
    if plain:
        kept = call(
            split_kernel, [portion] * extent, [delta_after, keep, stepped(send, 1)], loose=1
        )
        shares = [kept[0]] + [to_chan(kept[j], extent - j) for j in range(1, extent)]
        shares += [stepped(kept[j], 2, extent - j) for j in range(extent)]
        after = kept[0]
    else:
        after = keep
    made = call(
        functools.partial(field_kernel_back, pairs - 1, extent),
        [jax.ShapeDtypeStruct((share, planes, size, depth), BF16)] * extent,
        [after, second_back, first_back]
        + [delta_before, deltas[0], deltas[-1], delta_after, slopes[0], slopes[-1]]
        + inner,
        [room(share + 2), room(share + 2)],
        flops=work * (pairs + 2) * share,
        moved=space * 6,
        loose=1,
    )
    if plain:
        ahead = list(made[:1])
        (mine,) = call(
            functools.partial(add_kernel, len(ahead)), [portion], ahead + shares, loose=len(ahead)
        )
        made = list(made[:1]) + [relayed(value, mine) for value in made[1:]]
    pieces = exchanged(made)
    if plain:
        stride = 4
        while stride < slabs:
            got = [mine, stepped(mine, stride)]
            (mine,) = call(functools.partial(add_kernel, 0), [portion], got)
            stride *= 2
        other = stepped(mine, 1)
    else:
        mine, other = keep[0], send[0]
        for j in range(1, extent):
            mine, other = mine + to_chan(keep[j], extent - j), other + to_chan(send[j], extent - j)
        even = lax.rem(lax.axis_index("slab"), 2) == 0
        mine, other = jnp.where(even, mine, other), jnp.where(even, other, mine)
        mine, other = lax.psum((mine, other), "slab")
        mine, other = jnp.where(even, mine, other), jnp.where(even, other, mine)
    token, input_grad = call(
        functools.partial(merge_kernel, extent),
        [jax.ShapeDtypeStruct((8, 128), F32), jax.ShapeDtypeStruct(field.shape, BF16)],
        pieces,
        [pltpu.VMEM((rows * planes * size, depth), F32)],
        moved=4 * field.size,
    )
    first_grad, second_grad = call(
        functools.partial(finish_kernel, factor),
        [jax.ShapeDtypeStruct(by_tap, F32)] * 2,
        [token, mine, other],
        loose=1,
    )
    first_grad, second_grad = (jnp.transpose(g, (1, 0, 2)) for g in (first_grad, second_grad))
    return input_grad, first_grad, second_grad


def solution(mesh):
    placed = (
        P("chan", "slab", None, None),
        P(None, "slab", None, None),
        P("chan", None, None),
        P("chan", None, None),
    )
    return jax.shard_map(
        body,
        mesh=mesh,
        in_specs=placed,
        out_specs=(P("chan", "slab", None, None), P("chan", None, None), P("chan", None, None)),
        check_vma=False,
    )
```

```python
import functools
import math

import jax
import jax.numpy as jnp
from jax import lax
from jax.experimental import pallas as pl
from jax.experimental.pallas import tpu as pltpu
from jax.sharding import PartitionSpec as P

F32 = jnp.float32
BF16 = jnp.bfloat16
LIMIT = 16 * 1024 * 1024


def call(kernel, outs, args, scratch=(), flops=0, moved=0, loose=0, same=None):
    whole = pl.BlockSpec(memory_space=pltpu.VMEM)
    still = pl.BlockSpec(memory_space=pl.ANY)
    return pl.pallas_call(
        kernel,
        out_shape=outs,
        in_specs=[still] * loose + [whole] * (len(args) - loose),
        out_specs=[still if k in (same or {}).values() else whole for k in range(len(outs))],
        input_output_aliases=same or {},
        scratch_shapes=list(scratch),
        compiler_params=pltpu.CompilerParams(vmem_limit_bytes=LIMIT),
        cost_estimate=pl.CostEstimate(flops=flops, bytes_accessed=moved, transcendentals=0),
    )(*args)


def in_blocks(count, body):
    block = max(k for k in range(1, 17) if count % k == 0)

    def several(r, _):
        for k in range(block):
            body(r * block + k)
        return 0

    lax.fori_loop(0, count // block, several, 0)
    for k in range(count // block * block, count):
        body(k)


def widened(x_ref, wide, low, high):
    count, _, rows = x_ref.shape[:3]

    def widen(i):
        for x in range(low, high):
            start = pl.multiple_of((i * (high - low) + x - low) * rows, 8)
            wide[pl.ds(start, rows), :] = x_ref[i, x].astype(F32)

    in_blocks(count, widen)


def turn(wide, outs, shape, base, length):
    count, planes, rows = shape

    def one(f):
        y = lax.rem(base + f, rows)
        for x in range(planes):
            tile = wide[pl.ds(x * rows + y, count, stride=planes * rows), :]
            outs[x // 2][f, x % 2] = tile.astype(BF16)

    in_blocks(length, one)


def field_kernel(extent, margin, low, high, after, x_ref, *refs):
    del after
    outs, wide = refs[:-1], refs[-1]
    count, _, rows = x_ref.shape[:3]
    planes = high - low
    pairs = planes // 2
    share = rows // extent
    widened(x_ref, wide, low, high)
    me = lax.axis_index("chan")
    for s in range(extent):
        base = lax.rem(me + s, extent) * share - margin + rows
        turn(
            wide,
            outs[s * pairs : (s + 1) * pairs],
            (count, planes, rows),
            base,
            share + 2 * margin,
        )


def pack_kernel(after, first, second, packed):
    del after
    blank = jnp.zeros(first.shape[1:], F32)
    for h in range(packed.shape[0]):
        parts = []
        for ref in (first, second):
            for t in (2 * h, 2 * h + 1):
                parts.append(ref[t].astype(F32) if t < ref.shape[0] else blank)
        packed[h] = jnp.concatenate(parts, axis=1).astype(BF16)


def grad_kernel(extent, margin, after, x_ref, *refs):
    del after
    outs, wide = refs[:-1], refs[-1]
    count, planes, rows = x_ref.shape[:3]
    share = rows // extent
    widened(x_ref, wide, 0, planes)
    base = lax.axis_index("chan") * share - margin + rows
    turn(wide, outs, (count, planes, rows), base, share + 2 * margin)


def matrix_kernel(extent, *refs):
    packs, outs = refs[:extent], refs[extent:]
    me = lax.axis_index("chan")
    quarter = packs[0].shape[2] // 4
    taps = []
    turned = []
    for h in range(packs[0].shape[0]):
        tiles = [pack[h].astype(F32) for pack in packs]
        own = jnp.concatenate(tiles, axis=0)
        fixed = []
        for g in range(extent):
            place = lax.rem(me + extent - g, extent)
            tile = tiles[0]
            for j in range(1, extent):
                tile = jnp.where(place == j, tiles[j], tile)
            fixed.append(tile)
        both = jnp.concatenate(
            [own[:, : 2 * quarter], jnp.concatenate(fixed, axis=0)[:, 2 * quarter :]], axis=1
        )
        across = both.T
        for side in range(2):
            taps.append(
                [both[:, k * quarter : (k + 1) * quarter] for k in (side, side + 2)]
            )
            turned.append(
                [across[k * quarter : (k + 1) * quarter] for k in (side, side + 2)]
            )
    channels = quarter
    blank = jnp.zeros((channels, channels), F32)
    for k in range(2):
        for out, blocks, flip in ((outs[k], turned, False), (outs[2 + k], taps, True)):
            for e in range(3):
                for x in range(2):
                    chunks = []
                    for pair in range(2):
                        for b in range(3):
                            for side in range(2):
                                a = 2 * pair + side - x
                                t = 9 * a + 3 * b + e
                                inside = 0 <= a <= 2
                                t = 26 - t if flip else t
                                chunks.append(blocks[t][k] if inside else blank)
                    low = (2 * e + x) * channels
                    line = jnp.concatenate(chunks, axis=1).astype(BF16)
                    out[low : low + channels, :] = line
                    if k == 1 and flip:
                        half = line.shape[1] // 2
                        outs[4][low : low + channels, :] = line[:, :half]
                        outs[5][low : low + channels, :] = line[:, half:]


def stacked(refs, row, count):
    if len(refs) == 1:
        part = refs[0][pl.ds(row, count)]
        return part.reshape(-1, part.shape[-1])
    parts = [ref[row + b, x] for b in range(count) for x in range(2) for ref in refs]
    return jnp.concatenate(parts, axis=0)


def taps(weight, inputs, row):
    sides = []
    for pair in inputs:
        for q in range(2):
            parts = [stacked(refs, row + q, 3) for refs in pair]
            sides.append(jnp.concatenate(parts, axis=0) if len(parts) > 1 else parts[0])
    lifted = jnp.dot(weight, jnp.concatenate(sides, axis=1), preferred_element_type=F32)
    third = lifted.shape[0] // 3
    depth = sides[0].shape[1]
    sums = []
    for k in range(len(sides)):
        side = lifted[:, k * depth : (k + 1) * depth]
        sums.append(
            side[third : 2 * third]
            + pltpu.roll(side[:third], 1, 1)
            + pltpu.roll(side[2 * third :], depth - 1, 1)
        )
    return [sums[2 * p : 2 * p + 2] for p in range(len(inputs))]


def neighbours(pairs):
    return list(zip(pairs[:-1], pairs[1:]))


def silu_parts(v):
    sig = jax.nn.sigmoid(v)
    return sig, sig * (1.0 + v * (1.0 - sig))


def forward_kernel(groups, fresh, ready, *refs):
    refs = list(refs)
    fields = [[refs.pop(0) for _ in range(groups)] for _ in range(fresh + 1)]
    hiddens = [refs.pop(0) for _ in range(ready)]
    count = fresh + ready - 1
    grads = [refs.pop(0) for _ in range(count)]
    first, second = refs.pop(0), refs.pop(0)
    made = [refs.pop(0) for _ in range(fresh)]
    slopes = [refs.pop(0) for _ in range(fresh)]
    deltas = refs
    hiddens = hiddens + made

    def one(r):
        row = 2 * r
        for p, sums in enumerate(taps(first[...], neighbours(fields), row)):
            for q, v in enumerate(sums):
                sig, slope = silu_parts(v)
                shape = made[p].shape[1:]
                made[p][row + q] = (v * sig).astype(BF16).reshape(shape)
                slopes[p][row + q] = slope.astype(BF16).reshape(shape)

    in_blocks(made[0].shape[0] // 2, one)

    def two(r):
        row = 2 * r
        for p, sums in enumerate(taps(second[...], neighbours([[ref] for ref in hiddens]), row)):
            for q, v in enumerate(sums):
                shape = deltas[p].shape[1:]
                out_grad = grads[p][row + q].astype(F32)
                slope = silu_parts(v)[1].reshape(shape)
                deltas[p][row + q] = (out_grad * slope).astype(BF16)

    if count > 0:
        in_blocks(deltas[0].shape[0] // 2, two)


def planes_of(pairs):
    return [(refs, x) for refs in pairs for x in range(2)]


def weight_loop(total, pieces, first_row, deltas, delta_row, count):
    blocks = [k for k in range(1, 13) if count // 2 % k == 0 and k * len(deltas) <= 12]
    together = max(blocks, default=1)

    def product(r):
        left, right = [], []
        for k in range(together):
            row = 2 * (r * together + k)
            for x, ((delta,), place) in enumerate(deltas):
                rows = []
                for q in range(2):
                    wide = delta[delta_row + row + q, place]
                    depth = wide.shape[1]
                    rows += [pltpu.roll(wide, depth - 1, 1), wide, pltpu.roll(wide, 1, 1)]
                    rows.append(jnp.zeros_like(wide))
                right.append(jnp.concatenate(rows, axis=0))
                rows = []
                for refs, side in pieces[x : x + 3]:
                    for b in range(4):
                        for ref in refs:
                            rows.append(ref[first_row + row + b, side])
                left.append(jnp.concatenate(rows, axis=0))
        return lax.dot_general(
            jnp.concatenate(left, axis=1),
            jnp.concatenate(right, axis=1),
            (((1,), (1,)), ((), ())),
            preferred_element_type=F32,
        )

    value = total[...]
    for r in range(count // 2 // together):
        value = value + product(r)
    total[...] = value


def weight_fold(total, size):
    lanes = total.shape[1] // 2
    channels = total.shape[0] // 12
    upper, lower = total[:, :lanes], total[:, lanes:]
    groups = []
    for g in range(channels // size):
        taps_of = []
        for a in range(3):
            for b in range(3):
                start = (4 * a + b) * channels + g * size
                part = (
                    upper[start : start + size]
                    + lower[start + channels : start + channels + size]
                )
                taps_of += [part[:, e * channels : (e + 1) * channels] for e in range(3)]
        blank = jnp.zeros((size, channels), F32)
        taps_of.append(blank)
        groups.append([jnp.concatenate(taps_of[4 * h : 4 * h + 4], axis=1) for h in range(7)])
    return groups


def first_deltas(weight, inputs, slopes, firsts):
    def one(r):
        row = 2 * r
        for p, sums in enumerate(taps(weight[...], inputs, row)):
            for q, v in enumerate(sums):
                shape = firsts[p].shape[1:]
                slope = slopes[p][row + 2 + q].astype(F32)
                firsts[p][row + q] = (v.reshape(shape) * slope).astype(BF16)

    in_blocks(firsts[0].shape[0] // 2, one)


def gradient_kernel(share, groups, extent, pairs, *refs):
    refs = list(refs)
    hiddens = [[refs.pop(0)] for _ in range(pairs + 1)]
    deltas = [[refs.pop(0)] for _ in range(pairs)]
    weight, from_above, from_below = [refs.pop(0) for _ in range(3)]
    slopes = [refs.pop(0) for _ in range(pairs + 1)]
    fields = [[refs.pop(0) for _ in range(groups)] for _ in range(pairs + 2)]
    keep, send = refs.pop(0), refs.pop(0)
    inner = [refs.pop(0) for _ in range(pairs - 1)]
    head, tail, second_total, first_total = refs
    second_total[...] = jnp.zeros_like(second_total)
    first_total[...] = jnp.zeros_like(first_total)
    weight_loop(second_total, planes_of(hiddens), 2, planes_of(deltas), 2, share)
    firsts = [head] + inner + [tail]
    first_deltas(from_below, [(deltas[0],)], slopes[:1], [head])
    if inner:
        first_deltas(weight, neighbours(deltas), slopes[1:-1], inner)
    first_deltas(from_above, [(deltas[-1],)], slopes[-1:], [tail])
    parts = planes_of([[first] for first in firsts])
    weight_loop(first_total, planes_of(fields), 3, parts, 1, share)
    halves, size = keep.shape[1:3]
    me = lax.axis_index("chan")
    of_first = weight_fold(first_total, size)
    of_second = weight_fold(second_total, size)

    def place(ours, theirs):
        for g in range(extent):
            there = lax.rem(me + extent - g, extent)
            for h in range(halves):
                ours[g, h] = of_first[g][h]
                theirs[there, h] = of_second[g][h]

    odd = lax.rem(lax.axis_index("slab"), 2)

    @pl.when(odd == 0)
    def _():
        place(keep, send)

    @pl.when(odd == 1)
    def _():
        place(send, keep)


def tail_kernel(after, weight, above, below, slope, first):
    del after
    first_deltas(weight, [([above], [below])], [slope], [first])


def field_kernel_back(inner, groups, after, *refs):
    del after
    refs = list(refs)
    back, weight = refs.pop(0), refs.pop(0)
    above, below = [[refs.pop(0)] for _ in range(2)]
    slope = refs.pop(0)
    later = [refs.pop(0) for _ in range(inner + 1)]
    outs, head = refs[:groups], refs[groups]
    first_deltas(back, [(above, below)], [slope], [head])
    firsts = [head] + later

    def one(r):
        row = 2 * r
        size = outs[0].shape[2]
        channels = len(outs) * size
        for p, sums in enumerate(taps(weight[...], neighbours([[ref] for ref in firsts]), row)):
            for q, v in enumerate(sums):
                for x in range(2):
                    for j, out in enumerate(outs):
                        low = x * channels + j * size
                        out[row + q, 2 * p + x] = v[low : low + size].astype(BF16)

    in_blocks(outs[0].shape[0] // 2, one)


def split_kernel(after, one, two, *outs):
    del after
    for g, out in enumerate(outs):
        out[...] = one[g] + two[g]


def add_kernel(ahead, *refs):
    values = [ref[...] for ref in refs[ahead:-1]]
    while len(values) > 1:
        values = [sum(values[k + 1 : k + 2], values[k]) for k in range(0, len(values), 2)]
    refs[-1][...] = values[0]


def relay_kernel(*refs):
    pass


def finish_kernel(factor, after, mine, other, first, second):
    del after
    channels = first.shape[2]

    def place(ours, theirs):
        for result, sums in ((ours, mine), (theirs, other)):
            for t in range(27):
                low = t % 4 * channels
                result[t] = sums[t // 4, :, low : low + channels] * factor

    odd = lax.rem(lax.axis_index("slab"), 2)

    @pl.when(odd == 0)
    def _():
        place(first, second)

    @pl.when(odd == 1)
    def _():
        place(second, first)


def merge_kernel(extent, *refs):
    pieces, token, out, wide = refs[:-3], refs[-3], refs[-2], refs[-1]
    token[...] = jnp.zeros_like(token)
    size, planes, rows = out.shape[:3]
    share = rows // extent
    me = lax.axis_index("chan")
    for j in range(extent):
        base = lax.rem(me + extent - j, extent) * share

        def widen(f, mine=pieces[j::extent], base=base):
            x = 0
            for piece in mine:
                for k in range(piece.shape[1]):
                    start = ((base + f) * planes + x) * size
                    start = pl.multiple_of(start, 8) if size % 8 == 0 else start
                    wide[pl.ds(start, size), :] = piece[f, k].astype(F32)
                    x += 1

        in_blocks(share, widen)

    def back(i):
        for x in range(planes):
            tile = wide[pl.ds(x * size + i, rows, stride=planes * size), :]
            out[i, x] = tile.astype(BF16)

    in_blocks(size, back)


def body(field, out_grad, first_weight, second_weight):
    extent = lax.axis_size("chan")
    slabs = lax.axis_size("slab")
    me = lax.axis_index("chan")
    size, planes, rows, depth = field.shape
    channels = size * extent
    pairs = planes // 2
    share = rows // extent
    factor = 1.0 / math.sqrt(planes * slabs * rows * depth)

    def to_chan(value, shift):
        return lax.ppermute(value, "chan", [(i, (i + shift) % extent) for i in range(extent)])

    def to_next(value):
        return lax.ppermute(value, "slab", [(i, (i + 1) % slabs) for i in range(slabs)])

    def to_prev(value):
        return lax.ppermute(value, "slab", [((i + 1) % slabs, i) for i in range(slabs)])

    def relayed(value, *others):
        shape = jax.ShapeDtypeStruct(value.shape, value.dtype)
        early = [value, *others]
        return call(relay_kernel, [shape], early, loose=len(early), same={0: 0})[0]

    piece = jax.ShapeDtypeStruct((share + 8, 2, size, depth), BF16)
    by_tap = (27, size, channels)
    def field_pieces(low, high, after):
        count = (high - low) // 2
        made = call(
            functools.partial(field_kernel, extent, 4, low, high),
            [piece] * (extent * count),
            [after, field],
            [pltpu.VMEM((size * (high - low) * rows, depth), F32)],
            moved=field.size * 3,
            loose=1,
        )
        return [list(made[j * count : (j + 1) * count]) for j in range(extent)]

    made = field_pieces(planes - 2, planes, field)
    if pairs > 1:
        others = field_pieces(0, planes - 2, made[0][0])
        made = [first + last for first, last in zip(others, made)]
    parts = [made[0]]
    for j in range(1, extent):
        parts.append([to_chan(value, j) for value in made[j]])
    (pack,) = call(
        pack_kernel,
        [jax.ShapeDtypeStruct((14, size, 4 * channels), BF16)],
        [made[0][0], jnp.transpose(first_weight, (1, 0, 2)), jnp.transpose(second_weight, (1, 0, 2))],
        loose=1,
    )
    packs = [pack] + [to_chan(pack, j) for j in range(1, extent)]
    whole = size % 16 == 0
    own_before, own_after = [], []
    if whole:
        own_before, own_after = [to_next(parts[0][-1])], [to_prev(parts[0][0])]
    grad_piece = jax.ShapeDtypeStruct((share + 4, 2, channels, depth), BF16)
    grads = call(
        functools.partial(grad_kernel, extent, 2),
        [grad_piece] * pairs,
        [pack, out_grad],
        [pltpu.VMEM((channels * planes * rows, depth), F32)],
        moved=out_grad.size * 4,
        loose=1,
    )
    matrix = jax.ShapeDtypeStruct((6 * channels, 12 * channels), BF16)
    half = jax.ShapeDtypeStruct((6 * channels, 6 * channels), BF16)
    first_wide, second_wide, first_back, second_back, from_above, from_below = call(
        functools.partial(matrix_kernel, extent),
        [matrix] * 4 + [half] * 2,
        packs,
        moved=matrix.size * 8,
    )
    if whole and extent > 1 and pairs > 1:
        parts[1][-1] = relayed(parts[1][-1], pack)
        parts[1][0] = relayed(relayed(parts[1][0], grads[0], *packs[1:]), own_after[0])
    by_pair = [[parts[j][p] for j in range(extent)] for p in range(pairs)]
    groups = extent
    if not whole:
        by_pair = [[jnp.concatenate(pieces, axis=2)] for pieces in by_pair]
        groups = 1
    before = own_before + [to_next(piece) for piece in by_pair[-1][len(own_before) :]]
    after = own_after + [to_prev(piece) for piece in by_pair[0][len(own_after) :]]
    fields = [before] + by_pair + [after]

    def many(count, rows_each):
        return [jax.ShapeDtypeStruct((rows_each, 2, channels, depth), BF16)] * count

    def flat(lists):
        return [piece for pieces in lists for piece in pieces]

    work = 27 * 2 * channels * channels * depth * 2
    space = 4 * channels * depth * share

    made = call(
        functools.partial(forward_kernel, groups, pairs, 0),
        many(2 * pairs, share + 6) + many(pairs - 1, share + 4),
        flat(fields[: pairs + 1]) + list(grads[: pairs - 1]) + [first_wide, second_wide],
        flops=work * (2 * pairs - 1) * share,
        moved=space * 4 * pairs,
    )
    hiddens, slopes, deltas = made[:pairs], made[pairs : 2 * pairs], made[2 * pairs :]
    made = call(
        functools.partial(forward_kernel, groups, 1, 1),
        many(2, share + 6) + many(1, share + 4),
        flat(fields[pairs:]) + [hiddens[-1], grads[-1], first_wide, second_wide],
        flops=work * 2 * share,
        moved=space * 6,
    )
    hiddens = list(hiddens) + [made[0]]
    slopes = list(slopes) + [made[1]]
    deltas = list(deltas) + [made[2]]
    delta_after = to_prev(deltas[0])
    delta_before = to_next(deltas[-1])

    raw = jax.ShapeDtypeStruct((extent, 7, size, 4 * channels), F32)
    portion = jax.ShapeDtypeStruct(raw.shape[1:], F32)
    total = pltpu.VMEM((12 * channels, 8 * channels), F32)

    def room(rows_each):
        return pltpu.VMEM((rows_each, 2, channels, depth), BF16)

    made = call(
        functools.partial(gradient_kernel, share, groups, extent, pairs),
        [raw] * 2 + many(pairs - 1, share + 2),
        hiddens + deltas + [second_back, from_above, from_below] + slopes + flat(fields),
        [room(share + 2), room(share + 2), total, total],
    )
    keep, send, inner = made[0], made[1], list(made[2:])
    def exchanged(made):
        pieces = [made[0]] + [None] * (extent - 1)
        for j in range(1, extent):
            pieces[extent - j] = to_chan(made[j], extent - j)
        return pieces

    def stepped(value, stride, shift=0):
        if shift % extent == 0:
            return lax.ppermute(value, "slab", [(i, i ^ stride) for i in range(slabs)])
        pairs_of = []
        for i in range(slabs):
            for k in range(extent):
                there = (i ^ stride) * extent + (k + shift) % extent
                pairs_of.append((i * extent + k, there))
        return lax.ppermute(value, ("slab", "chan"), pairs_of)

    (tail,) = call(
        tail_kernel,
        many(1, share + 2),
        [keep, second_back, deltas[-1], delta_after, slopes[-1]],
        flops=work * share,
        moved=space * 2,
        loose=1,
    )
    plain = slabs & (slabs - 1) == 0 and slabs >= 4
    if plain:
        kept = call(
            split_kernel, [portion] * extent, [tail, keep, stepped(send, 1)], loose=1
        )
        shares = [kept[0]] + [to_chan(kept[j], extent - j) for j in range(1, extent)]
        shares += [stepped(kept[j], 2, extent - j) for j in range(extent)]
        after = kept[0]
    else:
        after = keep
    made = call(
        functools.partial(field_kernel_back, pairs - 1, extent),
        [jax.ShapeDtypeStruct((share, planes, size, depth), BF16)] * extent,
        [after, second_back, first_back, delta_before, deltas[0], slopes[0]] + inner + [tail],
        [room(share + 2)],
        flops=work * (pairs + 2) * share,
        moved=space * 6,
        loose=1,
    )
    if plain:
        ahead = list(made[:1])
        (mine,) = call(
            functools.partial(add_kernel, len(ahead)), [portion], ahead + shares, loose=len(ahead)
        )
        made = list(made[:1]) + [relayed(value, mine) for value in made[1:]]
    pieces = exchanged(made)
    if plain:
        stride = 4
        while stride < slabs:
            got = [mine, stepped(mine, stride)]
            (mine,) = call(functools.partial(add_kernel, 0), [portion], got)
            stride *= 2
        other = stepped(mine, 1)
    else:
        mine, other = keep[0], send[0]
        for j in range(1, extent):
            mine, other = mine + to_chan(keep[j], extent - j), other + to_chan(send[j], extent - j)
        even = lax.rem(lax.axis_index("slab"), 2) == 0
        mine, other = jnp.where(even, mine, other), jnp.where(even, other, mine)
        mine, other = lax.psum((mine, other), "slab")
        mine, other = jnp.where(even, mine, other), jnp.where(even, other, mine)
    token, input_grad = call(
        functools.partial(merge_kernel, extent),
        [jax.ShapeDtypeStruct((8, 128), F32), jax.ShapeDtypeStruct(field.shape, BF16)],
        pieces,
        [pltpu.VMEM((rows * planes * size, depth), F32)],
        moved=4 * field.size,
    )
    first_grad, second_grad = call(
        functools.partial(finish_kernel, factor),
        [jax.ShapeDtypeStruct(by_tap, F32)] * 2,
        [token, mine, other],
        loose=1,
    )
    first_grad, second_grad = (jnp.transpose(g, (1, 0, 2)) for g in (first_grad, second_grad))
    return input_grad, first_grad, second_grad


def solution(mesh):
    placed = (
        P("chan", "slab", None, None),
        P(None, "slab", None, None),
        P("chan", None, None),
        P("chan", None, None),
    )
    return jax.shard_map(
        body,
        mesh=mesh,
        in_specs=placed,
        out_specs=(P("chan", "slab", None, None), P("chan", None, None), P("chan", None, None)),
        check_vma=False,
    )
```

```python
import functools
import math

import jax
import jax.numpy as jnp
from jax import lax
from jax.experimental import pallas as pl
from jax.experimental.pallas import tpu as pltpu
from jax.sharding import PartitionSpec as P

F32 = jnp.float32
BF16 = jnp.bfloat16
LIMIT = 16 * 1024 * 1024


def call(kernel, outs, args, scratch=(), flops=0, moved=0, loose=0, same=None):
    whole = pl.BlockSpec(memory_space=pltpu.VMEM)
    still = pl.BlockSpec(memory_space=pl.ANY)
    return pl.pallas_call(
        kernel,
        out_shape=outs,
        in_specs=[still] * loose + [whole] * (len(args) - loose),
        out_specs=[still if k in (same or {}).values() else whole for k in range(len(outs))],
        input_output_aliases=same or {},
        scratch_shapes=list(scratch),
        compiler_params=pltpu.CompilerParams(vmem_limit_bytes=LIMIT),
        cost_estimate=pl.CostEstimate(flops=flops, bytes_accessed=moved, transcendentals=0),
    )(*args)


def in_blocks(count, body):
    block = max(k for k in range(1, 17) if count % k == 0)

    def several(r, _):
        for k in range(block):
            body(r * block + k)
        return 0

    lax.fori_loop(0, count // block, several, 0)
    for k in range(count // block * block, count):
        body(k)


def widened(x_ref, wide, low, high):
    count, _, rows = x_ref.shape[:3]

    def widen(i):
        for x in range(low, high):
            start = pl.multiple_of((i * (high - low) + x - low) * rows, 8)
            wide[pl.ds(start, rows), :] = x_ref[i, x].astype(F32)

    in_blocks(count, widen)


def turn(wide, outs, shape, base, length):
    count, planes, rows = shape

    def one(f):
        y = lax.rem(base + f, rows)
        for x in range(planes):
            tile = wide[pl.ds(x * rows + y, count, stride=planes * rows), :]
            outs[x // 2][f, x % 2] = tile.astype(BF16)

    in_blocks(length, one)


def field_kernel(extent, margin, low, high, after, x_ref, *refs):
    del after
    outs, wide = refs[:-1], refs[-1]
    count, _, rows = x_ref.shape[:3]
    planes = high - low
    pairs = planes // 2
    share = rows // extent
    widened(x_ref, wide, low, high)
    me = lax.axis_index("chan")
    for s in range(extent):
        base = lax.rem(me + s, extent) * share - margin + rows
        turn(
            wide,
            outs[s * pairs : (s + 1) * pairs],
            (count, planes, rows),
            base,
            share + 2 * margin,
        )


def pack_kernel(after, first, second, packed):
    del after
    blank = jnp.zeros(first.shape[1:], F32)
    for h in range(packed.shape[0]):
        parts = []
        for ref in (first, second):
            for t in (2 * h, 2 * h + 1):
                parts.append(ref[t].astype(F32) if t < ref.shape[0] else blank)
        packed[h] = jnp.concatenate(parts, axis=1).astype(BF16)


def grad_kernel(extent, margin, after, x_ref, *refs):
    del after
    outs, wide = refs[:-1], refs[-1]
    count, planes, rows = x_ref.shape[:3]
    share = rows // extent
    widened(x_ref, wide, 0, planes)
    base = lax.axis_index("chan") * share - margin + rows
    turn(wide, outs, (count, planes, rows), base, share + 2 * margin)


def matrix_kernel(extent, *refs):
    packs, outs = refs[:extent], refs[extent:]
    me = lax.axis_index("chan")
    quarter = packs[0].shape[2] // 4
    taps = []
    turned = []
    for h in range(packs[0].shape[0]):
        tiles = [pack[h].astype(F32) for pack in packs]
        own = jnp.concatenate(tiles, axis=0)
        fixed = []
        for g in range(extent):
            place = lax.rem(me + extent - g, extent)
            tile = tiles[0]
            for j in range(1, extent):
                tile = jnp.where(place == j, tiles[j], tile)
            fixed.append(tile)
        both = jnp.concatenate(
            [own[:, : 2 * quarter], jnp.concatenate(fixed, axis=0)[:, 2 * quarter :]], axis=1
        )
        across = both.T
        for side in range(2):
            taps.append(
                [both[:, k * quarter : (k + 1) * quarter] for k in (side, side + 2)]
            )
            turned.append(
                [across[k * quarter : (k + 1) * quarter] for k in (side, side + 2)]
            )
    channels = quarter
    blank = jnp.zeros((channels, channels), F32)
    for k in range(2):
        for out, blocks, flip in ((outs[k], turned, False), (outs[2 + k], taps, True)):
            for e in range(3):
                for x in range(2):
                    chunks = []
                    for pair in range(2):
                        for b in range(3):
                            for side in range(2):
                                a = 2 * pair + side - x
                                t = 9 * a + 3 * b + e
                                inside = 0 <= a <= 2
                                t = 26 - t if flip else t
                                chunks.append(blocks[t][k] if inside else blank)
                    low = (2 * e + x) * channels
                    line = jnp.concatenate(chunks, axis=1).astype(BF16)
                    out[low : low + channels, :] = line
                    if k == 1 and flip:
                        half = line.shape[1] // 2
                        outs[4][low : low + channels, :] = line[:, :half]
                        outs[5][low : low + channels, :] = line[:, half:]


def stacked(refs, row, count):
    if len(refs) == 1:
        part = refs[0][pl.ds(row, count)]
        return part.reshape(-1, part.shape[-1])
    parts = [ref[row + b, x] for b in range(count) for x in range(2) for ref in refs]
    return jnp.concatenate(parts, axis=0)


def taps(weight, inputs, row):
    sides = []
    for pair in inputs:
        for q in range(2):
            parts = [stacked(refs, row + q, 3) for refs in pair]
            sides.append(jnp.concatenate(parts, axis=0) if len(parts) > 1 else parts[0])
    lifted = jnp.dot(weight, jnp.concatenate(sides, axis=1), preferred_element_type=F32)
    third = lifted.shape[0] // 3
    depth = sides[0].shape[1]
    sums = []
    for k in range(len(sides)):
        side = lifted[:, k * depth : (k + 1) * depth]
        sums.append(
            side[third : 2 * third]
            + pltpu.roll(side[:third], 1, 1)
            + pltpu.roll(side[2 * third :], depth - 1, 1)
        )
    return [sums[2 * p : 2 * p + 2] for p in range(len(inputs))]


def neighbours(pairs):
    return list(zip(pairs[:-1], pairs[1:]))


def silu_parts(v):
    sig = jax.nn.sigmoid(v)
    return sig, sig * (1.0 + v * (1.0 - sig))


def forward_kernel(groups, fresh, ready, *refs):
    refs = list(refs)
    fields = [[refs.pop(0) for _ in range(groups)] for _ in range(fresh + 1)]
    hiddens = [refs.pop(0) for _ in range(ready)]
    count = fresh + ready - 1
    grads = [refs.pop(0) for _ in range(count)]
    first, second = refs.pop(0), refs.pop(0)
    made = [refs.pop(0) for _ in range(fresh)]
    slopes = [refs.pop(0) for _ in range(fresh)]
    deltas = refs
    hiddens = hiddens + made

    def one(r):
        row = 2 * r
        for p, sums in enumerate(taps(first[...], neighbours(fields), row)):
            for q, v in enumerate(sums):
                sig, slope = silu_parts(v)
                shape = made[p].shape[1:]
                made[p][row + q] = (v * sig).astype(BF16).reshape(shape)
                slopes[p][row + q] = slope.astype(BF16).reshape(shape)

    in_blocks(made[0].shape[0] // 2, one)

    def two(r):
        row = 2 * r
        for p, sums in enumerate(taps(second[...], neighbours([[ref] for ref in hiddens]), row)):
            for q, v in enumerate(sums):
                shape = deltas[p].shape[1:]
                out_grad = grads[p][row + q].astype(F32)
                slope = silu_parts(v)[1].reshape(shape)
                deltas[p][row + q] = (out_grad * slope).astype(BF16)

    if count > 0:
        in_blocks(deltas[0].shape[0] // 2, two)


def planes_of(pairs):
    return [(refs, x) for refs in pairs for x in range(2)]


def weight_loop(total, pieces, first_row, deltas, delta_row, count):
    blocks = [k for k in range(1, 13) if count // 2 % k == 0 and k * len(deltas) <= 24]
    together = max(blocks, default=1)

    def product(r):
        left, right = [], []
        for k in range(together):
            row = 2 * (r * together + k)
            for x, ((delta,), place) in enumerate(deltas):
                rows = []
                for q in range(2):
                    wide = delta[delta_row + row + q, place]
                    depth = wide.shape[1]
                    rows += [pltpu.roll(wide, depth - 1, 1), wide, pltpu.roll(wide, 1, 1)]
                    rows.append(jnp.zeros_like(wide))
                right.append(jnp.concatenate(rows, axis=0))
                rows = []
                for refs, side in pieces[x : x + 3]:
                    for b in range(4):
                        for ref in refs:
                            rows.append(ref[first_row + row + b, side])
                left.append(jnp.concatenate(rows, axis=0))
        return lax.dot_general(
            jnp.concatenate(left, axis=1),
            jnp.concatenate(right, axis=1),
            (((1,), (1,)), ((), ())),
            preferred_element_type=F32,
        )

    value = total[...]
    for r in range(count // 2 // together):
        value = value + product(r)
    total[...] = value


def weight_fold(total, size):
    lanes = total.shape[1] // 2
    channels = total.shape[0] // 12
    upper, lower = total[:, :lanes], total[:, lanes:]
    groups = []
    for g in range(channels // size):
        taps_of = []
        for a in range(3):
            for b in range(3):
                start = (4 * a + b) * channels + g * size
                part = (
                    upper[start : start + size]
                    + lower[start + channels : start + channels + size]
                )
                taps_of += [part[:, e * channels : (e + 1) * channels] for e in range(3)]
        blank = jnp.zeros((size, channels), F32)
        taps_of.append(blank)
        groups.append([jnp.concatenate(taps_of[4 * h : 4 * h + 4], axis=1) for h in range(7)])
    return groups


def first_deltas(weight, inputs, slopes, firsts):
    def one(r):
        row = 2 * r
        for p, sums in enumerate(taps(weight[...], inputs, row)):
            for q, v in enumerate(sums):
                shape = firsts[p].shape[1:]
                slope = slopes[p][row + 2 + q].astype(F32)
                firsts[p][row + q] = (v.reshape(shape) * slope).astype(BF16)

    in_blocks(firsts[0].shape[0] // 2, one)


def gradient_kernel(share, groups, extent, pairs, *refs):
    refs = list(refs)
    hiddens = [[refs.pop(0)] for _ in range(pairs + 1)]
    deltas = [[refs.pop(0)] for _ in range(pairs)]
    weight, from_above, from_below = [refs.pop(0) for _ in range(3)]
    slopes = [refs.pop(0) for _ in range(pairs + 1)]
    fields = [[refs.pop(0) for _ in range(groups)] for _ in range(pairs + 2)]
    keep, send = refs.pop(0), refs.pop(0)
    inner = [refs.pop(0) for _ in range(pairs - 1)]
    head, tail, second_total, first_total = refs
    second_total[...] = jnp.zeros_like(second_total)
    first_total[...] = jnp.zeros_like(first_total)
    weight_loop(second_total, planes_of(hiddens), 2, planes_of(deltas), 2, share)
    firsts = [head] + inner + [tail]
    first_deltas(from_below, [(deltas[0],)], slopes[:1], [head])
    if inner:
        first_deltas(weight, neighbours(deltas), slopes[1:-1], inner)
    first_deltas(from_above, [(deltas[-1],)], slopes[-1:], [tail])
    parts = planes_of([[first] for first in firsts])
    weight_loop(first_total, planes_of(fields), 3, parts, 1, share)
    halves, size = keep.shape[1:3]
    me = lax.axis_index("chan")
    of_first = weight_fold(first_total, size)
    of_second = weight_fold(second_total, size)

    def place(ours, theirs):
        for g in range(extent):
            there = lax.rem(me + extent - g, extent)
            for h in range(halves):
                ours[g, h] = of_first[g][h]
                theirs[there, h] = of_second[g][h]

    odd = lax.rem(lax.axis_index("slab"), 2)

    @pl.when(odd == 0)
    def _():
        place(keep, send)

    @pl.when(odd == 1)
    def _():
        place(send, keep)


def tail_kernel(after, weight, above, below, slope, first):
    del after
    first_deltas(weight, [([above], [below])], [slope], [first])


def field_kernel_back(inner, groups, after, *refs):
    del after
    refs = list(refs)
    back, weight = refs.pop(0), refs.pop(0)
    above, below = [[refs.pop(0)] for _ in range(2)]
    slope = refs.pop(0)
    later = [refs.pop(0) for _ in range(inner + 1)]
    outs, head = refs[:groups], refs[groups]
    first_deltas(back, [(above, below)], [slope], [head])
    firsts = [head] + later

    def one(r):
        row = 2 * r
        size = outs[0].shape[2]
        channels = len(outs) * size
        for p, sums in enumerate(taps(weight[...], neighbours([[ref] for ref in firsts]), row)):
            for q, v in enumerate(sums):
                for x in range(2):
                    for j, out in enumerate(outs):
                        low = x * channels + j * size
                        out[row + q, 2 * p + x] = v[low : low + size].astype(BF16)

    in_blocks(outs[0].shape[0] // 2, one)


def split_kernel(after, one, two, *outs):
    del after
    for g, out in enumerate(outs):
        out[...] = one[g] + two[g]


def add_kernel(ahead, *refs):
    values = [ref[...] for ref in refs[ahead:-1]]
    while len(values) > 1:
        values = [sum(values[k + 1 : k + 2], values[k]) for k in range(0, len(values), 2)]
    refs[-1][...] = values[0]


def relay_kernel(*refs):
    pass


def finish_kernel(factor, after, mine, other, first, second):
    del after
    channels = first.shape[2]

    def place(ours, theirs):
        for result, sums in ((ours, mine), (theirs, other)):
            for t in range(27):
                low = t % 4 * channels
                result[t] = sums[t // 4, :, low : low + channels] * factor

    odd = lax.rem(lax.axis_index("slab"), 2)

    @pl.when(odd == 0)
    def _():
        place(first, second)

    @pl.when(odd == 1)
    def _():
        place(second, first)


def merge_kernel(extent, *refs):
    pieces, token, out, wide = refs[:-3], refs[-3], refs[-2], refs[-1]
    token[...] = jnp.zeros_like(token)
    size, planes, rows = out.shape[:3]
    share = rows // extent
    me = lax.axis_index("chan")
    for j in range(extent):
        base = lax.rem(me + extent - j, extent) * share

        def widen(f, mine=pieces[j::extent], base=base):
            x = 0
            for piece in mine:
                for k in range(piece.shape[1]):
                    start = ((base + f) * planes + x) * size
                    start = pl.multiple_of(start, 8) if size % 8 == 0 else start
                    wide[pl.ds(start, size), :] = piece[f, k].astype(F32)
                    x += 1

        in_blocks(share, widen)

    def back(i):
        for x in range(planes):
            tile = wide[pl.ds(x * size + i, rows, stride=planes * size), :]
            out[i, x] = tile.astype(BF16)

    in_blocks(size, back)


def body(field, out_grad, first_weight, second_weight):
    extent = lax.axis_size("chan")
    slabs = lax.axis_size("slab")
    me = lax.axis_index("chan")
    size, planes, rows, depth = field.shape
    channels = size * extent
    pairs = planes // 2
    share = rows // extent
    factor = 1.0 / math.sqrt(planes * slabs * rows * depth)

    def to_chan(value, shift):
        return lax.ppermute(value, "chan", [(i, (i + shift) % extent) for i in range(extent)])

    def to_next(value):
        return lax.ppermute(value, "slab", [(i, (i + 1) % slabs) for i in range(slabs)])

    def to_prev(value):
        return lax.ppermute(value, "slab", [((i + 1) % slabs, i) for i in range(slabs)])

    def relayed(value, *others):
        shape = jax.ShapeDtypeStruct(value.shape, value.dtype)
        early = [value, *others]
        return call(relay_kernel, [shape], early, loose=len(early), same={0: 0})[0]

    piece = jax.ShapeDtypeStruct((share + 8, 2, size, depth), BF16)
    by_tap = (27, size, channels)
    def field_pieces(low, high, after):
        count = (high - low) // 2
        made = call(
            functools.partial(field_kernel, extent, 4, low, high),
            [piece] * (extent * count),
            [after, field],
            [pltpu.VMEM((size * (high - low) * rows, depth), F32)],
            moved=field.size * 3,
            loose=1,
        )
        return [list(made[j * count : (j + 1) * count]) for j in range(extent)]

    made = field_pieces(planes - 2, planes, field)
    if pairs > 1:
        others = field_pieces(0, planes - 2, made[0][0])
        made = [first + last for first, last in zip(others, made)]
    parts = [made[0]]
    for j in range(1, extent):
        parts.append([to_chan(value, j) for value in made[j]])
    (pack,) = call(
        pack_kernel,
        [jax.ShapeDtypeStruct((14, size, 4 * channels), BF16)],
        [made[0][0], jnp.transpose(first_weight, (1, 0, 2)), jnp.transpose(second_weight, (1, 0, 2))],
        loose=1,
    )
    packs = [pack] + [to_chan(pack, j) for j in range(1, extent)]
    whole = size % 16 == 0
    own_before, own_after = [], []
    if whole:
        own_before, own_after = [to_next(parts[0][-1])], [to_prev(parts[0][0])]
    grad_piece = jax.ShapeDtypeStruct((share + 4, 2, channels, depth), BF16)
    grads = call(
        functools.partial(grad_kernel, extent, 2),
        [grad_piece] * pairs,
        [pack, out_grad],
        [pltpu.VMEM((channels * planes * rows, depth), F32)],
        moved=out_grad.size * 4,
        loose=1,
    )
    matrix = jax.ShapeDtypeStruct((6 * channels, 12 * channels), BF16)
    half = jax.ShapeDtypeStruct((6 * channels, 6 * channels), BF16)
    first_wide, second_wide, first_back, second_back, from_above, from_below = call(
        functools.partial(matrix_kernel, extent),
        [matrix] * 4 + [half] * 2,
        packs,
        moved=matrix.size * 8,
    )
    if whole and extent > 1 and pairs > 1:
        parts[1][-1] = relayed(parts[1][-1], pack)
        parts[1][0] = relayed(relayed(parts[1][0], grads[0], *packs[1:]), own_after[0])
    by_pair = [[parts[j][p] for j in range(extent)] for p in range(pairs)]
    groups = extent
    if not whole:
        by_pair = [[jnp.concatenate(pieces, axis=2)] for pieces in by_pair]
        groups = 1
    before = own_before + [to_next(piece) for piece in by_pair[-1][len(own_before) :]]
    after = own_after + [to_prev(piece) for piece in by_pair[0][len(own_after) :]]
    fields = [before] + by_pair + [after]

    def many(count, rows_each):
        return [jax.ShapeDtypeStruct((rows_each, 2, channels, depth), BF16)] * count

    def flat(lists):
        return [piece for pieces in lists for piece in pieces]

    work = 27 * 2 * channels * channels * depth * 2
    space = 4 * channels * depth * share

    made = call(
        functools.partial(forward_kernel, groups, pairs, 0),
        many(2 * pairs, share + 6) + many(pairs - 1, share + 4),
        flat(fields[: pairs + 1]) + list(grads[: pairs - 1]) + [first_wide, second_wide],
        flops=work * (2 * pairs - 1) * share,
        moved=space * 4 * pairs,
    )
    hiddens, slopes, deltas = made[:pairs], made[pairs : 2 * pairs], made[2 * pairs :]
    made = call(
        functools.partial(forward_kernel, groups, 1, 1),
        many(2, share + 6) + many(1, share + 4),
        flat(fields[pairs:]) + [hiddens[-1], grads[-1], first_wide, second_wide],
        flops=work * 2 * share,
        moved=space * 6,
    )
    hiddens = list(hiddens) + [made[0]]
    slopes = list(slopes) + [made[1]]
    deltas = list(deltas) + [made[2]]
    delta_after = to_prev(deltas[0])
    delta_before = to_next(deltas[-1])

    raw = jax.ShapeDtypeStruct((extent, 7, size, 4 * channels), F32)
    portion = jax.ShapeDtypeStruct(raw.shape[1:], F32)
    total = pltpu.VMEM((12 * channels, 8 * channels), F32)

    def room(rows_each):
        return pltpu.VMEM((rows_each, 2, channels, depth), BF16)

    made = call(
        functools.partial(gradient_kernel, share, groups, extent, pairs),
        [raw] * 2 + many(pairs - 1, share + 2),
        hiddens + deltas + [second_back, from_above, from_below] + slopes + flat(fields),
        [room(share + 2), room(share + 2), total, total],
    )
    keep, send, inner = made[0], made[1], list(made[2:])
    def exchanged(made):
        pieces = [made[0]] + [None] * (extent - 1)
        for j in range(1, extent):
            pieces[extent - j] = to_chan(made[j], extent - j)
        return pieces

    def stepped(value, stride, shift=0):
        if shift % extent == 0:
            return lax.ppermute(value, "slab", [(i, i ^ stride) for i in range(slabs)])
        pairs_of = []
        for i in range(slabs):
            for k in range(extent):
                there = (i ^ stride) * extent + (k + shift) % extent
                pairs_of.append((i * extent + k, there))
        return lax.ppermute(value, ("slab", "chan"), pairs_of)

    (tail,) = call(
        tail_kernel,
        many(1, share + 2),
        [keep, second_back, deltas[-1], delta_after, slopes[-1]],
        flops=work * share,
        moved=space * 2,
        loose=1,
    )
    plain = slabs & (slabs - 1) == 0 and slabs >= 4
    if plain:
        kept = call(
            split_kernel, [portion] * extent, [tail, keep, stepped(send, 1)], loose=1
        )
        shares = [kept[0]] + [to_chan(kept[j], extent - j) for j in range(1, extent)]
        shares += [stepped(kept[j], 2, extent - j) for j in range(extent)]
        after = kept[0]
    else:
        after = keep
    made = call(
        functools.partial(field_kernel_back, pairs - 1, extent),
        [jax.ShapeDtypeStruct((share, planes, size, depth), BF16)] * extent,
        [after, second_back, first_back, delta_before, deltas[0], slopes[0]] + inner + [tail],
        [room(share + 2)],
        flops=work * (pairs + 2) * share,
        moved=space * 6,
        loose=1,
    )
    if plain:
        ahead = list(made[:1])
        (mine,) = call(
            functools.partial(add_kernel, len(ahead)), [portion], ahead + shares, loose=len(ahead)
        )
        made = list(made[:1]) + [relayed(value, mine) for value in made[1:]]
    pieces = exchanged(made)
    if plain:
        stride = 4
        while stride < slabs:
            got = [mine, stepped(mine, stride)]
            (mine,) = call(functools.partial(add_kernel, 0), [portion], got)
            stride *= 2
        other = stepped(mine, 1)
    else:
        mine, other = keep[0], send[0]
        for j in range(1, extent):
            mine, other = mine + to_chan(keep[j], extent - j), other + to_chan(send[j], extent - j)
        even = lax.rem(lax.axis_index("slab"), 2) == 0
        mine, other = jnp.where(even, mine, other), jnp.where(even, other, mine)
        mine, other = lax.psum((mine, other), "slab")
        mine, other = jnp.where(even, mine, other), jnp.where(even, other, mine)
    token, input_grad = call(
        functools.partial(merge_kernel, extent),
        [jax.ShapeDtypeStruct((8, 128), F32), jax.ShapeDtypeStruct(field.shape, BF16)],
        pieces,
        [pltpu.VMEM((rows * planes * size, depth), F32)],
        moved=4 * field.size,
    )
    first_grad, second_grad = call(
        functools.partial(finish_kernel, factor),
        [jax.ShapeDtypeStruct(by_tap, F32)] * 2,
        [token, mine, other],
        loose=1,
    )
    first_grad, second_grad = (jnp.transpose(g, (1, 0, 2)) for g in (first_grad, second_grad))
    return input_grad, first_grad, second_grad


def solution(mesh):
    placed = (
        P("chan", "slab", None, None),
        P(None, "slab", None, None),
        P("chan", None, None),
        P("chan", None, None),
    )
    return jax.shard_map(
        body,
        mesh=mesh,
        in_specs=placed,
        out_specs=(P("chan", "slab", None, None), P("chan", None, None), P("chan", None, None)),
        check_vma=False,
    )
```

```python
import functools
import math

import jax
import jax.numpy as jnp
from jax import lax
from jax.experimental import pallas as pl
from jax.experimental.pallas import tpu as pltpu
from jax.sharding import PartitionSpec as P

F32 = jnp.float32
BF16 = jnp.bfloat16
LIMIT = 16 * 1024 * 1024


def call(kernel, outs, args, scratch=(), flops=0, moved=0, loose=0, same=None, left=()):
    whole = pl.BlockSpec(memory_space=pltpu.VMEM)
    still = pl.BlockSpec(memory_space=pl.ANY)
    return pl.pallas_call(
        kernel,
        out_shape=outs,
        in_specs=[still] * loose + [whole] * (len(args) - loose),
        out_specs=[
            still if k in left or k in (same or {}).values() else whole for k in range(len(outs))
        ],
        input_output_aliases=same or {},
        scratch_shapes=list(scratch),
        compiler_params=pltpu.CompilerParams(vmem_limit_bytes=LIMIT),
        cost_estimate=pl.CostEstimate(flops=flops, bytes_accessed=moved, transcendentals=0),
    )(*args)


def in_blocks(count, body):
    block = max(k for k in range(1, 17) if count % k == 0)

    def several(r, _):
        for k in range(block):
            body(r * block + k)
        return 0

    lax.fori_loop(0, count // block, several, 0)
    for k in range(count // block * block, count):
        body(k)


def widened(x_ref, wide, low, high):
    count, _, rows = x_ref.shape[:3]

    def widen(i):
        for x in range(low, high):
            start = pl.multiple_of((i * (high - low) + x - low) * rows, 8)
            wide[pl.ds(start, rows), :] = x_ref[i, x].astype(F32)

    in_blocks(count, widen)


def turn(wide, outs, shape, base, length):
    count, planes, rows = shape

    def one(f):
        y = lax.rem(base + f, rows)
        for x in range(planes):
            tile = wide[pl.ds(x * rows + y, count, stride=planes * rows), :]
            outs[x // 2][f, x % 2] = tile.astype(BF16)

    in_blocks(length, one)


def field_kernel(extent, margin, low, high, after, x_ref, *refs):
    del after
    outs, wide = refs[:-1], refs[-1]
    count, _, rows = x_ref.shape[:3]
    planes = high - low
    pairs = planes // 2
    share = rows // extent
    widened(x_ref, wide, low, high)
    me = lax.axis_index("chan")
    for s in range(extent):
        base = lax.rem(me + s, extent) * share - margin + rows
        turn(
            wide,
            outs[s * pairs : (s + 1) * pairs],
            (count, planes, rows),
            base,
            share + 2 * margin,
        )


def pack_kernel(after, first, second, packed):
    del after
    blank = jnp.zeros(first.shape[1:], F32)
    for h in range(packed.shape[0]):
        parts = []
        for ref in (first, second):
            for t in (2 * h, 2 * h + 1):
                parts.append(ref[t].astype(F32) if t < ref.shape[0] else blank)
        packed[h] = jnp.concatenate(parts, axis=1).astype(BF16)


def grad_kernel(extent, margin, after, x_ref, *refs):
    del after
    outs, wide = refs[:-1], refs[-1]
    count, planes, rows = x_ref.shape[:3]
    share = rows // extent
    widened(x_ref, wide, 0, planes)
    base = lax.axis_index("chan") * share - margin + rows
    turn(wide, outs, (count, planes, rows), base, share + 2 * margin)


def matrix_kernel(extent, *refs):
    packs, outs = refs[:extent], refs[extent:]
    me = lax.axis_index("chan")
    quarter = packs[0].shape[2] // 4
    taps = []
    turned = []
    for h in range(packs[0].shape[0]):
        tiles = [pack[h].astype(F32) for pack in packs]
        own = jnp.concatenate(tiles, axis=0)
        fixed = []
        for g in range(extent):
            place = lax.rem(me + extent - g, extent)
            tile = tiles[0]
            for j in range(1, extent):
                tile = jnp.where(place == j, tiles[j], tile)
            fixed.append(tile)
        both = jnp.concatenate(
            [own[:, : 2 * quarter], jnp.concatenate(fixed, axis=0)[:, 2 * quarter :]], axis=1
        )
        across = both.T
        for side in range(2):
            taps.append(
                [both[:, k * quarter : (k + 1) * quarter] for k in (side, side + 2)]
            )
            turned.append(
                [across[k * quarter : (k + 1) * quarter] for k in (side, side + 2)]
            )
    channels = quarter
    blank = jnp.zeros((channels, channels), F32)
    for k in range(2):
        for out, blocks, flip in ((outs[k], turned, False), (outs[2 + k], taps, True)):
            for e in range(3):
                for x in range(2):
                    chunks = []
                    for pair in range(2):
                        for b in range(3):
                            for side in range(2):
                                a = 2 * pair + side - x
                                t = 9 * a + 3 * b + e
                                inside = 0 <= a <= 2
                                t = 26 - t if flip else t
                                chunks.append(blocks[t][k] if inside else blank)
                    low = (2 * e + x) * channels
                    line = jnp.concatenate(chunks, axis=1).astype(BF16)
                    out[low : low + channels, :] = line
                    if k == 1 and flip:
                        half = line.shape[1] // 2
                        outs[4][low : low + channels, :] = line[:, :half]
                        outs[5][low : low + channels, :] = line[:, half:]


def stacked(refs, row, count):
    if len(refs) == 1:
        part = refs[0][pl.ds(row, count)]
        return part.reshape(-1, part.shape[-1])
    parts = [ref[row + b, x] for b in range(count) for x in range(2) for ref in refs]
    return jnp.concatenate(parts, axis=0)


def taps(weight, inputs, row):
    sides = []
    for pair in inputs:
        for q in range(2):
            parts = [stacked(refs, row + q, 3) for refs in pair]
            sides.append(jnp.concatenate(parts, axis=0) if len(parts) > 1 else parts[0])
    lifted = jnp.dot(weight, jnp.concatenate(sides, axis=1), preferred_element_type=F32)
    third = lifted.shape[0] // 3
    depth = sides[0].shape[1]
    sums = []
    for k in range(len(sides)):
        side = lifted[:, k * depth : (k + 1) * depth]
        sums.append(
            side[third : 2 * third]
            + pltpu.roll(side[:third], 1, 1)
            + pltpu.roll(side[2 * third :], depth - 1, 1)
        )
    return [sums[2 * p : 2 * p + 2] for p in range(len(inputs))]


def neighbours(pairs):
    return list(zip(pairs[:-1], pairs[1:]))


def silu_parts(v):
    sig = jax.nn.sigmoid(v)
    return sig, sig * (1.0 + v * (1.0 - sig))


def forward_kernel(groups, fresh, ready, *refs):
    refs = list(refs)
    fields = [[refs.pop(0) for _ in range(groups)] for _ in range(fresh + 1)]
    hiddens = [refs.pop(0) for _ in range(ready)]
    count = fresh + ready - 1
    grads = [refs.pop(0) for _ in range(count)]
    first, second = refs.pop(0), refs.pop(0)
    made = [refs.pop(0) for _ in range(fresh)]
    slopes = [refs.pop(0) for _ in range(fresh)]
    deltas = refs
    hiddens = hiddens + made

    def one(r):
        row = 2 * r
        for p, sums in enumerate(taps(first[...], neighbours(fields), row)):
            for q, v in enumerate(sums):
                sig, slope = silu_parts(v)
                shape = made[p].shape[1:]
                made[p][row + q] = (v * sig).astype(BF16).reshape(shape)
                slopes[p][row + q] = slope.astype(BF16).reshape(shape)

    in_blocks(made[0].shape[0] // 2, one)

    def two(r):
        row = 2 * r
        for p, sums in enumerate(taps(second[...], neighbours([[ref] for ref in hiddens]), row)):
            for q, v in enumerate(sums):
                shape = deltas[p].shape[1:]
                out_grad = grads[p][row + q].astype(F32)
                slope = silu_parts(v)[1].reshape(shape)
                deltas[p][row + q] = (out_grad * slope).astype(BF16)

    if count > 0:
        in_blocks(deltas[0].shape[0] // 2, two)


def planes_of(pairs):
    return [(refs, x) for refs in pairs for x in range(2)]


def weight_loop(total, pieces, first_row, deltas, delta_row, count):
    blocks = [k for k in range(1, 13) if count // 2 % k == 0 and k * len(deltas) <= 12]
    together = max(blocks, default=1)

    def product(r):
        left, right = [], []
        for k in range(together):
            row = 2 * (r * together + k)
            for x, ((delta,), place) in enumerate(deltas):
                rows = []
                for q in range(2):
                    wide = delta[delta_row + row + q, place]
                    depth = wide.shape[1]
                    rows += [pltpu.roll(wide, depth - 1, 1), wide, pltpu.roll(wide, 1, 1)]
                    rows.append(jnp.zeros_like(wide))
                right.append(jnp.concatenate(rows, axis=0))
                rows = []
                for refs, side in pieces[x : x + 3]:
                    for b in range(4):
                        for ref in refs:
                            rows.append(ref[first_row + row + b, side])
                left.append(jnp.concatenate(rows, axis=0))
        return lax.dot_general(
            jnp.concatenate(left, axis=1),
            jnp.concatenate(right, axis=1),
            (((1,), (1,)), ((), ())),
            preferred_element_type=F32,
        )

    value = total[...]
    for r in range(count // 2 // together):
        value = value + product(r)
    total[...] = value


def weight_fold(total, size):
    lanes = total.shape[1] // 2
    channels = total.shape[0] // 12
    upper, lower = total[:, :lanes], total[:, lanes:]
    groups = []
    for g in range(channels // size):
        taps_of = []
        for a in range(3):
            for b in range(3):
                start = (4 * a + b) * channels + g * size
                part = (
                    upper[start : start + size]
                    + lower[start + channels : start + channels + size]
                )
                taps_of += [part[:, e * channels : (e + 1) * channels] for e in range(3)]
        blank = jnp.zeros((size, channels), F32)
        taps_of.append(blank)
        groups.append([jnp.concatenate(taps_of[4 * h : 4 * h + 4], axis=1) for h in range(7)])
    return groups


def first_deltas(weight, inputs, slopes, firsts):
    def one(r):
        row = 2 * r
        for p, sums in enumerate(taps(weight[...], inputs, row)):
            for q, v in enumerate(sums):
                shape = firsts[p].shape[1:]
                slope = slopes[p][row + 2 + q].astype(F32)
                firsts[p][row + q] = (v.reshape(shape) * slope).astype(BF16)

    in_blocks(firsts[0].shape[0] // 2, one)


def gradient_kernel(share, groups, extent, pairs, *refs):
    refs = list(refs)
    hiddens = [[refs.pop(0)] for _ in range(pairs + 1)]
    deltas = [[refs.pop(0)] for _ in range(pairs)]
    weight, from_above, from_below = [refs.pop(0) for _ in range(3)]
    slopes = [refs.pop(0) for _ in range(pairs + 1)]
    fields = [[refs.pop(0) for _ in range(groups)] for _ in range(pairs + 2)]
    keep, send = refs.pop(0), refs.pop(0)
    inner = [refs.pop(0) for _ in range(pairs - 1)]
    head, tail, second_total, first_total = refs
    second_total[...] = jnp.zeros_like(second_total)
    first_total[...] = jnp.zeros_like(first_total)
    weight_loop(second_total, planes_of(hiddens), 2, planes_of(deltas), 2, share)
    firsts = [head] + inner + [tail]
    first_deltas(from_below, [(deltas[0],)], slopes[:1], [head])
    if inner:
        first_deltas(weight, neighbours(deltas), slopes[1:-1], inner)
    first_deltas(from_above, [(deltas[-1],)], slopes[-1:], [tail])
    parts = planes_of([[first] for first in firsts])
    weight_loop(first_total, planes_of(fields), 3, parts, 1, share)
    halves, size = keep.shape[1:3]
    me = lax.axis_index("chan")
    of_first = weight_fold(first_total, size)
    of_second = weight_fold(second_total, size)

    def place(ours, theirs):
        for g in range(extent):
            there = lax.rem(me + extent - g, extent)
            for h in range(halves):
                ours[g, h] = of_first[g][h]
                theirs[there, h] = of_second[g][h]

    odd = lax.rem(lax.axis_index("slab"), 2)

    @pl.when(odd == 0)
    def _():
        place(keep, send)

    @pl.when(odd == 1)
    def _():
        place(send, keep)


def tail_kernel(after, weight, above, below, slope, first):
    del after
    first_deltas(weight, [([above], [below])], [slope], [first])


def field_kernel_back(inner, groups, after, *refs):
    del after
    refs = list(refs)
    back, weight = refs.pop(0), refs.pop(0)
    above, below = [[refs.pop(0)] for _ in range(2)]
    slope = refs.pop(0)
    later = [refs.pop(0) for _ in range(inner + 1)]
    outs, head = refs[:groups], refs[groups]
    first_deltas(back, [(above, below)], [slope], [head])
    firsts = [head] + later

    def one(r):
        row = 2 * r
        size = outs[0].shape[2]
        channels = len(outs) * size
        for p, sums in enumerate(taps(weight[...], neighbours([[ref] for ref in firsts]), row)):
            for q, v in enumerate(sums):
                for x in range(2):
                    for j, out in enumerate(outs):
                        low = x * channels + j * size
                        out[row + q, 2 * p + x] = v[low : low + size].astype(BF16)

    in_blocks(outs[0].shape[0] // 2, one)


def split_kernel(after, one, two, *outs):
    del after
    for g, out in enumerate(outs):
        out[...] = one[g] + two[g]


def add_kernel(ahead, *refs):
    values = [ref[...] for ref in refs[ahead:-1]]
    while len(values) > 1:
        values = [sum(values[k + 1 : k + 2], values[k]) for k in range(0, len(values), 2)]
    refs[-1][...] = values[0]


def relay_kernel(*refs):
    pass


def finish_kernel(factor, after, mine, other, first, second):
    del after
    channels = first.shape[2]

    def place(ours, theirs):
        for result, sums in ((ours, mine), (theirs, other)):
            for t in range(27):
                low = t % 4 * channels
                result[t] = sums[t // 4, :, low : low + channels] * factor

    odd = lax.rem(lax.axis_index("slab"), 2)

    @pl.when(odd == 0)
    def _():
        place(first, second)

    @pl.when(odd == 1)
    def _():
        place(second, first)


def merge_kernel(extent, *refs):
    pieces, (token, out, wide, held, done) = refs[:-5], refs[-5:]
    token[...] = jnp.zeros_like(token)
    size, planes, rows = out.shape[:3]
    share = rows // extent
    me = lax.axis_index("chan")
    for j in range(extent):
        base = lax.rem(me + extent - j, extent) * share

        def widen(f, mine=pieces[j::extent], base=base):
            x = 0
            for piece in mine:
                for k in range(piece.shape[1]):
                    start = ((base + f) * planes + x) * size
                    start = pl.multiple_of(start, 8) if size % 8 == 0 else start
                    wide[pl.ds(start, size), :] = piece[f, k].astype(F32)
                    x += 1

        in_blocks(share, widen)

    cuts = done.shape[0]
    copies = []
    for c in range(cuts):
        part = pl.ds(c * size // cuts, size // cuts)
        for i in range(c * size // cuts, (c + 1) * size // cuts):
            for x in range(planes):
                tile = wide[pl.ds(x * size + i, rows, stride=planes * size), :]
                held[i, x] = tile.astype(BF16)
        copies.append(pltpu.make_async_copy(held.at[part], out.at[part], done.at[c]))
        copies[-1].start()
    for copy in copies:
        copy.wait()


def body(field, out_grad, first_weight, second_weight):
    extent = lax.axis_size("chan")
    slabs = lax.axis_size("slab")
    me = lax.axis_index("chan")
    size, planes, rows, depth = field.shape
    channels = size * extent
    pairs = planes // 2
    share = rows // extent
    factor = 1.0 / math.sqrt(planes * slabs * rows * depth)

    def to_chan(value, shift):
        return lax.ppermute(value, "chan", [(i, (i + shift) % extent) for i in range(extent)])

    def to_next(value):
        return lax.ppermute(value, "slab", [(i, (i + 1) % slabs) for i in range(slabs)])

    def to_prev(value):
        return lax.ppermute(value, "slab", [((i + 1) % slabs, i) for i in range(slabs)])

    def relayed(value, *others):
        shape = jax.ShapeDtypeStruct(value.shape, value.dtype)
        early = [value, *others]
        return call(relay_kernel, [shape], early, loose=len(early), same={0: 0})[0]

    piece = jax.ShapeDtypeStruct((share + 8, 2, size, depth), BF16)
    by_tap = (27, size, channels)
    def field_pieces(low, high, after):
        count = (high - low) // 2
        made = call(
            functools.partial(field_kernel, extent, 4, low, high),
            [piece] * (extent * count),
            [after, field],
            [pltpu.VMEM((size * (high - low) * rows, depth), F32)],
            moved=field.size * 3,
            loose=1,
        )
        return [list(made[j * count : (j + 1) * count]) for j in range(extent)]

    made = field_pieces(planes - 2, planes, field)
    if pairs > 1:
        others = field_pieces(0, planes - 2, made[0][0])
        made = [first + last for first, last in zip(others, made)]
    parts = [made[0]]
    for j in range(1, extent):
        parts.append([to_chan(value, j) for value in made[j]])
    (pack,) = call(
        pack_kernel,
        [jax.ShapeDtypeStruct((14, size, 4 * channels), BF16)],
        [made[0][0], jnp.transpose(first_weight, (1, 0, 2)), jnp.transpose(second_weight, (1, 0, 2))],
        loose=1,
    )
    packs = [pack] + [to_chan(pack, j) for j in range(1, extent)]
    whole = size % 16 == 0
    own_before, own_after = [], []
    if whole:
        own_before, own_after = [to_next(parts[0][-1])], [to_prev(parts[0][0])]
    grad_piece = jax.ShapeDtypeStruct((share + 4, 2, channels, depth), BF16)
    grads = call(
        functools.partial(grad_kernel, extent, 2),
        [grad_piece] * pairs,
        [pack, out_grad],
        [pltpu.VMEM((channels * planes * rows, depth), F32)],
        moved=out_grad.size * 4,
        loose=1,
    )
    matrix = jax.ShapeDtypeStruct((6 * channels, 12 * channels), BF16)
    half = jax.ShapeDtypeStruct((6 * channels, 6 * channels), BF16)
    first_wide, second_wide, first_back, second_back, from_above, from_below = call(
        functools.partial(matrix_kernel, extent),
        [matrix] * 4 + [half] * 2,
        packs,
        moved=matrix.size * 8,
    )
    if whole and extent > 1 and pairs > 1:
        parts[1][-1] = relayed(parts[1][-1], pack)
        parts[1][0] = relayed(relayed(parts[1][0], grads[0], *packs[1:]), own_after[0])
    by_pair = [[parts[j][p] for j in range(extent)] for p in range(pairs)]
    groups = extent
    if not whole:
        by_pair = [[jnp.concatenate(pieces, axis=2)] for pieces in by_pair]
        groups = 1
    before = own_before + [to_next(piece) for piece in by_pair[-1][len(own_before) :]]
    after = own_after + [to_prev(piece) for piece in by_pair[0][len(own_after) :]]
    fields = [before] + by_pair + [after]

    def many(count, rows_each):
        return [jax.ShapeDtypeStruct((rows_each, 2, channels, depth), BF16)] * count

    def flat(lists):
        return [piece for pieces in lists for piece in pieces]

    work = 27 * 2 * channels * channels * depth * 2
    space = 4 * channels * depth * share

    made = call(
        functools.partial(forward_kernel, groups, pairs, 0),
        many(2 * pairs, share + 6) + many(pairs - 1, share + 4),
        flat(fields[: pairs + 1]) + list(grads[: pairs - 1]) + [first_wide, second_wide],
        flops=work * (2 * pairs - 1) * share,
        moved=space * 4 * pairs,
    )
    hiddens, slopes, deltas = made[:pairs], made[pairs : 2 * pairs], made[2 * pairs :]
    made = call(
        functools.partial(forward_kernel, groups, 1, 1),
        many(2, share + 6) + many(1, share + 4),
        flat(fields[pairs:]) + [hiddens[-1], grads[-1], first_wide, second_wide],
        flops=work * 2 * share,
        moved=space * 6,
    )
    hiddens = list(hiddens) + [made[0]]
    slopes = list(slopes) + [made[1]]
    deltas = list(deltas) + [made[2]]
    delta_after = to_prev(deltas[0])
    delta_before = to_next(deltas[-1])

    raw = jax.ShapeDtypeStruct((extent, 7, size, 4 * channels), F32)
    portion = jax.ShapeDtypeStruct(raw.shape[1:], F32)
    total = pltpu.VMEM((12 * channels, 8 * channels), F32)

    def room(rows_each):
        return pltpu.VMEM((rows_each, 2, channels, depth), BF16)

    made = call(
        functools.partial(gradient_kernel, share, groups, extent, pairs),
        [raw] * 2 + many(pairs - 1, share + 2),
        hiddens + deltas + [second_back, from_above, from_below] + slopes + flat(fields),
        [room(share + 2), room(share + 2), total, total],
    )
    keep, send, inner = made[0], made[1], list(made[2:])
    def exchanged(made):
        pieces = [made[0]] + [None] * (extent - 1)
        for j in range(1, extent):
            pieces[extent - j] = to_chan(made[j], extent - j)
        return pieces

    def stepped(value, stride, shift=0):
        if shift % extent == 0:
            return lax.ppermute(value, "slab", [(i, i ^ stride) for i in range(slabs)])
        pairs_of = []
        for i in range(slabs):
            for k in range(extent):
                there = (i ^ stride) * extent + (k + shift) % extent
                pairs_of.append((i * extent + k, there))
        return lax.ppermute(value, ("slab", "chan"), pairs_of)

    (tail,) = call(
        tail_kernel,
        many(1, share + 2),
        [keep, second_back, deltas[-1], delta_after, slopes[-1]],
        flops=work * share,
        moved=space * 2,
        loose=1,
    )
    plain = slabs & (slabs - 1) == 0 and slabs >= 4
    if plain:
        kept = call(
            split_kernel, [portion] * extent, [tail, keep, stepped(send, 1)], loose=1
        )
        shares = [kept[0]] + [to_chan(kept[j], extent - j) for j in range(1, extent)]
        shares += [stepped(kept[j], 2, extent - j) for j in range(extent)]
        after = kept[0]
    else:
        after = keep
    made = call(
        functools.partial(field_kernel_back, pairs - 1, extent),
        [jax.ShapeDtypeStruct((share, planes, size, depth), BF16)] * extent,
        [after, second_back, first_back, delta_before, deltas[0], slopes[0]] + inner + [tail],
        [room(share + 2)],
        flops=work * (pairs + 2) * share,
        moved=space * 6,
        loose=1,
    )
    if plain:
        ahead = list(made[:1])
        (mine,) = call(
            functools.partial(add_kernel, len(ahead)), [portion], ahead + shares, loose=len(ahead)
        )
        made = list(made[:1]) + [relayed(value, mine) for value in made[1:]]
    pieces = exchanged(made)
    if plain:
        stride = 4
        while stride < slabs:
            got = [mine, stepped(mine, stride)]
            (mine,) = call(functools.partial(add_kernel, 0), [portion], got)
            stride *= 2
        other = stepped(mine, 1)
    else:
        mine, other = keep[0], send[0]
        for j in range(1, extent):
            mine, other = mine + to_chan(keep[j], extent - j), other + to_chan(send[j], extent - j)
        even = lax.rem(lax.axis_index("slab"), 2) == 0
        mine, other = jnp.where(even, mine, other), jnp.where(even, other, mine)
        mine, other = lax.psum((mine, other), "slab")
        mine, other = jnp.where(even, mine, other), jnp.where(even, other, mine)
    token, input_grad = call(
        functools.partial(merge_kernel, extent),
        [jax.ShapeDtypeStruct((8, 128), F32), jax.ShapeDtypeStruct(field.shape, BF16)],
        pieces,
        [
            pltpu.VMEM((rows * planes * size, depth), F32),
            pltpu.VMEM(field.shape, BF16),
            pltpu.SemaphoreType.DMA((4 if size % 4 == 0 else 1,)),
        ],
        moved=4 * field.size,
        left=(1,),
    )
    first_grad, second_grad = call(
        functools.partial(finish_kernel, factor),
        [jax.ShapeDtypeStruct(by_tap, F32)] * 2,
        [token, mine, other],
        loose=1,
    )
    first_grad, second_grad = (jnp.transpose(g, (1, 0, 2)) for g in (first_grad, second_grad))
    return input_grad, first_grad, second_grad


def solution(mesh):
    placed = (
        P("chan", "slab", None, None),
        P(None, "slab", None, None),
        P("chan", None, None),
        P("chan", None, None),
    )
    return jax.shard_map(
        body,
        mesh=mesh,
        in_specs=placed,
        out_specs=(P("chan", "slab", None, None), P("chan", None, None), P("chan", None, None)),
        check_vma=False,
    )
```

```python
import functools
import math

import jax
import jax.numpy as jnp
from jax import lax
from jax.experimental import pallas as pl
from jax.experimental.pallas import tpu as pltpu
from jax.sharding import PartitionSpec as P

F32 = jnp.float32
BF16 = jnp.bfloat16
LIMIT = 16 * 1024 * 1024


def call(kernel, outs, args, scratch=(), flops=0, moved=0, loose=0, same=None, left=()):
    whole = pl.BlockSpec(memory_space=pltpu.VMEM)
    still = pl.BlockSpec(memory_space=pl.ANY)
    return pl.pallas_call(
        kernel,
        out_shape=outs,
        in_specs=[still] * loose + [whole] * (len(args) - loose),
        out_specs=[
            still if k in left or k in (same or {}).values() else whole for k in range(len(outs))
        ],
        input_output_aliases=same or {},
        scratch_shapes=list(scratch),
        compiler_params=pltpu.CompilerParams(vmem_limit_bytes=LIMIT),
        cost_estimate=pl.CostEstimate(flops=flops, bytes_accessed=moved, transcendentals=0),
    )(*args)


def in_blocks(count, body):
    block = max(k for k in range(1, 17) if count % k == 0)

    def several(r, _):
        for k in range(block):
            body(r * block + k)
        return 0

    lax.fori_loop(0, count // block, several, 0)
    for k in range(count // block * block, count):
        body(k)


def widened(x_ref, wide, low, high):
    count, _, rows = x_ref.shape[:3]

    def widen(i):
        for x in range(low, high):
            start = pl.multiple_of((i * (high - low) + x - low) * rows, 8)
            wide[pl.ds(start, rows), :] = x_ref[i, x].astype(F32)

    in_blocks(count, widen)


def turn(wide, outs, shape, base, length):
    count, planes, rows = shape

    def one(f):
        y = lax.rem(base + f, rows)
        for x in range(planes):
            tile = wide[pl.ds(x * rows + y, count, stride=planes * rows), :]
            outs[x // 2][f, x % 2] = tile.astype(BF16)

    in_blocks(length, one)


def field_kernel(extent, margin, low, high, after, x_ref, *refs):
    del after
    outs, wide = refs[:-1], refs[-1]
    count, _, rows = x_ref.shape[:3]
    planes = high - low
    pairs = planes // 2
    share = rows // extent
    widened(x_ref, wide, low, high)
    me = lax.axis_index("chan")
    for s in range(extent):
        base = lax.rem(me + s, extent) * share - margin + rows
        turn(
            wide,
            outs[s * pairs : (s + 1) * pairs],
            (count, planes, rows),
            base,
            share + 2 * margin,
        )


def pack_kernel(after, first, second, packed):
    del after
    blank = jnp.zeros(first.shape[1:], F32)
    for h in range(packed.shape[0]):
        parts = []
        for ref in (first, second):
            for t in (2 * h, 2 * h + 1):
                parts.append(ref[t].astype(F32) if t < ref.shape[0] else blank)
        packed[h] = jnp.concatenate(parts, axis=1).astype(BF16)


def grad_kernel(extent, margin, after, x_ref, *refs):
    del after
    outs, wide = refs[:-1], refs[-1]
    count, planes, rows = x_ref.shape[:3]
    share = rows // extent
    widened(x_ref, wide, 0, planes)
    base = lax.axis_index("chan") * share - margin + rows
    turn(wide, outs, (count, planes, rows), base, share + 2 * margin)


def matrix_kernel(extent, *refs):
    packs, outs = refs[:extent], refs[extent:]
    me = lax.axis_index("chan")
    quarter = packs[0].shape[2] // 4
    taps = []
    turned = []
    for h in range(packs[0].shape[0]):
        tiles = [pack[h].astype(F32) for pack in packs]
        own = jnp.concatenate(tiles, axis=0)
        fixed = []
        for g in range(extent):
            place = lax.rem(me + extent - g, extent)
            tile = tiles[0]
            for j in range(1, extent):
                tile = jnp.where(place == j, tiles[j], tile)
            fixed.append(tile)
        both = jnp.concatenate(
            [own[:, : 2 * quarter], jnp.concatenate(fixed, axis=0)[:, 2 * quarter :]], axis=1
        )
        across = both.T
        for side in range(2):
            taps.append(
                [both[:, k * quarter : (k + 1) * quarter] for k in (side, side + 2)]
            )
            turned.append(
                [across[k * quarter : (k + 1) * quarter] for k in (side, side + 2)]
            )
    channels = quarter
    blank = jnp.zeros((channels, channels), F32)
    for k in range(2):
        for out, blocks, flip in ((outs[k], turned, False), (outs[2 + k], taps, True)):
            for e in range(3):
                for x in range(2):
                    chunks = []
                    for pair in range(2):
                        for b in range(3):
                            for side in range(2):
                                a = 2 * pair + side - x
                                t = 9 * a + 3 * b + e
                                inside = 0 <= a <= 2
                                t = 26 - t if flip else t
                                chunks.append(blocks[t][k] if inside else blank)
                    low = (2 * e + x) * channels
                    line = jnp.concatenate(chunks, axis=1).astype(BF16)
                    out[low : low + channels, :] = line
                    if k == 1 and flip:
                        half = line.shape[1] // 2
                        outs[4][low : low + channels, :] = line[:, :half]
                        outs[5][low : low + channels, :] = line[:, half:]


def stacked(refs, row, count):
    if len(refs) == 1:
        part = refs[0][pl.ds(row, count)]
        return part.reshape(-1, part.shape[-1])
    parts = [ref[row + b, x] for b in range(count) for x in range(2) for ref in refs]
    return jnp.concatenate(parts, axis=0)


def taps(weight, inputs, row):
    sides = []
    for pair in inputs:
        for q in range(2):
            parts = [stacked(refs, row + q, 3) for refs in pair]
            sides.append(jnp.concatenate(parts, axis=0) if len(parts) > 1 else parts[0])
    lifted = jnp.dot(weight, jnp.concatenate(sides, axis=1), preferred_element_type=F32)
    third = lifted.shape[0] // 3
    depth = sides[0].shape[1]
    sums = []
    for k in range(len(sides)):
        side = lifted[:, k * depth : (k + 1) * depth]
        sums.append(
            side[third : 2 * third]
            + pltpu.roll(side[:third], 1, 1)
            + pltpu.roll(side[2 * third :], depth - 1, 1)
        )
    return [sums[2 * p : 2 * p + 2] for p in range(len(inputs))]


def neighbours(pairs):
    return list(zip(pairs[:-1], pairs[1:]))


def silu_parts(v):
    sig = jax.nn.sigmoid(v)
    return sig, sig * (1.0 + v * (1.0 - sig))


def forward_kernel(groups, fresh, ready, *refs):
    refs = list(refs)
    fields = [[refs.pop(0) for _ in range(groups)] for _ in range(fresh + 1)]
    hiddens = [refs.pop(0) for _ in range(ready)]
    count = fresh + ready - 1
    grads = [refs.pop(0) for _ in range(count)]
    first, second = refs.pop(0), refs.pop(0)
    made = [refs.pop(0) for _ in range(fresh)]
    slopes = [refs.pop(0) for _ in range(fresh)]
    deltas = refs
    hiddens = hiddens + made

    def one(r):
        row = 2 * r
        for p, sums in enumerate(taps(first[...], neighbours(fields), row)):
            for q, v in enumerate(sums):
                sig, slope = silu_parts(v)
                shape = made[p].shape[1:]
                made[p][row + q] = (v * sig).astype(BF16).reshape(shape)
                slopes[p][row + q] = slope.astype(BF16).reshape(shape)

    in_blocks(made[0].shape[0] // 2, one)

    def two(r):
        row = 2 * r
        for p, sums in enumerate(taps(second[...], neighbours([[ref] for ref in hiddens]), row)):
            for q, v in enumerate(sums):
                shape = deltas[p].shape[1:]
                out_grad = grads[p][row + q].astype(F32)
                slope = silu_parts(v)[1].reshape(shape)
                deltas[p][row + q] = (out_grad * slope).astype(BF16)

    if count > 0:
        in_blocks(deltas[0].shape[0] // 2, two)


def planes_of(pairs):
    return [(refs, x) for refs in pairs for x in range(2)]


def weight_loop(total, pieces, first_row, deltas, delta_row, count):
    blocks = [k for k in range(1, 13) if count // 2 % k == 0 and k * len(deltas) <= 12]
    together = max(blocks, default=1)

    def product(r):
        left, right = [], []
        for k in range(together):
            row = 2 * (r * together + k)
            for x, ((delta,), place) in enumerate(deltas):
                rows = []
                for q in range(2):
                    wide = delta[delta_row + row + q, place]
                    depth = wide.shape[1]
                    rows += [pltpu.roll(wide, depth - 1, 1), wide, pltpu.roll(wide, 1, 1)]
                    rows.append(jnp.zeros_like(wide))
                right.append(jnp.concatenate(rows, axis=0))
                rows = []
                for refs, side in pieces[x : x + 3]:
                    for b in range(4):
                        for ref in refs:
                            rows.append(ref[first_row + row + b, side])
                left.append(jnp.concatenate(rows, axis=0))
        return lax.dot_general(
            jnp.concatenate(left, axis=1),
            jnp.concatenate(right, axis=1),
            (((1,), (1,)), ((), ())),
            preferred_element_type=F32,
        )

    value = total[...]
    for r in range(count // 2 // together):
        value = value + product(r)
    total[...] = value


def weight_fold(total, size):
    lanes = total.shape[1] // 2
    channels = total.shape[0] // 12
    upper, lower = total[:, :lanes], total[:, lanes:]
    groups = []
    for g in range(channels // size):
        taps_of = []
        for a in range(3):
            for b in range(3):
                start = (4 * a + b) * channels + g * size
                part = (
                    upper[start : start + size]
                    + lower[start + channels : start + channels + size]
                )
                taps_of += [part[:, e * channels : (e + 1) * channels] for e in range(3)]
        blank = jnp.zeros((size, channels), F32)
        taps_of.append(blank)
        groups.append([jnp.concatenate(taps_of[4 * h : 4 * h + 4], axis=1) for h in range(7)])
    return groups


def first_deltas(weight, inputs, slopes, firsts):
    def one(r):
        row = 2 * r
        for p, sums in enumerate(taps(weight[...], inputs, row)):
            for q, v in enumerate(sums):
                shape = firsts[p].shape[1:]
                slope = slopes[p][row + 2 + q].astype(F32)
                firsts[p][row + q] = (v.reshape(shape) * slope).astype(BF16)

    in_blocks(firsts[0].shape[0] // 2, one)


def gradient_kernel(share, groups, extent, pairs, *refs):
    refs = list(refs)
    hiddens = [[refs.pop(0)] for _ in range(pairs + 1)]
    deltas = [[refs.pop(0)] for _ in range(pairs)]
    weight, from_above, from_below = [refs.pop(0) for _ in range(3)]
    slopes = [refs.pop(0) for _ in range(pairs + 1)]
    fields = [[refs.pop(0) for _ in range(groups)] for _ in range(pairs + 2)]
    keep, send = refs.pop(0), refs.pop(0)
    inner = [refs.pop(0) for _ in range(pairs - 1)]
    head, tail, second_total, first_total = refs
    second_total[...] = jnp.zeros_like(second_total)
    first_total[...] = jnp.zeros_like(first_total)
    weight_loop(second_total, planes_of(hiddens), 2, planes_of(deltas), 2, share)
    firsts = [head] + inner + [tail]
    first_deltas(from_below, [(deltas[0],)], slopes[:1], [head])
    if inner:
        first_deltas(weight, neighbours(deltas), slopes[1:-1], inner)
    first_deltas(from_above, [(deltas[-1],)], slopes[-1:], [tail])
    parts = planes_of([[first] for first in firsts])
    weight_loop(first_total, planes_of(fields), 3, parts, 1, share)
    halves, size = keep.shape[1:3]
    me = lax.axis_index("chan")
    of_first = weight_fold(first_total, size)
    of_second = weight_fold(second_total, size)

    def place(ours, theirs):
        for g in range(extent):
            there = lax.rem(me + extent - g, extent)
            for h in range(halves):
                ours[g, h] = of_first[g][h]
                theirs[there, h] = of_second[g][h]

    odd = lax.rem(lax.axis_index("slab"), 2)

    @pl.when(odd == 0)
    def _():
        place(keep, send)

    @pl.when(odd == 1)
    def _():
        place(send, keep)


def tail_kernel(after, weight, above, below, slope, first):
    del after
    first_deltas(weight, [([above], [below])], [slope], [first])


def field_kernel_back(inner, groups, after, *refs):
    del after
    refs = list(refs)
    back, weight = refs.pop(0), refs.pop(0)
    above, below = [[refs.pop(0)] for _ in range(2)]
    slope = refs.pop(0)
    later = [refs.pop(0) for _ in range(inner + 1)]
    outs, head = refs[:groups], refs[groups]
    first_deltas(back, [(above, below)], [slope], [head])
    firsts = [head] + later

    def one(r):
        row = 2 * r
        size = outs[0].shape[2]
        channels = len(outs) * size
        for p, sums in enumerate(taps(weight[...], neighbours([[ref] for ref in firsts]), row)):
            for q, v in enumerate(sums):
                for x in range(2):
                    for j, out in enumerate(outs):
                        low = x * channels + j * size
                        out[row + q, 2 * p + x] = v[low : low + size].astype(BF16)

    in_blocks(outs[0].shape[0] // 2, one)


def split_kernel(after, one, two, *outs):
    del after
    for g, out in enumerate(outs):
        out[...] = one[g] + two[g]


def add_kernel(ahead, *refs):
    values = [ref[...] for ref in refs[ahead:-1]]
    while len(values) > 1:
        values = [sum(values[k + 1 : k + 2], values[k]) for k in range(0, len(values), 2)]
    refs[-1][...] = values[0]


def relay_kernel(*refs):
    pass


def by_taps(sums, result, factor):
    channels = result.shape[2]
    for t in range(27):
        low = t % 4 * channels
        result[t] = sums[t // 4, :, low : low + channels] * factor


def finish_kernel(factor, first_in, second_in, other, first, second, held, done):
    del first_in, second_in
    by_taps(other, held, factor)
    odd = lax.rem(lax.axis_index("slab"), 2)

    @pl.when(odd == 0)
    def _():
        copy = pltpu.make_async_copy(held, second, done.at[0])
        copy.start()
        copy.wait()

    @pl.when(odd == 1)
    def _():
        copy = pltpu.make_async_copy(held, first, done.at[0])
        copy.start()
        copy.wait()


def merge_kernel(extent, factor, mine, *refs):
    pieces, (out, first, second, wide, held, own, done, own_done) = refs[:-8], refs[-8:]
    by_taps(mine, own, factor)
    odd = lax.rem(lax.axis_index("slab"), 2)

    @pl.when(odd == 0)
    def _():
        pltpu.make_async_copy(own, first, own_done.at[0]).start()

    @pl.when(odd == 1)
    def _():
        pltpu.make_async_copy(own, second, own_done.at[0]).start()

    size, planes, rows = out.shape[:3]
    share = rows // extent
    me = lax.axis_index("chan")
    for j in range(extent):
        base = lax.rem(me + extent - j, extent) * share

        def widen(f, mine=pieces[j::extent], base=base):
            x = 0
            for piece in mine:
                for k in range(piece.shape[1]):
                    start = ((base + f) * planes + x) * size
                    start = pl.multiple_of(start, 8) if size % 8 == 0 else start
                    wide[pl.ds(start, size), :] = piece[f, k].astype(F32)
                    x += 1

        in_blocks(share, widen)

    cuts = done.shape[0]
    copies = []
    for c in range(cuts):
        part = pl.ds(c * size // cuts, size // cuts)
        for i in range(c * size // cuts, (c + 1) * size // cuts):
            for x in range(planes):
                tile = wide[pl.ds(x * size + i, rows, stride=planes * size), :]
                held[i, x] = tile.astype(BF16)
        copies.append(pltpu.make_async_copy(held.at[part], out.at[part], done.at[c]))
        copies[-1].start()
    for copy in copies:
        copy.wait()

    @pl.when(odd == 0)
    def _():
        pltpu.make_async_copy(own, first, own_done.at[0]).wait()

    @pl.when(odd == 1)
    def _():
        pltpu.make_async_copy(own, second, own_done.at[0]).wait()


def body(field, out_grad, first_weight, second_weight):
    extent = lax.axis_size("chan")
    slabs = lax.axis_size("slab")
    me = lax.axis_index("chan")
    size, planes, rows, depth = field.shape
    channels = size * extent
    pairs = planes // 2
    share = rows // extent
    factor = 1.0 / math.sqrt(planes * slabs * rows * depth)

    def to_chan(value, shift):
        return lax.ppermute(value, "chan", [(i, (i + shift) % extent) for i in range(extent)])

    def to_next(value):
        return lax.ppermute(value, "slab", [(i, (i + 1) % slabs) for i in range(slabs)])

    def to_prev(value):
        return lax.ppermute(value, "slab", [((i + 1) % slabs, i) for i in range(slabs)])

    def relayed(value, *others):
        shape = jax.ShapeDtypeStruct(value.shape, value.dtype)
        early = [value, *others]
        return call(relay_kernel, [shape], early, loose=len(early), same={0: 0})[0]

    piece = jax.ShapeDtypeStruct((share + 8, 2, size, depth), BF16)
    by_tap = (27, size, channels)
    def field_pieces(low, high, after):
        count = (high - low) // 2
        made = call(
            functools.partial(field_kernel, extent, 4, low, high),
            [piece] * (extent * count),
            [after, field],
            [pltpu.VMEM((size * (high - low) * rows, depth), F32)],
            moved=field.size * 3,
            loose=1,
        )
        return [list(made[j * count : (j + 1) * count]) for j in range(extent)]

    made = field_pieces(planes - 2, planes, field)
    if pairs > 1:
        others = field_pieces(0, planes - 2, made[0][0])
        made = [first + last for first, last in zip(others, made)]
    parts = [made[0]]
    for j in range(1, extent):
        parts.append([to_chan(value, j) for value in made[j]])
    (pack,) = call(
        pack_kernel,
        [jax.ShapeDtypeStruct((14, size, 4 * channels), BF16)],
        [made[0][0], jnp.transpose(first_weight, (1, 0, 2)), jnp.transpose(second_weight, (1, 0, 2))],
        loose=1,
    )
    packs = [pack] + [to_chan(pack, j) for j in range(1, extent)]
    whole = size % 16 == 0
    own_before, own_after = [], []
    if whole:
        own_before, own_after = [to_next(parts[0][-1])], [to_prev(parts[0][0])]
    grad_piece = jax.ShapeDtypeStruct((share + 4, 2, channels, depth), BF16)
    grads = call(
        functools.partial(grad_kernel, extent, 2),
        [grad_piece] * pairs,
        [pack, out_grad],
        [pltpu.VMEM((channels * planes * rows, depth), F32)],
        moved=out_grad.size * 4,
        loose=1,
    )
    matrix = jax.ShapeDtypeStruct((6 * channels, 12 * channels), BF16)
    half = jax.ShapeDtypeStruct((6 * channels, 6 * channels), BF16)
    first_wide, second_wide, first_back, second_back, from_above, from_below = call(
        functools.partial(matrix_kernel, extent),
        [matrix] * 4 + [half] * 2,
        packs,
        moved=matrix.size * 8,
    )
    if whole and extent > 1 and pairs > 1:
        parts[1][-1] = relayed(parts[1][-1], pack)
        parts[1][0] = relayed(relayed(parts[1][0], grads[0], *packs[1:]), own_after[0])
    by_pair = [[parts[j][p] for j in range(extent)] for p in range(pairs)]
    groups = extent
    if not whole:
        by_pair = [[jnp.concatenate(pieces, axis=2)] for pieces in by_pair]
        groups = 1
    before = own_before + [to_next(piece) for piece in by_pair[-1][len(own_before) :]]
    after = own_after + [to_prev(piece) for piece in by_pair[0][len(own_after) :]]
    fields = [before] + by_pair + [after]

    def many(count, rows_each):
        return [jax.ShapeDtypeStruct((rows_each, 2, channels, depth), BF16)] * count

    def flat(lists):
        return [piece for pieces in lists for piece in pieces]

    work = 27 * 2 * channels * channels * depth * 2
    space = 4 * channels * depth * share

    made = call(
        functools.partial(forward_kernel, groups, pairs, 0),
        many(2 * pairs, share + 6) + many(pairs - 1, share + 4),
        flat(fields[: pairs + 1]) + list(grads[: pairs - 1]) + [first_wide, second_wide],
        flops=work * (2 * pairs - 1) * share,
        moved=space * 4 * pairs,
    )
    hiddens, slopes, deltas = made[:pairs], made[pairs : 2 * pairs], made[2 * pairs :]
    made = call(
        functools.partial(forward_kernel, groups, 1, 1),
        many(2, share + 6) + many(1, share + 4),
        flat(fields[pairs:]) + [hiddens[-1], grads[-1], first_wide, second_wide],
        flops=work * 2 * share,
        moved=space * 6,
    )
    hiddens = list(hiddens) + [made[0]]
    slopes = list(slopes) + [made[1]]
    deltas = list(deltas) + [made[2]]
    delta_after = to_prev(deltas[0])
    delta_before = to_next(deltas[-1])

    raw = jax.ShapeDtypeStruct((extent, 7, size, 4 * channels), F32)
    portion = jax.ShapeDtypeStruct(raw.shape[1:], F32)
    total = pltpu.VMEM((12 * channels, 8 * channels), F32)

    def room(rows_each):
        return pltpu.VMEM((rows_each, 2, channels, depth), BF16)

    made = call(
        functools.partial(gradient_kernel, share, groups, extent, pairs),
        [raw] * 2 + many(pairs - 1, share + 2),
        hiddens + deltas + [second_back, from_above, from_below] + slopes + flat(fields),
        [room(share + 2), room(share + 2), total, total],
    )
    keep, send, inner = made[0], made[1], list(made[2:])
    def exchanged(made):
        pieces = [made[0]] + [None] * (extent - 1)
        for j in range(1, extent):
            pieces[extent - j] = to_chan(made[j], extent - j)
        return pieces

    def stepped(value, stride, shift=0):
        if shift % extent == 0:
            return lax.ppermute(value, "slab", [(i, i ^ stride) for i in range(slabs)])
        pairs_of = []
        for i in range(slabs):
            for k in range(extent):
                there = (i ^ stride) * extent + (k + shift) % extent
                pairs_of.append((i * extent + k, there))
        return lax.ppermute(value, ("slab", "chan"), pairs_of)

    (tail,) = call(
        tail_kernel,
        many(1, share + 2),
        [keep, second_back, deltas[-1], delta_after, slopes[-1]],
        flops=work * share,
        moved=space * 2,
        loose=1,
    )
    plain = slabs & (slabs - 1) == 0 and slabs >= 4
    if plain:
        kept = call(
            split_kernel, [portion] * extent, [tail, keep, stepped(send, 1)], loose=1
        )
        shares = [kept[0]] + [to_chan(kept[j], extent - j) for j in range(1, extent)]
        shares += [stepped(kept[j], 2, extent - j) for j in range(extent)]
        after = kept[0]
    else:
        after = keep
    made = call(
        functools.partial(field_kernel_back, pairs - 1, extent),
        [jax.ShapeDtypeStruct((share, planes, size, depth), BF16)] * extent,
        [after, second_back, first_back, delta_before, deltas[0], slopes[0]] + inner + [tail],
        [room(share + 2)],
        flops=work * (pairs + 2) * share,
        moved=space * 6,
        loose=1,
    )
    if plain:
        ahead = list(made[:1])
        (mine,) = call(
            functools.partial(add_kernel, len(ahead)), [portion], ahead + shares, loose=len(ahead)
        )
        made = list(made[:1]) + [relayed(value, mine) for value in made[1:]]
    pieces = exchanged(made)
    if plain:
        stride = 4
        while stride < slabs:
            got = [mine, stepped(mine, stride)]
            (mine,) = call(functools.partial(add_kernel, 0), [portion], got)
            stride *= 2
        other = stepped(mine, 1)
    else:
        mine, other = keep[0], send[0]
        for j in range(1, extent):
            mine, other = mine + to_chan(keep[j], extent - j), other + to_chan(send[j], extent - j)
        even = lax.rem(lax.axis_index("slab"), 2) == 0
        mine, other = jnp.where(even, mine, other), jnp.where(even, other, mine)
        mine, other = lax.psum((mine, other), "slab")
        mine, other = jnp.where(even, mine, other), jnp.where(even, other, mine)
    result = jax.ShapeDtypeStruct(by_tap, F32)
    input_grad, first_grad, second_grad = call(
        functools.partial(merge_kernel, extent, factor),
        [jax.ShapeDtypeStruct(field.shape, BF16), result, result],
        [mine] + pieces,
        [
            pltpu.VMEM((rows * planes * size, depth), F32),
            pltpu.VMEM(field.shape, BF16),
            pltpu.VMEM(by_tap, F32),
            pltpu.SemaphoreType.DMA((4 if size % 4 == 0 else 1,)),
            pltpu.SemaphoreType.DMA((1,)),
        ],
        moved=4 * field.size,
        left=(0, 1, 2),
    )
    first_grad, second_grad = call(
        functools.partial(finish_kernel, factor),
        [result, result],
        [first_grad, second_grad, other],
        [pltpu.VMEM(by_tap, F32), pltpu.SemaphoreType.DMA((1,))],
        loose=2,
        same={0: 0, 1: 1},
    )
    first_grad, second_grad = (jnp.transpose(g, (1, 0, 2)) for g in (first_grad, second_grad))
    return input_grad, first_grad, second_grad


def solution(mesh):
    placed = (
        P("chan", "slab", None, None),
        P(None, "slab", None, None),
        P("chan", None, None),
        P("chan", None, None),
    )
    return jax.shard_map(
        body,
        mesh=mesh,
        in_specs=placed,
        out_specs=(P("chan", "slab", None, None), P("chan", None, None), P("chan", None, None)),
        check_vma=False,
    )
```

```python
import functools
import math

import jax
import jax.numpy as jnp
from jax import lax
from jax.experimental import pallas as pl
from jax.experimental.pallas import tpu as pltpu
from jax.sharding import PartitionSpec as P

F32 = jnp.float32
BF16 = jnp.bfloat16
LIMIT = 16 * 1024 * 1024


def call(kernel, outs, args, scratch=(), flops=0, moved=0, loose=0, same=None, left=()):
    whole = pl.BlockSpec(memory_space=pltpu.VMEM)
    still = pl.BlockSpec(memory_space=pl.ANY)
    return pl.pallas_call(
        kernel,
        out_shape=outs,
        in_specs=[still] * loose + [whole] * (len(args) - loose),
        out_specs=[
            still if k in left or k in (same or {}).values() else whole for k in range(len(outs))
        ],
        input_output_aliases=same or {},
        scratch_shapes=list(scratch),
        compiler_params=pltpu.CompilerParams(vmem_limit_bytes=LIMIT),
        cost_estimate=pl.CostEstimate(flops=flops, bytes_accessed=moved, transcendentals=0),
    )(*args)


def in_blocks(count, body):
    block = max(k for k in range(1, 17) if count % k == 0)

    def several(r, _):
        for k in range(block):
            body(r * block + k)
        return 0

    lax.fori_loop(0, count // block, several, 0)
    for k in range(count // block * block, count):
        body(k)


def widened(x_ref, wide, low, high):
    count, _, rows = x_ref.shape[:3]

    def widen(i):
        for x in range(low, high):
            start = pl.multiple_of((i * (high - low) + x - low) * rows, 8)
            wide[pl.ds(start, rows), :] = x_ref[i, x].astype(F32)

    in_blocks(count, widen)


def turn(wide, outs, shape, base, length):
    count, planes, rows = shape

    def one(f):
        y = lax.rem(base + f, rows)
        for x in range(planes):
            tile = wide[pl.ds(x * rows + y, count, stride=planes * rows), :]
            outs[x // 2][f, x % 2] = tile.astype(BF16)

    in_blocks(length, one)


def field_kernel(extent, margin, low, high, after, x_ref, *refs):
    del after
    outs, wide = refs[:-1], refs[-1]
    count, _, rows = x_ref.shape[:3]
    planes = high - low
    pairs = planes // 2
    share = rows // extent
    widened(x_ref, wide, low, high)
    me = lax.axis_index("chan")
    for s in range(extent):
        base = lax.rem(me + s, extent) * share - margin + rows
        turn(
            wide,
            outs[s * pairs : (s + 1) * pairs],
            (count, planes, rows),
            base,
            share + 2 * margin,
        )


def pack_kernel(after, first, second, packed):
    del after
    blank = jnp.zeros(first.shape[1:], F32)
    for h in range(packed.shape[0]):
        parts = []
        for ref in (first, second):
            for t in (2 * h, 2 * h + 1):
                parts.append(ref[t].astype(F32) if t < ref.shape[0] else blank)
        packed[h] = jnp.concatenate(parts, axis=1).astype(BF16)


def grad_kernel(extent, margin, after, x_ref, *refs):
    del after
    outs, wide = refs[:-1], refs[-1]
    count, planes, rows = x_ref.shape[:3]
    share = rows // extent
    widened(x_ref, wide, 0, planes)
    base = lax.axis_index("chan") * share - margin + rows
    turn(wide, outs, (count, planes, rows), base, share + 2 * margin)


def matrix_kernel(extent, *refs):
    packs, outs = refs[:extent], refs[extent:]
    me = lax.axis_index("chan")
    quarter = packs[0].shape[2] // 4
    taps = []
    turned = []
    for h in range(packs[0].shape[0]):
        tiles = [pack[h].astype(F32) for pack in packs]
        own = jnp.concatenate(tiles, axis=0)
        fixed = []
        for g in range(extent):
            place = lax.rem(me + extent - g, extent)
            tile = tiles[0]
            for j in range(1, extent):
                tile = jnp.where(place == j, tiles[j], tile)
            fixed.append(tile)
        both = jnp.concatenate(
            [own[:, : 2 * quarter], jnp.concatenate(fixed, axis=0)[:, 2 * quarter :]], axis=1
        )
        across = both.T
        for side in range(2):
            taps.append(
                [both[:, k * quarter : (k + 1) * quarter] for k in (side, side + 2)]
            )
            turned.append(
                [across[k * quarter : (k + 1) * quarter] for k in (side, side + 2)]
            )
    channels = quarter
    blank = jnp.zeros((channels, channels), F32)
    for k in range(2):
        for out, blocks, flip in ((outs[k], turned, False), (outs[2 + k], taps, True)):
            for e in range(3):
                for x in range(2):
                    chunks = []
                    for pair in range(2):
                        for b in range(3):
                            for side in range(2):
                                a = 2 * pair + side - x
                                t = 9 * a + 3 * b + e
                                inside = 0 <= a <= 2
                                t = 26 - t if flip else t
                                chunks.append(blocks[t][k] if inside else blank)
                    low = (2 * e + x) * channels
                    line = jnp.concatenate(chunks, axis=1).astype(BF16)
                    out[low : low + channels, :] = line
                    if k == 1 and flip:
                        half = line.shape[1] // 2
                        outs[4][low : low + channels, :] = line[:, :half]
                        outs[5][low : low + channels, :] = line[:, half:]


def stacked(refs, row, count):
    if len(refs) == 1:
        part = refs[0][pl.ds(row, count)]
        return part.reshape(-1, part.shape[-1])
    parts = [ref[row + b, x] for b in range(count) for x in range(2) for ref in refs]
    return jnp.concatenate(parts, axis=0)


def taps(weight, inputs, row):
    sides = []
    for pair in inputs:
        for q in range(2):
            parts = [stacked(refs, row + q, 3) for refs in pair]
            sides.append(jnp.concatenate(parts, axis=0) if len(parts) > 1 else parts[0])
    lifted = jnp.dot(weight, jnp.concatenate(sides, axis=1), preferred_element_type=F32)
    third = lifted.shape[0] // 3
    depth = sides[0].shape[1]
    sums = []
    for k in range(len(sides)):
        side = lifted[:, k * depth : (k + 1) * depth]
        sums.append(
            side[third : 2 * third]
            + pltpu.roll(side[:third], 1, 1)
            + pltpu.roll(side[2 * third :], depth - 1, 1)
        )
    return [sums[2 * p : 2 * p + 2] for p in range(len(inputs))]


def neighbours(pairs):
    return list(zip(pairs[:-1], pairs[1:]))


def silu_parts(v):
    sig = jax.nn.sigmoid(v)
    return sig, sig * (1.0 + v * (1.0 - sig))


def forward_kernel(groups, fresh, ready, *refs):
    refs = list(refs)
    fields = [[refs.pop(0) for _ in range(groups)] for _ in range(fresh + 1)]
    hiddens = [refs.pop(0) for _ in range(ready)]
    count = fresh + ready - 1
    grads = [refs.pop(0) for _ in range(count)]
    first, second = refs.pop(0), refs.pop(0)
    made = [refs.pop(0) for _ in range(fresh)]
    slopes = [refs.pop(0) for _ in range(fresh)]
    deltas = refs
    hiddens = hiddens + made

    def one(r):
        row = 2 * r
        for p, sums in enumerate(taps(first[...], neighbours(fields), row)):
            for q, v in enumerate(sums):
                sig, slope = silu_parts(v)
                shape = made[p].shape[1:]
                made[p][row + q] = (v * sig).astype(BF16).reshape(shape)
                slopes[p][row + q] = slope.astype(BF16).reshape(shape)

    in_blocks(made[0].shape[0] // 2, one)

    def two(r):
        row = 2 * r
        for p, sums in enumerate(taps(second[...], neighbours([[ref] for ref in hiddens]), row)):
            for q, v in enumerate(sums):
                shape = deltas[p].shape[1:]
                out_grad = grads[p][row + q].astype(F32)
                slope = silu_parts(v)[1].reshape(shape)
                deltas[p][row + q] = (out_grad * slope).astype(BF16)

    if count > 0:
        in_blocks(deltas[0].shape[0] // 2, two)


def planes_of(pairs):
    return [(refs, x) for refs in pairs for x in range(2)]


def weight_loop(total, pieces, first_row, deltas, delta_row, count):
    blocks = [k for k in range(1, 13) if count // 2 % k == 0 and k * len(deltas) <= 12]
    together = max(blocks, default=1)

    def product(r):
        left, right = [], []
        for k in range(together):
            row = 2 * (r * together + k)
            for x, ((delta,), place) in enumerate(deltas):
                rows = []
                for q in range(2):
                    wide = delta[delta_row + row + q, place]
                    depth = wide.shape[1]
                    rows += [pltpu.roll(wide, depth - 1, 1), wide, pltpu.roll(wide, 1, 1)]
                right.append(jnp.concatenate(rows, axis=0))
                rows = []
                for refs, side in pieces[x : x + 3]:
                    for b in range(4):
                        for ref in refs:
                            rows.append(ref[first_row + row + b, side])
                left.append(jnp.concatenate(rows, axis=0))
        return lax.dot_general(
            jnp.concatenate(left, axis=1),
            jnp.concatenate(right, axis=1),
            (((1,), (1,)), ((), ())),
            preferred_element_type=F32,
        )

    value = total[...]
    for r in range(count // 2 // together):
        value = value + product(r)
    total[...] = value


def weight_fold(total, size):
    lanes = total.shape[1] // 2
    channels = total.shape[0] // 12
    upper, lower = total[:, :lanes], total[:, lanes:]
    groups = []
    for g in range(channels // size):
        taps_of = []
        for a in range(3):
            for b in range(3):
                start = (4 * a + b) * channels + g * size
                part = (
                    upper[start : start + size]
                    + lower[start + channels : start + channels + size]
                )
                taps_of += [part[:, e * channels : (e + 1) * channels] for e in range(3)]
        blank = jnp.zeros((size, channels), F32)
        taps_of.append(blank)
        groups.append([jnp.concatenate(taps_of[4 * h : 4 * h + 4], axis=1) for h in range(7)])
    return groups


def first_deltas(weight, inputs, slopes, firsts):
    def one(r):
        row = 2 * r
        for p, sums in enumerate(taps(weight[...], inputs, row)):
            for q, v in enumerate(sums):
                shape = firsts[p].shape[1:]
                slope = slopes[p][row + 2 + q].astype(F32)
                firsts[p][row + q] = (v.reshape(shape) * slope).astype(BF16)

    in_blocks(firsts[0].shape[0] // 2, one)


def gradient_kernel(share, groups, extent, pairs, *refs):
    refs = list(refs)
    hiddens = [[refs.pop(0)] for _ in range(pairs + 1)]
    deltas = [[refs.pop(0)] for _ in range(pairs)]
    weight, from_above, from_below = [refs.pop(0) for _ in range(3)]
    slopes = [refs.pop(0) for _ in range(pairs + 1)]
    fields = [[refs.pop(0) for _ in range(groups)] for _ in range(pairs + 2)]
    keep, send = refs.pop(0), refs.pop(0)
    inner = [refs.pop(0) for _ in range(pairs - 1)]
    head, tail, second_total, first_total = refs
    second_total[...] = jnp.zeros_like(second_total)
    first_total[...] = jnp.zeros_like(first_total)
    weight_loop(second_total, planes_of(hiddens), 2, planes_of(deltas), 2, share)
    firsts = [head] + inner + [tail]
    first_deltas(from_below, [(deltas[0],)], slopes[:1], [head])
    if inner:
        first_deltas(weight, neighbours(deltas), slopes[1:-1], inner)
    first_deltas(from_above, [(deltas[-1],)], slopes[-1:], [tail])
    parts = planes_of([[first] for first in firsts])
    weight_loop(first_total, planes_of(fields), 3, parts, 1, share)
    halves, size = keep.shape[1:3]
    me = lax.axis_index("chan")
    of_first = weight_fold(first_total, size)
    of_second = weight_fold(second_total, size)

    def place(ours, theirs):
        for g in range(extent):
            there = lax.rem(me + extent - g, extent)
            for h in range(halves):
                ours[g, h] = of_first[g][h]
                theirs[there, h] = of_second[g][h]

    odd = lax.rem(lax.axis_index("slab"), 2)

    @pl.when(odd == 0)
    def _():
        place(keep, send)

    @pl.when(odd == 1)
    def _():
        place(send, keep)


def tail_kernel(after, weight, above, below, slope, first):
    del after
    first_deltas(weight, [([above], [below])], [slope], [first])


def field_kernel_back(inner, groups, after, *refs):
    del after
    refs = list(refs)
    back, weight = refs.pop(0), refs.pop(0)
    above, below = [[refs.pop(0)] for _ in range(2)]
    slope = refs.pop(0)
    later = [refs.pop(0) for _ in range(inner + 1)]
    outs, head = refs[:groups], refs[groups]
    first_deltas(back, [(above, below)], [slope], [head])
    firsts = [head] + later

    def one(r):
        row = 2 * r
        size = outs[0].shape[2]
        channels = len(outs) * size
        for p, sums in enumerate(taps(weight[...], neighbours([[ref] for ref in firsts]), row)):
            for q, v in enumerate(sums):
                for x in range(2):
                    for j, out in enumerate(outs):
                        low = x * channels + j * size
                        out[row + q, 2 * p + x] = v[low : low + size].astype(BF16)

    in_blocks(outs[0].shape[0] // 2, one)


def split_kernel(after, one, two, *outs):
    del after
    for g, out in enumerate(outs):
        out[...] = one[g] + two[g]


def add_kernel(ahead, *refs):
    values = [ref[...] for ref in refs[ahead:-1]]
    while len(values) > 1:
        values = [sum(values[k + 1 : k + 2], values[k]) for k in range(0, len(values), 2)]
    refs[-1][...] = values[0]


def relay_kernel(*refs):
    pass


def finish_kernel(factor, after, mine, other, first, second):
    del after
    channels = first.shape[2]

    def place(ours, theirs):
        for result, sums in ((ours, mine), (theirs, other)):
            for t in range(27):
                low = t % 4 * channels
                result[t] = sums[t // 4, :, low : low + channels] * factor

    odd = lax.rem(lax.axis_index("slab"), 2)

    @pl.when(odd == 0)
    def _():
        place(first, second)

    @pl.when(odd == 1)
    def _():
        place(second, first)


def merge_kernel(extent, *refs):
    pieces, (token, out, wide, held, done) = refs[:-5], refs[-5:]
    token[...] = jnp.zeros_like(token)
    size, planes, rows = out.shape[:3]
    share = rows // extent
    me = lax.axis_index("chan")
    for j in range(extent):
        base = lax.rem(me + extent - j, extent) * share

        def widen(f, mine=pieces[j::extent], base=base):
            x = 0
            for piece in mine:
                for k in range(piece.shape[1]):
                    start = ((base + f) * planes + x) * size
                    start = pl.multiple_of(start, 8) if size % 8 == 0 else start
                    wide[pl.ds(start, size), :] = piece[f, k].astype(F32)
                    x += 1

        in_blocks(share, widen)

    cuts = done.shape[0]
    copies = []
    for c in range(cuts):
        part = pl.ds(c * size // cuts, size // cuts)
        for i in range(c * size // cuts, (c + 1) * size // cuts):
            for x in range(planes):
                tile = wide[pl.ds(x * size + i, rows, stride=planes * size), :]
                held[i, x] = tile.astype(BF16)
        copies.append(pltpu.make_async_copy(held.at[part], out.at[part], done.at[c]))
        copies[-1].start()
    for copy in copies:
        copy.wait()


def body(field, out_grad, first_weight, second_weight):
    extent = lax.axis_size("chan")
    slabs = lax.axis_size("slab")
    me = lax.axis_index("chan")
    size, planes, rows, depth = field.shape
    channels = size * extent
    pairs = planes // 2
    share = rows // extent
    factor = 1.0 / math.sqrt(planes * slabs * rows * depth)

    def to_chan(value, shift):
        return lax.ppermute(value, "chan", [(i, (i + shift) % extent) for i in range(extent)])

    def to_next(value):
        return lax.ppermute(value, "slab", [(i, (i + 1) % slabs) for i in range(slabs)])

    def to_prev(value):
        return lax.ppermute(value, "slab", [((i + 1) % slabs, i) for i in range(slabs)])

    def relayed(value, *others):
        shape = jax.ShapeDtypeStruct(value.shape, value.dtype)
        early = [value, *others]
        return call(relay_kernel, [shape], early, loose=len(early), same={0: 0})[0]

    piece = jax.ShapeDtypeStruct((share + 8, 2, size, depth), BF16)
    by_tap = (27, size, channels)
    def field_pieces(low, high, after):
        count = (high - low) // 2
        made = call(
            functools.partial(field_kernel, extent, 4, low, high),
            [piece] * (extent * count),
            [after, field],
            [pltpu.VMEM((size * (high - low) * rows, depth), F32)],
            moved=field.size * 3,
            loose=1,
        )
        return [list(made[j * count : (j + 1) * count]) for j in range(extent)]

    made = field_pieces(planes - 2, planes, field)
    if pairs > 1:
        others = field_pieces(0, planes - 2, made[0][0])
        made = [first + last for first, last in zip(others, made)]
    parts = [made[0]]
    for j in range(1, extent):
        parts.append([to_chan(value, j) for value in made[j]])
    (pack,) = call(
        pack_kernel,
        [jax.ShapeDtypeStruct((14, size, 4 * channels), BF16)],
        [made[0][0], jnp.transpose(first_weight, (1, 0, 2)), jnp.transpose(second_weight, (1, 0, 2))],
        loose=1,
    )
    packs = [pack] + [to_chan(pack, j) for j in range(1, extent)]
    whole = size % 16 == 0
    own_before, own_after = [], []
    if whole:
        own_before, own_after = [to_next(parts[0][-1])], [to_prev(parts[0][0])]
    grad_piece = jax.ShapeDtypeStruct((share + 4, 2, channels, depth), BF16)
    grads = call(
        functools.partial(grad_kernel, extent, 2),
        [grad_piece] * pairs,
        [pack, out_grad],
        [pltpu.VMEM((channels * planes * rows, depth), F32)],
        moved=out_grad.size * 4,
        loose=1,
    )
    matrix = jax.ShapeDtypeStruct((6 * channels, 12 * channels), BF16)
    half = jax.ShapeDtypeStruct((6 * channels, 6 * channels), BF16)
    first_wide, second_wide, first_back, second_back, from_above, from_below = call(
        functools.partial(matrix_kernel, extent),
        [matrix] * 4 + [half] * 2,
        packs,
        moved=matrix.size * 8,
    )
    if whole and extent > 1 and pairs > 1:
        parts[1][-1] = relayed(parts[1][-1], pack)
        parts[1][0] = relayed(relayed(parts[1][0], grads[0], *packs[1:]), own_after[0])
    by_pair = [[parts[j][p] for j in range(extent)] for p in range(pairs)]
    groups = extent
    if not whole:
        by_pair = [[jnp.concatenate(pieces, axis=2)] for pieces in by_pair]
        groups = 1
    before = own_before + [to_next(piece) for piece in by_pair[-1][len(own_before) :]]
    after = own_after + [to_prev(piece) for piece in by_pair[0][len(own_after) :]]
    fields = [before] + by_pair + [after]

    def many(count, rows_each):
        return [jax.ShapeDtypeStruct((rows_each, 2, channels, depth), BF16)] * count

    def flat(lists):
        return [piece for pieces in lists for piece in pieces]

    work = 27 * 2 * channels * channels * depth * 2
    space = 4 * channels * depth * share

    made = call(
        functools.partial(forward_kernel, groups, pairs, 0),
        many(2 * pairs, share + 6) + many(pairs - 1, share + 4),
        flat(fields[: pairs + 1]) + list(grads[: pairs - 1]) + [first_wide, second_wide],
        flops=work * (2 * pairs - 1) * share,
        moved=space * 4 * pairs,
    )
    hiddens, slopes, deltas = made[:pairs], made[pairs : 2 * pairs], made[2 * pairs :]
    made = call(
        functools.partial(forward_kernel, groups, 1, 1),
        many(2, share + 6) + many(1, share + 4),
        flat(fields[pairs:]) + [hiddens[-1], grads[-1], first_wide, second_wide],
        flops=work * 2 * share,
        moved=space * 6,
    )
    hiddens = list(hiddens) + [made[0]]
    slopes = list(slopes) + [made[1]]
    deltas = list(deltas) + [made[2]]
    delta_after = to_prev(deltas[0])
    delta_before = to_next(deltas[-1])

    raw = jax.ShapeDtypeStruct((extent, 7, size, 4 * channels), F32)
    portion = jax.ShapeDtypeStruct(raw.shape[1:], F32)
    total = pltpu.VMEM((12 * channels, 6 * channels), F32)

    def room(rows_each):
        return pltpu.VMEM((rows_each, 2, channels, depth), BF16)

    made = call(
        functools.partial(gradient_kernel, share, groups, extent, pairs),
        [raw] * 2 + many(pairs - 1, share + 2),
        hiddens + deltas + [second_back, from_above, from_below] + slopes + flat(fields),
        [room(share + 2), room(share + 2), total, total],
    )
    keep, send, inner = made[0], made[1], list(made[2:])
    def exchanged(made):
        pieces = [made[0]] + [None] * (extent - 1)
        for j in range(1, extent):
            pieces[extent - j] = to_chan(made[j], extent - j)
        return pieces

    def stepped(value, stride, shift=0):
        if shift % extent == 0:
            return lax.ppermute(value, "slab", [(i, i ^ stride) for i in range(slabs)])
        pairs_of = []
        for i in range(slabs):
            for k in range(extent):
                there = (i ^ stride) * extent + (k + shift) % extent
                pairs_of.append((i * extent + k, there))
        return lax.ppermute(value, ("slab", "chan"), pairs_of)

    (tail,) = call(
        tail_kernel,
        many(1, share + 2),
        [keep, second_back, deltas[-1], delta_after, slopes[-1]],
        flops=work * share,
        moved=space * 2,
        loose=1,
    )
    plain = slabs & (slabs - 1) == 0 and slabs >= 4
    if plain:
        kept = call(
            split_kernel, [portion] * extent, [tail, keep, stepped(send, 1)], loose=1
        )
        shares = [kept[0]] + [to_chan(kept[j], extent - j) for j in range(1, extent)]
        shares += [stepped(kept[j], 2, extent - j) for j in range(extent)]
        after = kept[0]
    else:
        after = keep
    made = call(
        functools.partial(field_kernel_back, pairs - 1, extent),
        [jax.ShapeDtypeStruct((share, planes, size, depth), BF16)] * extent,
        [after, second_back, first_back, delta_before, deltas[0], slopes[0]] + inner + [tail],
        [room(share + 2)],
        flops=work * (pairs + 2) * share,
        moved=space * 6,
        loose=1,
    )
    if plain:
        ahead = list(made[:1])
        (mine,) = call(
            functools.partial(add_kernel, len(ahead)), [portion], ahead + shares, loose=len(ahead)
        )
        made = list(made[:1]) + [relayed(value, mine) for value in made[1:]]
    pieces = exchanged(made)
    if plain:
        stride = 4
        while stride < slabs:
            got = [mine, stepped(mine, stride)]
            (mine,) = call(functools.partial(add_kernel, 0), [portion], got)
            stride *= 2
        other = stepped(mine, 1)
    else:
        mine, other = keep[0], send[0]
        for j in range(1, extent):
            mine, other = mine + to_chan(keep[j], extent - j), other + to_chan(send[j], extent - j)
        even = lax.rem(lax.axis_index("slab"), 2) == 0
        mine, other = jnp.where(even, mine, other), jnp.where(even, other, mine)
        mine, other = lax.psum((mine, other), "slab")
        mine, other = jnp.where(even, mine, other), jnp.where(even, other, mine)
    token, input_grad = call(
        functools.partial(merge_kernel, extent),
        [jax.ShapeDtypeStruct((8, 128), F32), jax.ShapeDtypeStruct(field.shape, BF16)],
        pieces,
        [
            pltpu.VMEM((rows * planes * size, depth), F32),
            pltpu.VMEM(field.shape, BF16),
            pltpu.SemaphoreType.DMA((4 if size % 4 == 0 else 1,)),
        ],
        moved=4 * field.size,
        left=(1,),
    )
    first_grad, second_grad = call(
        functools.partial(finish_kernel, factor),
        [jax.ShapeDtypeStruct(by_tap, F32)] * 2,
        [token, mine, other],
        loose=1,
    )
    first_grad, second_grad = (jnp.transpose(g, (1, 0, 2)) for g in (first_grad, second_grad))
    return input_grad, first_grad, second_grad


def solution(mesh):
    placed = (
        P("chan", "slab", None, None),
        P(None, "slab", None, None),
        P("chan", None, None),
        P("chan", None, None),
    )
    return jax.shard_map(
        body,
        mesh=mesh,
        in_specs=placed,
        out_specs=(P("chan", "slab", None, None), P("chan", None, None), P("chan", None, None)),
        check_vma=False,
    )
```
